32 devices in a mesh: seq: 8 (over y, x, core), head: 4 (over z).
Axes of the slice: x: 2, y: 2, z: 4, core: 2. Of those that a mesh axis runs over, the one named last changes fastest.
Arguments:
- tokens: bfloat16 [6144, 2048], P('seq', 'head'), may hold values from -6 to 6
- cotangent: bfloat16 [6144, 2048], P('seq', 'head'), may hold values from -6 to 6
- lengths: int32 [3, 4], replicated, may hold values from 1 to 2048, as said below
- deal_order: int32 [6144], P('seq'), may hold values from 0 to 255, as said below
- norm_gain: float32 [2048], replicated, may hold values from 0.5 to 1.5
- proj_gate: bfloat16 [2048, 4096], P('seq', 'head'), may hold values from -0.125 to 0.125
- proj_inner: bfloat16 [2048, 4096], P('seq', 'head'), may hold values from -0.125 to 0.125
- proj_state: bfloat16 [2048, 256], P('seq'), may hold values from -0.125 to 0.125
- proj_step: bfloat16 [2048, 64], P('seq', 'head'), may hold values from -0.125 to 0.125
- conv_inner: float32 [4, 4096], P(None, 'head'), may hold values from -3 to 3
- conv_inner_bias: float32 [4096], P('head'), may hold values from -3 to 3
- conv_state: float32 [4, 256], replicated, may hold values from -3 to 3
- conv_state_bias: float32 [256], replicated, may hold values from -3 to 3
- step_bias: float32 [64], P('head'), may hold values from -12 to -3
- decay_log: float32 [64], P('head'), may hold values from -2 to 1
- skip_gain: float32 [64], P('head'), may hold values from 0.5 to 1.5
- inner_gain: float32 [4096], P('head'), may hold values from 0.5 to 1.5
- proj_out: bfloat16 [4096, 2048], P('head', 'seq'), may hold values from -0.09375 to 0.09375
Outputs:
- output: bfloat16 [6144, 2048], P('seq', 'head')
- grad_input: bfloat16 [6144, 2048], P('seq', 'head')
- grad_norm_gain: float32 [2048], P('head')
- grad_proj_gate: float32 [2048, 4096], P('seq', 'head')
- grad_proj_inner: float32 [2048, 4096], P('seq', 'head')
- grad_proj_state: float32 [2048, 256], P('head')
- grad_proj_step: float32 [2048, 64], P('seq', 'head')
- grad_conv_inner: float32 [4, 4096], P(None, 'head')
- grad_conv_inner_bias: float32 [4096], P('head')
- grad_conv_state: float32 [4, 256], P(None, 'head')
- grad_conv_state_bias: float32 [256], P('head')
- grad_step_bias: float32 [64], P('head')
- grad_decay_log: float32 [64], P('head')
- grad_skip_gain: float32 [64], P('head')
- grad_inner_gain: float32 [4096], P('head')
- grad_proj_out: float32 [4096, 2048], P('head', 'seq')
The draws below stay inside these ranges and needn't reach their ends.
Inputs may be any that keep to these rules, and one draw needn't show every extreme that they name: Each row of lengths sums to 2048; its entries are positive. `deal_order`: every aligned block of 256 entries is a permutation of 0 to 255.
All inputs are finite; a program needn't handle non-finite values.
Results may differ from the reference program's by a relative error of at most 0.015.
Values may be sent and summed in bfloat16 or wider, within the bound.
No kernel may reach another device: no remote copies, remote signals or barrier semaphores. Data moves between devices by JAX's collectives and lax.ppermute only.
A program may use at most 256 MiB of HBM per device.

```python
import math
import jax
import jax.numpy as jnp
from jax import lax

D = 2048
INNER = 4096
HEADS = 64
HEAD_DIM = 64
STATE = 128
CONV = 4
BLOCK = 256
MICRO = 3
SEQ_MB = 4
TOK_DEV = 256
PIECE = 32
TOK_MB = 2048
TOKENS = 6144
SEQ_MIN = 256
N_SEQ = 8


def draw_lengths(key, part):
    key = jax.random.fold_in(key, 11)
    subkeys = jax.random.split(key, 3)
    leftover = TOK_MB - SEQ_MB * SEQ_MIN
    cut_points = jnp.sort(jax.random.randint(subkeys[0], (MICRO, SEQ_MB - 1), 0, leftover + 1), axis=1)
    boundary = jnp.concatenate([jnp.zeros((MICRO, 1), jnp.int32), cut_points.astype(jnp.int32), jnp.full((MICRO, 1), leftover, jnp.int32)], axis=1)
    even_rows = SEQ_MIN + boundary[:, 1:] - boundary[:, :-1]
    short_lengths = jax.random.randint(subkeys[1], (SEQ_MB - 1,), 1, TOK_DEV // (2 * (SEQ_MB - 1)) + 1)
    longest = TOK_MB - jnp.sum(short_lengths)
    spanning = jnp.concatenate([short_lengths[:1], jnp.reshape(longest, (1,)), short_lengths[1:]])
    chosen = jax.random.randint(subkeys[2], (), 0, MICRO)
    chosen_row = (jnp.arange(MICRO) == chosen)[:, None]
    return jnp.where(chosen_row, spanning[None, :], even_rows).astype(jnp.int32)


def draw_deal_order(key, part):
    key = jax.random.fold_in(key, 23)
    subkeys = jax.random.split(key, TOKENS // TOK_DEV)
    shuffled = jax.vmap(lambda subkey: jax.random.permutation(subkey, TOK_DEV))(subkeys)
    return shuffled.reshape(TOKENS).astype(jnp.int32)


def decay_plan(key, slow_low, slow_high, fast_share):
    level_draw = jax.random.uniform(jax.random.fold_in(key, 1), (HEADS,), jnp.float32)
    toss_up = jax.random.uniform(jax.random.fold_in(key, 2), (HEADS,), jnp.float32)
    slow_rate = slow_low + (slow_high - slow_low) * level_draw
    fast_rate = math.log(0.02) + (math.log(0.05) - math.log(0.02)) * level_draw
    log_rate = jnp.where(toss_up < fast_share, fast_rate, slow_rate)
    span_rows = jnp.minimum(jnp.exp(-log_rate), TOK_MB * 1.0)
    return (log_rate, span_rows)


def draw_decay_log(key, part):
    log_rate, span_rows = decay_plan(key, math.log(0.3 / TOK_MB), math.log(0.05), 0.25)
    return (math.log(2.0) + log_rate + jnp.log(span_rows)).astype(jnp.float32)


def draw_step_bias(key, part):
    log_rate, span_rows = decay_plan(key, math.log(0.3 / TOK_MB), math.log(0.05), 0.25)
    return jnp.log(jnp.expm1(0.5 / span_rows)).astype(jnp.float32)


def block_levels(rng, dims, shards, low, largest):
    def one(dim, blocks):
        draws = jax.random.uniform(jax.random.fold_in(jax.random.fold_in(rng, 6), dim), (blocks,), jnp.float32, low / len(shards), largest / len(shards))
        return jnp.repeat(jnp.exp(draws), dims[dim] // blocks).reshape((-1,) + (1,) * (len(dims) - dim - 1))

    gain = one(*shards[0])
    for cut in shards[1:]:
        gain = gain * one(*cut)
    return gain


def scatter_about(stream_key, dims, spread, bound, cuts=(), kind=jnp.bfloat16):
    loudness = block_levels(stream_key, dims, cuts, -0.22, 0.18) if cuts else 1.0
    values = jax.random.normal(stream_key, dims, jnp.float32) * spread * loudness
    return jnp.minimum(jnp.maximum(values, -bound), bound).astype(kind)


def setup_inputs(seed: int = 0) -> dict:
    key_list = jax.random.split(jax.random.key(seed), 19)
    tokens = scatter_about(key_list[0], (TOKENS, D), 1.0, 6.0, ((0, 8), (1, 4)))
    cotangent = scatter_about(key_list[1], (TOKENS, D), 1.0, 6.0, ((0, 8), (1, 4)))
    lengths = draw_lengths(jax.random.fold_in(key_list[18], 71), 0)
    deal_order = draw_deal_order(jax.random.fold_in(key_list[18], 71), 0)
    norm_gain = jnp.clip(1.0 + 0.1 * jax.random.normal(key_list[4], (D,), jnp.float32), 0.5, 1.5)
    proj_gate = scatter_about(key_list[5], (D, INNER), D ** -0.5, 0.125, ((0, 8), (1, 4)))
    proj_inner = scatter_about(key_list[6], (D, INNER), D ** -0.5, 0.125, ((0, 8), (1, 4)))
    proj_state = scatter_about(key_list[7], (D, 2 * STATE), D ** -0.5, 0.125, ((0, 8),))
    proj_step = scatter_about(key_list[8], (D, HEADS), D ** -0.5, 0.125, ((0, 8), (1, 4)))
    conv_inner = scatter_about(key_list[9], (CONV, INNER), CONV ** -0.5, 3.0, ((1, 4),), jnp.float32)
    conv_inner_bias = scatter_about(key_list[10], (INNER,), 0.5, 3.0, ((0, 4),), jnp.float32)
    conv_state = scatter_about(key_list[11], (CONV, 2 * STATE), CONV ** -0.5, 3.0, (), jnp.float32)
    conv_state_bias = scatter_about(key_list[12], (2 * STATE,), 0.5, 3.0, (), jnp.float32)
    step_bias = draw_step_bias(jax.random.fold_in(key_list[18], 71), 0)
    decay_log = draw_decay_log(jax.random.fold_in(key_list[18], 71), 0)
    skip_gain = jnp.clip(0.5 + 1.0 * jax.random.uniform(key_list[15], (HEADS,), jnp.float32) ** block_levels(key_list[15], (HEADS,), ((0, 4),), -0.2, 0.2), 0.5, 1.5)
    inner_gain = jnp.clip(1.0 + 0.1 * jax.random.normal(key_list[16], (INNER,), jnp.float32), 0.5, 1.5)
    proj_out = scatter_about(key_list[17], (INNER, D), INNER ** -0.5, 0.09375, ((0, 4), (1, 8)))
    return dict(tokens=tokens, cotangent=cotangent, lengths=lengths, deal_order=deal_order, norm_gain=norm_gain, proj_gate=proj_gate, proj_inner=proj_inner, proj_state=proj_state, proj_step=proj_step, conv_inner=conv_inner, conv_inner_bias=conv_inner_bias, conv_state=conv_state, conv_state_bias=conv_state_bias, step_bias=step_bias, decay_log=decay_log, skip_gain=skip_gain, inner_gain=inner_gain, proj_out=proj_out)


epsilon = 1e-05
highest = lax.Precision.HIGHEST

@jax.custom_vjp
def low(v):
    return lax.optimization_barrier(v.astype(jnp.bfloat16)).astype(jnp.float32)

@jax.custom_vjp
def low_back(v):
    return v

def low_keep(v):
    return (low(v), None)

def low_pass(kept, grad):
    return (grad,)

def back_keep(v):
    return (v, None)

def back_low(kept, grad):
    return (low(grad),)
low.defvjp(low_keep, low_pass)
low_back.defvjp(back_keep, back_low)

def matmul_hi(left, right):
    return jnp.dot(left, right, precision=highest, preferred_element_type=jnp.float32)

def row_segments(lengths_row, row_count):
    starts = jnp.cumsum(lengths_row) - lengths_row
    position = jnp.arange(row_count, dtype=jnp.int32)
    return (lax.optimization_barrier(jnp.sum((position[:, None] >= starts[None, :]).astype(jnp.int32), axis=1)) - 1).astype(jnp.int32)

def source_rows(deal_order):
    blocks = jnp.transpose(deal_order.reshape(N_SEQ, MICRO, N_SEQ, PIECE), (1, 2, 0, 3))
    sender = jnp.arange(N_SEQ, dtype=jnp.int32)[None, None, :, None]
    batch_index = jnp.arange(MICRO, dtype=jnp.int32)[:, None, None, None]
    return (sender * (MICRO * TOK_DEV) + batch_index * TOK_DEV + blocks).reshape(TOKENS).astype(jnp.int32)

def causal_conv(values, weight, offset_bias, segment):
    row_count = values.shape[0]
    taps_total = weight.shape[0]
    padded = jnp.concatenate([jnp.zeros((taps_total - 1, values.shape[1]), jnp.float32), values], axis=0)
    seg_pad = jnp.concatenate([jnp.full((taps_total - 1,), -1, jnp.int32), segment])
    result = jnp.zeros_like(values) + offset_bias[None, :]
    for tap_index in range(taps_total):
        same_seq = (seg_pad[tap_index:tap_index + row_count] == segment).astype(jnp.float32)
        result = result + weight[tap_index][None, :] * padded[tap_index:tap_index + row_count] * same_seq[:, None]
    return result

def state_space(heads_x, step_size, rate_scale, input_map, output_map, segment):
    blocks_total = heads_x.shape[0] // BLOCK
    previous = jnp.concatenate([jnp.full((1,), -1, jnp.int32), segment[:-1]])
    offsets = jnp.arange(BLOCK)
    causal = offsets[:, None] >= offsets[None, :]

    def advance(carry_state, pieces):
        part_x, part_step, part_in, part_out, part_seg, before = pieces
        cumulative = jnp.cumsum(part_step * rate_scale[None, :], axis=0)
        same_seq = ((part_seg[:, None] == part_seg[None, :]) & causal)[:, :, None]
        difference = cumulative[:, None, :] - cumulative[None, :, :]
        decay_mat = jnp.where(same_seq, jnp.exp(jnp.where(same_seq, difference, 0.0)), 0.0)
        scores = matmul_hi(part_out, part_in.T)
        inputs = part_step[:, :, None] * part_x
        inner_out = jnp.einsum('ijh,ij,jhp->ihp', decay_mat, scores, inputs, precision=highest)
        inflow = (part_seg == before).astype(jnp.float32)[:, None] * jnp.exp(cumulative)
        carried = inflow[:, :, None] * jnp.einsum('in,hpn->ihp', part_out, carry_state, precision=highest)
        kept_rows = (part_seg == part_seg[-1]).astype(jnp.float32)[:, None]
        fading = kept_rows * jnp.exp(cumulative[-1][None, :] - cumulative)
        through = (part_seg[-1] == before).astype(jnp.float32) * jnp.exp(cumulative[-1])
        fresh_state = jnp.einsum('jh,jhp,jn->hpn', fading, inputs, part_in, precision=highest)
        return (through[:, None, None] * carry_state + fresh_state, inner_out + carried)
    pieces = (heads_x.reshape(blocks_total, BLOCK, HEADS, HEAD_DIM), step_size.reshape(blocks_total, BLOCK, HEADS), input_map.reshape(blocks_total, BLOCK, STATE), output_map.reshape(blocks_total, BLOCK, STATE), segment.reshape(blocks_total, BLOCK), previous.reshape(blocks_total, BLOCK)[:, 0])
    initial = jnp.zeros((HEADS, HEAD_DIM, STATE), jnp.float32)
    final_state, result = lax.scan(jax.checkpoint(advance), initial, pieces)
    return result.reshape(blocks_total * BLOCK, HEADS, HEAD_DIM)

def block_forward(rows_all, norm_gain, proj_gate, proj_inner, proj_state, proj_step, conv_inner, conv_inner_bias, conv_state, conv_state_bias, step_bias, decay_log, skip_gain, inner_gain, proj_out, segments):
    conv_weight = jnp.concatenate([conv_inner, conv_state], axis=1)
    conv_offset = jnp.concatenate([conv_inner_bias, conv_state_bias])
    rate_scale = -jnp.exp(decay_log)

    def one_batch(rows_mb, segment):
        inv_rms = lax.rsqrt(lax.optimization_barrier(jnp.mean(rows_mb * rows_mb, axis=1, keepdims=True)) + epsilon)
        normed = low(rows_mb * inv_rms * norm_gain[None, :])
        gate_pre = low_back(matmul_hi(normed, proj_gate))
        inner_pre = low_back(matmul_hi(normed, proj_inner))
        state_pre = matmul_hi(normed, proj_state)
        step_pre = low_back(matmul_hi(normed, proj_step))
        conv_out = causal_conv(jnp.concatenate([inner_pre, state_pre], axis=1), conv_weight, conv_offset, segment)
        mixed_act = jax.nn.silu(conv_out)
        heads_x = mixed_act[:, :INNER].reshape(TOK_MB, HEADS, HEAD_DIM)
        input_map = mixed_act[:, INNER:INNER + STATE]
        output_map = mixed_act[:, INNER + STATE:]
        step_size = jax.nn.softplus(step_pre + step_bias[None, :])
        scanned = state_space(heads_x, step_size, rate_scale, input_map, output_map, segment)
        mixer_out = (scanned + skip_gain[None, :, None] * heads_x).reshape(TOK_MB, INNER)
        gated_y = mixer_out * jax.nn.silu(gate_pre)
        inner_inv = lax.rsqrt(lax.optimization_barrier(jnp.mean(gated_y * gated_y, axis=1, keepdims=True)) + epsilon)
        normed_y = low(gated_y * inner_inv * inner_gain[None, :])
        return rows_mb + matmul_hi(normed_y, proj_out)
    batches = rows_all.reshape(MICRO, TOK_MB, D)
    results = lax.map(lambda operands: jax.checkpoint(one_batch)(operands[0], operands[1]), (batches, segments))
    return results.reshape(TOKENS, D)

def reference(tokens, cotangent, lengths, deal_order, norm_gain, proj_gate, proj_inner, proj_state, proj_step, conv_inner, conv_inner_bias, conv_state, conv_state_bias, step_bias, decay_log, skip_gain, inner_gain, proj_out):
    source = source_rows(deal_order)
    rows_in = tokens[source].astype(jnp.float32)
    grad_rows = cotangent[source].astype(jnp.float32)
    segments = jax.vmap(lambda lengths_row: row_segments(lengths_row, TOK_MB))(lengths)
    params = tuple((value.astype(jnp.float32) for value in (norm_gain, proj_gate, proj_inner, proj_state, proj_step, conv_inner, conv_inner_bias, conv_state, conv_state_bias, step_bias, decay_log, skip_gain, inner_gain, proj_out)))

    def forward(rows_proc, param_set):
        return block_forward(rows_proc, *param_set, segments)
    result, pullback = jax.vjp(forward, rows_in, params)
    grad_in_rows, grads = pullback(grad_rows)
    output = jnp.zeros_like(tokens).at[source].set(result.astype(jnp.bfloat16))
    grad_input = jnp.zeros_like(tokens).at[source].set(grad_in_rows.astype(jnp.bfloat16))
    return (output, grad_input, grads[0], grads[1], grads[2], grads[3], grads[4], grads[5], grads[6], grads[7], grads[8], grads[9], grads[10], grads[11], grads[12], grads[13])
```

```python
import jax
import jax.numpy as jnp
from jax import lax
from jax.sharding import PartitionSpec as P

epsilon = 1e-05
highest = lax.Precision.HIGHEST
f32 = jnp.float32
bf16 = jnp.bfloat16


def swapped(value, axis, bit):
    return lax.ppermute(value, axis, [(i, i ^ bit) for i in range(lax.axis_size(axis))])


def axis_bits(axis):
    count = lax.axis_size(axis)
    return [1 << k for k in range(count.bit_length() - 1)]


def gather_relative(first, second):
    links = axis_bits("seq")[1:]
    grown = []
    for part, order in ((first, links), (second, links[::-1])):
        grown.append([part[None], [0], order])
    for step in range(len(links)):
        for item in grown:
            held, labels, order = item
            bit = order[step]
            item[0] = jnp.concatenate([held, swapped(held, "seq", bit)], axis=0)
            item[1] = labels + [label ^ bit for label in labels]
    (left, left_labels, _), (right, right_labels, _) = grown
    right = jnp.stack([right[right_labels.index(label)] for label in left_labels])
    own = jnp.concatenate([left, right], axis=2)
    other = swapped(own, "seq", 1)
    full = jnp.stack([own, other], axis=1)
    order = sorted(range(len(left_labels)), key=lambda at: left_labels[at])
    if order != list(range(len(order))):
        full = full[jnp.array(order)]
    return full.reshape((-1,) + own.shape[1:])


def scatter_relative(partial):
    count, rows, columns = partial.shape
    links = axis_bits("seq")[1:]
    pairs = partial.reshape(count // 2, 2, rows, columns)
    mine = added(pairs[:, 0], swapped(pairs[:, 1], "seq", 1))
    parts = []
    for piece, order in (
        (mine[:, :, : columns // 2], links[::-1]),
        (mine[:, :, columns // 2 :], links),
    ):
        parts.append([piece, [2 * at for at in range(count // 2)], order])
    for step in range(len(links)):
        for item in parts:
            held, labels, order = item
            bit = order[step]
            keep = [at for at, label in enumerate(labels) if not label & bit]
            give = [labels.index(labels[at] ^ bit) for at in keep]
            sent = jnp.concatenate([held[at : at + 1] for at in give], axis=0)
            kept = jnp.concatenate([held[at : at + 1] for at in keep], axis=0)
            got = swapped(sent, "seq", bit)
            last = step == len(links) - 1
            item[0] = kept.astype(f32) + got.astype(f32) if last else added(kept, got)
            item[1] = [labels[at] for at in keep]
    return jnp.concatenate([item[0][0] for item in parts], axis=1)


def added(left, right):
    return (left.astype(f32) + right.astype(f32)).astype(left.dtype)


def line_gather(own):
    size, here = lax.axis_size("head"), lax.axis_index("head")
    ups, downs = [], []
    up = down = own
    for step in range(1, size):
        up = lax.ppermute(up, "head", [(i, i + 1) for i in range(step - 1, size - 1)])
        down = lax.ppermute(down, "head", [(i, i - 1) for i in range(1, size - step + 1)])
        ups.append(up)
        downs.append(down)
    slots = [own]
    for step in range(1, size):
        slots.append(jnp.where(here >= step, ups[step - 1], downs[size - step - 1]))
    return slots


def line_scatter(block_of):
    size, here = lax.axis_size("head"), lax.axis_index("head")
    up = down = None
    for step in range(1, size):
        give_up = block_of(jnp.clip(here + size - step, 0, size - 1))
        give_down = block_of(jnp.clip(here - size + step, 0, size - 1))
        if up is not None:
            give_up, give_down = added(give_up, up), added(give_down, down)
        up = lax.ppermute(give_up, "head", [(i, i + 1) for i in range(step)])
        down = lax.ppermute(give_down, "head", [(i, i - 1) for i in range(size - step, size)])
    return block_of(here).astype(f32) + up.astype(f32) + down.astype(f32)


def head_sum(value):
    for bit in axis_bits("head"):
        value = value + swapped(value, "head", bit)
    return value


def seq_sum(value):
    for bit in axis_bits("seq"):
        value = value + swapped(value, "seq", bit)
    return value


def scan_before(decay, state, reverse):
    here = lax.axis_index("seq")
    m, h, p, n = state.shape
    total_decay, total = decay, state
    ahead = jnp.zeros_like(state)
    ahead_decay = jnp.ones_like(decay)
    bits = axis_bits("seq")
    for bit in bits:
        got = swapped(total.astype(bf16), "seq", bit).astype(f32)
        got_decay = swapped(total_decay, "seq", bit)
        later = ((here & bit) == 0) if reverse else ((here & bit) != 0)
        ahead = jnp.where(later, ahead_decay[..., None, None] * got + ahead, ahead)
        ahead_decay = jnp.where(later, ahead_decay * got_decay, ahead_decay)
        if bit != bits[-1]:
            total = jnp.where(
                later,
                total_decay[..., None, None] * got + total,
                got_decay[..., None, None] * total + got,
            )
            total_decay = total_decay * got_decay
    return ahead


def passed_along(value, axis, steps):
    count = lax.axis_size(axis)
    initial, last = (max(0, -steps), min(count, count - steps))
    return lax.ppermute(value, axis, [(source, source + steps) for source in range(initial, last)])


def dot_last(left, right):
    return lax.dot_general(
        left, right, (((1,), (1,)), ((), ())), preferred_element_type=f32
    )


def dot_first(left, right):
    return lax.dot_general(
        left, right, (((0,), (0,)), ((), ())), preferred_element_type=f32
    )


def exact_sum(form, left, right):
    return jnp.einsum(form, left, right, precision=highest, preferred_element_type=f32)


def silu_slope(values):
    logistic = jax.nn.sigmoid(values)
    return logistic * (1.0 + values * (1.0 - logistic))


def segment_ids(lengths_row, first_row, row_count):
    starts = jnp.cumsum(lengths_row) - lengths_row
    position = first_row + jnp.arange(row_count, dtype=jnp.int32)
    found_seq = jnp.sum((position[:, None] >= starts[None, :]).astype(jnp.int32), axis=1) - 1
    inside = (position >= 0) & (position < jnp.sum(lengths_row))
    return jnp.where(inside, found_seq, jnp.where(position < 0, -1, -2))


def block_terms(heads_x, step_size, rate_scale, input_map, output_map, segment, before):
    block_width = segment.shape[1]
    cumulative = jnp.cumsum(step_size * rate_scale[None, None, :], axis=1)
    cum_heads = jnp.swapaxes(cumulative, 1, 2)
    offsets = jnp.arange(block_width)
    same_seq = (
        (segment[:, :, None] == segment[:, None, :]) & (offsets[:, None] >= offsets[None, :])
    )[:, None]
    difference = cum_heads[:, :, :, None] - cum_heads[:, :, None, :]
    decay_mat = jnp.where(same_seq, jnp.exp(jnp.where(same_seq, difference, 0.0)), 0.0)
    scores = exact_sum("cin,cjn->cij", output_map, input_map)
    mixing = decay_mat * scores[:, None]
    inputs = step_size[..., None] * heads_x
    inner_out = exact_sum("chij,cjhp->cihp", mixing, inputs)
    last_seg = segment[:, -1]
    fading = (segment == last_seg[:, None]).astype(jnp.float32)[:, :, None] * jnp.exp(
        cumulative[:, -1:, :] - cumulative
    )
    fresh_state = exact_sum("cjhp,cjn->chpn", fading[..., None] * inputs, input_map)
    through = (last_seg == before).astype(jnp.float32)[:, None] * jnp.exp(cumulative[:, -1, :])
    inflow = (segment == before[:, None]).astype(jnp.float32)[:, :, None] * jnp.exp(cumulative)
    return (decay_mat, mixing, inputs, fading, through, inflow, inner_out, fresh_state)


def block_grads(
    grad_y,
    heads_x,
    step_size,
    rate_scale,
    input_map,
    output_map,
    block_parts,
    entering,
    leaving,
    weighted,
    read_back,
):
    decay_mat, mixing, inputs, fading, through, inflow, inner_out, fresh_state = block_parts
    grad_mix = exact_sum("cihp,cjhp->chij", grad_y, inputs)
    pulled = exact_sum("chpn,cjn->cjhp", leaving, input_map)
    grad_inputs = exact_sum("chij,cihp->cjhp", mixing, grad_y) + fading[..., None] * pulled
    grad_scores = jnp.sum(decay_mat * grad_mix, axis=1)
    grad_output_map = exact_sum("cij,cjn->cin", grad_scores, input_map) + exact_sum(
        "cihp,chpn->cin", weighted, entering
    )
    grad_input_map = exact_sum("cij,cin->cjn", grad_scores, output_map) + exact_sum(
        "cjhp,chpn->cjn", fading[..., None] * inputs, leaving
    )
    paired = grad_mix * mixing
    grad_cum = jnp.swapaxes(jnp.sum(paired, axis=3) - jnp.sum(paired, axis=2), 1, 2)
    grad_cum = grad_cum + inflow * jnp.sum(grad_y * read_back, axis=3)
    fade_grad = fading * jnp.sum(inputs * pulled, axis=3)
    through_grad = through * jnp.sum(leaving * entering, axis=(2, 3))
    grad_cum = grad_cum - fade_grad
    grad_cum = grad_cum.at[:, -1, :].add(jnp.sum(fade_grad, axis=1) + through_grad)
    grad_rate = jnp.flip(jnp.cumsum(jnp.flip(grad_cum, axis=1), axis=1), axis=1)
    grad_step = grad_rate * rate_scale[None, None, :] + jnp.sum(grad_inputs * heads_x, axis=3)
    grad_scale = jnp.sum(grad_rate * step_size, axis=(0, 1))
    grad_x = grad_inputs * step_size[..., None]
    return (grad_x, grad_step, grad_scale, grad_input_map, grad_output_map)


def per_device(
    tokens,
    cotangent,
    lengths,
    deal_order,
    norm_gain,
    proj_gate,
    proj_inner,
    proj_state,
    proj_step,
    conv_inner,
    conv_inner_bias,
    conv_state,
    conv_state_bias,
    step_bias,
    decay_log,
    skip_gain,
    inner_gain,
    proj_out,
):
    batch_count = lengths.shape[0]
    rows_local, width_own = tokens.shape
    tok_dev = rows_local // batch_count
    seq_index = lax.axis_index("seq")
    head_index = lax.axis_index("head")
    seq_size = lax.axis_size("seq")
    head_size = lax.axis_size("head")
    heads_own = proj_step.shape[1]
    inner_own = proj_inner.shape[1]
    head_width = inner_own // heads_own
    state_width = proj_state.shape[1] // 2
    taps_total = conv_inner.shape[0]
    width_all = width_own * head_size
    inner_all = inner_own * head_size
    depth = width_all // seq_size
    per_quarter = seq_size // head_size

    slot_order = deal_order.reshape(batch_count, tok_dev)
    picks = (slot_order[:, :, None] == jnp.arange(tok_dev)[None, None, :]).astype(bf16)

    def dealt(values):
        rows = jnp.einsum(
            "mij,mjf->mif", picks, values.reshape(batch_count, tok_dev, width_own),
            preferred_element_type=f32,
        ).astype(bf16)
        return lax.all_to_all(rows, "seq", split_axis=1, concat_axis=1, tiled=True)

    def returned(values):
        rows = lax.all_to_all(values, "seq", split_axis=1, concat_axis=1, tiled=True)
        rows = jnp.einsum("mij,mif->mjf", picks, rows, preferred_element_type=f32)
        return rows.astype(bf16).reshape(rows_local, width_own)

    def turn_quarter(values):
        lead = values.shape[:-1]
        values = values.reshape(lead + (per_quarter, depth))
        for bit in axis_bits("seq"):
            if bit < per_quarter:
                halves = values.reshape(lead + (per_quarter // (2 * bit), 2, bit, depth))
                turned = jnp.where((seq_index & bit) != 0, jnp.flip(halves, -3), halves)
                values = turned.reshape(lead + (per_quarter, depth))
        return values.reshape(lead + (width_own,))

    def quarter_start(quarter):
        return ((quarter * per_quarter) ^ (seq_index & ~(per_quarter - 1))) * depth

    def all_features(own):
        slots = line_gather(own)
        full = jnp.zeros(own.shape[:-1] + (width_all,), own.dtype)
        for step, slot in enumerate(slots):
            quarter = jnp.remainder(head_index - step + head_size, head_size)
            full = lax.dynamic_update_slice_in_dim(full, slot, quarter_start(quarter), 1)
        return full

    def own_features(partial):
        def block_of(quarter):
            return lax.dynamic_slice_in_dim(partial, quarter_start(quarter), width_own, 1)
        return line_scatter(block_of)

    tokens_in = dealt(tokens)
    cot_in = dealt(cotangent)
    rows = batch_count * tok_dev
    flat_tokens = tokens_in.reshape(rows, width_own)
    flat_cot = cot_in.reshape(rows, width_own)

    half = inner_own // 2
    first = jnp.concatenate([proj_inner[:, :half], proj_state[:, :state_width]], axis=1)
    second = jnp.concatenate([proj_inner[:, half:], proj_state[:, state_width:], proj_step], axis=1)
    full_main = gather_relative(first, second).reshape(width_all, -1)
    cut = half + state_width
    full_inner = jnp.concatenate([full_main[:, :half], full_main[:, cut : cut + half]], axis=1)
    full_state = jnp.concatenate(
        [full_main[:, half:cut], full_main[:, cut + half : cut + half + state_width]], axis=1
    )
    full_step = full_main[:, cut + half + state_width :]
    full_gate = gather_relative(proj_gate[:, :half], proj_gate[:, half:]).reshape(width_all, -1)
    out_t = proj_out.T
    full_out_t = gather_relative(out_t[:, :half], out_t[:, half:]).reshape(width_all, -1)

    rows_bf = all_features(turn_quarter(flat_tokens))
    cot_full = all_features(turn_quarter(flat_cot))

    gain_quarters = turn_quarter(norm_gain.reshape(head_size, width_own))
    gain_rel = jnp.zeros((width_all,), f32)
    for quarter in range(head_size):
        gain_rel = lax.dynamic_update_slice_in_dim(
            gain_rel, gain_quarters[quarter], quarter_start(quarter), 0
        )
    own_start = quarter_start(head_index)
    gain_own = lax.dynamic_slice_in_dim(gain_rel, own_start, width_own, 0)

    first_row = seq_index * tok_dev
    segs = [segment_ids(lengths[b], first_row - (taps_total - 1), tok_dev + 2 * (taps_total - 1)) for b in range(batch_count)]
    seg_all = jnp.stack(segs)
    segment = seg_all[:, taps_total - 1 : taps_total - 1 + tok_dev]
    before = seg_all[:, taps_total - 2]

    rows_full = rows_bf.astype(f32)
    inv_rms = lax.rsqrt(jnp.mean(rows_full * rows_full, axis=1, keepdims=True) + epsilon)
    unit_rows = rows_full * inv_rms
    normed = (unit_rows * gain_rel[None, :]).astype(bf16)
    inner_pre = jnp.dot(normed, full_inner, preferred_element_type=f32)
    state_pre = jnp.dot(normed, full_state, preferred_element_type=f32)
    step_pre = jnp.dot(normed, full_step, preferred_element_type=f32)
    gate_pre = jnp.dot(normed, full_gate, preferred_element_type=f32)
    conv_in = jnp.concatenate([inner_pre, state_pre], axis=1).reshape(batch_count, tok_dev, -1)
    before_rows = passed_along(conv_in[:, tok_dev - (taps_total - 1) :], "seq", 1)

    conv_weight = jnp.concatenate([conv_inner, conv_state], axis=1)
    conv_offset = jnp.concatenate([conv_inner_bias, conv_state_bias])
    rate_scale = -jnp.exp(decay_log)

    extended = jnp.concatenate([before_rows, conv_in], axis=1)
    conv_out = jnp.zeros_like(conv_in) + conv_offset
    for tap in range(taps_total):
        same = (seg_all[:, tap : tap + tok_dev] == segment).astype(f32)
        conv_out = conv_out + conv_weight[tap] * extended[:, tap : tap + tok_dev] * same[..., None]
    mixed_act = jax.nn.silu(conv_out)
    heads_x = mixed_act[:, :, :inner_own].reshape(batch_count, tok_dev, heads_own, head_width)
    input_map = mixed_act[:, :, inner_own : inner_own + state_width]
    output_map = mixed_act[:, :, inner_own + state_width :]
    step_size = jax.nn.softplus(step_pre + step_bias).reshape(batch_count, tok_dev, heads_own)
    block_parts = block_terms(heads_x, step_size, rate_scale, input_map, output_map, segment, before)
    inflow, through, fresh_state = block_parts[5], block_parts[4], block_parts[7]
    entering = scan_before(through, fresh_state, False)
    read_back = exact_sum("cin,chpn->cihp", output_map, entering)
    heads_y = block_parts[6] + inflow[..., None] * read_back + skip_gain[:, None] * heads_x
    mixer_out = heads_y.reshape(rows, inner_own)
    gate_act = jax.nn.silu(gate_pre)
    gated_y = mixer_out * gate_act
    grad_normed_y = jnp.dot(cot_full, full_out_t, preferred_element_type=f32)
    scaled = grad_normed_y * inner_gain
    stats = head_sum(jnp.stack([jnp.sum(gated_y * gated_y, axis=1), jnp.sum(scaled * gated_y, axis=1)]))
    square_sum, inner_dot = stats[0], stats[1]
    inner_inv = lax.rsqrt(square_sum / inner_all + epsilon)[:, None]
    normed_y = (gated_y * inner_inv * inner_gain).astype(bf16)
    branch = own_features(dot_last(normed_y, full_out_t).astype(bf16))
    out_rows = (flat_tokens.astype(f32) + turn_quarter(branch)).astype(bf16)
    out_back = returned(out_rows.reshape(batch_count, tok_dev, width_own))
    grad_out_t = scatter_relative(
        dot_first(cot_full, normed_y).astype(bf16).reshape(seq_size, depth, inner_own)
    )
    grad_gated = (
        inner_inv * scaled
        - gated_y * (inner_inv * inner_inv * inner_inv) * (inner_dot / inner_all)[:, None]
    )
    grad_inner_gain = jnp.sum(grad_normed_y * gated_y * inner_inv, axis=0)
    grad_heads_y = (grad_gated * gate_act).reshape(batch_count, tok_dev, heads_own, head_width)
    grad_gate = (grad_gated * mixer_out * silu_slope(gate_pre)).astype(bf16)
    grad_w_gate = scatter_relative(
        dot_first(normed, grad_gate).astype(bf16).reshape(seq_size, depth, inner_own)
    )
    grad_skip = jnp.sum(grad_heads_y * heads_x, axis=(0, 1, 3))
    weighted = inflow[..., None] * grad_heads_y
    local_in = exact_sum("cihp,cin->chpn", weighted, output_map)
    leaving = scan_before(through, local_in, True)
    grad_x, grad_step, grad_scale, grad_input_map, grad_output_map = block_grads(
        grad_heads_y, heads_x, step_size, rate_scale, input_map, output_map, block_parts,
        entering, leaving, weighted, read_back,
    )
    grad_x = grad_x + skip_gain[:, None] * grad_heads_y
    grad_step_pre = grad_step.reshape(rows, heads_own) * jax.nn.sigmoid(step_pre + step_bias)
    grad_mixed = jnp.concatenate(
        [grad_x.reshape(batch_count, tok_dev, inner_own), grad_input_map, grad_output_map], axis=2
    )
    grad_conv_out = grad_mixed * silu_slope(conv_out)
    after_rows = passed_along(grad_conv_out[:, : taps_total - 1], "seq", -1)
    grad_ext = jnp.concatenate([grad_conv_out, after_rows], axis=1)
    grad_conv_in = jnp.zeros_like(conv_in)
    weight_rows = []
    for tap in range(taps_total):
        lag = taps_total - 1 - tap
        ahead = seg_all[:, taps_total - 1 + lag : taps_total - 1 + lag + tok_dev] == segment
        grad_conv_in = grad_conv_in + conv_weight[tap] * grad_ext[:, lag : lag + tok_dev] * ahead.astype(f32)[..., None]
        behind = (seg_all[:, tap : tap + tok_dev] == segment).astype(f32)
        weight_rows.append(jnp.sum(grad_conv_out * extended[:, tap : tap + tok_dev] * behind[..., None], axis=(0, 1)))
    grad_conv_w = jnp.stack(weight_rows)
    grad_conv_b = jnp.sum(grad_conv_out, axis=(0, 1))
    grad_conv_in = grad_conv_in.reshape(rows, -1)
    grad_inner_low = grad_conv_in[:, :inner_own].astype(bf16)
    grad_state_pre = grad_conv_in[:, inner_own:]
    grad_step_low = grad_step_pre.astype(bf16)
    state_hi = grad_state_pre.astype(bf16)
    rows_part = (
        dot_last(grad_gate, full_gate)
        + dot_last(grad_inner_low, full_inner)
        + dot_last(grad_step_low, full_step)
        + dot_last(state_hi, full_state)
    )
    unit_own = lax.dynamic_slice_in_dim(unit_rows, own_start, width_own, 1)
    row_dot = head_sum(jnp.sum(rows_part * gain_rel * unit_rows, axis=1))
    rows_own = own_features(rows_part.astype(bf16))
    grad_norm_gain = turn_quarter(jnp.sum(rows_own * unit_own, axis=0))
    grad_own = inv_rms * (rows_own * gain_own - unit_own * (row_dot / width_all)[:, None])
    grad_rows_in = (turn_quarter(grad_own) + flat_cot.astype(f32)).astype(bf16)
    grad_back = returned(grad_rows_in.reshape(batch_count, tok_dev, width_own))
    grad_main = scatter_relative(
        dot_first(
            normed,
            jnp.concatenate([grad_inner_low, grad_step_low], axis=1),
        ).astype(bf16).reshape(seq_size, depth, inner_own + heads_own)
    )
    state_part = dot_first(state_hi, normed).astype(bf16)
    grad_w_state = own_features(state_part)
    packed = jnp.concatenate([
        grad_conv_w[:, :inner_own].reshape(-1), grad_conv_b[:inner_own], grad_inner_gain,
        jnp.sum(grad_step_pre, axis=0), grad_scale * rate_scale, grad_skip, grad_norm_gain,
    ])
    packed = seq_sum(packed)
    state_small = head_sum(seq_sum(jnp.concatenate([grad_conv_w[:, inner_own:], grad_conv_b[None, inner_own:]])))
    state_own = state_small.shape[1] // head_size
    state_small = lax.dynamic_slice_in_dim(state_small, head_index * state_own, state_own, 1)
    grad_w_state = seq_sum(turn_quarter(grad_w_state).T.astype(bf16)).astype(f32)
    sizes = [taps_total * inner_own, inner_own, inner_own, heads_own, heads_own, heads_own, width_own]
    pieces, at = [], 0
    for size in sizes:
        pieces.append(packed[at : at + size])
        at += size
    return (
        out_back,
        grad_back,
        pieces[6],
        grad_w_gate,
        grad_main[:, :inner_own],
        grad_w_state,
        grad_main[:, inner_own:],
        pieces[0].reshape(taps_total, inner_own),
        pieces[1],
        state_small[:taps_total],
        state_small[taps_total],
        pieces[3],
        pieces[4],
        pieces[5],
        pieces[2],
        grad_out_t.T,
    )


def solution(mesh):
    return jax.shard_map(
        per_device,
        mesh=mesh,
        in_specs=(
            P("seq", "head"),
            P("seq", "head"),
            P(),
            P("seq"),
            P(),
            P("seq", "head"),
            P("seq", "head"),
            P("seq", None),
            P("seq", "head"),
            P(None, "head"),
            P("head"),
            P(),
            P(),
            P("head"),
            P("head"),
            P("head"),
            P("head"),
            P("head", "seq"),
        ),
        out_specs=(
            P("seq", "head"),
            P("seq", "head"),
            P("head"),
            P("seq", "head"),
            P("seq", "head"),
            P("head", None),
            P("seq", "head"),
            P(None, "head"),
            P("head"),
            P(None, "head"),
            P("head"),
            P("head"),
            P("head"),
            P("head"),
            P("head"),
            P("head", "seq"),
        ),
        check_vma=False,
    )
```

```python
import functools
import jax
import jax.numpy as jnp
from jax import lax
from jax.experimental import pallas as pl
from jax.experimental.pallas import tpu as pltpu
from jax.sharding import PartitionSpec as P

epsilon = 1e-05
highest = lax.Precision.HIGHEST
f32 = jnp.float32
bf16 = jnp.bfloat16
LANES = 128
HALO = 8
STATE_PAD = 16
VMEM_BYTES = 56 * 1024 * 1024


def swapped(value, axis, bit):
    return lax.ppermute(value, axis, [(i, i ^ bit) for i in range(lax.axis_size(axis))])


def axis_bits(axis):
    count = lax.axis_size(axis)
    return [1 << k for k in range(count.bit_length() - 1)]


def added(left, right):
    return (left.astype(f32) + right.astype(f32)).astype(left.dtype)


def gathered(part, order):
    held, labels = part[None], [0]
    for bit in order:
        held = jnp.concatenate([held, swapped(held, "seq", bit)], axis=0)
        labels = labels + [label ^ bit for label in labels]
    if labels != sorted(labels):
        held = jnp.concatenate([held[at : at + 1] for at in map(labels.index, sorted(labels))])
    return held.reshape(-1, part.shape[1])


def gather_weight(first, second):
    links = axis_bits("seq")[1:]
    own = (gathered(first, links), gathered(second, links[::-1]))
    return own, tuple(swapped(half, "seq", 1) for half in own)


def scattered(keep, send, labels, order):
    rows = keep.shape[0] // len(labels)
    kept = keep.reshape(len(labels), rows, -1)
    sent = send.reshape(len(labels), rows, -1)
    for step, bit in enumerate(order):
        got = swapped(sent, "seq", bit)
        if step == len(order) - 1:
            return kept[0].astype(f32) + got[0].astype(f32)
        total = added(kept, got)
        after = order[step + 1]
        keep_at = [at for at, label in enumerate(labels) if not label & after]
        send_at = [labels.index(labels[at] ^ after) for at in keep_at]
        kept = jnp.concatenate([total[at : at + 1] for at in keep_at])
        sent = jnp.concatenate([total[at : at + 1] for at in send_at])
        labels = [labels[at] for at in keep_at]


def line_gather(own):
    size = lax.axis_size("head")
    ups, downs = [], []
    up = down = own
    for step in range(1, size):
        up = lax.ppermute(up, "head", [(i, i + 1) for i in range(step - 1, size - 1)])
        down = lax.ppermute(down, "head", [(i, i - 1) for i in range(1, size - step + 1)])
        ups.append(up)
        downs.append(down)
    return ups, downs


def line_scatter(blocks):
    size, here = lax.axis_size("head"), lax.axis_index("head")

    def block_of(at):
        return lax.dynamic_index_in_dim(blocks, jnp.clip(at, 0, size - 1), 0, keepdims=False)

    up = down = None
    for step in range(1, size):
        give_up = blocks[size - 1] if step == 1 else block_of(here + size - step)
        give_down = blocks[0] if step == 1 else block_of(here - size + step)
        if up is not None:
            give_up, give_down = added(give_up, up), added(give_down, down)
        up = lax.ppermute(give_up, "head", [(i, i + 1) for i in range(step)])
        down = lax.ppermute(give_down, "head", [(i, i - 1) for i in range(size - step, size)])
    return block_of(here).astype(f32) + up.astype(f32) + down.astype(f32)


def axis_sum(value, axis):
    for bit in axis_bits(axis):
        value = value + swapped(value, axis, bit)
    return value


def scan_before(local, states, reverse):
    here = lax.axis_index("seq")
    state_row = (jnp.arange(local.shape[1]) < states).astype(f32)[None, :, None]
    total = local.astype(f32)
    ahead = jnp.broadcast_to(1.0 - state_row, local.shape)
    bits = axis_bits("seq")
    sent = local
    for bit in bits:
        got = swapped(sent, "seq", bit).astype(f32)
        later = ((here & bit) == 0) if reverse else ((here & bit) != 0)
        ahead = jnp.where(later, ahead[:, states : states + 1] * got + state_row * ahead, ahead)
        if bit != bits[-1]:
            total = jnp.where(
                later,
                total[:, states : states + 1] * got + state_row * total,
                got[:, states : states + 1] * total + state_row * got,
            )
            sent = total.astype(bf16)
    return ahead.astype(bf16)


def passed_along(value, axis, steps):
    count = lax.axis_size(axis)
    initial, last = (max(0, -steps), min(count, count - steps))
    return lax.ppermute(value, axis, [(source, source + steps) for source in range(initial, last)])


def dot(left, right, precision=None):
    return jnp.dot(left, right, preferred_element_type=f32, precision=precision)


def dot_nt(left, right, precision=None):
    return lax.dot_general(
        left, right, (((1,), (1,)), ((), ())), preferred_element_type=f32, precision=precision
    )


def dot_tn(left, right, precision=None):
    return lax.dot_general(
        left, right, (((0,), (0,)), ((), ())), preferred_element_type=f32, precision=precision
    )


def both_parts(values):
    high = values.astype(bf16)
    return jnp.concatenate([high, (values - high.astype(f32)).astype(bf16)], axis=1)


def silu_slope(values):
    logistic = jax.nn.sigmoid(values)
    return logistic * (1.0 + values * (1.0 - logistic))


def call(kernel, grid, scalars, ins, outs, scratch=(), flops=0, bytes_accessed=0):
    return pl.pallas_call(
        kernel,
        grid_spec=pltpu.PrefetchScalarGridSpec(
            num_scalar_prefetch=len(scalars),
            grid=grid,
            in_specs=[pl.BlockSpec(block, index) for _, block, index in ins],
            out_specs=[pl.BlockSpec(block, index) for _, _, block, index in outs],
            scratch_shapes=list(scratch),
        ),
        out_shape=[jax.ShapeDtypeStruct(shape, dtype) for shape, dtype, _, _ in outs],
        compiler_params=pltpu.CompilerParams(vmem_limit_bytes=VMEM_BYTES),
        cost_estimate=pl.CostEstimate(
            flops=int(flops), bytes_accessed=int(bytes_accessed), transcendentals=0
        ),
    )(*scalars, *[array for array, _, _ in ins])


def per_row(array, rows):
    return (array, (rows,) + array.shape[1:], lambda m, *_: (m,) + (0,) * (array.ndim - 1))


def per_step(array):
    return (array, (1,) + array.shape[1:], lambda m, *_: (m,) + (0,) * (array.ndim - 1))


def entire(array):
    return (array, array.shape, lambda *_: (0,) * array.ndim)


def row_out(total, rows, width, dtype):
    return ((total, width), dtype, (rows, width), lambda m, *_: (m, 0))


def step_out(count, shape, dtype):
    return ((count,) + shape, dtype, (1,) + shape, lambda m, *_: (m,) + (0,) * len(shape))


def sum_out(shape, dtype=f32):
    return (shape, dtype, shape, lambda *_: (0,) * len(shape))


def segment_of(position, plan, place, m):
    found = jnp.full(jnp.shape(position), -1, jnp.int32)
    for k in range(plan.shape[1]):
        found = found + (position >= plan[m, k]).astype(jnp.int32)
    return jnp.where(position >= place[3], -2, found)


def column_position(rows, place, shift=0):
    return place[2] + shift + lax.broadcasted_iota(jnp.int32, (rows, 1), 0)


def row_position(rows, place):
    return place[2] + lax.broadcasted_iota(jnp.int32, (1, rows), 1)


def by_core(values, me, depth):
    count = values.shape[1] // depth
    blocks = [values[:, k * depth : (k + 1) * depth] for k in range(count)]
    odd = (me & 1) != 0
    halves = []
    for at in (0, 1):
        straight, turned = blocks[at::2], blocks[1 - at :: 2]
        half = [jnp.where(odd, b, a) for a, b in zip(straight, turned)]
        bit = 1
        while bit < count // 2:
            flip = ((me >> 1) & bit) != 0
            half = [jnp.where(flip, half[k ^ bit], half[k]) for k in range(len(half))]
            bit *= 2
        halves.append(half[0] if len(half) == 1 else jnp.concatenate(half, axis=1))
    return halves


def from_core(first, second, me, depth):
    count = 2 * first.shape[1] // depth
    odd = (me & 1) != 0
    halves = []
    for values in (first, second):
        half = [values[:, k * depth : (k + 1) * depth] for k in range(count // 2)]
        bit = 1
        while bit < count // 2:
            flip = ((me >> 1) & bit) != 0
            half = [jnp.where(flip, half[k ^ bit], half[k]) for k in range(len(half))]
            bit *= 2
        halves.append(half)
    blocks = []
    for k in range(count // 2):
        blocks.append(jnp.where(odd, halves[1][k], halves[0][k]))
        blocks.append(jnp.where(odd, halves[0][k], halves[1][k]))
    return jnp.concatenate(blocks, axis=1)


def half_start(quarter, me, width, depth):
    count = width // depth // 2
    return pl.multiple_of(((quarter * count) ^ ((me >> 1) & ~(count - 1))) * depth, width // 2)


def features_kernel(norm, size, depth, place, *refs):
    own, ups, downs = refs[0], refs[1:size], refs[size : 2 * size - 1]
    refs = refs[2 * size - 1 :]
    if norm:
        gain, even, odd, even_t, odd_t, inverse = refs
    else:
        even, odd, even_t, odd_t = refs
    z, me = place[0], place[1]
    width = own.shape[1]
    slots = [own[...].astype(f32)]
    for step in range(1, size):
        up, down = ups[step - 1][...].astype(f32), downs[size - step - 1][...].astype(f32)
        slots.append(jnp.where(z >= step, up, down))
    if norm:
        square = sum(jnp.sum(slot * slot, axis=1, keepdims=True) for slot in slots)
        inv = lax.rsqrt(square / (width * size) + epsilon)
        inverse[...] = inv
    for step, slot in enumerate(slots):
        quarter = lax.rem(z - step + size, size)
        if norm:
            start = pl.multiple_of(quarter * width, width)
            slot = slot * inv * gain[:, pl.ds(start, width)]
        first, second = by_core(slot, me, depth)
        at = pl.ds(half_start(quarter, me, width, depth), width // 2)
        even[:, at] = first.astype(bf16)
        odd[:, at] = second.astype(bf16)
        even_t[at, :] = first.T.astype(bf16)
        odd_t[at, :] = second.T.astype(bf16)


def all_features(own, place, gain, rows, depth):
    total, width = own.shape
    size = lax.axis_size("head")
    ups, downs = line_gather(own)
    half = width * size // 2
    ins = [per_row(array, rows) for array in [own] + ups + downs]
    outs = [row_out(total, rows, half, bf16)] * 2
    outs += [((half, total), bf16, (half, rows), lambda m, *_: (0, m))] * 2
    if gain is not None:
        ins.append(entire(gain))
        outs.append(row_out(total, rows, 1, f32))
    kernel = functools.partial(features_kernel, gain is not None, size, depth)
    return call(
        kernel, (total // rows,), (place,), ins, outs, bytes_accessed=total * width * 2 * 11
    )


def project_kernel(outs_of, even, odd, *refs):
    count = 2 * sum(len(group) for group in outs_of)
    weights, outs = refs[:count], refs[count:]
    at = 0
    for out, group in zip(outs, outs_of):
        start = 0
        for _ in group:
            first, second = weights[at], weights[at + 1]
            width = first.shape[1]
            out[:, start : start + width] = dot(even[...], first[...]) + dot(odd[...], second[...])
            start += width
            at += 2


def project(even, odd, groups, rows):
    total = even.shape[0]
    ins = [per_row(even, rows), per_row(odd, rows)]
    outs, moved, flops = [], 0, 0
    for group in groups:
        width = 0
        for first, second in group:
            ins += [entire(first), entire(second)]
            width += first.shape[1]
        outs.append(row_out(total, rows, width, f32))
        moved += width * (2 * even.shape[1] * 2 + total * 4)
        flops += 4 * total * even.shape[1] * width
    kernel = functools.partial(project_kernel, [len(group) * [0] for group in groups])
    return call(kernel, (total // rows,), (), ins, outs, flops=flops, bytes_accessed=moved)


def conv_kernel(
    width, heads, place, plan, first_pre, second_pre, first_halo, second_halo, taps, bias, step_bias,
    scale, spread, conv_out, small, inputs, maps, fresh, extended, padded,
):
    m = pl.program_id(0)
    rows = first_pre.shape[0]
    states = maps.shape[1] // 2
    half = width // 2
    taps_total = taps.shape[0]
    here = segment_of(column_position(rows, place), plan, place, m)
    same = [
        (segment_of(column_position(rows, place, tap + 1 - taps_total), plan, place, m) == here).astype(f32)
        for tap in range(taps_total)
    ]
    before = segment_of(place[2] - 1, plan, place, m)
    last = segment_of(place[2] + rows - 1, plan, place, m)

    padded[...] = jnp.zeros_like(padded)
    padded[:, :heads] = second_pre[:, half + states :]
    pre = padded[...] + step_bias[...]
    rest = jnp.exp(-jnp.abs(pre))
    series = rest * (
        1.0 - rest * (1 / 2 - rest * (1 / 3 - rest * (1 / 4 - rest * (1 / 5 - rest * (1 / 6)))))
    )
    step = jnp.maximum(pre, 0.0) + jnp.where(rest < 0.03, series, jnp.log(1.0 + rest))
    row = lax.broadcasted_iota(jnp.int32, (rows, rows), 0)
    col = lax.broadcasted_iota(jnp.int32, (rows, rows), 1)
    lower = (row >= col).astype(f32)
    cumulative = dot(lower, step * scale[...], highest)
    small[:, :LANES] = cumulative
    small[:, LANES : 2 * LANES] = step
    small[:, 2 * LANES :] = pre
    ending = cumulative[rows - 1 :, :]
    fading = (here == last).astype(f32) * jnp.exp(ending - cumulative)
    through = (last == before).astype(f32) * jnp.exp(ending)
    step_parts, fading_parts = both_parts(step), both_parts(fading)
    through_parts = both_parts(jnp.broadcast_to(through, (STATE_PAD, LANES)))

    def conv(source, halo, at, out_at):
        tile = slice(at, at + LANES)
        extended[:HALO, :] = halo[0, :, tile]
        extended[HALO:, :] = source[:, tile]
        out_tile = slice(out_at, out_at + LANES)
        result = jnp.broadcast_to(bias[:, out_tile], (rows, LANES))
        for tap in range(taps_total):
            start = HALO + tap + 1 - taps_total
            result = result + taps[tap : tap + 1, out_tile] * extended[start : start + rows, :] * same[tap]
        conv_out[:, out_tile] = result
        return result * jax.nn.sigmoid(result)

    for at in range(0, states, LANES):
        maps[:, at : at + LANES] = conv(first_pre, first_halo, half + at, half + at)
        maps[:, states + at : states + at + LANES] = conv(
            second_pre, second_halo, half + at, width + states + at
        )
    input_map = maps[:, :states].astype(bf16)
    for at in range(0, width, LANES):
        if at < half:
            heads_x = conv(first_pre, first_halo, at, at)
        else:
            heads_x = conv(second_pre, second_halo, at - half, at + states)
        tile = slice(at, at + LANES)
        values = heads_x * dot(step_parts, spread[:, tile])
        inputs[:, tile] = values.astype(bf16)
        faded = (values * dot(fading_parts, spread[:, tile])).astype(bf16)
        fresh[0, :states, tile] = dot_tn(input_map, faded).astype(bf16)
        fresh[0, states:, tile] = dot(through_parts, spread[:, tile]).astype(bf16)


def allowed_mask(rows, place, plan, m, transposed):
    column = segment_of(column_position(rows, place), plan, place, m)
    across = segment_of(row_position(rows, place), plan, place, m)
    row = lax.broadcasted_iota(jnp.int32, (rows, rows), 0)
    col = lax.broadcasted_iota(jnp.int32, (rows, rows), 1)
    order = (row <= col) if transposed else (row >= col)
    return jnp.where(order & (column == across), 0.0, -1e30)


def lane_select(parts, per):
    lane = lax.broadcasted_iota(jnp.int32, parts[0].shape, 1)
    result = parts[0]
    for at in range(1, per):
        result = jnp.where(lane >= at * (LANES // per), parts[at], result)
    return result


def mix_kernel(per, place, plan, small, maps, inputs, out):
    m = pl.program_id(0)
    rows, width = inputs.shape
    states = maps.shape[1] // 2
    cumulative = small[:, :LANES]
    flat = cumulative.T
    mask = allowed_mask(rows, place, plan, m, False)
    scores = dot_nt(maps[:, states:], maps[:, :states], highest)
    for at in range(0, width, LANES):
        tile = slice(at, at + LANES)
        for low in range(0, rows, LANES):
            end = low + LANES
            parts = []
            for sub in range(per):
                head = at // LANES * per + sub
                decay = jnp.exp(
                    (cumulative[low:end, head : head + 1] - flat[head : head + 1, :end])
                    + mask[low:end, :end]
                )
                mixing = (decay * scores[low:end, :end]).astype(bf16)
                parts.append(dot(mixing, inputs[:end, tile]))
            out[low:end, tile] = lane_select(parts, per)


def unmix_kernel(per, place, plan, small, maps, inputs, grads, grad_inputs, grad_maps, total):
    m = pl.program_id(0)
    rows, width = inputs.shape
    states = maps.shape[1] // 2
    cumulative = small[:, :LANES]
    flat = cumulative.T
    mask = allowed_mask(rows, place, plan, m, True)
    scores = dot_nt(maps[:, :states], maps[:, states:], highest)
    lane = lax.broadcasted_iota(jnp.int32, (LANES, LANES), 1)
    total[...] = jnp.zeros_like(total)
    for at in range(0, width, LANES):
        tile = slice(at, at + LANES)
        for low in range(0, rows, LANES):
            end = low + LANES
            later = grads[low:, tile]
            parts = []
            gathered_sum = total[low:end, low:]
            for sub in range(per):
                head = at // LANES * per + sub
                decay = jnp.exp(
                    (flat[head : head + 1, low:] - cumulative[low:end, head : head + 1])
                    + mask[low:end, low:]
                )
                mixing = (decay * scores[low:end, low:]).astype(bf16)
                parts.append(dot(mixing, later))
                inside = (lane // (LANES // per)) == sub
                own = jnp.where(inside, inputs[low:end, tile].astype(f32), 0.0).astype(bf16)
                gathered_sum = gathered_sum + decay * dot_nt(own, later)
            total[low:end, low:] = gathered_sum
            grad_inputs[low:end, tile] = lane_select(parts, per)
    grad_scores = total[...].astype(bf16)
    grad_maps[:, :states] = dot(grad_scores, maps[:, states:].astype(bf16))
    grad_maps[:, states:] = dot_tn(grad_scores, maps[:, :states].astype(bf16))


def inner_tile(ref, at, states):
    half = (ref.shape[1] - 2 * states) // 2
    start = at if at < half else at + states
    return ref[:, start : start + LANES]


def inflow_of(cumulative, rows, place, plan, m):
    here = segment_of(column_position(rows, place), plan, place, m)
    before = segment_of(place[2] - 1, plan, place, m)
    return (here == before).astype(f32) * jnp.exp(cumulative)


def gated_kernel(
    place, plan, small, maps, mixed, entering, conv_out, gate, grad_y, gain, skip, spread, scanned, sums
):
    m = pl.program_id(0)
    rows, width = mixed.shape
    states = maps.shape[1] // 2
    inflow = both_parts(inflow_of(small[:, :LANES], rows, place, plan, m))
    output_map = maps[:, states:].astype(bf16)
    square = jnp.zeros((rows, LANES), f32)
    product = jnp.zeros((rows, LANES), f32)
    for at in range(0, width, LANES):
        tile = slice(at, at + LANES)
        carried = dot(output_map, entering[0, :states, tile]) * dot(inflow, spread[:, tile])
        scan = mixed[:, tile] + carried
        scanned[:, tile] = scan
        conv = inner_tile(conv_out, at, states)
        gates = gate[:, tile]
        gated = (scan + skip[:, tile] * (conv * jax.nn.sigmoid(conv))) * (gates * jax.nn.sigmoid(gates))
        square = square + gated * gated
        product = product + grad_y[:, tile] * gain[:, tile] * gated
    ones = jnp.ones((HALO, LANES), f32)
    pick = lax.broadcasted_iota(jnp.int32, (HALO, rows), 0)
    sums[0] = jnp.where(pick == 0, dot_nt(ones, square, highest), dot_nt(ones, product, highest))


def ungated_kernel(
    inner_all, place, plan, small, maps, scanned, conv_out, gate, grad_y, sums, gain, skip, spread,
    normed_y, grads, grad_gate, local, grad_gain, grad_skip,
):
    m = pl.program_id(0)
    rows, width = scanned.shape
    states = maps.shape[1] // 2
    row = lax.broadcasted_iota(jnp.int32, (rows, rows), 0)
    col = lax.broadcasted_iota(jnp.int32, (rows, rows), 1)
    columns = dot_nt((row == col).astype(f32), sums[0], highest)
    inv = lax.rsqrt(columns[:, :1] / inner_all + epsilon)
    pull = inv * inv * inv * (columns[:, 1:2] / inner_all)
    cumulative = small[:, :LANES]
    inflow = both_parts(inflow_of(cumulative, rows, place, plan, m))
    before = segment_of(place[2] - 1, plan, place, m)
    last = segment_of(place[2] + rows - 1, plan, place, m)
    through = (last == before).astype(f32) * jnp.exp(cumulative[rows - 1 :, :])
    through_parts = both_parts(jnp.broadcast_to(through, (STATE_PAD, LANES)))
    output_map = maps[:, states:].astype(bf16)

    @pl.when(m == 0)
    def _():
        grad_gain[...] = jnp.zeros_like(grad_gain)
        grad_skip[...] = jnp.zeros_like(grad_skip)

    for at in range(0, width, LANES):
        tile = slice(at, at + LANES)
        conv = inner_tile(conv_out, at, states)
        heads_x = conv * jax.nn.sigmoid(conv)
        mixer = scanned[:, tile] + skip[:, tile] * heads_x
        gates = gate[:, tile]
        logistic = jax.nn.sigmoid(gates)
        act = gates * logistic
        gated = mixer * act
        normed = gated * inv
        normed_y[:, tile] = (normed * gain[:, tile]).astype(bf16)
        grad = grad_y[:, tile]
        grad_gain[:, tile] += jnp.sum(grad * normed, axis=0, keepdims=True)
        grad_gated = inv * (grad * gain[:, tile]) - gated * pull
        grad_mixer = grad_gated * act
        grads[:, tile] = grad_mixer.astype(bf16)
        grad_skip[:, tile] += jnp.sum(grad_mixer * heads_x, axis=0, keepdims=True)
        grad_gate[:, tile] = (
            grad_gated * mixer * (logistic * (1.0 + gates * (1.0 - logistic)))
        ).astype(bf16)
        weighted = (grad_mixer * dot(inflow, spread[:, tile])).astype(bf16)
        local[0, :states, tile] = dot_tn(output_map, weighted).astype(bf16)
        local[0, states:, tile] = dot(through_parts, spread[:, tile]).astype(bf16)


def unscan_kernel(
    place, plan, small, maps, scanned, conv_out, inputs, grads, grad_inputs, grad_maps, entering, leaving,
    skip, scale, spread, grad_conv_out, grad_step, grad_bias, grad_heads,
):
    m = pl.program_id(0)
    rows, width = scanned.shape
    states = maps.shape[1] // 2
    half = width // 2
    cumulative, step, pre = (small[:, k * LANES : (k + 1) * LANES] for k in range(3))
    here = segment_of(column_position(rows, place), plan, place, m)
    before = segment_of(place[2] - 1, plan, place, m)
    last = segment_of(place[2] + rows - 1, plan, place, m)
    ending = cumulative[rows - 1 :, :]
    fading = both_parts((here == last).astype(f32) * jnp.exp(ending - cumulative))
    inflow = both_parts((here == before).astype(f32) * jnp.exp(cumulative))
    through = (last == before).astype(f32) * jnp.exp(ending)
    step_parts = both_parts(step)
    input_map = maps[:, :states].astype(bf16)

    @pl.when(m == 0)
    def _():
        grad_bias[...] = jnp.zeros_like(grad_bias)
        grad_heads[...] = jnp.zeros_like(grad_heads)

    grad_in, grad_out = grad_maps[:, :states], grad_maps[:, states:]
    grad_cum = jnp.zeros((rows, LANES), f32)
    grad_own = jnp.zeros((rows, LANES), f32)
    ends = jnp.zeros((HALO, LANES), f32)
    for at in range(0, width, LANES):
        tile = slice(at, at + LANES)
        spread_tile = spread[:, tile]
        leave, enter = leaving[0, :states, tile], entering[0, :states, tile]
        fade = dot(fading, spread_tile)
        pulled = fade * dot(input_map, leave)
        values = inputs[:, tile].astype(f32)
        grad = grads[:, tile].astype(f32)
        total = grad_inputs[:, tile] + pulled
        faded = (values * fade).astype(bf16)
        weighted = (grad * dot(inflow, spread_tile)).astype(bf16)
        grad_in = grad_in + dot_nt(faded, leave)
        grad_out = grad_out + dot_nt(weighted, enter)
        conv = inner_tile(conv_out, at, states)
        logistic = jax.nn.sigmoid(conv)
        heads_x = conv * logistic
        first = both_parts(grad * scanned[:, tile] - values * total)
        second = both_parts(total * heads_x)
        grad_cum = grad_cum + dot_nt(first[:, :LANES], spread[:LANES, tile]) + dot_nt(
            first[:, LANES:], spread[:LANES, tile]
        )
        grad_own = grad_own + dot_nt(second[:, :LANES], spread[:LANES, tile]) + dot_nt(
            second[:, LANES:], spread[:LANES, tile]
        )
        fade_sum = jnp.sum(values * pulled, axis=0, keepdims=True)
        through_sum = jnp.sum(leave.astype(f32) * enter.astype(f32), axis=0, keepdims=True)
        pick = lax.broadcasted_iota(jnp.int32, (HALO, LANES), 0)
        edge = both_parts(jnp.where(pick == 0, fade_sum, through_sum))
        ends = ends + dot_nt(edge[:, :LANES], spread[:LANES, tile]) + dot_nt(
            edge[:, LANES:], spread[:LANES, tile]
        )
        grad_x = total * dot(step_parts, spread_tile) + skip[:, tile] * grad
        start = at if at < half else at + states
        result = grad_x * (logistic * (1.0 + conv * (1.0 - logistic)))
        grad_conv_out[:, start : start + LANES] = result
        grad_bias[:, start : start + LANES] += jnp.sum(result, axis=0, keepdims=True)
    for values, start in ((grad_in, half), (grad_out, width + states)):
        conv = conv_out[:, start : start + states]
        result = values * silu_slope(conv)
        grad_conv_out[:, start : start + states] = result
        grad_bias[:, start : start + states] += jnp.sum(result, axis=0, keepdims=True)
    row = lax.broadcasted_iota(jnp.int32, (rows, rows), 0)
    col = lax.broadcasted_iota(jnp.int32, (rows, rows), 1)
    upper = (row <= col).astype(f32)
    grad_rate = dot(upper, grad_cum, highest) + (ends[:1] + through * ends[1:2])
    rate = step * scale[...]
    grad_pre = (grad_rate * scale[...] + grad_own) * jax.nn.sigmoid(pre)
    grad_step[...] = grad_pre
    grad_heads[0:1, :] += jnp.sum(grad_rate * rate, axis=0, keepdims=True)
    grad_heads[1:2, :] += jnp.sum(grad_pre, axis=0, keepdims=True)


def unconv_kernel(
    heads, place, plan, first_pre, second_pre, first_halo, second_halo, grad_out, after, grad_step, taps,
    first_grad, second_grad, grad_taps, extended, extended_grad,
):
    m = pl.program_id(0)
    rows = first_pre.shape[0]
    first_width = first_pre.shape[1]
    channels = grad_out.shape[1]
    taps_total = taps.shape[0]
    here = segment_of(column_position(rows, place), plan, place, m)
    behind, ahead = [], []
    for tap in range(taps_total):
        lag = taps_total - 1 - tap
        behind.append((segment_of(column_position(rows, place, -lag), plan, place, m) == here).astype(f32))
        ahead.append((segment_of(column_position(rows, place, lag), plan, place, m) == here).astype(f32))

    @pl.when(m == 0)
    def _():
        grad_taps[...] = jnp.zeros_like(grad_taps)

    for at in range(0, channels, LANES):
        tile = slice(at, at + LANES)
        if at < first_width:
            source, halo, target, start = first_pre, first_halo, first_grad, at
        else:
            source, halo, target, start = second_pre, second_halo, second_grad, at - first_width
        own = slice(start, start + LANES)
        extended[:HALO, :] = halo[0, :, own]
        extended[HALO:, :] = source[:, own]
        grad = grad_out[:, tile]
        extended_grad[:rows, :] = grad
        extended_grad[rows:, :] = after[0, :, tile]
        result = jnp.zeros((rows, LANES), f32)
        for tap in range(taps_total):
            lag = taps_total - 1 - tap
            result = result + taps[tap : tap + 1, tile] * extended_grad[lag : lag + rows, :] * ahead[tap]
            begin = HALO - lag
            product = grad * extended[begin : begin + rows, :] * behind[tap]
            grad_taps[tap : tap + 1, tile] += jnp.sum(product, axis=0, keepdims=True)
        target[:, own] = result.astype(bf16)
    second_grad[:, channels - first_width :] = grad_step[:, :heads].astype(bf16)


def spread_kernel(count, with_sums, size, depth, place, *refs):
    values, refs = refs[:count], refs[count:]
    even_w, odd_w, refs = refs[:count], refs[count : 2 * count], refs[2 * count :]
    if with_sums:
        even, odd, out, sums, even_s, odd_s = refs
    else:
        out, even_s, odd_s = refs
    z, me = place[0], place[1]
    even_s[...] = sum(dot_nt(v[...], w[...]) for v, w in zip(values, even_w))
    odd_s[...] = sum(dot_nt(v[...], w[...]) for v, w in zip(values, odd_w))
    rows, half = even_s.shape
    if with_sums:
        product = jnp.zeros((rows, LANES), f32)
        for scratch, normed in ((even_s, even), (odd_s, odd)):
            for at in range(0, half, LANES):
                product = product + scratch[:, at : at + LANES] * normed[:, at : at + LANES].astype(f32)
        sums[0] = dot_nt(jnp.ones((HALO, LANES), f32), product, highest)
    width = 2 * half // size
    for quarter in range(size):
        at = pl.ds(half_start(quarter, me, width, depth), width // 2)
        out[quarter] = from_core(even_s[:, at], odd_s[:, at], me, depth).astype(bf16)


def spread_features(values, even_w, odd_w, place, rows, depth, normed=None):
    total = values[0].shape[0]
    size = lax.axis_size("head")
    half = even_w[0].shape[0]
    width = 2 * half // size
    ins = [per_row(v, rows) for v in values] + [entire(w) for w in even_w + odd_w]
    outs = [((size, total, width), bf16, (size, rows, width), lambda m, *_: (0, m, 0))]
    if normed is not None:
        ins += [per_row(array, rows) for array in normed]
        outs.append(step_out(total // rows, (HALO, rows), f32))
    kernel = functools.partial(spread_kernel, len(values), normed is not None, size, depth)
    inner = sum(v.shape[1] for v in values)
    return call(
        kernel, (total // rows,), (place,), ins, outs,
        scratch=[pltpu.VMEM((rows, half), f32)] * 2,
        flops=4 * total * inner * half,
        bytes_accessed=inner * half * 4 + total * half * 4 + total * inner * 2,
    )


def weight_kernel(count, keep_and_send, *refs):
    left, rights, refs = refs[0], refs[1 : 1 + count], refs[1 + count :]
    if not keep_and_send:
        for right, out in zip(rights, refs):
            out[...] = dot(left[...], right[...]).astype(bf16)
        return
    others, refs = refs[:count], refs[count:]
    step = pl.program_id(0)
    blocks = pl.num_programs(0)
    for at, (right, other) in enumerate(zip(rights, others)):
        keep, send = refs[2 * at], refs[2 * at + 1]
        result = (dot(left[...], right[...]) + other[...].astype(f32)).astype(bf16)
        sending = (step >= blocks // 2) if at % 2 == 0 else (lax.rem(step, 2) == 1)

        @pl.when(sending)
        def _():
            send[...] = result

        @pl.when(jnp.logical_not(sending))
        def _():
            keep[...] = result


def weight_gradient(even_t, odd_t, halves, depth):
    blocks = even_t.shape[0] // depth
    total = even_t.shape[1]
    left = lambda array: (array, (depth, total), lambda l: (l, 0))
    flops = 2 * even_t.shape[0] * total * sum(h.shape[1] for h in halves)
    moved = even_t.shape[0] * (total + sum(h.shape[1] for h in halves)) * 2
    sent = call(
        functools.partial(weight_kernel, 2, False), (blocks,), (),
        [left(odd_t)] + [entire(h) for h in halves],
        [((even_t.shape[0], h.shape[1]), bf16, (depth, h.shape[1]), lambda l: (l, 0)) for h in halves],
        flops=flops, bytes_accessed=moved,
    )
    got = [swapped(value, "seq", 1) for value in sent]
    outs = []
    top = blocks // 2
    for at, h in enumerate(halves):
        shape = (even_t.shape[0] // 2, h.shape[1])
        block = (depth, h.shape[1])
        if at == 0:
            outs.append((shape, bf16, block, lambda l: (jnp.minimum(l, top - 1), 0)))
            outs.append((shape, bf16, block, lambda l: (jnp.maximum(l - top, 0), 0)))
        else:
            outs.append((shape, bf16, block, lambda l: (l // 2, 0)))
            outs.append((shape, bf16, block, lambda l: (l // 2, 0)))
    mine = call(
        functools.partial(weight_kernel, 2, True), (blocks,), (),
        [left(even_t)] + [entire(h) for h in halves]
        + [(g, (depth, g.shape[1]), lambda l: (l, 0)) for g in got],
        outs, flops=flops, bytes_accessed=moved,
    )
    links = axis_bits("seq")[1:]
    labels = [bit << 1 for bit in range(blocks)]
    first = scattered(mine[0], mine[1], [x for x in labels if not x & links[-1]], links[::-1])
    second = scattered(mine[2], mine[3], [x for x in labels if not x & links[0]], links)
    return first, second


def per_device(
    tokens,
    cotangent,
    lengths,
    deal_order,
    norm_gain,
    proj_gate,
    proj_inner,
    proj_state,
    proj_step,
    conv_inner,
    conv_inner_bias,
    conv_state,
    conv_state_bias,
    step_bias,
    decay_log,
    skip_gain,
    inner_gain,
    proj_out,
):
    batch_count = lengths.shape[0]
    rows_local, width_own = tokens.shape
    tok_dev = rows_local // batch_count
    seq_index = lax.axis_index("seq")
    head_index = lax.axis_index("head")
    seq_size = lax.axis_size("seq")
    head_size = lax.axis_size("head")
    heads_own = proj_step.shape[1]
    inner_own = proj_inner.shape[1]
    head_width = inner_own // heads_own
    states = proj_state.shape[1] // 2
    taps_total = conv_inner.shape[0]
    width_all = width_own * head_size
    inner_all = inner_own * head_size
    depth = width_all // seq_size
    per_quarter = seq_size // head_size
    half = inner_own // 2
    channels = inner_own + 2 * states
    per = LANES // head_width
    rows = tok_dev
    grid = (batch_count,)

    place = jnp.stack(
        [head_index, seq_index, seq_index * tok_dev, jnp.int32(tok_dev * seq_size)]
    ).astype(jnp.int32)
    plan = (jnp.cumsum(lengths, axis=1) - lengths).astype(jnp.int32)
    scalars = (place, plan)

    slot_order = deal_order.reshape(batch_count, tok_dev)
    picks = (slot_order[:, :, None] == jnp.arange(tok_dev)[None, None, :]).astype(bf16)

    def dealt(values):
        values = jnp.einsum(
            "mij,mjf->mif", picks, values.reshape(batch_count, tok_dev, width_own),
            preferred_element_type=f32,
        ).astype(bf16)
        values = lax.all_to_all(values, "seq", split_axis=1, concat_axis=1, tiled=True)
        return values.reshape(rows_local, width_own)

    def returned(values):
        values = values.reshape(batch_count, tok_dev, width_own)
        values = lax.all_to_all(values, "seq", split_axis=1, concat_axis=1, tiled=True)
        values = jnp.einsum("mij,mif->mjf", picks, values, preferred_element_type=f32)
        return values.astype(bf16).reshape(rows_local, width_own)

    flat_tokens = dealt(tokens)
    flat_cot = dealt(cotangent)

    main_even, main_odd = gather_weight(
        jnp.concatenate([proj_inner[:, :half], proj_state[:, :states]], axis=1),
        jnp.concatenate([proj_inner[:, half:], proj_state[:, states:], proj_step], axis=1),
    )
    gate_even, gate_odd = gather_weight(proj_gate[:, :half], proj_gate[:, half:])
    out_t = proj_out.T
    out_even, out_odd = gather_weight(out_t[:, :half], out_t[:, half:])

    even, odd, even_t, odd_t, inv_rms = all_features(
        flat_tokens, place, norm_gain[None, :], tok_dev, depth
    )
    cot_even, cot_odd, cot_even_t, cot_odd_t = all_features(flat_cot, place, None, tok_dev, depth)

    def in_order(inner, state):
        return jnp.concatenate(
            [inner[:, :half], state[:, :states], inner[:, half:], state[:, states:]], axis=1
        )

    taps = in_order(conv_inner, conv_state)
    bias = in_order(conv_inner_bias[None, :], conv_state_bias[None, :])
    pad = LANES - heads_own
    step_bias_row = jnp.pad(step_bias, (0, pad))[None, :]
    scale = jnp.pad(-jnp.exp(decay_log), (0, pad))[None, :]
    spread = (
        jnp.arange(2 * LANES)[:, None] % LANES == jnp.arange(inner_own)[None, :] // head_width
    ).astype(bf16)
    skip = jnp.repeat(skip_gain, head_width)[None, :]
    gain = inner_gain[None, :]

    first_pre, second_pre = project(
        even, odd, [[(main_even[0], main_odd[0])], [(main_even[1], main_odd[1])]], tok_dev
    )

    def halo_before(values):
        values = values.reshape(batch_count, tok_dev, -1)[:, tok_dev - HALO :]
        return passed_along(values, "seq", 1)

    first_halo, second_halo = halo_before(first_pre), halo_before(second_pre)
    (gate,) = project(
        even, odd, [[(gate_even[0], gate_odd[0]), (gate_even[1], gate_odd[1])]], tok_dev
    )
    pres = [per_row(first_pre, rows), per_row(second_pre, rows), per_step(first_halo), per_step(second_halo)]
    conv_out, small, inputs, maps, fresh = call(
        functools.partial(conv_kernel, inner_own, heads_own), grid, scalars,
        pres + [entire(a) for a in (taps, bias, step_bias_row, scale, spread)],
        [
            row_out(rows_local, rows, channels, f32),
            row_out(rows_local, rows, 3 * LANES, f32),
            row_out(rows_local, rows, inner_own, bf16),
            row_out(rows_local, rows, 2 * states, f32),
            step_out(batch_count, (states + STATE_PAD, inner_own), bf16),
        ],
        scratch=[pltpu.VMEM((rows + HALO, LANES), f32), pltpu.VMEM((rows, LANES), f32)],
        flops=rows_local * inner_own * 2000, bytes_accessed=rows_local * inner_own * 12,
    )
    entering = scan_before(fresh, states, False)
    scan_ins = [per_row(small, rows), per_row(maps, rows)]
    (mixed,) = call(
        functools.partial(mix_kernel, per), grid, scalars, scan_ins + [per_row(inputs, rows)],
        [row_out(rows_local, rows, inner_own, f32)],
        flops=rows_local * inner_own * 6000, bytes_accessed=rows_local * inner_own * 6,
    )
    (grad_y,) = project(
        cot_even, cot_odd, [[(out_even[0], out_odd[0]), (out_even[1], out_odd[1])]], tok_dev
    )
    vectors = [entire(gain), entire(skip), entire(spread)]
    scanned, sums = call(
        gated_kernel, grid, scalars,
        scan_ins
        + [per_row(mixed, rows), per_step(entering), per_row(conv_out, rows), per_row(gate, rows)]
        + [per_row(grad_y, rows)] + vectors,
        [row_out(rows_local, rows, inner_own, f32), step_out(batch_count, (HALO, rows), f32)],
        flops=rows_local * inner_own * 1500, bytes_accessed=rows_local * inner_own * 20,
    )
    sums = axis_sum(sums, "head")
    normed_y, grads, grad_gate, local, grad_gain, grad_skip = call(
        functools.partial(ungated_kernel, inner_all), grid, scalars,
        scan_ins
        + [per_row(array, rows) for array in (scanned, conv_out, gate, grad_y)]
        + [per_step(sums)] + vectors,
        [row_out(rows_local, rows, inner_own, bf16)] * 3
        + [step_out(batch_count, (states + STATE_PAD, inner_own), bf16)]
        + [sum_out((1, inner_own))] * 2,
        flops=rows_local * inner_own * 2000, bytes_accessed=rows_local * inner_own * 24,
    )
    leaving = scan_before(local, states, True)

    (out_blocks,) = spread_features(
        [normed_y[:, :half], normed_y[:, half:]], list(out_even), list(out_odd), place, tok_dev, depth
    )
    branch = line_scatter(out_blocks)
    out_back = returned((flat_tokens.astype(f32) + branch).astype(bf16))

    grad_out_parts = weight_gradient(cot_even_t, cot_odd_t, [normed_y[:, :half], normed_y[:, half:]], depth)
    grad_gate_halves = [grad_gate[:, :half], grad_gate[:, half:]]
    grad_gate_parts = weight_gradient(even_t, odd_t, grad_gate_halves, depth)
    grad_inputs, grad_maps = call(
        functools.partial(unmix_kernel, per), grid, scalars,
        scan_ins + [per_row(inputs, rows), per_row(grads, rows)],
        [row_out(rows_local, rows, inner_own, f32), row_out(rows_local, rows, 2 * states, f32)],
        scratch=[pltpu.VMEM((rows, rows), f32)],
        flops=rows_local * inner_own * 12000, bytes_accessed=rows_local * inner_own * 8,
    )
    grad_conv_out, grad_step, grad_bias, grad_heads = call(
        unscan_kernel, grid, scalars,
        scan_ins
        + [per_row(a, rows) for a in (scanned, conv_out, inputs, grads, grad_inputs, grad_maps)]
        + [per_step(entering), per_step(leaving), entire(skip), entire(scale), entire(spread)],
        [
            row_out(rows_local, rows, channels, f32),
            row_out(rows_local, rows, LANES, f32),
            sum_out((1, channels)),
            sum_out((HALO, LANES)),
        ],
        flops=rows_local * inner_own * 4000, bytes_accessed=rows_local * inner_own * 28,
    )
    after = passed_along(grad_conv_out.reshape(batch_count, tok_dev, channels)[:, :HALO], "seq", -1)
    first_grad, second_grad, grad_taps = call(
        functools.partial(unconv_kernel, heads_own), grid, scalars,
        pres + [per_row(grad_conv_out, rows), per_step(after), per_row(grad_step, rows), entire(taps)],
        [
            row_out(rows_local, rows, first_pre.shape[1], bf16),
            row_out(rows_local, rows, second_pre.shape[1], bf16),
            sum_out((taps_total, channels)),
        ],
        scratch=[pltpu.VMEM((rows + HALO, LANES), f32)] * 2,
        flops=rows_local * inner_own * 100, bytes_accessed=rows_local * inner_own * 14,
    )
    grad_blocks, row_dots = spread_features(
        [first_grad, second_grad] + grad_gate_halves,
        list(main_even) + list(gate_even), list(main_odd) + list(gate_odd),
        place, tok_dev, depth, normed=(even, odd),
    )
    row_dots = axis_sum(row_dots, "head")[:, 0, :].reshape(rows_local, 1)
    rows_own = line_scatter(grad_blocks)
    unit_own = flat_tokens.astype(f32) * inv_rms
    gain_own = lax.dynamic_slice_in_dim(norm_gain, head_index * width_own, width_own, 0)
    grad_norm_gain = jnp.sum(rows_own * unit_own, axis=0)
    grad_rows_in = inv_rms * (rows_own * gain_own - unit_own * (row_dots / width_all))
    grad_back = returned((grad_rows_in + flat_cot.astype(f32)).astype(bf16))
    first_main, second_main = weight_gradient(even_t, odd_t, [first_grad, second_grad], depth)

    grad_w_state = axis_sum(
        jnp.concatenate([first_main[:, half:], second_main[:, half : half + states]], axis=1), "head"
    ).astype(bf16)
    mine = (seq_index // per_quarter) == head_index
    place_rows = (seq_index % per_quarter) * depth
    grad_w_state = lax.dynamic_update_slice_in_dim(
        jnp.zeros((width_own, 2 * states), bf16),
        jnp.where(mine, grad_w_state, jnp.zeros_like(grad_w_state)), place_rows, 0,
    )
    grad_w_state = axis_sum(grad_w_state, "seq").astype(f32)

    def fill(row):
        return jnp.pad(row, ((0, 0), (0, channels - row.shape[1])))

    packed = jnp.concatenate(
        [
            grad_taps,
            grad_bias,
            fill(grad_gain),
            fill(grad_skip),
            fill(jnp.concatenate([grad_heads[0:1], grad_heads[1:2], grad_norm_gain[None, :]], axis=1)),
        ]
    )
    packed = axis_sum(packed, "seq")

    def inner_of(values):
        return jnp.concatenate([values[:, :half], values[:, half + states : inner_own + states]], axis=1)

    state_sums = jnp.concatenate(
        [packed[: taps_total + 1, half : half + states], packed[: taps_total + 1, inner_own + states :]],
        axis=1,
    )
    state_sums = axis_sum(state_sums, "head")
    state_own = 2 * states // head_size
    state_sums = lax.dynamic_slice_in_dim(state_sums, head_index * state_own, state_own, 1)
    conv_sums = inner_of(packed[: taps_total + 1])
    return (
        out_back,
        grad_back,
        packed[taps_total + 3, 2 * LANES : 2 * LANES + width_own],
        jnp.concatenate(grad_gate_parts, axis=1),
        jnp.concatenate([first_main[:, :half], second_main[:, :half]], axis=1),
        grad_w_state,
        second_main[:, half + states :],
        conv_sums[:taps_total],
        conv_sums[taps_total],
        state_sums[:taps_total],
        state_sums[taps_total],
        packed[taps_total + 3, LANES : LANES + heads_own],
        packed[taps_total + 3, :heads_own],
        jnp.sum(packed[taps_total + 2, :inner_own].reshape(heads_own, head_width), axis=1),
        packed[taps_total + 1, :inner_own],
        jnp.concatenate(grad_out_parts, axis=1).T,
    )


def solution(mesh):
    return jax.shard_map(
        per_device,
        mesh=mesh,
        in_specs=(
            P("seq", "head"),
            P("seq", "head"),
            P(),
            P("seq"),
            P(),
            P("seq", "head"),
            P("seq", "head"),
            P("seq", None),
            P("seq", "head"),
            P(None, "head"),
            P("head"),
            P(),
            P(),
            P("head"),
            P("head"),
            P("head"),
            P("head"),
            P("head", "seq"),
        ),
        out_specs=(
            P("seq", "head"),
            P("seq", "head"),
            P("head"),
            P("seq", "head"),
            P("seq", "head"),
            P("head", None),
            P("seq", "head"),
            P(None, "head"),
            P("head"),
            P(None, "head"),
            P("head"),
            P("head"),
            P("head"),
            P("head"),
            P("head"),
            P("head", "seq"),
        ),
        check_vma=False,
    )
```

```python
import functools
import jax
import jax.numpy as jnp
from jax import lax
from jax.experimental import pallas as pl
from jax.experimental.pallas import tpu as pltpu
from jax.sharding import PartitionSpec as P

epsilon = 1e-05
highest = lax.Precision.HIGHEST
f32 = jnp.float32
bf16 = jnp.bfloat16
LANES = 128
HALO = 8
STATE_PAD = 16
COST_SCALE = 64
VMEM_SPARE = 4 * 1024 * 1024


def swapped(value, axis, bit):
    return lax.ppermute(value, axis, [(i, i ^ bit) for i in range(lax.axis_size(axis))])


def axis_bits(axis):
    count = lax.axis_size(axis)
    return [1 << k for k in range(count.bit_length() - 1)]


def added(left, right):
    return (left.astype(f32) + right.astype(f32)).astype(left.dtype)


def after(value, *others):
    return lax.optimization_barrier((value, *others))[0]


def after_all(values, others):
    return lax.optimization_barrier((tuple(values), tuple(others)))[0]


class Scattered:
    def __init__(self, keep, send, labels, order):
        rows = keep.shape[0] // len(labels)
        self.pair = (keep.reshape(len(labels), rows, -1), send.reshape(len(labels), rows, -1))
        self.labels, self.left = labels, list(order)

    def advance(self):
        kept, sent = self.pair
        total = added(kept, swapped(sent, "seq", self.left.pop(0)))
        if not self.left:
            self.pair = (total,)
            return
        following, labels = self.left[0], self.labels
        keep_at = [at for at, label in enumerate(labels) if not label & following]
        send_at = [labels.index(labels[at] ^ following) for at in keep_at]
        kept = jnp.concatenate([total[at : at + 1] for at in keep_at])
        sent = jnp.concatenate([total[at : at + 1] for at in send_at])
        self.pair = (kept, sent)
        self.labels = [labels[at] for at in keep_at]

    def finish(self):
        return [self.pair[0][0]]


class LineGather:
    def __init__(self, own):
        self.size = lax.axis_size("head")
        self.up = self.down = own
        self.ups, self.downs = [], []

    def advance(self, *beside):
        step = len(self.ups) + 1
        if step < self.size:
            up = lax.ppermute(self.up, "head", [(i, i + 1) for i in range(step - 1, self.size - 1)])
            down = lax.ppermute(self.down, "head", [(i, i - 1) for i in range(1, self.size - step + 1)])
            if beside:
                (up, down), beside = lax.optimization_barrier(((up, down), beside))
            self.up, self.down = up, down
            self.ups.append(up)
            self.downs.append(down)
        return beside

    def finish(self):
        while len(self.ups) + 1 < self.size:
            self.advance()
        return self.ups, self.downs


class LineScatter:
    def __init__(self, edges, middle):
        self.size, self.here = lax.axis_size("head"), lax.axis_index("head")
        self.edges, self.middle = edges, middle
        self.up = self.down = None
        self.step = 0

    def block_of(self, at):
        last = self.size - 1
        inner = lax.dynamic_index_in_dim(self.middle, jnp.clip(at - 1, 0, last - 2), 0, keepdims=False)
        return jnp.where(at <= 0, self.edges[0], jnp.where(at >= last, self.edges[1], inner))

    def advance(self, *beside):
        self.step += 1
        step, size, here = self.step, self.size, self.here
        if step < size:
            if step == 1:
                up, down = self.edges[1], self.edges[0]
            else:
                up = added(self.block_of(here + size - step), self.up)
                down = added(self.block_of(here - size + step), self.down)
            up = lax.ppermute(up, "head", [(i, i + 1) for i in range(step)])
            down = lax.ppermute(down, "head", [(i, i - 1) for i in range(size - step, size)])
            if beside:
                (up, down), beside = lax.optimization_barrier(((up, down), beside))
            self.up, self.down = up, down
        return beside

    def finish(self):
        while self.step + 1 < self.size:
            self.advance()
        return self.block_of(self.here).astype(f32) + self.up.astype(f32) + self.down.astype(f32)


def axis_sum(value, axis):
    for bit in axis_bits(axis):
        value = value + swapped(value, axis, bit)
    return value


def passed_along(value, axis, steps):
    count = lax.axis_size(axis)
    initial, last = (max(0, -steps), min(count, count - steps))
    return lax.ppermute(value, axis, [(source, source + steps) for source in range(initial, last)])


def dot(left, right, precision=None):
    return jnp.dot(left, right, preferred_element_type=f32, precision=precision)


def dot_nt(left, right, precision=None):
    return lax.dot_general(
        left, right, (((1,), (1,)), ((), ())), preferred_element_type=f32, precision=precision
    )


def dot_tn(left, right, precision=None):
    return lax.dot_general(
        left, right, (((0,), (0,)), ((), ())), preferred_element_type=f32, precision=precision
    )


def both_parts(values):
    high = values.astype(bf16)
    return jnp.concatenate([high, (values - high.astype(f32)).astype(bf16)], axis=1)


def silu_slope(values):
    logistic = jax.nn.sigmoid(values)
    return logistic * (1.0 + values * (1.0 - logistic))


def tiled_bytes(shape, dtype):
    *lead, rows, lanes = shape
    size = -(-rows // 8) * 8 * -(-lanes // LANES) * LANES * jnp.dtype(dtype).itemsize
    for count in lead:
        size *= count
    return size


def call(kernel, grid, scalars, ins, outs, scratch=(), flops=0, bytes_accessed=0):
    held = [block == array.shape for array, block, _ in ins]
    need = sum(
        (1 if whole else 2) * tiled_bytes(block, array.dtype) for (array, block, _), whole in zip(ins, held)
    )
    need += sum(2 * tiled_bytes(block, dtype) for _, dtype, block, _ in outs)
    need += sum(tiled_bytes(item.shape, item.dtype) for item in scratch)
    return pl.pallas_call(
        kernel,
        grid_spec=pltpu.PrefetchScalarGridSpec(
            num_scalar_prefetch=len(scalars),
            grid=grid,
            in_specs=[
                pl.BlockSpec(block, index, pipeline_mode=pl.Buffered(1) if whole else None)
                for (_, block, index), whole in zip(ins, held)
            ],
            out_specs=[pl.BlockSpec(block, index) for _, _, block, index in outs],
            scratch_shapes=list(scratch),
        ),
        out_shape=[jax.ShapeDtypeStruct(shape, dtype) for shape, dtype, _, _ in outs],
        compiler_params=pltpu.CompilerParams(vmem_limit_bytes=need + VMEM_SPARE),
        cost_estimate=pl.CostEstimate(
            flops=int(flops) // COST_SCALE, bytes_accessed=int(bytes_accessed) // COST_SCALE, transcendentals=0
        ),
    )(*scalars, *[array for array, _, _ in ins])


def per_row(array, rows):
    return (array, (rows,) + array.shape[1:], lambda m, *_: (m,) + (0,) * (array.ndim - 1))


def per_deal(array):
    return (array, (array.shape[0], 1) + array.shape[2:], lambda m, *_: (0, m, 0, 0))


def deal_out(senders, count, rows, width, dtype):
    return ((senders, count, rows, width), dtype, (senders, 1, rows, width), lambda m, *_: (0, m, 0, 0))


def deal_rows(ref, tile):
    values = ref[:, 0, :, tile].astype(f32)
    return values.reshape(values.shape[0] * values.shape[1], values.shape[2])


def put_deal_rows(ref, tile, values):
    shape = (ref.shape[0], ref.shape[2], values.shape[1])
    ref[:, 0, :, tile] = values.reshape(shape).astype(ref.dtype)


def per_step(array):
    return (array, (1,) + array.shape[1:], lambda m, *_: (m,) + (0,) * (array.ndim - 1))


def entire(array):
    return (array, array.shape, lambda *_: (0,) * array.ndim)


def row_out(total, rows, width, dtype):
    return ((total, width), dtype, (rows, width), lambda m, *_: (m, 0))


def step_out(count, shape, dtype):
    return ((count,) + shape, dtype, (1,) + shape, lambda m, *_: (m,) + (0,) * len(shape))


def sum_out(shape, dtype=f32):
    return (shape, dtype, shape, lambda *_: (0,) * len(shape))


def joined(earlier, following, states):
    row = lax.broadcasted_iota(jnp.int32, earlier.shape, 0)
    return following[states : states + 1] * earlier + jnp.where(row < states, following, 0.0)


def chip_kernel(states, flags, own, other, total):
    for at in range(own.shape[0]):
        mine, theirs = own[at].astype(f32), other[at].astype(f32)
        later = flags[0] != 0
        first, second = jnp.where(later, theirs, mine), jnp.where(later, mine, theirs)
        total[at] = joined(first, second, states).astype(bf16)


def link_kernel(states, step, last, flags, *refs):
    total, other, refs = refs[0], refs[1], refs[2:]
    later = flags[step] != 0
    if step > 1:
        before, refs = refs[0], refs[1:]
    for at in range(total.shape[0]):
        mine, theirs = total[at].astype(f32), other[at].astype(f32)
        if step == 1:
            row = lax.broadcasted_iota(jnp.int32, mine.shape, 0)
            ahead = jnp.where(row < states, 0.0, 1.0)
            refs[0][at] = jnp.where(later, theirs, ahead).astype(bf16)
        else:
            ahead = before[at].astype(f32)
            refs[0][at] = jnp.where(later, joined(theirs, ahead, states), ahead).astype(bf16)
        if not last:
            first, second = jnp.where(later, theirs, mine), jnp.where(later, mine, theirs)
            refs[1][at] = joined(first, second, states).astype(bf16)


def enter_kernel(states, flags, ahead, ahead_other, sibling, entering):
    odd = flags[flags.shape[0] - 1] != 0
    half = ahead.shape[2]
    for at in range(ahead.shape[0]):
        mine, theirs = ahead[at], ahead_other[at]
        left, right = jnp.where(odd, theirs, mine), jnp.where(odd, mine, theirs)
        for start, values in ((0, left), (half, right)):
            values = values.astype(f32)
            near = sibling[at, :, start : start + half].astype(f32)
            entering[at, :, start : start + half] = jnp.where(
                flags[0] != 0, joined(values, near, states), values
            ).astype(bf16)


def scan_before(local, states, reverse, fillers):
    here = lax.axis_index("seq")
    bits = axis_bits("seq")
    count, height, width = local.shape
    passed = [((here & bit) == 0) if reverse else ((here & bit) != 0) for bit in bits]
    flags = jnp.stack(passed + [(here & 1) != 0]).astype(jnp.int32)
    whole = local.shape
    piece = (count, height, width // 2)
    at_step = lambda *_: (0, 0, 0)
    at_core = lambda _, flags: (0, 0, flags[len(bits)])
    half_out = (piece, bf16, piece, at_step)
    moved = local.size * 4
    sibling = swapped(local, "seq", 1)
    (total,) = call(
        functools.partial(chip_kernel, states), (1,), (flags,),
        [(local, piece, at_core), (sibling, piece, at_core)], [half_out], bytes_accessed=moved,
    )
    ahead, filled, beside = None, [], ()
    for step, bit in enumerate(bits[1:], 1):
        other = swapped(total, "seq", bit)
        if step <= len(fillers):
            other, value = lax.optimization_barrier((other, fillers[step - 1](*beside)))
            beside = (value,)
            filled.append(value)
        last = step == len(bits) - 1
        ins = [total, other] + ([] if ahead is None else [ahead])
        results = call(
            functools.partial(link_kernel, states, step, last), (1,), (flags,),
            [(array, piece, at_step) for array in ins], [half_out] * (1 if last else 2),
            bytes_accessed=moved,
        )
        ahead = results[0]
        total = None if last else results[1]
    ahead_other = swapped(ahead, "seq", 1)
    (entering,) = call(
        functools.partial(enter_kernel, states), (1,), (flags,),
        [(ahead, piece, at_step), (ahead_other, piece, at_step), (sibling, whole, at_step)],
        [(local.shape, bf16, whole, at_step)], bytes_accessed=moved * 2,
    )
    return [entering] + filled


def segment_of(position, plan, place, m):
    found = jnp.full(jnp.shape(position), -1, jnp.int32)
    for k in range(plan.shape[1]):
        found = found + (position >= plan[m, k]).astype(jnp.int32)
    return jnp.where(position >= place[3], -2, found)


def column_position(rows, place, shift=0):
    return place[2] + shift + lax.broadcasted_iota(jnp.int32, (rows, 1), 0)


def row_position(rows, place):
    return place[2] + lax.broadcasted_iota(jnp.int32, (1, rows), 1)


def by_core(values, me, depth):
    count = values.shape[1] // depth
    blocks = [values[:, k * depth : (k + 1) * depth] for k in range(count)]
    odd = (me & 1) != 0
    halves = []
    for at in (0, 1):
        straight, turned = blocks[at::2], blocks[1 - at :: 2]
        half = [jnp.where(odd, b, a) for a, b in zip(straight, turned)]
        bit = 1
        while bit < count // 2:
            flip = ((me >> 1) & bit) != 0
            half = [jnp.where(flip, half[k ^ bit], half[k]) for k in range(len(half))]
            bit *= 2
        halves.append(half[0] if len(half) == 1 else jnp.concatenate(half, axis=1))
    return halves


def half_start(quarter, me, width, depth):
    count = width // depth // 2
    return pl.multiple_of(((quarter * count) ^ ((me >> 1) & ~(count - 1))) * depth, width // 2)


def line_slot(own, ups, downs, z, step):
    if step == 0:
        return deal_rows(own, slice(None))
    up, down = ups[step - 1], downs[len(downs) - step]
    return jnp.where(z >= step, deal_rows(up, slice(None)), deal_rows(down, slice(None)))


def features_kernel(size, depth, place, *refs):
    own, ups, downs = refs[0], refs[1:size], refs[size : 2 * size - 1]
    gain, normed, even_t, odd_t, inverse = refs[2 * size - 1 :]
    z, me = place[0], place[1]
    width = own.shape[3]
    slots = [line_slot(own, ups, downs, z, step) for step in range(size)]
    square = sum(jnp.sum(slot * slot, axis=1, keepdims=True) for slot in slots)
    inv = lax.rsqrt(square / (width * size) + epsilon)
    put_deal_rows(inverse, slice(None), inv)
    for step, slot in enumerate(slots):
        quarter = lax.rem(z - step + size, size)
        place_at = pl.ds(pl.multiple_of(quarter * width, width), width)
        slot = slot * inv * gain[:, place_at]
        normed[:, place_at] = slot.astype(bf16)
        first, second = by_core(slot, me, depth)
        at = pl.ds(half_start(quarter, me, width, depth), width // 2)
        even_t[at, :] = first.T.astype(bf16)
        odd_t[at, :] = second.T.astype(bf16)


def all_features(own, lines, place, gain, depth):
    senders, count, piece, width = own.shape
    rows = senders * piece
    total = rows * count
    size = lax.axis_size("head")
    ups, downs = lines
    half = width * size // 2
    outs = [row_out(total, rows, 2 * half, bf16)]
    outs += [((half, total), bf16, (half, rows), lambda m, *_: (0, m))] * 2
    outs.append(deal_out(senders, count, piece, 1, f32))
    return call(
        functools.partial(features_kernel, size, depth), (count,), (place,),
        [per_deal(array) for array in [own] + ups + downs] + [entire(gain)], outs,
        bytes_accessed=total * width * 2 * 15,
    )


def cotangent_kernel(size, place, *refs):
    own, ups, downs = refs[0], refs[1:size], refs[size : 2 * size - 1]
    weight, every, grad_y = refs[2 * size - 1 :]
    z = place[0]
    width = own.shape[3]
    total = None
    for step in range(size):
        slot = line_slot(own, ups, downs, z, step)
        quarter = lax.rem(z - step + size, size)
        place_at = pl.ds(pl.multiple_of(quarter * width, width), width)
        every[:, place_at] = slot.astype(bf16)
        part = dot_nt(slot.astype(bf16), weight[:, place_at])
        total = part if total is None else total + part
    grad_y[...] = total


def cotangent_products(own, lines, place, weight):
    senders, count, piece, width = own.shape
    rows = senders * piece
    total = rows * count
    size = lax.axis_size("head")
    ups, downs = lines
    return call(
        functools.partial(cotangent_kernel, size), (count,), (place,),
        [per_deal(array) for array in [own] + ups + downs] + [entire(weight)],
        [
            row_out(total, rows, width * size, bf16),
            row_out(total, rows, weight.shape[0], f32),
        ],
        flops=2 * total * width * size * weight.shape[0],
        bytes_accessed=total * width * 2 * 11 + weight.size * 2 + total * weight.shape[0] * 4,
    )


def conv_kernel(
    width, place, plan, pre, halo, taps, bias, step_bias, scale, spread, conv_out, small, inputs, maps, fresh,
    extended,
):
    m = pl.program_id(0)
    rows = pre.shape[0]
    states = maps.shape[1] // 2
    taps_total = taps.shape[0]
    here = segment_of(column_position(rows, place), plan, place, m)
    same = [
        (segment_of(column_position(rows, place, tap + 1 - taps_total), plan, place, m) == here).astype(f32)
        for tap in range(taps_total)
    ]
    before = segment_of(place[2] - 1, plan, place, m)
    last = segment_of(place[2] + rows - 1, plan, place, m)

    step_pre = pre[:, width + 2 * states : width + 2 * states + LANES] + step_bias[...]
    rest = jnp.exp(-jnp.abs(step_pre))
    series = rest * (
        1.0 - rest * (1 / 2 - rest * (1 / 3 - rest * (1 / 4 - rest * (1 / 5 - rest * (1 / 6)))))
    )
    step = jnp.maximum(step_pre, 0.0) + jnp.where(rest < 0.03, series, jnp.log(1.0 + rest))
    row = lax.broadcasted_iota(jnp.int32, (rows, rows), 0)
    col = lax.broadcasted_iota(jnp.int32, (rows, rows), 1)
    lower = (row >= col).astype(f32)
    cumulative = dot(lower, step * scale[...], highest)
    small[:, :LANES] = cumulative
    small[:, LANES : 2 * LANES] = step
    small[:, 2 * LANES :] = step_pre
    ending = cumulative[rows - 1 :, :]
    fading = (here == last).astype(f32) * jnp.exp(ending - cumulative)
    through = (last == before).astype(f32) * jnp.exp(ending)
    step_parts, fading_parts = both_parts(step), both_parts(fading)
    through_parts = both_parts(jnp.broadcast_to(through, (STATE_PAD, LANES)))

    def conv(at):
        tile = slice(at, at + LANES)
        extended[:HALO, :] = halo[0, :, tile]
        extended[HALO:, :] = pre[:, tile]
        result = jnp.broadcast_to(bias[:, tile], (rows, LANES))
        for tap in range(taps_total):
            start = HALO + tap + 1 - taps_total
            result = result + taps[tap : tap + 1, tile] * extended[start : start + rows, :] * same[tap]
        conv_out[:, tile] = result
        return result * jax.nn.sigmoid(result)

    for at in range(0, 2 * states, LANES):
        maps[:, at : at + LANES] = conv(width + at)
    input_map_t = maps[:, :states].T.astype(bf16)
    for at in range(0, width, LANES):
        tile = slice(at, at + LANES)
        values = conv(at) * dot(step_parts, spread[:, tile])
        inputs[:, tile] = values.astype(bf16)
        faded = (values * dot(fading_parts, spread[:, tile])).astype(bf16)
        fresh[0, :states, tile] = dot(input_map_t, faded).astype(bf16)
        fresh[0, states:, tile] = dot(through_parts, spread[:, tile]).astype(bf16)


def allowed_mask(rows, place, plan, m, transposed):
    column = segment_of(column_position(rows, place), plan, place, m)
    across = segment_of(row_position(rows, place), plan, place, m)
    row = lax.broadcasted_iota(jnp.int32, (rows, rows), 0)
    col = lax.broadcasted_iota(jnp.int32, (rows, rows), 1)
    order = (row <= col) if transposed else (row >= col)
    return jnp.where(order & (column == across), 0.0, -1e30)


def lane_select(parts, per):
    lane = lax.broadcasted_iota(jnp.int32, parts[0].shape, 1)
    result = parts[0]
    for at in range(1, per):
        result = jnp.where(lane >= at * (LANES // per), parts[at], result)
    return result


def mix_kernel(per, place, plan, small, maps, inputs, out):
    m = pl.program_id(0)
    rows, width = inputs.shape
    states = maps.shape[1] // 2
    cumulative = small[:, :LANES]
    flat = cumulative.T
    mask = allowed_mask(rows, place, plan, m, False)
    scores = dot_nt(maps[:, states:], maps[:, :states], highest)
    for at in range(0, width, LANES):
        tile = slice(at, at + LANES)
        for low in range(0, rows, LANES):
            end = low + LANES
            parts = []
            for sub in range(per):
                head = at // LANES * per + sub
                decay = jnp.exp(
                    (cumulative[low:end, head : head + 1] - flat[head : head + 1, :end])
                    + mask[low:end, :end]
                )
                mixing = (decay * scores[low:end, :end]).astype(bf16)
                parts.append(dot(mixing, inputs[:end, tile]))
            out[low:end, tile] = lane_select(parts, per)


def unmix_kernel(per, place, plan, small, maps, inputs, grads, grad_inputs, grad_maps, total):
    m = pl.program_id(0)
    rows, width = inputs.shape
    states = maps.shape[1] // 2
    cumulative = small[:, :LANES]
    flat = cumulative.T
    mask = allowed_mask(rows, place, plan, m, True)
    scores = dot_nt(maps[:, :states], maps[:, states:], highest)
    lane = lax.broadcasted_iota(jnp.int32, (LANES, LANES), 1)
    total[...] = jnp.zeros_like(total)
    for at in range(0, width, LANES):
        tile = slice(at, at + LANES)
        for low in range(0, rows, LANES):
            end = low + LANES
            later = grads[low:, tile]
            parts = []
            gathered_sum = total[low:end, low:]
            for sub in range(per):
                head = at // LANES * per + sub
                decay = jnp.exp(
                    (flat[head : head + 1, low:] - cumulative[low:end, head : head + 1])
                    + mask[low:end, low:]
                )
                mixing = (decay * scores[low:end, low:]).astype(bf16)
                parts.append(dot(mixing, later))
                inside = (lane // (LANES // per)) == sub
                own = jnp.where(inside, inputs[low:end, tile].astype(f32), 0.0).astype(bf16)
                gathered_sum = gathered_sum + decay * dot_nt(own, later)
            total[low:end, low:] = gathered_sum
            grad_inputs[low:end, tile] = lane_select(parts, per)
    grad_scores = total[...].astype(bf16)
    grad_maps[:, :states] = dot(grad_scores, maps[:, states:].astype(bf16))
    grad_maps[:, states:] = dot_tn(grad_scores, maps[:, :states].astype(bf16))


def inflow_of(cumulative, rows, place, plan, m):
    here = segment_of(column_position(rows, place), plan, place, m)
    before = segment_of(place[2] - 1, plan, place, m)
    return (here == before).astype(f32) * jnp.exp(cumulative)


def gated_kernel(
    place, plan, small, maps, mixed, entering, conv_out, gate, grad_y, gain, skip, spread, scanned, scaled_y, sums
):
    m = pl.program_id(0)
    rows, width = mixed.shape
    states = maps.shape[1] // 2
    inflow = both_parts(inflow_of(small[:, :LANES], rows, place, plan, m))
    output_map = maps[:, states:].astype(bf16)
    square = jnp.zeros((rows, LANES), f32)
    product = jnp.zeros((rows, LANES), f32)
    for at in range(0, width, LANES):
        tile = slice(at, at + LANES)
        carried = dot(output_map, entering[0, :states, tile]) * dot(inflow, spread[:, tile])
        scan = mixed[:, tile] + carried
        scanned[:, tile] = scan
        conv = conv_out[:, tile]
        gates = gate[:, tile]
        gated = (scan + skip[:, tile] * (conv * jax.nn.sigmoid(conv))) * (gates * jax.nn.sigmoid(gates))
        square = square + gated * gated
        scaled = gain[:, tile] * gated
        put_deal_rows(scaled_y, tile, scaled)
        product = product + grad_y[:, tile] * scaled
    ones = jnp.ones((HALO, LANES), f32)
    pick = lax.broadcasted_iota(jnp.int32, (HALO, rows), 0)
    sums[0] = jnp.where(pick == 0, dot_nt(ones, square, highest), dot_nt(ones, product, highest))


def ungated_kernel(
    inner_all, place, plan, small, maps, scanned, conv_out, gate, grad_y, sums, gain, skip, spread,
    normed_y_t, grads, grad_gate, local, row_part, grad_gain, grad_skip,
):
    m = pl.program_id(0)
    rows, width = scanned.shape
    states = maps.shape[1] // 2
    row = lax.broadcasted_iota(jnp.int32, (rows, rows), 0)
    col = lax.broadcasted_iota(jnp.int32, (rows, rows), 1)
    columns = dot_nt((row == col).astype(f32), sums[0], highest)
    inv = lax.rsqrt(columns[:, :1] / inner_all + epsilon)
    pull = inv * inv * inv * (columns[:, 1:2] / inner_all)
    cumulative = small[:, :LANES]
    inflow = both_parts(inflow_of(cumulative, rows, place, plan, m))
    before = segment_of(place[2] - 1, plan, place, m)
    last = segment_of(place[2] + rows - 1, plan, place, m)
    through = (last == before).astype(f32) * jnp.exp(cumulative[rows - 1 :, :])
    through_parts = both_parts(jnp.broadcast_to(through, (STATE_PAD, LANES)))
    output_map_t = maps[:, states:].T.astype(bf16)

    @pl.when(m == 0)
    def _():
        grad_gain[...] = jnp.zeros_like(grad_gain)
        grad_skip[...] = jnp.zeros_like(grad_skip)

    product = jnp.zeros((rows, LANES), f32)
    for at in range(0, width, LANES):
        tile = slice(at, at + LANES)
        conv = conv_out[:, tile]
        heads_x = conv * jax.nn.sigmoid(conv)
        mixer = scanned[:, tile] + skip[:, tile] * heads_x
        gates = gate[:, tile]
        logistic = jax.nn.sigmoid(gates)
        act = gates * logistic
        gated = mixer * act
        normed = gated * inv
        normed_y_t[tile, :] = (normed * gain[:, tile]).T.astype(bf16)
        grad = grad_y[:, tile]
        grad_gain[:, tile] += jnp.sum(grad * normed, axis=0, keepdims=True)
        grad_gated = inv * (grad * gain[:, tile]) - gated * pull
        grad_mixer = grad_gated * act
        grads[:, tile] = grad_mixer.astype(bf16)
        grad_skip[:, tile] += jnp.sum(grad_mixer * heads_x, axis=0, keepdims=True)
        grad_gates = grad_gated * mixer * (logistic * (1.0 + gates * (1.0 - logistic)))
        grad_gate[:, tile] = grad_gates.astype(bf16)
        product = product + grad_gates * gates
        weighted = (grad_mixer * dot(inflow, spread[:, tile])).astype(bf16)
        local[0, :states, tile] = dot(output_map_t, weighted).astype(bf16)
        local[0, states:, tile] = dot(through_parts, spread[:, tile]).astype(bf16)
    row_part[0] = dot_nt(jnp.ones((HALO, LANES), f32), product, highest)


def unscan_kernel(
    place, plan, small, maps, scanned, conv_out, inputs, grads, grad_inputs, grad_maps, entering, leaving,
    skip, scale, spread, grad_conv_out, grad_step, grad_bias, grad_heads,
):
    m = pl.program_id(0)
    rows, width = scanned.shape
    states = maps.shape[1] // 2
    cumulative, step, pre = (small[:, k * LANES : (k + 1) * LANES] for k in range(3))
    here = segment_of(column_position(rows, place), plan, place, m)
    before = segment_of(place[2] - 1, plan, place, m)
    last = segment_of(place[2] + rows - 1, plan, place, m)
    ending = cumulative[rows - 1 :, :]
    fading = both_parts((here == last).astype(f32) * jnp.exp(ending - cumulative))
    inflow = both_parts((here == before).astype(f32) * jnp.exp(cumulative))
    through = (last == before).astype(f32) * jnp.exp(ending)
    step_parts = both_parts(step)
    input_map = maps[:, :states].astype(bf16)

    @pl.when(m == 0)
    def _():
        grad_bias[...] = jnp.zeros_like(grad_bias)
        grad_heads[...] = jnp.zeros_like(grad_heads)

    grad_in, grad_out = grad_maps[:, :states], grad_maps[:, states:]
    grad_cum = jnp.zeros((rows, LANES), f32)
    grad_own = jnp.zeros((rows, LANES), f32)
    ends = jnp.zeros((HALO, LANES), f32)
    for at in range(0, width, LANES):
        tile = slice(at, at + LANES)
        spread_tile = spread[:, tile]
        leave, enter = leaving[0, :states, tile], entering[0, :states, tile]
        fade = dot(fading, spread_tile)
        pulled = fade * dot(input_map, leave)
        values = inputs[:, tile].astype(f32)
        grad = grads[:, tile].astype(f32)
        total = grad_inputs[:, tile] + pulled
        faded = (values * fade).astype(bf16)
        weighted = (grad * dot(inflow, spread_tile)).astype(bf16)
        grad_in = grad_in + dot_nt(faded, leave)
        grad_out = grad_out + dot_nt(weighted, enter)
        conv = conv_out[:, tile]
        logistic = jax.nn.sigmoid(conv)
        heads_x = conv * logistic
        first = both_parts(grad * scanned[:, tile] - values * total)
        second = both_parts(total * heads_x)
        grad_cum = grad_cum + dot_nt(first[:, :LANES], spread[:LANES, tile]) + dot_nt(
            first[:, LANES:], spread[:LANES, tile]
        )
        grad_own = grad_own + dot_nt(second[:, :LANES], spread[:LANES, tile]) + dot_nt(
            second[:, LANES:], spread[:LANES, tile]
        )
        fade_sum = jnp.sum(values * pulled, axis=0, keepdims=True)
        through_sum = jnp.sum(leave.astype(f32) * enter.astype(f32), axis=0, keepdims=True)
        pick = lax.broadcasted_iota(jnp.int32, (HALO, LANES), 0)
        edge = both_parts(jnp.where(pick == 0, fade_sum, through_sum))
        ends = ends + dot_nt(edge[:, :LANES], spread[:LANES, tile]) + dot_nt(
            edge[:, LANES:], spread[:LANES, tile]
        )
        grad_x = total * dot(step_parts, spread_tile) + skip[:, tile] * grad
        result = grad_x * (logistic * (1.0 + conv * (1.0 - logistic)))
        grad_conv_out[:, tile] = result
        grad_bias[:, tile] += jnp.sum(result, axis=0, keepdims=True)
    for values, start in ((grad_in, width), (grad_out, width + states)):
        conv = conv_out[:, start : start + states]
        result = values * silu_slope(conv)
        grad_conv_out[:, start : start + states] = result
        grad_bias[:, start : start + states] += jnp.sum(result, axis=0, keepdims=True)
    row = lax.broadcasted_iota(jnp.int32, (rows, rows), 0)
    col = lax.broadcasted_iota(jnp.int32, (rows, rows), 1)
    upper = (row <= col).astype(f32)
    grad_rate = dot(upper, grad_cum, highest) + (ends[:1] + through * ends[1:2])
    rate = step * scale[...]
    grad_pre = (grad_rate * scale[...] + grad_own) * jax.nn.sigmoid(pre)
    grad_step[...] = grad_pre
    grad_heads[0:1, :] += jnp.sum(grad_rate * rate, axis=0, keepdims=True)
    grad_heads[1:2, :] += jnp.sum(grad_pre, axis=0, keepdims=True)


def unconv_kernel(
    place, plan, pre, halo, grad_out, after_rows, grad_step, row_part, taps, grad_pre, row_sums, grad_taps,
    extended, extended_grad,
):
    m = pl.program_id(0)
    rows = pre.shape[0]
    channels = grad_out.shape[1]
    taps_total = taps.shape[0]
    here = segment_of(column_position(rows, place), plan, place, m)
    behind, ahead = [], []
    for tap in range(taps_total):
        lag = taps_total - 1 - tap
        behind.append((segment_of(column_position(rows, place, -lag), plan, place, m) == here).astype(f32))
        ahead.append((segment_of(column_position(rows, place, lag), plan, place, m) == here).astype(f32))

    @pl.when(m == 0)
    def _():
        grad_taps[...] = jnp.zeros_like(grad_taps)

    total = jnp.zeros((rows, LANES), f32)
    for at in range(0, channels, LANES):
        tile = slice(at, at + LANES)
        extended[:HALO, :] = halo[0, :, tile]
        extended[HALO:, :] = pre[:, tile]
        grad = grad_out[:, tile]
        extended_grad[:rows, :] = grad
        extended_grad[rows:, :] = after_rows[0, :, tile]
        result = jnp.zeros((rows, LANES), f32)
        for tap in range(taps_total):
            lag = taps_total - 1 - tap
            result = result + taps[tap : tap + 1, tile] * extended_grad[lag : lag + rows, :] * ahead[tap]
            begin = HALO - lag
            product = grad * extended[begin : begin + rows, :] * behind[tap]
            grad_taps[tap : tap + 1, tile] += jnp.sum(product, axis=0, keepdims=True)
        grad_pre[:, tile] = result.astype(bf16)
        total = total + result * pre[:, tile]
    grad_pre[:, channels:] = grad_step[...].astype(bf16)
    total = total + grad_step[...] * pre[:, channels : channels + LANES]
    row_sums[0] = row_part[0] + dot_nt(jnp.ones((HALO, LANES), f32), total, highest)


def rows_kernel(first, second, weight, out):
    cut = weight.shape[1] - second.shape[1]
    result = dot_nt(first[...], weight[:, : first.shape[1]]) + dot_nt(second[...], weight[:, cut:])
    put_deal_rows(out.at[0], slice(None), result)


def rows_gradient(first, second, weight, quarters, senders, count):
    total = first.shape[0]
    start, stride, number = quarters
    size = lax.axis_size("head")
    width = weight.shape[0] // size
    rows = total // count
    row_block = lambda array: (array, (rows, array.shape[1]), lambda q, m: (m, 0))
    shape = (number, senders, count, rows // senders, width)
    block = (1, senders, 1, rows // senders, width)
    return call(
        rows_kernel, (number, count), (),
        [row_block(first), row_block(second)]
        + [(weight, (width, weight.shape[1]), lambda q, m: (start + stride * q, 0))],
        [(shape, bf16, block, lambda q, m: (q, 0, m, 0, 0))],
        flops=2 * total * (first.shape[1] + second.shape[1]) * width * number,
        bytes_accessed=(weight.size + (first.size + second.size) * number) * 2,
    )[0]


def state_kernel(depth, place, even_t, odd_t, grads, out):
    me = place[1]
    quarter = pl.program_id(0)
    height = out.shape[0]
    at = pl.ds(half_start(quarter, me, height, depth), height // 2)
    parts = [dot(left[at, :], grads[...]) for left in (even_t, odd_t)]
    odd = (me & 1) != 0
    count = height // depth
    halves = []
    for values in parts:
        half = [values[k * depth : (k + 1) * depth, :] for k in range(count // 2)]
        bit = 1
        while bit < count // 2:
            flip = ((me >> 1) & bit) != 0
            half = [jnp.where(flip, half[k ^ bit], half[k]) for k in range(len(half))]
            bit *= 2
        halves.append(half)
    for k in range(count // 2):
        base = 2 * k * depth
        out[base : base + depth, :] = jnp.where(odd, halves[1][k], halves[0][k]).astype(bf16)
        out[base + depth : base + 2 * depth, :] = jnp.where(odd, halves[0][k], halves[1][k]).astype(bf16)


def out_kernel(left, right, out):
    depth = out.shape[2]
    for block in range(out.shape[0]):
        out[block] = dot(left[...], right[:, block * depth : (block + 1) * depth]).astype(bf16)


def sent_kernel(columns, count, left, *refs):
    rights, out = refs[:count], refs[count]
    for which, source, target, size in columns:
        out[:, target : target + size] = dot(left[...], rights[which][:, source : source + size]).astype(bf16)


def kept_kernel(columns, count, cut, left, *refs):
    rights, other, outs = refs[:count], refs[count], refs[count + 1 :]
    step = pl.program_id(0)
    high, odd = step >= pl.num_programs(0) // 2, lax.rem(step, 2) == 1
    for which, source, target, size in columns:
        result = dot(left[...], rights[which][:, source : source + size])
        result = (result + other[:, target : target + size].astype(f32)).astype(bf16)
        if target < cut:
            keep, send, sending, start = outs[0], outs[1], high, target
        else:
            keep, send, sending, start = outs[2], outs[3], odd, target - cut
        tile = slice(start, start + size)

        @pl.when(sending)
        def _():
            send[:, tile] = result

        @pl.when(jnp.logical_not(sending))
        def _():
            keep[:, tile] = result


def total_kernel(targets, *refs):
    ins, outs = refs[:2], refs[2:]
    for out, (which, source, target, size) in zip([outs[t[0]] for t in targets], [t[1] for t in targets]):
        tile = slice(source, source + size)
        out[:, target : target + size] = ins[which][:, tile].astype(f32)


def weight_gradient_sent(odd_t, rights, columns, depth):
    total = odd_t.shape[1]
    width = max(target + size for _, _, target, size in columns)
    (sent,) = call(
        functools.partial(sent_kernel, columns, len(rights)), (odd_t.shape[0] // depth,), (),
        [(odd_t, (depth, total), lambda l: (l, 0))] + [entire(right) for right in rights],
        [((odd_t.shape[0], width), bf16, (depth, width), lambda l: (l, 0))],
        flops=2 * odd_t.shape[0] * total * width,
        bytes_accessed=odd_t.shape[0] * (total + width) * 2 + sum(right.size for right in rights) * 2,
    )
    return sent, swapped(sent, "seq", 1)


def weight_gradient(line, other, even_t, got, rights, columns, cut, results, depth):
    blocks = even_t.shape[0] // depth
    total = even_t.shape[1]
    width = got.shape[1]
    left = lambda array: (array, (depth, total), lambda l: (l, 0))
    flops = 2 * even_t.shape[0] * total * width
    moved = even_t.shape[0] * (total + width) * 2 + sum(right.size for right in rights) * 2
    top = blocks // 2
    rows = even_t.shape[0] // 2
    half = lambda size, index: ((rows, size), bf16, (depth, size), index)
    mine = call(
        functools.partial(kept_kernel, columns, len(rights), cut), (blocks,), (),
        [left(even_t)] + [entire(right) for right in rights] + [(got, (depth, width), lambda l: (l, 0))],
        [
            half(cut, lambda l: (jnp.minimum(l, top - 1), 0)),
            half(cut, lambda l: (jnp.maximum(l - top, 0), 0)),
            half(width - cut, lambda l: (l // 2, 0)),
            half(width - cut, lambda l: (l // 2, 0)),
        ],
        flops=flops, bytes_accessed=moved,
    )
    links = axis_bits("seq")[1:]
    labels = [bit << 1 for bit in range(blocks)]
    *mine, other = line.advance(*mine, other)
    parts = [
        Scattered(mine[0], mine[1], [x for x in labels if not x & links[-1]], links[::-1]),
        Scattered(mine[2], mine[3], [x for x in labels if not x & links[0]], links),
    ]
    while parts[0].left:
        for part in parts:
            part.advance()
        for part, pair in zip(parts, line.advance(*[part.pair for part in parts])):
            part.pair = pair
    first, second = [part.finish() for part in parts]
    targets = [(at, column) for at, (_, parts) in enumerate(results) for column in parts]
    return *call(
        functools.partial(total_kernel, targets), (1,), (), [entire(a) for a in first + second],
        [((depth, size), f32, (depth, size), lambda *_: (0, 0)) for size, _ in results],
        bytes_accessed=depth * width * 8,
    ), other


def per_device(
    tokens,
    cotangent,
    lengths,
    deal_order,
    norm_gain,
    proj_gate,
    proj_inner,
    proj_state,
    proj_step,
    conv_inner,
    conv_inner_bias,
    conv_state,
    conv_state_bias,
    step_bias,
    decay_log,
    skip_gain,
    inner_gain,
    proj_out,
):
    batch_count = lengths.shape[0]
    rows_local, width_own = tokens.shape
    tok_dev = rows_local // batch_count
    seq_index = lax.axis_index("seq")
    head_index = lax.axis_index("head")
    seq_size = lax.axis_size("seq")
    head_size = lax.axis_size("head")
    heads_own = proj_step.shape[1]
    inner_own = proj_inner.shape[1]
    head_width = inner_own // heads_own
    states = proj_state.shape[1] // 2
    taps_total = conv_inner.shape[0]
    width_all = width_own * head_size
    inner_all = inner_own * head_size
    depth = width_all // seq_size
    channels = inner_own + 2 * states
    per = LANES // head_width
    rows = tok_dev
    grid = (batch_count,)

    place = jnp.stack(
        [head_index, seq_index, seq_index * tok_dev, jnp.int32(tok_dev * seq_size)]
    ).astype(jnp.int32)
    plan = (jnp.cumsum(lengths, axis=1) - lengths).astype(jnp.int32)
    scalars = (place, plan)

    piece = tok_dev // seq_size
    dealt_row = deal_order.reshape(batch_count, seq_size, piece) + (
        jnp.arange(batch_count, dtype=jnp.int32) * tok_dev
    )[:, None, None]
    picks = (
        jnp.transpose(dealt_row, (1, 0, 2)).reshape(rows_local, 1) == jnp.arange(rows_local)[None, :]
    ).astype(bf16)
    deal_shape = (seq_size, batch_count, piece, width_own)

    def dealt(values):
        values = dot(picks, values).astype(bf16).reshape(seq_size, batch_count * piece, width_own)
        values = lax.all_to_all(values, "seq", split_axis=0, concat_axis=0, tiled=True)
        return values.reshape(deal_shape)

    def returned(values):
        values = values.reshape(seq_size, batch_count * piece, width_own)
        values = lax.all_to_all(values, "seq", split_axis=0, concat_axis=0, tiled=True)
        return dot_tn(picks, values.reshape(rows_local, width_own)).astype(bf16)

    deal_tokens = dealt(tokens)
    lines = LineGather(deal_tokens)
    lines.advance()
    deal_cot = dealt(cotangent)

    full_in = lax.all_gather(
        jnp.concatenate(
            [proj_inner, proj_state, proj_step, jnp.zeros((depth, 2 * LANES - heads_own), bf16), proj_gate],
            axis=1,
        ),
        "seq", axis=0, tiled=True,
    )
    full_out = lax.all_gather(after(proj_out, lines.up, lines.down), "seq", axis=1, tiled=True)

    lines = lines.finish()
    normed, even_t, odd_t, inv_rms = all_features(deal_tokens, lines, place, norm_gain[None, :], depth)
    cot_lines = LineGather(after(deal_cot, lines[0][-1], lines[1][-1]))

    taps = jnp.concatenate([conv_inner, conv_state], axis=1)
    bias = jnp.concatenate([conv_inner_bias, conv_state_bias])[None, :]
    pad = LANES - heads_own
    step_bias_row = jnp.pad(step_bias, (0, pad))[None, :]
    scale = jnp.pad(-jnp.exp(decay_log), (0, pad))[None, :]
    spread = (
        jnp.arange(2 * LANES)[:, None] % LANES == jnp.arange(inner_own)[None, :] // head_width
    ).astype(bf16)
    skip = jnp.repeat(skip_gain, head_width)[None, :]
    gain = inner_gain[None, :]

    pre_width = channels + 2 * LANES
    (pre,) = cot_lines.advance(dot(normed, full_in[:, :pre_width]))
    halo = passed_along(pre.reshape(batch_count, tok_dev, -1)[:, tok_dev - HALO :], "seq", 1)
    gate = dot(normed, full_in[:, pre_width:])
    halo, gate = lax.optimization_barrier((halo, gate))
    conv_out, small, inputs, maps, fresh = call(
        functools.partial(conv_kernel, inner_own), grid, scalars,
        [per_row(pre, rows), per_step(halo)]
        + [entire(a) for a in (taps, bias, step_bias_row, scale, spread)],
        [
            row_out(rows_local, rows, channels, f32),
            row_out(rows_local, rows, 3 * LANES, f32),
            row_out(rows_local, rows, inner_own, bf16),
            row_out(rows_local, rows, 2 * states, f32),
            step_out(batch_count, (states + STATE_PAD, inner_own), bf16),
        ],
        scratch=[pltpu.VMEM((rows + HALO, LANES), f32)],
        flops=rows_local * inner_own * 2000, bytes_accessed=rows_local * inner_own * 12,
    )
    conv_out, small, inputs, maps, fresh = cot_lines.advance(conv_out, small, inputs, maps, fresh)
    scan_ins = [per_row(small, rows), per_row(maps, rows)]
    (mixed,) = call(
        functools.partial(mix_kernel, per), grid, scalars, scan_ins + [per_row(inputs, rows)],
        [row_out(rows_local, rows, inner_own, f32)],
        flops=rows_local * inner_own * 6000, bytes_accessed=rows_local * inner_own * 6,
    )
    cot_lines.advance()

    def with_cotangent(beside):
        cot_lines.ups[-1], cot_lines.downs[-1] = cot_lines.up, cot_lines.down = beside[1:]
        return cotangent_products(deal_cot, cot_lines.finish(), place, full_out)

    entering, (mixed, _, _), (flat_cot, grad_y) = scan_before(
        fresh, states, False, [lambda: (mixed, cot_lines.up, cot_lines.down), with_cotangent]
    )
    vectors = [entire(gain), entire(skip), entire(spread)]
    scanned, scaled_y, sums = call(
        gated_kernel, grid, scalars,
        scan_ins
        + [per_row(mixed, rows), per_step(entering), per_row(conv_out, rows), per_row(gate, rows)]
        + [per_row(grad_y, rows)] + vectors,
        [
            row_out(rows_local, rows, inner_own, f32),
            deal_out(seq_size, batch_count, piece, inner_own, bf16),
            step_out(batch_count, (HALO, rows), f32),
        ],
        flops=rows_local * inner_own * 1500, bytes_accessed=rows_local * inner_own * 20,
    )
    out_rows = dot(scaled_y.reshape(rows_local, inner_own), full_out).astype(bf16)
    sums = sums + swapped(sums, "head", 1)
    for bit in axis_bits("head")[1:]:
        other, out_rows = lax.optimization_barrier((swapped(sums, "head", bit), out_rows))
        sums = sums + other
    branch = lax.psum_scatter(
        out_rows.reshape(deal_shape[:3] + (width_all,)), "head", scatter_dimension=3, tiled=True
    )

    def deal_column(values):
        return jnp.transpose(values.reshape(batch_count, seq_size, piece), (1, 0, 2))[..., None]

    inner_inv = deal_column(lax.rsqrt(sums[:, 0, :] / inner_all + epsilon))
    normed_y_t, grads, grad_gate, local, row_part, grad_gain, grad_skip = call(
        functools.partial(ungated_kernel, inner_all), grid, scalars,
        scan_ins
        + [per_row(array, rows) for array in (scanned, conv_out, gate, grad_y)]
        + [per_step(sums)] + vectors,
        [((inner_own, rows_local), bf16, (inner_own, rows), lambda m, *_: (0, m))]
        + [row_out(rows_local, rows, inner_own, bf16)] * 2
        + [step_out(batch_count, (states + STATE_PAD, inner_own), bf16)]
        + [step_out(batch_count, (HALO, rows), f32)]
        + [sum_out((1, inner_own))] * 2,
        flops=rows_local * inner_own * 2000, bytes_accessed=rows_local * inner_own * 24,
    )
    grad_inputs, grad_maps = call(
        functools.partial(unmix_kernel, per), grid, scalars,
        scan_ins + [per_row(inputs, rows), per_row(grads, rows)],
        [row_out(rows_local, rows, inner_own, f32), row_out(rows_local, rows, 2 * states, f32)],
        scratch=[pltpu.VMEM((rows, rows), f32)],
        flops=rows_local * inner_own * 12000, bytes_accessed=rows_local * inner_own * 8,
    )
    (grad_out,) = call(
        out_kernel, (1,), (), [entire(normed_y_t), entire(flat_cot)],
        [sum_out((seq_size, inner_own, depth), bf16)],
        flops=2 * rows_local * inner_own * width_all, bytes_accessed=rows_local * width_all * 6,
    )
    leaving, grad_inputs, grad_out = scan_before(
        local, states, True, [lambda: grad_inputs, lambda _: grad_out]
    )

    grad_out = lax.all_to_all(grad_out, "seq", split_axis=0, concat_axis=0, tiled=True)
    grad_conv_out, grad_step, grad_bias, grad_heads = call(
        unscan_kernel, grid, scalars,
        scan_ins
        + [per_row(a, rows) for a in (scanned, conv_out, inputs, grads, grad_inputs, grad_maps)]
        + [per_step(entering), per_step(leaving), entire(skip), entire(scale), entire(spread)],
        [
            row_out(rows_local, rows, channels, f32),
            row_out(rows_local, rows, LANES, f32),
            sum_out((1, channels)),
            sum_out((HALO, LANES)),
        ],
        flops=rows_local * inner_own * 4000, bytes_accessed=rows_local * inner_own * 28,
    )
    after_rows = passed_along(grad_conv_out.reshape(batch_count, tok_dev, channels)[:, :HALO], "seq", -1)
    after_rows, branch = lax.optimization_barrier((after_rows, branch))
    grad_pre, row_dots, grad_taps = call(
        unconv_kernel, grid, scalars,
        [per_row(pre, rows), per_step(halo), per_row(grad_conv_out, rows), per_step(after_rows)]
        + [per_row(grad_step, rows), per_step(row_part), entire(taps)],
        [
            row_out(rows_local, rows, channels + LANES, bf16),
            step_out(batch_count, (HALO, rows), f32),
            sum_out((taps_total, channels)),
        ],
        scratch=[pltpu.VMEM((rows + HALO, LANES), f32)] * 2,
        flops=rows_local * inner_own * 100, bytes_accessed=rows_local * inner_own * 14,
    )
    columns = [(0, 0, 0, inner_own), (1, 0, inner_own, inner_own), (0, channels, 2 * inner_own, LANES)]
    sent, got = weight_gradient_sent(odd_t, [grad_pre, grad_gate], columns, depth)
    (state_part,) = call(
        functools.partial(state_kernel, depth), (head_size,), (place,),
        [
            entire(even_t), entire(odd_t),
            (grad_pre, (rows_local, 2 * states), lambda m, *_: (0, inner_own // (2 * states))),
        ],
        [row_out(width_all, width_own, 2 * states, bf16)],
        flops=4 * width_all * rows_local * states, bytes_accessed=width_all * rows_local * 2,
    )
    shared_size = (taps_total + 1) * 2 * states
    headed = jnp.concatenate(
        [grad_taps[:, inner_own:].reshape(1, -1), grad_bias[:, inner_own:], row_dots[:, 0, :].reshape(1, -1)],
        axis=1,
    )
    headed = axis_sum(headed, "head")
    row_dots = deal_column(headed[0, shared_size:])
    state_part = state_part.reshape(head_size, width_own, 2 * states)
    last = head_size - 1
    state_line = LineScatter([state_part[0], state_part[last]], state_part[1:last])
    sent, got, headed = state_line.advance(sent, got, headed)
    grad_rows = lambda quarters: rows_gradient(
        after(grad_pre, sent), grad_gate, full_in, quarters, seq_size, batch_count
    )
    edges = grad_rows((0, last, 2))
    (edges,) = state_line.advance(edges)
    rows_line = LineScatter([edges[0], edges[1]], grad_rows((1, 1, last - 1)))
    grad_w_state = state_line.finish()

    lines_of = lambda values: jnp.pad(values, (0, -values.size % (2 * states))).reshape(-1, 2 * states)
    small = [
        grad_taps[:, :inner_own], grad_bias[:, :inner_own], grad_gain, grad_skip, grad_heads[:2],
        headed[0, :shared_size],
    ]
    small_rows = [lines_of(values.reshape(-1)) for values in small]
    together = jnp.concatenate([grad_w_state] + small_rows).astype(bf16)
    grad_w_state = axis_sum(together, "seq")
    grad_inner, grad_w_gate, grad_w_step, grad_w_state = weight_gradient(
        rows_line, grad_w_state, even_t, got, [grad_pre, grad_gate], columns,
        inner_own,
        [
            (inner_own, [(0, 0, 0, inner_own)]),
            (inner_own, [(1, 0, 0, inner_own)]),
            (LANES, [(1, inner_own, 0, LANES)]),
        ],
        depth,
    )
    grad_out = jnp.sum(grad_out.astype(f32), axis=0)
    out_back = returned((deal_tokens.astype(f32) + branch.astype(f32) * inner_inv).astype(bf16))
    rows_own = rows_line.finish()
    unit_own = deal_tokens.astype(f32) * inv_rms
    gain_own = lax.dynamic_slice_in_dim(norm_gain, head_index * width_own, width_own, 0)
    grad_norm_gain = jnp.sum(rows_own * unit_own, axis=(0, 1, 2))
    grad_rows_in = inv_rms * (rows_own * gain_own - unit_own * (row_dots / width_all))
    grad_back = returned((grad_rows_in + deal_cot.astype(f32)).astype(bf16))

    grad_norm_gain = axis_sum(grad_norm_gain[None, :], "seq")[0]
    summed = []
    at = width_own
    for values, lines in zip(small, small_rows):
        part = grad_w_state[at : at + lines.shape[0]].astype(f32).reshape(-1)[: values.size]
        summed.append(part.reshape(values.shape))
        at += lines.shape[0]
    state_sums = summed[5].reshape(taps_total + 1, 2 * states)
    state_own = 2 * states // head_size
    state_sums = lax.dynamic_slice_in_dim(state_sums, head_index * state_own, state_own, 1)
    return (
        out_back,
        grad_back,
        grad_norm_gain,
        grad_w_gate,
        grad_inner,
        grad_w_state[:width_own].astype(f32),
        grad_w_step[:, :heads_own],
        summed[0],
        summed[1][0],
        state_sums[:taps_total],
        state_sums[taps_total],
        summed[4][1, :heads_own],
        summed[4][0, :heads_own],
        jnp.sum(summed[3].reshape(heads_own, head_width), axis=1),
        summed[2][0],
        grad_out,
    )


def solution(mesh):
    return jax.shard_map(
        per_device,
        mesh=mesh,
        in_specs=(
            P("seq", "head"),
            P("seq", "head"),
            P(),
            P("seq"),
            P(),
            P("seq", "head"),
            P("seq", "head"),
            P("seq", None),
            P("seq", "head"),
            P(None, "head"),
            P("head"),
            P(),
            P(),
            P("head"),
            P("head"),
            P("head"),
            P("head"),
            P("head", "seq"),
        ),
        out_specs=(
            P("seq", "head"),
            P("seq", "head"),
            P("head"),
            P("seq", "head"),
            P("seq", "head"),
            P("head", None),
            P("seq", "head"),
            P(None, "head"),
            P("head"),
            P(None, "head"),
            P("head"),
            P("head"),
            P("head"),
            P("head"),
            P("head"),
            P("head", "seq"),
        ),
        check_vma=False,
    )
```

```python
import functools
import math
import jax
import jax.numpy as jnp
from jax import lax
from jax.experimental import pallas as pl
from jax.experimental.pallas import tpu as pltpu
from jax.sharding import PartitionSpec as P

epsilon = 1e-05
highest = lax.Precision.HIGHEST
f32 = jnp.float32
bf16 = jnp.bfloat16
LANES = 128
HALO = 8
STATE_PAD = 16
HBM_BYTES = 700000
VMEM_SPARE = 10 * 1024 * 1024


def swapped(value, axis, bit):
    return lax.ppermute(value, axis, [(i, i ^ bit) for i in range(lax.axis_size(axis))])


def axis_bits(axis):
    count = lax.axis_size(axis)
    return [1 << k for k in range(count.bit_length() - 1)]


def added(left, right):
    return (left.astype(f32) + right.astype(f32)).astype(left.dtype)


def after(value, *others):
    return lax.optimization_barrier((value, *others))[0]


def after_all(values, others):
    return lax.optimization_barrier((tuple(values), tuple(others)))[0]


class Scattered:
    def __init__(self, keep, send, labels, order):
        rows = keep.shape[0] // len(labels)
        self.pair = (keep.reshape(len(labels), rows, -1), send.reshape(len(labels), rows, -1))
        self.labels, self.left = labels, list(order)

    def send(self):
        self.got = swapped(self.pair[1], "seq", self.left.pop(0))

    def receive(self):
        total = added(self.pair[0], self.got)
        if not self.left:
            self.pair = (total,)
            return
        following, labels = self.left[0], self.labels
        keep_at = [at for at, label in enumerate(labels) if not label & following]
        send_at = [labels.index(labels[at] ^ following) for at in keep_at]
        kept = jnp.concatenate([total[at : at + 1] for at in keep_at])
        sent = jnp.concatenate([total[at : at + 1] for at in send_at])
        self.pair = (kept, sent)
        self.labels = [labels[at] for at in keep_at]

    def finish(self):
        return [self.pair[0][0]]


class LineGather:
    def __init__(self, own):
        self.size = lax.axis_size("head")
        self.up = self.down = own
        self.ups, self.downs = [], []

    def advance(self, *beside):
        step = len(self.ups) + 1
        if step < self.size:
            up = lax.ppermute(self.up, "head", [(i, i + 1) for i in range(step - 1, self.size - 1)])
            down = lax.ppermute(self.down, "head", [(i, i - 1) for i in range(1, self.size - step + 1)])
            if beside:
                (up, down), beside = lax.optimization_barrier(((up, down), beside))
            self.up, self.down = up, down
            self.ups.append(up)
            self.downs.append(down)
        return beside

    def finish(self):
        while len(self.ups) + 1 < self.size:
            self.advance()
        return self.ups, self.downs


class LineScatter:
    def __init__(self, edges, middle=None):
        self.size, self.here = lax.axis_size("head"), lax.axis_index("head")
        self.edges, self.middle = edges, middle
        self.up = self.down = None
        self.step = 0

    def block_of(self, at):
        last = self.size - 1
        inner = lax.dynamic_index_in_dim(self.middle, jnp.clip(at - 1, 0, last - 2), 0, keepdims=False)
        return jnp.where(at <= 0, self.edges[0], jnp.where(at >= last, self.edges[1], inner))

    def advance(self, *beside):
        self.step += 1
        step, size, here = self.step, self.size, self.here
        if step < size:
            if step == 1:
                up, down = self.edges[1], self.edges[0]
            else:
                up = added(self.block_of(here + size - step), self.up)
                down = added(self.block_of(here - size + step), self.down)
            up = lax.ppermute(up, "head", [(i, i + 1) for i in range(step)])
            down = lax.ppermute(down, "head", [(i, i - 1) for i in range(size - step, size)])
            if beside:
                (up, down), beside = lax.optimization_barrier(((up, down), beside))
            self.up, self.down = up, down
        return beside

    def finish(self):
        while self.step + 1 < self.size:
            self.advance()
        return self.up, self.down


def axis_sum(value, axis):
    for bit in axis_bits(axis):
        value = value + swapped(value, axis, bit)
    return value


def passed_along(value, axis, steps):
    count = lax.axis_size(axis)
    initial, last = (max(0, -steps), min(count, count - steps))
    return lax.ppermute(value, axis, [(source, source + steps) for source in range(initial, last)])


def dot(left, right, precision=None):
    return jnp.dot(left, right, preferred_element_type=f32, precision=precision)


def dot_nt(left, right, precision=None):
    return lax.dot_general(
        left, right, (((1,), (1,)), ((), ())), preferred_element_type=f32, precision=precision
    )


def dot_tn(left, right, precision=None):
    return lax.dot_general(
        left, right, (((0,), (0,)), ((), ())), preferred_element_type=f32, precision=precision
    )


def both_parts(values):
    high = values.astype(bf16)
    return jnp.concatenate([high, (values - high.astype(f32)).astype(bf16)], axis=1)


def silu_slope(values):
    logistic = jax.nn.sigmoid(values)
    return logistic * (1.0 + values * (1.0 - logistic))


def big(shape, dtype):
    return math.prod(shape) * jnp.dtype(dtype).itemsize > HBM_BYTES


def tiled_bytes(shape, dtype):
    *lead, rows, lanes = shape
    size = -(-rows // 8) * 8 * -(-lanes // LANES) * LANES * jnp.dtype(dtype).itemsize
    for count in lead:
        size *= count
    return size


def call(kernel, grid, scalars, ins, outs, scratch=(), flops=0, bytes_accessed=0):
    ins = [(streamed(a) if big(a.shape, a.dtype) else a, block, index) for a, block, index in ins]
    held = [block == array.shape for array, block, _ in ins]
    need = sum(
        (1 if whole else 2) * tiled_bytes(block, array.dtype) for (array, block, _), whole in zip(ins, held)
    )
    need += sum(2 * tiled_bytes(block, dtype) for _, dtype, block, _ in outs)
    need += sum(tiled_bytes(item.shape, item.dtype) for item in scratch)
    return pl.pallas_call(
        kernel,
        grid_spec=pltpu.PrefetchScalarGridSpec(
            num_scalar_prefetch=len(scalars),
            grid=grid,
            in_specs=[
                pl.BlockSpec(block, index, pipeline_mode=pl.Buffered(1) if whole else None)
                for (_, block, index), whole in zip(ins, held)
            ],
            out_specs=[pl.BlockSpec(block, index) for _, _, block, index in outs],
            scratch_shapes=list(scratch),
        ),
        out_shape=[
            (pltpu.HBM if big(shape, dtype) else jax.ShapeDtypeStruct)(shape, dtype) for shape, dtype, _, _ in outs
        ],
        compiler_params=pltpu.CompilerParams(vmem_limit_bytes=need + VMEM_SPARE),
        cost_estimate=pl.CostEstimate(
            flops=int(flops), bytes_accessed=int(bytes_accessed), transcendentals=0
        ),
    )(*scalars, *[array for array, _, _ in ins])


def streamed(array):
    return pltpu.with_memory_space_constraint(array, pltpu.HBM)


def per_row(array, rows):
    return (array, (rows,) + array.shape[1:], lambda m, *_: (m,) + (0,) * (array.ndim - 1))


def per_deal(array):
    return (array, (array.shape[0], 1) + array.shape[2:], lambda m, *_: (0, m, 0, 0))


def per_deal_of(array):
    return (array, (1, array.shape[1], 1) + array.shape[3:], lambda m, *_: (0, 0, m, 0, 0))


def deal_out(senders, count, rows, width, dtype):
    return ((senders, count, rows, width), dtype, (senders, 1, rows, width), lambda m, *_: (0, m, 0, 0))


def deal_rows(ref, tile):
    values = ref[:, 0, :, tile].astype(f32)
    return values.reshape(values.shape[0] * values.shape[1], values.shape[2])


def put_deal_rows(ref, tile, values):
    shape = (ref.shape[0], ref.shape[2], values.shape[1])
    ref[:, 0, :, tile] = values.reshape(shape).astype(ref.dtype)


def per_step(array):
    return (array, (1,) + array.shape[1:], lambda m, *_: (m,) + (0,) * (array.ndim - 1))


def entire(array):
    return (array, array.shape, lambda *_: (0,) * array.ndim)


def row_out(total, rows, width, dtype):
    return ((total, width), dtype, (rows, width), lambda m, *_: (m, 0))


def step_out(count, shape, dtype):
    return ((count,) + shape, dtype, (1,) + shape, lambda m, *_: (m,) + (0,) * len(shape))


def sum_out(shape, dtype=f32):
    return (shape, dtype, shape, lambda *_: (0,) * len(shape))


def joined(earlier, following, states):
    row = lax.broadcasted_iota(jnp.int32, earlier.shape, 0)
    return following[states : states + 1] * earlier + jnp.where(row < states, following, 0.0)


def chip_kernel(states, flags, own, other, total):
    for at in range(own.shape[0]):
        mine, theirs = own[at].astype(f32), other[at].astype(f32)
        later = flags[0] != 0
        first, second = jnp.where(later, theirs, mine), jnp.where(later, mine, theirs)
        total[at] = joined(first, second, states).astype(bf16)


def link_kernel(states, step, last, flags, *refs):
    total, other, refs = refs[0], refs[1], refs[2:]
    later = flags[step] != 0
    if step > 1:
        before, refs = refs[0], refs[1:]
    for at in range(total.shape[0]):
        mine, theirs = total[at].astype(f32), other[at].astype(f32)
        if step == 1:
            row = lax.broadcasted_iota(jnp.int32, mine.shape, 0)
            ahead = jnp.where(row < states, 0.0, 1.0)
            refs[0][at] = jnp.where(later, theirs, ahead).astype(bf16)
        else:
            ahead = before[at].astype(f32)
            refs[0][at] = jnp.where(later, joined(theirs, ahead, states), ahead).astype(bf16)
        if not last:
            first, second = jnp.where(later, theirs, mine), jnp.where(later, mine, theirs)
            refs[1][at] = joined(first, second, states).astype(bf16)


def enter_kernel(states, flags, ahead, ahead_other, sibling, entering):
    odd = flags[flags.shape[0] - 1] != 0
    half = ahead.shape[2]
    for at in range(ahead.shape[0]):
        mine, theirs = ahead[at], ahead_other[at]
        left, right = jnp.where(odd, theirs, mine), jnp.where(odd, mine, theirs)
        for start, values in ((0, left), (half, right)):
            values = values.astype(f32)
            near = sibling[at, :, start : start + half].astype(f32)
            entering[at, :, start : start + half] = jnp.where(
                flags[0] != 0, joined(values, near, states), values
            ).astype(bf16)


def scan_before(local, states, reverse, fillers):
    here = lax.axis_index("seq")
    bits = axis_bits("seq")
    count, height, width = local.shape
    passed = [((here & bit) == 0) if reverse else ((here & bit) != 0) for bit in bits]
    flags = jnp.stack(passed + [(here & 1) != 0]).astype(jnp.int32)
    whole = local.shape
    piece = (count, height, width // 2)
    at_step = lambda *_: (0, 0, 0)
    at_core = lambda _, flags: (0, 0, flags[len(bits)])
    half_out = (piece, bf16, piece, at_step)
    moved = local.size * 4
    sibling = swapped(local, "seq", 1)
    (total,) = call(
        functools.partial(chip_kernel, states), (1,), (flags,),
        [(local, piece, at_core), (sibling, piece, at_core)], [half_out], bytes_accessed=moved,
    )
    ahead, filled, beside = None, [], ()
    for step, bit in enumerate(bits[1:], 1):
        other = swapped(total, "seq", bit)
        if step <= len(fillers):
            other, value = lax.optimization_barrier((other, fillers[step - 1](*beside)))
            beside = (value,)
            filled.append(value)
        last = step == len(bits) - 1
        ins = [total, other] + ([] if ahead is None else [ahead])
        results = call(
            functools.partial(link_kernel, states, step, last), (1,), (flags,),
            [(array, piece, at_step) for array in ins], [half_out] * (1 if last else 2),
            bytes_accessed=moved,
        )
        ahead = results[0]
        total = None if last else results[1]
    ahead_other = swapped(ahead, "seq", 1)
    (entering,) = call(
        functools.partial(enter_kernel, states), (1,), (flags,),
        [(ahead, piece, at_step), (ahead_other, piece, at_step), (sibling, whole, at_step)],
        [(local.shape, bf16, whole, at_step)], bytes_accessed=moved * 2,
    )
    return [entering] + filled


def segment_of(position, plan, place, m):
    found = jnp.full(jnp.shape(position), -1, jnp.int32)
    for k in range(plan.shape[1]):
        found = found + (position >= plan[m, k]).astype(jnp.int32)
    return jnp.where(position >= place[3], -2, found)


def column_position(rows, place, shift=0):
    return place[2] + shift + lax.broadcasted_iota(jnp.int32, (rows, 1), 0)


def row_position(rows, place):
    return place[2] + lax.broadcasted_iota(jnp.int32, (1, rows), 1)


def by_core(values, me, depth):
    count = values.shape[1] // depth
    blocks = [values[:, k * depth : (k + 1) * depth] for k in range(count)]
    odd = (me & 1) != 0
    halves = []
    for at in (0, 1):
        straight, turned = blocks[at::2], blocks[1 - at :: 2]
        half = [jnp.where(odd, b, a) for a, b in zip(straight, turned)]
        bit = 1
        while bit < count // 2:
            flip = ((me >> 1) & bit) != 0
            half = [jnp.where(flip, half[k ^ bit], half[k]) for k in range(len(half))]
            bit *= 2
        halves.append(half[0] if len(half) == 1 else jnp.concatenate(half, axis=1))
    return halves


def half_start(quarter, me, width, depth):
    count = width // depth // 2
    return pl.multiple_of(((quarter * count) ^ ((me >> 1) & ~(count - 1))) * depth, width // 2)


def line_slot(own, ups, downs, z, step):
    if step == 0:
        return deal_rows(own, slice(None))
    up, down = ups[step - 1], downs[len(downs) - step]
    return jnp.where(z >= step, deal_rows(up, slice(None)), deal_rows(down, slice(None)))


def features_kernel(size, depth, place, *refs):
    own, ups, downs = refs[0], refs[1:size], refs[size : 2 * size - 1]
    gain, normed, even_t, odd_t, own_t, inverse = refs[2 * size - 1 :]
    z, me = place[0], place[1]
    width = own.shape[3]
    slots = [line_slot(own, ups, downs, z, step) for step in range(size)]
    square = sum(jnp.sum(slot * slot, axis=1, keepdims=True) for slot in slots)
    inv = lax.rsqrt(square / (width * size) + epsilon)
    put_deal_rows(inverse, slice(None), inv)
    for step, slot in enumerate(slots):
        quarter = lax.rem(z - step + size, size)
        place_at = pl.ds(pl.multiple_of(quarter * width, width), width)
        slot = slot * inv * gain[:, place_at]
        normed[:, place_at] = slot.astype(bf16)
        if step == 0:
            own_t[...] = slot.T.astype(bf16)
        first, second = by_core(slot, me, depth)
        at = pl.ds(half_start(quarter, me, width, depth), width // 2)
        even_t[at, :] = first.T.astype(bf16)
        odd_t[at, :] = second.T.astype(bf16)


def all_features(own, lines, place, gain, depth):
    senders, count, piece, width = own.shape
    rows = senders * piece
    total = rows * count
    size = lax.axis_size("head")
    ups, downs = lines
    half = width * size // 2
    outs = [row_out(total, rows, 2 * half, bf16)]
    outs += [((half, total), bf16, (half, rows), lambda m, *_: (0, m))] * 2
    outs.append(((width, total), bf16, (width, rows), lambda m, *_: (0, m)))
    outs.append(deal_out(senders, count, piece, 1, f32))
    return call(
        functools.partial(features_kernel, size, depth), (count,), (place,),
        [per_deal(array) for array in [own] + ups + downs] + [entire(gain)], outs,
        bytes_accessed=total * width * 2 * 15,
    )


def cotangent_kernel(size, place, *refs):
    own, ups, downs = refs[0], refs[1:size], refs[size : 2 * size - 1]
    weight, every, grad_y = refs[2 * size - 1 :]
    z = place[0]
    width = own.shape[3]
    total = None
    for step in range(size):
        slot = line_slot(own, ups, downs, z, step)
        quarter = lax.rem(z - step + size, size)
        place_at = pl.ds(pl.multiple_of(quarter * width, width), width)
        every[:, place_at] = slot.astype(bf16)
        part = dot_nt(slot.astype(bf16), weight[:, place_at])
        total = part if total is None else total + part
    grad_y[...] = total.astype(bf16)


def cotangent_products(own, lines, place, weight):
    senders, count, piece, width = own.shape
    rows = senders * piece
    total = rows * count
    size = lax.axis_size("head")
    ups, downs = lines
    return call(
        functools.partial(cotangent_kernel, size), (count,), (place,),
        [per_deal(array) for array in [own] + ups + downs] + [entire(weight)],
        [
            row_out(total, rows, width * size, bf16),
            row_out(total, rows, weight.shape[0], bf16),
        ],
        flops=2 * total * width * size * weight.shape[0],
        bytes_accessed=total * width * 2 * 11 + weight.size * 2 + total * weight.shape[0] * 4,
    )


def conv_kernel(
    width, place, plan, pre, halo, taps, bias, step_bias, scale, spread, conv_out, small, inputs, maps, fresh,
    extended,
):
    m = pl.program_id(0)
    rows = pre.shape[0]
    states = maps.shape[1] // 2
    taps_total = taps.shape[0]
    here = segment_of(column_position(rows, place), plan, place, m)
    same = [
        (segment_of(column_position(rows, place, tap + 1 - taps_total), plan, place, m) == here).astype(f32)
        for tap in range(taps_total)
    ]
    before = segment_of(place[2] - 1, plan, place, m)
    last = segment_of(place[2] + rows - 1, plan, place, m)

    step_pre = pre[:, width + 2 * states : width + 2 * states + LANES] + step_bias[...]
    rest = jnp.exp(-jnp.abs(step_pre))
    series = rest * (
        1.0 - rest * (1 / 2 - rest * (1 / 3 - rest * (1 / 4 - rest * (1 / 5 - rest * (1 / 6)))))
    )
    step = jnp.maximum(step_pre, 0.0) + jnp.where(rest < 0.03, series, jnp.log(1.0 + rest))
    row = lax.broadcasted_iota(jnp.int32, (rows, rows), 0)
    col = lax.broadcasted_iota(jnp.int32, (rows, rows), 1)
    lower = (row >= col).astype(f32)
    cumulative = dot(lower, step * scale[...], highest)
    small[:, :LANES] = cumulative
    small[:, LANES : 2 * LANES] = step
    small[:, 2 * LANES :] = step_pre
    ending = cumulative[rows - 1 :, :]
    fading = (here == last).astype(f32) * jnp.exp(ending - cumulative)
    through = (last == before).astype(f32) * jnp.exp(ending)
    step_parts, fading_parts = both_parts(step), both_parts(fading)
    through_parts = both_parts(jnp.broadcast_to(through, (STATE_PAD, LANES)))

    def conv(at):
        tile = slice(at, at + LANES)
        extended[:HALO, :] = halo[0, :, tile]
        extended[HALO:, :] = pre[:, tile]
        result = jnp.broadcast_to(bias[:, tile], (rows, LANES))
        for tap in range(taps_total):
            start = HALO + tap + 1 - taps_total
            result = result + taps[tap : tap + 1, tile] * extended[start : start + rows, :] * same[tap]
        conv_out[:, tile] = result
        return result * jax.nn.sigmoid(result)

    for at in range(0, 2 * states, LANES):
        maps[:, at : at + LANES] = conv(width + at)
    input_map_t = maps[:, :states].T.astype(bf16)
    for at in range(0, width, LANES):
        tile = slice(at, at + LANES)
        values = conv(at) * dot(step_parts, spread[:, tile])
        inputs[:, tile] = values.astype(bf16)
        faded = (values * dot(fading_parts, spread[:, tile])).astype(bf16)
        fresh[0, :states, tile] = dot(input_map_t, faded).astype(bf16)
        fresh[0, states:, tile] = dot(through_parts, spread[:, tile]).astype(bf16)


def allowed_mask(rows, place, plan, m, transposed):
    column = segment_of(column_position(rows, place), plan, place, m)
    across = segment_of(row_position(rows, place), plan, place, m)
    row = lax.broadcasted_iota(jnp.int32, (rows, rows), 0)
    col = lax.broadcasted_iota(jnp.int32, (rows, rows), 1)
    order = (row <= col) if transposed else (row >= col)
    return jnp.where(order & (column == across), 0.0, -1e30)


def lane_select(parts, per):
    lane = lax.broadcasted_iota(jnp.int32, parts[0].shape, 1)
    result = parts[0]
    for at in range(1, per):
        result = jnp.where(lane >= at * (LANES // per), parts[at], result)
    return result


def mix_kernel(per, place, plan, small, maps, inputs, out):
    m = pl.program_id(0)
    rows, width = inputs.shape
    states = maps.shape[1] // 2
    cumulative = small[:, :LANES]
    flat = cumulative.T
    mask = allowed_mask(rows, place, plan, m, False)
    scores = dot_nt(maps[:, states:], maps[:, :states], highest)
    for at in range(0, width, LANES):
        tile = slice(at, at + LANES)
        for low in range(0, rows, LANES):
            end = low + LANES
            parts = []
            for sub in range(per):
                head = at // LANES * per + sub
                decay = jnp.exp(
                    (cumulative[low:end, head : head + 1] - flat[head : head + 1, :end])
                    + mask[low:end, :end]
                )
                mixing = (decay * scores[low:end, :end]).astype(bf16)
                parts.append(dot(mixing, inputs[:end, tile]))
            out[low:end, tile] = lane_select(parts, per)


def unmix_kernel(per, place, plan, small, maps, inputs, grads, grad_inputs, grad_maps, total):
    m = pl.program_id(0)
    rows, width = inputs.shape
    states = maps.shape[1] // 2
    cumulative = small[:, :LANES]
    flat = cumulative.T
    mask = allowed_mask(rows, place, plan, m, True)
    scores = dot_nt(maps[:, :states], maps[:, states:], highest)
    lane = lax.broadcasted_iota(jnp.int32, (LANES, LANES), 1)
    total[...] = jnp.zeros_like(total)
    for at in range(0, width, LANES):
        tile = slice(at, at + LANES)
        for low in range(0, rows, LANES):
            end = low + LANES
            later = grads[low:, tile]
            parts = []
            gathered_sum = total[low:end, low:]
            for sub in range(per):
                head = at // LANES * per + sub
                decay = jnp.exp(
                    (flat[head : head + 1, low:] - cumulative[low:end, head : head + 1])
                    + mask[low:end, low:]
                )
                mixing = (decay * scores[low:end, low:]).astype(bf16)
                parts.append(dot(mixing, later))
                inside = (lane // (LANES // per)) == sub
                own = jnp.where(inside, inputs[low:end, tile].astype(f32), 0.0).astype(bf16)
                gathered_sum = gathered_sum + decay * dot_nt(own, later)
            total[low:end, low:] = gathered_sum
            grad_inputs[low:end, tile] = lane_select(parts, per)
    grad_scores = total[...].astype(bf16)
    grad_maps[:, :states] = dot(grad_scores, maps[:, states:].astype(bf16))
    grad_maps[:, states:] = dot_tn(grad_scores, maps[:, :states].astype(bf16))


def inflow_of(cumulative, rows, place, plan, m):
    here = segment_of(column_position(rows, place), plan, place, m)
    before = segment_of(place[2] - 1, plan, place, m)
    return (here == before).astype(f32) * jnp.exp(cumulative)


def gated_kernel(
    place, plan, small, maps, mixed, entering, conv_out, gate, grad_y, gain, skip, spread, scanned, scaled_y, sums
):
    m = pl.program_id(0)
    rows, width = mixed.shape
    states = maps.shape[1] // 2
    inflow = both_parts(inflow_of(small[:, :LANES], rows, place, plan, m))
    output_map = maps[:, states:].astype(bf16)
    square = jnp.zeros((rows, LANES), f32)
    product = jnp.zeros((rows, LANES), f32)
    for at in range(0, width, LANES):
        tile = slice(at, at + LANES)
        carried = dot(output_map, entering[0, :states, tile]) * dot(inflow, spread[:, tile])
        scan = mixed[:, tile] + carried
        scanned[:, tile] = scan
        conv = conv_out[:, tile]
        gates = gate[:, tile].astype(f32)
        gated = (scan + skip[:, tile] * (conv * jax.nn.sigmoid(conv))) * (gates * jax.nn.sigmoid(gates))
        square = square + gated * gated
        scaled = gain[:, tile] * gated
        put_deal_rows(scaled_y, tile, scaled)
        product = product + grad_y[:, tile].astype(f32) * scaled
    ones = jnp.ones((HALO, LANES), f32)
    pick = lax.broadcasted_iota(jnp.int32, (HALO, rows), 0)
    sums[0] = jnp.where(pick == 0, dot_nt(ones, square, highest), dot_nt(ones, product, highest))


def ungated_kernel(
    inner_all, place, plan, small, maps, scanned, conv_out, gate, grad_y, sums, gain, skip, spread,
    normed_y_t, grads, grad_gate, local, row_part, grad_gain, grad_skip,
):
    m = pl.program_id(0)
    rows, width = scanned.shape
    states = maps.shape[1] // 2
    row = lax.broadcasted_iota(jnp.int32, (rows, rows), 0)
    col = lax.broadcasted_iota(jnp.int32, (rows, rows), 1)
    columns = dot_nt((row == col).astype(f32), sums[0], highest)
    inv = lax.rsqrt(columns[:, :1] / inner_all + epsilon)
    pull = inv * inv * inv * (columns[:, 1:2] / inner_all)
    cumulative = small[:, :LANES]
    inflow = both_parts(inflow_of(cumulative, rows, place, plan, m))
    before = segment_of(place[2] - 1, plan, place, m)
    last = segment_of(place[2] + rows - 1, plan, place, m)
    through = (last == before).astype(f32) * jnp.exp(cumulative[rows - 1 :, :])
    through_parts = both_parts(jnp.broadcast_to(through, (STATE_PAD, LANES)))
    output_map_t = maps[:, states:].T.astype(bf16)

    @pl.when(m == 0)
    def _():
        grad_gain[...] = jnp.zeros_like(grad_gain)
        grad_skip[...] = jnp.zeros_like(grad_skip)

    product = jnp.zeros((rows, LANES), f32)
    for at in range(0, width, LANES):
        tile = slice(at, at + LANES)
        conv = conv_out[:, tile]
        heads_x = conv * jax.nn.sigmoid(conv)
        mixer = scanned[:, tile] + skip[:, tile] * heads_x
        gates = gate[:, tile].astype(f32)
        logistic = jax.nn.sigmoid(gates)
        act = gates * logistic
        gated = mixer * act
        normed = gated * inv
        normed_y_t[tile, :] = (normed * gain[:, tile]).T.astype(bf16)
        grad = grad_y[:, tile].astype(f32)
        grad_gain[:, tile] += jnp.sum(grad * normed, axis=0, keepdims=True)
        grad_gated = inv * (grad * gain[:, tile]) - gated * pull
        grad_mixer = grad_gated * act
        grads[:, tile] = grad_mixer.astype(bf16)
        grad_skip[:, tile] += jnp.sum(grad_mixer * heads_x, axis=0, keepdims=True)
        grad_gates = grad_gated * mixer * (logistic * (1.0 + gates * (1.0 - logistic)))
        grad_gate[:, tile] = grad_gates.astype(bf16)
        product = product + grad_gates * gates
        weighted = (grad_mixer * dot(inflow, spread[:, tile])).astype(bf16)
        local[0, :states, tile] = dot(output_map_t, weighted).astype(bf16)
        local[0, states:, tile] = dot(through_parts, spread[:, tile]).astype(bf16)
    row_part[0] = dot_nt(jnp.ones((HALO, LANES), f32), product, highest)


def unscan_kernel(
    place, plan, small, maps, scanned, conv_out, inputs, grads, grad_inputs, grad_maps, entering, leaving,
    skip, scale, spread, grad_conv_out, grad_step, grad_bias, grad_heads,
):
    m = pl.program_id(0)
    rows, width = scanned.shape
    states = maps.shape[1] // 2
    cumulative, step, pre = (small[:, k * LANES : (k + 1) * LANES] for k in range(3))
    here = segment_of(column_position(rows, place), plan, place, m)
    before = segment_of(place[2] - 1, plan, place, m)
    last = segment_of(place[2] + rows - 1, plan, place, m)
    ending = cumulative[rows - 1 :, :]
    fading = both_parts((here == last).astype(f32) * jnp.exp(ending - cumulative))
    inflow = both_parts((here == before).astype(f32) * jnp.exp(cumulative))
    through = (last == before).astype(f32) * jnp.exp(ending)
    step_parts = both_parts(step)
    input_map = maps[:, :states].astype(bf16)

    @pl.when(m == 0)
    def _():
        grad_bias[...] = jnp.zeros_like(grad_bias)
        grad_heads[...] = jnp.zeros_like(grad_heads)

    grad_in, grad_out = grad_maps[:, :states], grad_maps[:, states:]
    grad_cum = jnp.zeros((rows, LANES), f32)
    grad_own = jnp.zeros((rows, LANES), f32)
    ends = jnp.zeros((HALO, LANES), f32)
    for at in range(0, width, LANES):
        tile = slice(at, at + LANES)
        spread_tile = spread[:, tile]
        leave, enter = leaving[0, :states, tile], entering[0, :states, tile]
        fade = dot(fading, spread_tile)
        pulled = fade * dot(input_map, leave)
        values = inputs[:, tile].astype(f32)
        grad = grads[:, tile].astype(f32)
        total = grad_inputs[:, tile] + pulled
        faded = (values * fade).astype(bf16)
        weighted = (grad * dot(inflow, spread_tile)).astype(bf16)
        grad_in = grad_in + dot_nt(faded, leave)
        grad_out = grad_out + dot_nt(weighted, enter)
        conv = conv_out[:, tile]
        logistic = jax.nn.sigmoid(conv)
        heads_x = conv * logistic
        first = both_parts(grad * scanned[:, tile] - values * total)
        second = both_parts(total * heads_x)
        grad_cum = grad_cum + dot_nt(first[:, :LANES], spread[:LANES, tile]) + dot_nt(
            first[:, LANES:], spread[:LANES, tile]
        )
        grad_own = grad_own + dot_nt(second[:, :LANES], spread[:LANES, tile]) + dot_nt(
            second[:, LANES:], spread[:LANES, tile]
        )
        fade_sum = jnp.sum(values * pulled, axis=0, keepdims=True)
        through_sum = jnp.sum(leave.astype(f32) * enter.astype(f32), axis=0, keepdims=True)
        pick = lax.broadcasted_iota(jnp.int32, (HALO, LANES), 0)
        edge = both_parts(jnp.where(pick == 0, fade_sum, through_sum))
        ends = ends + dot_nt(edge[:, :LANES], spread[:LANES, tile]) + dot_nt(
            edge[:, LANES:], spread[:LANES, tile]
        )
        grad_x = total * dot(step_parts, spread_tile) + skip[:, tile] * grad
        result = grad_x * (logistic * (1.0 + conv * (1.0 - logistic)))
        grad_conv_out[:, tile] = result
        grad_bias[:, tile] += jnp.sum(result, axis=0, keepdims=True)
    for values, start in ((grad_in, width), (grad_out, width + states)):
        conv = conv_out[:, start : start + states]
        result = values * silu_slope(conv)
        grad_conv_out[:, start : start + states] = result
        grad_bias[:, start : start + states] += jnp.sum(result, axis=0, keepdims=True)
    row = lax.broadcasted_iota(jnp.int32, (rows, rows), 0)
    col = lax.broadcasted_iota(jnp.int32, (rows, rows), 1)
    upper = (row <= col).astype(f32)
    grad_rate = dot(upper, grad_cum, highest) + (ends[:1] + through * ends[1:2])
    rate = step * scale[...]
    grad_pre = (grad_rate * scale[...] + grad_own) * jax.nn.sigmoid(pre)
    grad_step[...] = grad_pre
    grad_heads[0:1, :] += jnp.sum(grad_rate * rate, axis=0, keepdims=True)
    grad_heads[1:2, :] += jnp.sum(grad_pre, axis=0, keepdims=True)


def unconv_kernel(
    place, plan, pre, halo, grad_out, after_rows, grad_step, row_part, taps, grad_pre, grad_state, row_sums,
    grad_taps, extended, extended_grad,
):
    m = pl.program_id(0)
    rows = pre.shape[0]
    channels = grad_out.shape[1]
    taps_total = taps.shape[0]
    here = segment_of(column_position(rows, place), plan, place, m)
    behind, ahead = [], []
    for tap in range(taps_total):
        lag = taps_total - 1 - tap
        behind.append((segment_of(column_position(rows, place, -lag), plan, place, m) == here).astype(f32))
        ahead.append((segment_of(column_position(rows, place, lag), plan, place, m) == here).astype(f32))

    @pl.when(m == 0)
    def _():
        grad_taps[...] = jnp.zeros_like(grad_taps)

    total = jnp.zeros((rows, LANES), f32)
    for at in range(0, channels, LANES):
        tile = slice(at, at + LANES)
        extended[:HALO, :] = halo[0, :, tile]
        extended[HALO:, :] = pre[:, tile]
        grad = grad_out[:, tile]
        extended_grad[:rows, :] = grad
        extended_grad[rows:, :] = after_rows[0, :, tile]
        result = jnp.zeros((rows, LANES), f32)
        for tap in range(taps_total):
            lag = taps_total - 1 - tap
            result = result + taps[tap : tap + 1, tile] * extended_grad[lag : lag + rows, :] * ahead[tap]
            begin = HALO - lag
            product = grad * extended[begin : begin + rows, :] * behind[tap]
            grad_taps[tap : tap + 1, tile] += jnp.sum(product, axis=0, keepdims=True)
        grad_pre[:, tile] = result.astype(bf16)
        total = total + result * pre[:, tile]
    grad_pre[:, channels:] = grad_step[...].astype(bf16)
    grad_state[...] = grad_pre[:, channels - grad_state.shape[1] : channels]
    total = total + grad_step[...] * pre[:, channels : channels + LANES]
    row_sums[0] = row_part[0] + dot_nt(jnp.ones((HALO, LANES), f32), total, highest)


def rows_kernel(quarters, first, second, *refs):
    for weight, out in zip(refs[:quarters], refs[quarters:]):
        cut = weight.shape[1] - second.shape[1]
        result = dot_nt(first[...], weight[:, : first.shape[1]]) + dot_nt(second[...], weight[:, cut:])
        put_deal_rows(out.at[0], slice(None), result)


def rows_gradient(first, second, weight, senders, count, edges):
    total = first.shape[0]
    size = lax.axis_size("head")
    width = weight.shape[0] // size
    rows = total // count
    flops = total * (first.shape[1] + second.shape[1]) * width * size
    moved = weight.size + (first.size + second.size) * size
    block = (1, senders, 1, rows // senders, width)
    if edges:
        shape = (1, senders, count, rows // senders, width)
        return call(
            functools.partial(rows_kernel, 2), (count,), (),
            [per_row(first, rows), per_row(second, rows)]
            + [(weight, (width, weight.shape[1]), lambda m, at=at: (at, 0)) for at in (0, size - 1)],
            [(shape, bf16, block, lambda m: (0, 0, m, 0, 0))] * 2, flops=flops, bytes_accessed=moved,
        )
    row_block = lambda array: (array, (rows, array.shape[1]), lambda q, m: (m, 0))
    return call(
        functools.partial(rows_kernel, 1), (size - 2, count), (),
        [row_block(first), row_block(second), (weight, (width, weight.shape[1]), lambda q, m: (q + 1, 0))],
        [
            (
                (size - 2, senders, count, rows // senders, width), bf16, block,
                lambda q, m: (q, 0, m, 0, 0),
            )
        ],
        flops=flops, bytes_accessed=moved,
    )[0]


def column_of(rows_form):
    rows = rows_form.shape[1]
    row = lax.broadcasted_iota(jnp.int32, (rows, rows), 0)
    col = lax.broadcasted_iota(jnp.int32, (rows, rows), 1)
    return dot_nt((row == col).astype(f32), rows_form, highest)[:, :1]


def output_kernel(inner_all, tokens, branch, sums, out):
    inv = lax.rsqrt(column_of(sums[0]) / inner_all + epsilon)
    every = slice(None)
    put_deal_rows(out, every, deal_rows(tokens, every) + deal_rows(branch, every) * inv)


def input_kernel(
    size, place, low, high, middle, up, down, tokens, cot, inverse, sums, gain, out, grad_gain
):
    every = slice(None)
    here = place[0]
    width = tokens.shape[3]
    own = jnp.where(
        here == 0,
        deal_rows(low.at[0], every),
        jnp.where(here == size - 1, deal_rows(high.at[0], every), deal_rows(middle.at[0], every)),
    )
    rows_own = own + deal_rows(up, every) + deal_rows(down, every)
    inv = deal_rows(inverse, every)
    unit = deal_rows(tokens, every) * inv
    own_gain = gain[:, pl.ds(pl.multiple_of(here * width, width), width)]
    total = column_of(sums[0]) / (width * size)
    put_deal_rows(out, every, inv * (rows_own * own_gain - unit * total) + deal_rows(cot, every))
    product = jnp.sum(rows_own * unit, axis=0, keepdims=True)

    @pl.when(pl.program_id(0) == 0)
    def _():
        grad_gain[...] = product

    @pl.when(pl.program_id(0) > 0)
    def _():
        grad_gain[...] += product


def out_kernel(left, right, out):
    out[...] = dot(left[...], right[...]).astype(bf16)


def sent_kernel(columns, count, left, *refs):
    rights, out = refs[:count], refs[count]
    for which, source, target, size in columns:
        out[:, target : target + size] = dot(left[...], rights[which][:, source : source + size]).astype(bf16)


def kept_kernel(columns, count, cut, left, *refs):
    rights, other, outs = refs[:count], refs[count], refs[count + 1 :]
    step = pl.program_id(0)
    high, odd = step >= pl.num_programs(0) // 2, lax.rem(step, 2) == 1
    for which, source, target, size in columns:
        result = dot(left[...], rights[which][:, source : source + size])
        result = (result + other[:, target : target + size].astype(f32)).astype(bf16)
        if target < cut:
            keep, send, sending, start = outs[0], outs[1], high, target
        else:
            keep, send, sending, start = outs[2], outs[3], odd, target - cut
        tile = slice(start, start + size)

        @pl.when(sending)
        def _():
            send[:, tile] = result

        @pl.when(jnp.logical_not(sending))
        def _():
            keep[:, tile] = result


def total_kernel(targets, *refs):
    ins, outs = refs[:2], refs[2:]
    for out, (which, source, target, size) in zip([outs[t[0]] for t in targets], [t[1] for t in targets]):
        tile = slice(source, source + size)
        out[:, target : target + size] = ins[which][:, tile].astype(f32)


def weight_gradient_sent(odd_t, rights, columns, depth):
    total = odd_t.shape[1]
    width = max(target + size for _, _, target, size in columns)
    (sent,) = call(
        functools.partial(sent_kernel, columns, len(rights)), (odd_t.shape[0] // depth,), (),
        [(odd_t, (depth, total), lambda l: (l, 0))] + [entire(right) for right in rights],
        [((odd_t.shape[0], width), bf16, (depth, width), lambda l: (l, 0))],
        flops=2 * odd_t.shape[0] * total * width,
        bytes_accessed=odd_t.shape[0] * (total + width) * 2 + sum(right.size for right in rights) * 2,
    )
    return sent


def weight_gradient_kept(even_t, got, rights, columns, cut, depth):
    blocks = even_t.shape[0] // depth
    total = even_t.shape[1]
    width = got.shape[1]
    top = blocks // 2
    rows = even_t.shape[0] // 2
    half = lambda size, index: ((rows, size), bf16, (depth, size), index)
    return call(
        functools.partial(kept_kernel, columns, len(rights), cut), (blocks,), (),
        [(even_t, (depth, total), lambda l: (l, 0))] + [entire(right) for right in rights]
        + [(got, (depth, width), lambda l: (l, 0))],
        [
            half(cut, lambda l: (jnp.minimum(l, top - 1), 0)),
            half(cut, lambda l: (jnp.maximum(l - top, 0), 0)),
            half(width - cut, lambda l: (l // 2, 0)),
            half(width - cut, lambda l: (l // 2, 0)),
        ],
        flops=2 * even_t.shape[0] * total * width,
        bytes_accessed=even_t.shape[0] * (total + width) * 2 + sum(right.size for right in rights) * 2,
    )


def weight_gradient_parts(mine):
    links = axis_bits("seq")[1:]
    labels = [bit << 1 for bit in range(2 ** len(links))]
    return [
        Scattered(mine[0], mine[1], [x for x in labels if not x & links[-1]], links[::-1]),
        Scattered(mine[2], mine[3], [x for x in labels if not x & links[0]], links),
    ]


def weight_gradient_total(parts, results, depth):
    ins = [array for part in parts for array in part.finish()]
    targets = [(at, column) for at, (_, columns) in enumerate(results) for column in columns]
    return call(
        functools.partial(total_kernel, targets), (1,), (), [entire(a) for a in ins],
        [((depth, size), f32, (depth, size), lambda *_: (0, 0)) for size, _ in results],
        bytes_accessed=sum(a.size for a in ins) * 6,
    )


def per_device(
    tokens,
    cotangent,
    lengths,
    deal_order,
    norm_gain,
    proj_gate,
    proj_inner,
    proj_state,
    proj_step,
    conv_inner,
    conv_inner_bias,
    conv_state,
    conv_state_bias,
    step_bias,
    decay_log,
    skip_gain,
    inner_gain,
    proj_out,
):
    batch_count = lengths.shape[0]
    rows_local, width_own = tokens.shape
    tok_dev = rows_local // batch_count
    seq_index = lax.axis_index("seq")
    head_index = lax.axis_index("head")
    seq_size = lax.axis_size("seq")
    head_size = lax.axis_size("head")
    heads_own = proj_step.shape[1]
    inner_own = proj_inner.shape[1]
    head_width = inner_own // heads_own
    states = proj_state.shape[1] // 2
    taps_total = conv_inner.shape[0]
    width_all = width_own * head_size
    inner_all = inner_own * head_size
    depth = width_all // seq_size
    channels = inner_own + 2 * states
    per = LANES // head_width
    rows = tok_dev
    grid = (batch_count,)

    place = jnp.stack(
        [head_index, seq_index, seq_index * tok_dev, jnp.int32(tok_dev * seq_size)]
    ).astype(jnp.int32)
    plan = (jnp.cumsum(lengths, axis=1) - lengths).astype(jnp.int32)
    scalars = (place, plan)

    piece = tok_dev // seq_size
    dealt_row = deal_order.reshape(batch_count, seq_size, piece) + (
        jnp.arange(batch_count, dtype=jnp.int32) * tok_dev
    )[:, None, None]
    picks = (
        jnp.transpose(dealt_row, (1, 0, 2)).reshape(rows_local, 1) == jnp.arange(rows_local)[None, :]
    ).astype(bf16)
    deal_shape = (seq_size, batch_count, piece, width_own)

    def dealt(values):
        values = dot(picks, values).astype(bf16).reshape(seq_size, batch_count * piece, width_own)
        values = lax.all_to_all(values, "seq", split_axis=0, concat_axis=0, tiled=True)
        return values.reshape(deal_shape)

    def sent_back(values):
        values = values.reshape(seq_size, -1, width_own)
        return lax.all_to_all(values, "seq", split_axis=0, concat_axis=0, tiled=True)

    def put_back(values):
        return dot_tn(picks, values.reshape(rows_local, width_own)).astype(bf16)

    deal_tokens = dealt(tokens)
    lines = LineGather(deal_tokens)
    lines.advance()
    deal_cot = dealt(cotangent)

    full_in = lax.all_gather(
        jnp.concatenate(
            [proj_inner, proj_state, proj_step, jnp.zeros((depth, 2 * LANES - heads_own), bf16), proj_gate],
            axis=1,
        ),
        "seq", axis=0, tiled=True,
    )
    full_out = lax.all_gather(after(proj_out, lines.up, lines.down), "seq", axis=1, tiled=True)

    lines = lines.finish()
    normed, even_t, odd_t, own_t, inv_rms = all_features(deal_tokens, lines, place, norm_gain[None, :], depth)
    cot_lines = LineGather(after(deal_cot, lines[0][-1], lines[1][-1]))

    taps = jnp.concatenate([conv_inner, conv_state], axis=1)
    bias = jnp.concatenate([conv_inner_bias, conv_state_bias])[None, :]
    pad = LANES - heads_own
    step_bias_row = jnp.pad(step_bias, (0, pad))[None, :]
    scale = jnp.pad(-jnp.exp(decay_log), (0, pad))[None, :]
    spread = (
        jnp.arange(2 * LANES)[:, None] % LANES == jnp.arange(inner_own)[None, :] // head_width
    ).astype(bf16)
    skip = jnp.repeat(skip_gain, head_width)[None, :]
    gain = inner_gain[None, :]

    pre_width = channels + 2 * LANES
    (pre,) = cot_lines.advance(dot(normed, full_in[:, :pre_width]))
    halo = passed_along(pre.reshape(batch_count, tok_dev, -1)[:, tok_dev - HALO :], "seq", 1)
    gate = dot(normed, full_in[:, pre_width:]).astype(bf16)
    halo, gate = lax.optimization_barrier((halo, gate))
    conv_out, small, inputs, maps, fresh = call(
        functools.partial(conv_kernel, inner_own), grid, scalars,
        [per_row(pre, rows), per_step(halo)]
        + [entire(a) for a in (taps, bias, step_bias_row, scale, spread)],
        [
            row_out(rows_local, rows, channels, f32),
            row_out(rows_local, rows, 3 * LANES, f32),
            row_out(rows_local, rows, inner_own, bf16),
            row_out(rows_local, rows, 2 * states, f32),
            step_out(batch_count, (states + STATE_PAD, inner_own), bf16),
        ],
        scratch=[pltpu.VMEM((rows + HALO, LANES), f32)],
        flops=rows_local * inner_own * 2000, bytes_accessed=rows_local * inner_own * 20,
    )
    conv_out, small, inputs, maps, fresh = cot_lines.advance(conv_out, small, inputs, maps, fresh)
    scan_ins = [per_row(small, rows), per_row(maps, rows)]
    (mixed,) = call(
        functools.partial(mix_kernel, per), grid, scalars, scan_ins + [per_row(inputs, rows)],
        [row_out(rows_local, rows, inner_own, f32)],
        flops=rows_local * inner_own * 2500, bytes_accessed=rows_local * inner_own * 6,
    )
    cot_lines.advance()

    def with_cotangent(beside):
        cot_lines.ups[-1], cot_lines.downs[-1] = cot_lines.up, cot_lines.down = beside[1:]
        return cotangent_products(deal_cot, cot_lines.finish(), place, full_out)

    entering, (mixed, _, _), (flat_cot, grad_y) = scan_before(
        fresh, states, False, [lambda: (mixed, cot_lines.up, cot_lines.down), with_cotangent]
    )
    vectors = [entire(gain), entire(skip), entire(spread)]
    scanned, scaled_y, sums = call(
        gated_kernel, grid, scalars,
        scan_ins
        + [per_row(mixed, rows), per_step(entering), per_row(conv_out, rows), per_row(gate, rows)]
        + [per_row(grad_y, rows)] + vectors,
        [
            row_out(rows_local, rows, inner_own, f32),
            deal_out(seq_size, batch_count, piece, inner_own, bf16),
            step_out(batch_count, (HALO, rows), f32),
        ],
        flops=rows_local * inner_own * 1500, bytes_accessed=rows_local * inner_own * 8,
    )
    out_rows = dot(scaled_y.reshape(rows_local, inner_own), full_out).astype(bf16)
    sums = sums + swapped(sums, "head", 1)
    for bit in axis_bits("head")[1:]:
        other, out_rows = lax.optimization_barrier((swapped(sums, "head", bit), out_rows))
        sums = sums + other
    branch = lax.psum_scatter(
        out_rows.reshape(deal_shape[:3] + (width_all,)), "head", scatter_dimension=3, tiled=True
    )

    normed_y_t, grads, grad_gate, local, row_part, grad_gain, grad_skip = call(
        functools.partial(ungated_kernel, inner_all), grid, scalars,
        scan_ins
        + [per_row(array, rows) for array in (scanned, conv_out, gate, grad_y)]
        + [per_step(sums)] + vectors,
        [((inner_own, rows_local), bf16, (inner_own, rows), lambda m, *_: (0, m))]
        + [row_out(rows_local, rows, inner_own, bf16)] * 2
        + [step_out(batch_count, (states + STATE_PAD, inner_own), bf16)]
        + [step_out(batch_count, (HALO, rows), f32)]
        + [sum_out((1, inner_own))] * 2,
        flops=rows_local * inner_own * 2000, bytes_accessed=rows_local * inner_own * 24,
    )
    grad_inputs, grad_maps = call(
        functools.partial(unmix_kernel, per), grid, scalars,
        scan_ins + [per_row(inputs, rows), per_row(grads, rows)],
        [row_out(rows_local, rows, inner_own, f32), row_out(rows_local, rows, 2 * states, f32)],
        scratch=[pltpu.VMEM((rows, rows), f32)],
        flops=rows_local * inner_own * 4000, bytes_accessed=rows_local * inner_own * 8,
    )
    (grad_out,) = call(
        out_kernel, (head_size,), (),
        [entire(normed_y_t), (flat_cot, (rows_local, width_own), lambda q: (0, q))],
        [((inner_own, width_all), bf16, (inner_own, width_own), lambda q: (0, q))],
        flops=2 * rows_local * inner_own * width_all, bytes_accessed=rows_local * width_all * 6,
    )
    leaving, grad_inputs, grad_out = scan_before(
        local, states, True, [lambda: grad_inputs, lambda _: grad_out]
    )

    grad_out = lax.psum_scatter(grad_out, "seq", scatter_dimension=1, tiled=True)
    grad_conv_out, grad_step, grad_bias, grad_heads = call(
        unscan_kernel, grid, scalars,
        scan_ins
        + [per_row(a, rows) for a in (scanned, conv_out, inputs, grads)]
        + [per_row(grad_inputs, rows), per_row(grad_maps, rows)]
        + [per_step(entering), per_step(leaving), entire(skip), entire(scale), entire(spread)],
        [
            row_out(rows_local, rows, channels, f32),
            row_out(rows_local, rows, LANES, f32),
            sum_out((1, channels)),
            sum_out((HALO, LANES)),
        ],
        flops=rows_local * inner_own * 4000, bytes_accessed=rows_local * inner_own * 28,
    )
    after_rows = passed_along(grad_conv_out.reshape(batch_count, tok_dev, channels)[:, :HALO], "seq", -1)
    after_rows, branch = lax.optimization_barrier((after_rows, branch))
    grad_pre, grad_state, row_dots, grad_taps = call(
        unconv_kernel, grid, scalars,
        [per_row(pre, rows), per_step(halo), per_row(grad_conv_out, rows), per_step(after_rows)]
        + [per_row(grad_step, rows), per_step(row_part), entire(taps)],
        [
            row_out(rows_local, rows, channels + LANES, bf16),
            row_out(rows_local, rows, 2 * states, bf16),
            step_out(batch_count, (HALO, rows), f32),
            sum_out((taps_total, channels)),
        ],
        scratch=[pltpu.VMEM((rows + HALO, LANES), f32)] * 2,
        flops=rows_local * inner_own * 100, bytes_accessed=rows_local * inner_own * 14,
    )
    columns = [
        (0, 0, 0, inner_own), (1, 0, inner_own, inner_own), (0, channels, 2 * inner_own, LANES)
    ]
    fill = lambda row: jnp.pad(row, ((0, 0), (0, channels - row.shape[1])))
    state_small = jnp.concatenate([grad_taps[:, inner_own:], grad_bias[:, inner_own:]])
    row_dots = jnp.concatenate([row_dots[:, 0, :], state_small.reshape(-1, rows)])
    packed = jnp.concatenate(
        [grad_taps, grad_bias, fill(grad_gain), fill(grad_skip), fill(grad_heads[:2].reshape(1, 2 * LANES))]
    )
    packed = packed + swapped(packed, "seq", 1)
    seq_bits, head_bits = axis_bits("seq"), axis_bits("head")
    sent = weight_gradient_sent(odd_t, [grad_pre, grad_gate], columns, depth)
    others = [
        swapped(row_dots, "head", head_bits[0]), swapped(packed, "seq", seq_bits[1]),
        swapped(grad_state, "head", head_bits[0]),
    ]
    others, sent = lax.optimization_barrier((others, sent))
    row_dots, packed, grad_state = row_dots + others[0], packed + others[1], added(grad_state, others[2])
    got = swapped(sent, "seq", 1)
    grad_rows = lambda first, edges: rows_gradient(
        first, grad_gate, full_in, seq_size, batch_count, edges
    )
    low, high = grad_rows(after(grad_pre, sent), True)
    other, low, high = lax.optimization_barrier((swapped(packed, "seq", seq_bits[2]), low, high))
    packed = packed + other
    for bit in seq_bits[3:]:
        packed = packed + swapped(packed, "seq", bit)
    rows_line = LineScatter([low[0], high[0]])
    mine = weight_gradient_kept(even_t, after(got, low), [grad_pre, grad_gate], columns, inner_own, depth)
    rows_line.middle = grad_rows(after(grad_pre, mine[0]), False)
    others = [swapped(row_dots, "head", head_bits[1]), swapped(grad_state, "head", head_bits[1])]
    *mine, rows_line.middle, branch, others = rows_line.advance(*mine, rows_line.middle, branch, others)
    row_dots, grad_state = row_dots + others[0], added(grad_state, others[1])
    for bit in head_bits[2:]:
        row_dots = row_dots + swapped(row_dots, "head", bit)
        grad_state = added(grad_state, swapped(grad_state, "head", bit))
    (grad_w_state,) = call(
        out_kernel, (1,), (), [entire(own_t), entire(grad_state)], [sum_out((width_own, 2 * states), bf16)],
        flops=2 * rows_local * width_own * 2 * states, bytes_accessed=rows_local * (width_own + 2 * states) * 2,
    )
    state_small = row_dots[batch_count:].reshape(-1, 2 * states).astype(bf16)
    row_dots = row_dots[:batch_count, None, :]
    pad_rows = -state_small.shape[0] % 16
    grad_w_state = jnp.concatenate([grad_w_state, jnp.pad(state_small, ((0, pad_rows), (0, 0)))])
    grad_w_state = added(grad_w_state, swapped(grad_w_state, "seq", 1))
    parts = weight_gradient_parts(mine)
    for part in parts:
        part.send()
    grad_w_state, grad_out = rows_line.advance(grad_w_state, grad_out)
    other = swapped(grad_w_state, "seq", seq_bits[1])
    (out_rows,) = call(
        functools.partial(output_kernel, inner_all), grid, (),
        [per_deal(deal_tokens), per_deal(branch), per_step(sums)],
        [deal_out(seq_size, batch_count, piece, width_own, bf16)],
        bytes_accessed=rows_local * width_own * 6,
    )
    out_rows = sent_back(out_rows)
    (out_rows,) = rows_line.advance(out_rows)
    grad_out = grad_out.astype(f32)
    up, down = rows_line.finish()
    middle = rows_line.middle
    grad_rows_in, grad_norm_gain = call(
        functools.partial(input_kernel, head_size), grid, (place,),
        [per_deal_of(low), per_deal_of(high)]
        + [
            (
                middle, (1, seq_size, 1, piece, width_own),
                lambda m, place: (jnp.clip(place[0] - 1, 0, head_size - 3), 0, m, 0, 0),
            )
        ]
        + [per_deal(a) for a in (up, down, deal_tokens, deal_cot, inv_rms)]
        + [per_step(row_dots), entire(norm_gain[None, :])],
        [deal_out(seq_size, batch_count, piece, width_own, bf16), sum_out((1, width_own))],
        bytes_accessed=rows_local * width_own * 16,
    )
    (parts[0].got, parts[1].got, other), grad_rows_in = lax.optimization_barrier(
        ((parts[0].got, parts[1].got, other), grad_rows_in)
    )
    grad_w_state = added(grad_w_state, other)
    for part in parts:
        part.receive()
    while parts[0].left:
        for part in parts:
            part.send()
            part.receive()
    grad_inner, grad_w_gate, grad_w_step = weight_gradient_total(
        parts,
        [
            (inner_own, [(0, 0, 0, inner_own)]),
            (inner_own, [(1, 0, 0, inner_own)]),
            (LANES, [(1, inner_own, 0, LANES)]),
        ],
        depth,
    )
    for bit in seq_bits[2:]:
        grad_w_state = added(grad_w_state, swapped(grad_w_state, "seq", bit))
    out_back = put_back(out_rows)
    grad_w_state = grad_w_state.astype(f32)
    state_sums = grad_w_state[width_own : width_own + taps_total + 1]
    gain_high = grad_norm_gain.astype(bf16)
    gain_low = (grad_norm_gain - gain_high.astype(f32)).astype(bf16)
    gain_rows = jnp.pad(jnp.concatenate([gain_high, gain_low]), ((0, HALO - 2), (0, 0)))
    own_rows = batch_count * piece
    grad_back = sent_back(
        jnp.concatenate(
            [
                grad_rows_in.reshape(seq_size, own_rows, width_own),
                jnp.broadcast_to(gain_rows, (seq_size, HALO, width_own)),
            ],
            axis=1,
        )
    )
    grad_norm_gain = jnp.sum(grad_back[:, own_rows : own_rows + 2].astype(f32), axis=(0, 1))
    grad_back = put_back(grad_back[:, :own_rows])
    state_own = 2 * states // head_size
    state_sums = lax.dynamic_slice_in_dim(state_sums, head_index * state_own, state_own, 1)
    return (
        out_back,
        grad_back,
        grad_norm_gain,
        grad_w_gate,
        grad_inner,
        grad_w_state[:width_own],
        grad_w_step[:, :heads_own],
        packed[:taps_total, :inner_own],
        packed[taps_total, :inner_own],
        state_sums[:taps_total],
        state_sums[taps_total],
        packed[taps_total + 3, LANES : LANES + heads_own],
        packed[taps_total + 3, :heads_own],
        jnp.sum(packed[taps_total + 2, :inner_own].reshape(heads_own, head_width), axis=1),
        packed[taps_total + 1, :inner_own],
        grad_out,
    )


def solution(mesh):
    return jax.shard_map(
        per_device,
        mesh=mesh,
        in_specs=(
            P("seq", "head"),
            P("seq", "head"),
            P(),
            P("seq"),
            P(),
            P("seq", "head"),
            P("seq", "head"),
            P("seq", None),
            P("seq", "head"),
            P(None, "head"),
            P("head"),
            P(),
            P(),
            P("head"),
            P("head"),
            P("head"),
            P("head"),
            P("head", "seq"),
        ),
        out_specs=(
            P("seq", "head"),
            P("seq", "head"),
            P("head"),
            P("seq", "head"),
            P("seq", "head"),
            P("head", None),
            P("seq", "head"),
            P(None, "head"),
            P("head"),
            P(None, "head"),
            P("head"),
            P("head"),
            P("head"),
            P("head"),
            P("head"),
            P("head", "seq"),
        ),
        check_vma=False,
    )
```

```python
import functools
import math
import jax
import jax.numpy as jnp
from jax import lax
from jax.experimental import pallas as pl
from jax.experimental.pallas import tpu as pltpu
from jax.sharding import PartitionSpec as P

epsilon = 1e-05
highest = lax.Precision.HIGHEST
f32 = jnp.float32
bf16 = jnp.bfloat16
LANES = 128
HALO = 8
STATE_PAD = 16
HBM_BYTES = 700000
VMEM_SPARE = 10 * 1024 * 1024


def swapped(value, axis, bit):
    return lax.ppermute(value, axis, [(i, i ^ bit) for i in range(lax.axis_size(axis))])


def axis_bits(axis):
    count = lax.axis_size(axis)
    return [1 << k for k in range(count.bit_length() - 1)]


def added(left, right):
    return (left.astype(f32) + right.astype(f32)).astype(left.dtype)


def after(value, *others):
    return lax.optimization_barrier((value, *others))[0]


def after_all(values, others):
    return lax.optimization_barrier((tuple(values), tuple(others)))[0]


class Scattered:
    def __init__(self, keep, send, labels, order):
        rows = keep.shape[0] // len(labels)
        self.pair = (keep.reshape(len(labels), rows, -1), send.reshape(len(labels), rows, -1))
        self.labels, self.left = labels, list(order)

    def send(self):
        self.got = swapped(self.pair[1], "seq", self.left.pop(0))

    def receive(self):
        total = added(self.pair[0], self.got)
        if not self.left:
            self.pair = (total,)
            return
        following, labels = self.left[0], self.labels
        keep_at = [at for at, label in enumerate(labels) if not label & following]
        send_at = [labels.index(labels[at] ^ following) for at in keep_at]
        kept = jnp.concatenate([total[at : at + 1] for at in keep_at])
        sent = jnp.concatenate([total[at : at + 1] for at in send_at])
        self.pair = (kept, sent)
        self.labels = [labels[at] for at in keep_at]

    def finish(self):
        return [self.pair[0][0]]


class LineGather:
    def __init__(self, own):
        self.size = lax.axis_size("head")
        self.up = self.down = own
        self.ups, self.downs = [], []

    def advance(self, *beside):
        step = len(self.ups) + 1
        if step < self.size:
            up = lax.ppermute(self.up, "head", [(i, i + 1) for i in range(step - 1, self.size - 1)])
            down = lax.ppermute(self.down, "head", [(i, i - 1) for i in range(1, self.size - step + 1)])
            if beside:
                (up, down), beside = lax.optimization_barrier(((up, down), beside))
            self.up, self.down = up, down
            self.ups.append(up)
            self.downs.append(down)
        return beside

    def finish(self):
        while len(self.ups) + 1 < self.size:
            self.advance()
        return self.ups, self.downs


class LineScatter:
    def __init__(self, edges, middle=None):
        self.size, self.here = lax.axis_size("head"), lax.axis_index("head")
        self.edges, self.middle = edges, middle
        self.up = self.down = None
        self.step = 0

    def block_of(self, at):
        last = self.size - 1
        inner = lax.dynamic_index_in_dim(self.middle, jnp.clip(at - 1, 0, last - 2), 0, keepdims=False)
        return jnp.where(at <= 0, self.edges[0], jnp.where(at >= last, self.edges[1], inner))

    def advance(self, *beside):
        self.step += 1
        step, size, here = self.step, self.size, self.here
        if step < size:
            if step == 1:
                up, down = self.edges[1], self.edges[0]
            else:
                up = added(self.block_of(here + size - step), self.up)
                down = added(self.block_of(here - size + step), self.down)
            up = lax.ppermute(up, "head", [(i, i + 1) for i in range(step)])
            down = lax.ppermute(down, "head", [(i, i - 1) for i in range(size - step, size)])
            if beside:
                (up, down), beside = lax.optimization_barrier(((up, down), beside))
            self.up, self.down = up, down
        return beside

    def finish(self):
        while self.step + 1 < self.size:
            self.advance()
        return self.up, self.down


def axis_sum(value, axis):
    for bit in axis_bits(axis):
        value = value + swapped(value, axis, bit)
    return value


def passed_along(value, axis, steps):
    count = lax.axis_size(axis)
    initial, last = (max(0, -steps), min(count, count - steps))
    return lax.ppermute(value, axis, [(source, source + steps) for source in range(initial, last)])


def dot(left, right, precision=None):
    return jnp.dot(left, right, preferred_element_type=f32, precision=precision)


def dot_nt(left, right, precision=None):
    return lax.dot_general(
        left, right, (((1,), (1,)), ((), ())), preferred_element_type=f32, precision=precision
    )


def dot_tn(left, right, precision=None):
    return lax.dot_general(
        left, right, (((0,), (0,)), ((), ())), preferred_element_type=f32, precision=precision
    )


def both_parts(values):
    high = values.astype(bf16)
    return jnp.concatenate([high, (values - high.astype(f32)).astype(bf16)], axis=1)


def silu_slope(values):
    logistic = jax.nn.sigmoid(values)
    return logistic * (1.0 + values * (1.0 - logistic))


def big(shape, dtype):
    return math.prod(shape) * jnp.dtype(dtype).itemsize > HBM_BYTES


def tiled_bytes(shape, dtype):
    *lead, rows, lanes = shape
    size = -(-rows // 8) * 8 * -(-lanes // LANES) * LANES * jnp.dtype(dtype).itemsize
    for count in lead:
        size *= count
    return size


def call(kernel, grid, scalars, ins, outs, scratch=(), flops=0, bytes_accessed=0):
    ins = [(streamed(a) if big(a.shape, a.dtype) else a, block, index) for a, block, index in ins]
    held = [block == array.shape for array, block, _ in ins]
    need = sum(
        (1 if whole else 2) * tiled_bytes(block, array.dtype) for (array, block, _), whole in zip(ins, held)
    )
    need += sum(2 * tiled_bytes(block, dtype) for _, dtype, block, _ in outs)
    need += sum(tiled_bytes(item.shape, item.dtype) for item in scratch)
    return pl.pallas_call(
        kernel,
        grid_spec=pltpu.PrefetchScalarGridSpec(
            num_scalar_prefetch=len(scalars),
            grid=grid,
            in_specs=[
                pl.BlockSpec(block, index, pipeline_mode=pl.Buffered(1) if whole else None)
                for (_, block, index), whole in zip(ins, held)
            ],
            out_specs=[pl.BlockSpec(block, index) for _, _, block, index in outs],
            scratch_shapes=list(scratch),
        ),
        out_shape=[
            (pltpu.HBM if big(shape, dtype) else jax.ShapeDtypeStruct)(shape, dtype) for shape, dtype, _, _ in outs
        ],
        compiler_params=pltpu.CompilerParams(vmem_limit_bytes=need + VMEM_SPARE),
        cost_estimate=pl.CostEstimate(
            flops=int(flops), bytes_accessed=int(bytes_accessed), transcendentals=0
        ),
    )(*scalars, *[array for array, _, _ in ins])


def streamed(array):
    return pltpu.with_memory_space_constraint(array, pltpu.HBM)


def per_row(array, rows):
    return (array, (rows,) + array.shape[1:], lambda m, *_: (m,) + (0,) * (array.ndim - 1))


def per_deal(array):
    return (array, (array.shape[0], 1) + array.shape[2:], lambda m, *_: (0, m, 0, 0))


def per_deal_of(array):
    return (array, (1, array.shape[1], 1) + array.shape[3:], lambda m, *_: (0, 0, m, 0, 0))


def deal_out(senders, count, rows, width, dtype):
    return ((senders, count, rows, width), dtype, (senders, 1, rows, width), lambda m, *_: (0, m, 0, 0))


def deal_rows(ref, tile):
    values = ref[:, 0, :, tile].astype(f32)
    return values.reshape(values.shape[0] * values.shape[1], values.shape[2])


def put_deal_rows(ref, tile, values):
    shape = (ref.shape[0], ref.shape[2], values.shape[1])
    ref[:, 0, :, tile] = values.reshape(shape).astype(ref.dtype)


def per_step(array):
    return (array, (1,) + array.shape[1:], lambda m, *_: (m,) + (0,) * (array.ndim - 1))


def entire(array):
    return (array, array.shape, lambda *_: (0,) * array.ndim)


def row_out(total, rows, width, dtype):
    return ((total, width), dtype, (rows, width), lambda m, *_: (m, 0))


def step_out(count, shape, dtype):
    return ((count,) + shape, dtype, (1,) + shape, lambda m, *_: (m,) + (0,) * len(shape))


def sum_out(shape, dtype=f32):
    return (shape, dtype, shape, lambda *_: (0,) * len(shape))


def joined(earlier, following, states):
    row = lax.broadcasted_iota(jnp.int32, earlier.shape, 0)
    return following[states : states + 1] * earlier + jnp.where(row < states, following, 0.0)


def chip_kernel(states, flags, own, other, total):
    for at in range(own.shape[0]):
        mine, theirs = own[at].astype(f32), other[at].astype(f32)
        later = flags[0] != 0
        first, second = jnp.where(later, theirs, mine), jnp.where(later, mine, theirs)
        total[at] = joined(first, second, states).astype(bf16)


def link_kernel(states, step, last, flags, *refs):
    total, other, refs = refs[0], refs[1], refs[2:]
    later = flags[step] != 0
    if step > 1:
        before, refs = refs[0], refs[1:]
    for at in range(total.shape[0]):
        mine, theirs = total[at].astype(f32), other[at].astype(f32)
        if step == 1:
            row = lax.broadcasted_iota(jnp.int32, mine.shape, 0)
            ahead = jnp.where(row < states, 0.0, 1.0)
            refs[0][at] = jnp.where(later, theirs, ahead).astype(bf16)
        else:
            ahead = before[at].astype(f32)
            refs[0][at] = jnp.where(later, joined(theirs, ahead, states), ahead).astype(bf16)
        if not last:
            first, second = jnp.where(later, theirs, mine), jnp.where(later, mine, theirs)
            refs[1][at] = joined(first, second, states).astype(bf16)


def enter_kernel(states, flags, ahead, ahead_other, sibling, entering):
    odd = flags[flags.shape[0] - 1] != 0
    half = ahead.shape[2]
    for at in range(ahead.shape[0]):
        mine, theirs = ahead[at], ahead_other[at]
        left, right = jnp.where(odd, theirs, mine), jnp.where(odd, mine, theirs)
        for start, values in ((0, left), (half, right)):
            values = values.astype(f32)
            near = sibling[at, :, start : start + half].astype(f32)
            entering[at, :, start : start + half] = jnp.where(
                flags[0] != 0, joined(values, near, states), values
            ).astype(bf16)


def scan_before(local, states, reverse, fillers):
    here = lax.axis_index("seq")
    bits = axis_bits("seq")
    count, height, width = local.shape
    passed = [((here & bit) == 0) if reverse else ((here & bit) != 0) for bit in bits]
    flags = jnp.stack(passed + [(here & 1) != 0]).astype(jnp.int32)
    whole = local.shape
    piece = (count, height, width // 2)
    at_step = lambda *_: (0, 0, 0)
    at_core = lambda _, flags: (0, 0, flags[len(bits)])
    half_out = (piece, bf16, piece, at_step)
    moved = local.size * 4
    sibling = swapped(local, "seq", 1)
    (total,) = call(
        functools.partial(chip_kernel, states), (1,), (flags,),
        [(local, piece, at_core), (sibling, piece, at_core)], [half_out], bytes_accessed=moved,
    )
    ahead, filled, beside = None, [], ()
    for step, bit in enumerate(bits[1:], 1):
        other = swapped(total, "seq", bit)
        if step <= len(fillers):
            other, value = lax.optimization_barrier((other, fillers[step - 1](*beside)))
            beside = (value,)
            filled.append(value)
        last = step == len(bits) - 1
        ins = [total, other] + ([] if ahead is None else [ahead])
        results = call(
            functools.partial(link_kernel, states, step, last), (1,), (flags,),
            [(array, piece, at_step) for array in ins], [half_out] * (1 if last else 2),
            bytes_accessed=moved,
        )
        ahead = results[0]
        total = None if last else results[1]
    ahead_other = swapped(ahead, "seq", 1)
    (entering,) = call(
        functools.partial(enter_kernel, states), (1,), (flags,),
        [(ahead, piece, at_step), (ahead_other, piece, at_step), (sibling, whole, at_step)],
        [(local.shape, bf16, whole, at_step)], bytes_accessed=moved * 2,
    )
    return [entering] + filled


def segment_of(position, plan, place, m):
    found = jnp.full(jnp.shape(position), -1, jnp.int32)
    for k in range(plan.shape[1]):
        found = found + (position >= plan[m, k]).astype(jnp.int32)
    return jnp.where(position >= place[3], -2, found)


def column_position(rows, place, shift=0):
    return place[2] + shift + lax.broadcasted_iota(jnp.int32, (rows, 1), 0)


def row_position(rows, place):
    return place[2] + lax.broadcasted_iota(jnp.int32, (1, rows), 1)


def by_core(values, me, depth):
    count = values.shape[1] // depth
    blocks = [values[:, k * depth : (k + 1) * depth] for k in range(count)]
    odd = (me & 1) != 0
    halves = []
    for at in (0, 1):
        straight, turned = blocks[at::2], blocks[1 - at :: 2]
        half = [jnp.where(odd, b, a) for a, b in zip(straight, turned)]
        bit = 1
        while bit < count // 2:
            flip = ((me >> 1) & bit) != 0
            half = [jnp.where(flip, half[k ^ bit], half[k]) for k in range(len(half))]
            bit *= 2
        halves.append(half[0] if len(half) == 1 else jnp.concatenate(half, axis=1))
    return halves


def half_start(quarter, me, width, depth):
    count = width // depth // 2
    return pl.multiple_of(((quarter * count) ^ ((me >> 1) & ~(count - 1))) * depth, width // 2)


def line_slot(own, ups, downs, z, step):
    if step == 0:
        return deal_rows(own, slice(None))
    up, down = ups[step - 1], downs[len(downs) - step]
    return jnp.where(z >= step, deal_rows(up, slice(None)), deal_rows(down, slice(None)))


def features_kernel(size, depth, place, *refs):
    own, ups, downs = refs[0], refs[1:size], refs[size : 2 * size - 1]
    gain, normed, even_t, odd_t, own_t, inverse = refs[2 * size - 1 :]
    z, me = place[0], place[1]
    width = own.shape[3]
    slots = [line_slot(own, ups, downs, z, step) for step in range(size)]
    square = sum(jnp.sum(slot * slot, axis=1, keepdims=True) for slot in slots)
    inv = lax.rsqrt(square / (width * size) + epsilon)
    put_deal_rows(inverse, slice(None), inv)
    for step, slot in enumerate(slots):
        quarter = lax.rem(z - step + size, size)
        place_at = pl.ds(pl.multiple_of(quarter * width, width), width)
        slot = slot * inv * gain[:, place_at]
        normed[:, place_at] = slot.astype(bf16)
        if step == 0:
            own_t[...] = slot.astype(bf16).T
        first, second = by_core(slot, me, depth)
        at = pl.ds(half_start(quarter, me, width, depth), width // 2)
        even_t[at, :] = first.astype(bf16).T
        odd_t[at, :] = second.astype(bf16).T


def all_features(own, lines, place, gain, depth):
    senders, count, piece, width = own.shape
    rows = senders * piece
    total = rows * count
    size = lax.axis_size("head")
    ups, downs = lines
    half = width * size // 2
    outs = [row_out(total, rows, 2 * half, bf16)]
    outs += [((half, total), bf16, (half, rows), lambda m, *_: (0, m))] * 2
    outs.append(((width, total), bf16, (width, rows), lambda m, *_: (0, m)))
    outs.append(deal_out(senders, count, piece, 1, f32))
    return call(
        functools.partial(features_kernel, size, depth), (count,), (place,),
        [per_deal(array) for array in [own] + ups + downs] + [entire(gain)], outs,
        bytes_accessed=total * width * 2 * 15,
    )


def cotangent_kernel(size, place, *refs):
    own, ups, downs = refs[0], refs[1:size], refs[size : 2 * size - 1]
    weight, every, grad_y = refs[2 * size - 1 :]
    z = place[0]
    width = own.shape[3]
    total = None
    for step in range(size):
        slot = line_slot(own, ups, downs, z, step)
        quarter = lax.rem(z - step + size, size)
        place_at = pl.ds(pl.multiple_of(quarter * width, width), width)
        every[:, place_at] = slot.astype(bf16)
        part = dot_nt(slot.astype(bf16), weight[:, place_at])
        total = part if total is None else total + part
    grad_y[...] = total.astype(bf16)


def cotangent_products(own, lines, place, weight):
    senders, count, piece, width = own.shape
    rows = senders * piece
    total = rows * count
    size = lax.axis_size("head")
    ups, downs = lines
    return call(
        functools.partial(cotangent_kernel, size), (count,), (place,),
        [per_deal(array) for array in [own] + ups + downs] + [entire(weight)],
        [
            row_out(total, rows, width * size, bf16),
            row_out(total, rows, weight.shape[0], bf16),
        ],
        flops=2 * total * width * size * weight.shape[0],
        bytes_accessed=total * width * 2 * 11 + weight.size * 2 + total * weight.shape[0] * 4,
    )


def conv_kernel(
    width, place, plan, pre, halo, taps, bias, step_bias, scale, spread, conv_out, small, inputs, maps, fresh,
    extended,
):
    m = pl.program_id(0)
    rows = pre.shape[0]
    states = maps.shape[1] // 2
    taps_total = taps.shape[0]
    here = segment_of(column_position(rows, place), plan, place, m)
    same = [
        (segment_of(column_position(rows, place, tap + 1 - taps_total), plan, place, m) == here).astype(f32)
        for tap in range(taps_total)
    ]
    before = segment_of(place[2] - 1, plan, place, m)
    last = segment_of(place[2] + rows - 1, plan, place, m)

    step_pre = pre[:, width + 2 * states : width + 2 * states + LANES] + step_bias[...]
    rest = jnp.exp(-jnp.abs(step_pre))
    series = rest * (
        1.0 - rest * (1 / 2 - rest * (1 / 3 - rest * (1 / 4 - rest * (1 / 5 - rest * (1 / 6)))))
    )
    step = jnp.maximum(step_pre, 0.0) + jnp.where(rest < 0.03, series, jnp.log(1.0 + rest))
    row = lax.broadcasted_iota(jnp.int32, (rows, rows), 0)
    col = lax.broadcasted_iota(jnp.int32, (rows, rows), 1)
    lower = (row >= col).astype(f32)
    cumulative = dot(lower, step * scale[...], highest)
    small[:, :LANES] = cumulative
    small[:, LANES : 2 * LANES] = step
    small[:, 2 * LANES :] = step_pre
    ending = cumulative[rows - 1 :, :]
    fading = (here == last).astype(f32) * jnp.exp(ending - cumulative)
    through = (last == before).astype(f32) * jnp.exp(ending)
    step_parts, fading_parts = both_parts(step), both_parts(fading)
    through_parts = both_parts(jnp.broadcast_to(through, (STATE_PAD, LANES)))

    def conv(at):
        tile = slice(at, at + LANES)
        extended[:HALO, :] = halo[0, :, tile]
        extended[HALO:, :] = pre[:, tile]
        result = jnp.broadcast_to(bias[:, tile], (rows, LANES))
        for tap in range(taps_total):
            start = HALO + tap + 1 - taps_total
            result = result + taps[tap : tap + 1, tile] * extended[start : start + rows, :] * same[tap]
        conv_out[:, tile] = result
        return result * jax.nn.sigmoid(result)

    for at in range(0, 2 * states, LANES):
        maps[:, at : at + LANES] = conv(width + at)
    input_map_t = maps[:, :states].T.astype(bf16)
    for at in range(0, width, LANES):
        tile = slice(at, at + LANES)
        values = conv(at) * dot(step_parts, spread[:, tile])
        inputs[:, tile] = values.astype(bf16)
        faded = (values * dot(fading_parts, spread[:, tile])).astype(bf16)
        fresh[0, :states, tile] = dot(input_map_t, faded).astype(bf16)
        fresh[0, states:, tile] = dot(through_parts, spread[:, tile]).astype(bf16)


def allowed_mask(rows, place, plan, m, transposed):
    column = segment_of(column_position(rows, place), plan, place, m)
    across = segment_of(row_position(rows, place), plan, place, m)
    row = lax.broadcasted_iota(jnp.int32, (rows, rows), 0)
    col = lax.broadcasted_iota(jnp.int32, (rows, rows), 1)
    order = (row <= col) if transposed else (row >= col)
    return jnp.where(order & (column == across), 0.0, -1e30)


def lane_select(parts, per):
    lane = lax.broadcasted_iota(jnp.int32, parts[0].shape, 1)
    result = parts[0]
    for at in range(1, per):
        result = jnp.where(lane >= at * (LANES // per), parts[at], result)
    return result


def mix_kernel(per, place, plan, small, maps, inputs, out):
    m = pl.program_id(0)
    rows, width = inputs.shape
    states = maps.shape[1] // 2
    cumulative = small[:, :LANES]
    flat = cumulative.T
    mask = allowed_mask(rows, place, plan, m, False)
    scores = dot_nt(maps[:, states:], maps[:, :states], highest)
    for at in range(0, width, LANES):
        tile = slice(at, at + LANES)
        for low in range(0, rows, LANES):
            end = low + LANES
            parts = []
            for sub in range(per):
                head = at // LANES * per + sub
                decay = jnp.exp(
                    (cumulative[low:end, head : head + 1] - flat[head : head + 1, :end])
                    + mask[low:end, :end]
                )
                mixing = (decay * scores[low:end, :end]).astype(bf16)
                parts.append(dot(mixing, inputs[:end, tile]))
            out[low:end, tile] = lane_select(parts, per)


def unmix_kernel(per, place, plan, small, maps, inputs, grads, grad_inputs, grad_maps, total):
    m = pl.program_id(0)
    rows, width = inputs.shape
    states = maps.shape[1] // 2
    cumulative = small[:, :LANES]
    flat = cumulative.T
    mask = allowed_mask(rows, place, plan, m, True)
    scores = dot_nt(maps[:, :states], maps[:, states:], highest)
    lane = lax.broadcasted_iota(jnp.int32, (LANES, LANES), 1)
    total[...] = jnp.zeros_like(total)
    for at in range(0, width, LANES):
        tile = slice(at, at + LANES)
        for low in range(0, rows, LANES):
            end = low + LANES
            later = grads[low:, tile]
            parts = []
            gathered_sum = total[low:end, low:]
            for sub in range(per):
                head = at // LANES * per + sub
                decay = jnp.exp(
                    (flat[head : head + 1, low:] - cumulative[low:end, head : head + 1])
                    + mask[low:end, low:]
                )
                mixing = (decay * scores[low:end, low:]).astype(bf16)
                parts.append(dot(mixing, later))
                inside = (lane // (LANES // per)) == sub
                own = jnp.where(inside, inputs[low:end, tile].astype(f32), 0.0).astype(bf16)
                gathered_sum = gathered_sum + decay * dot_nt(own, later)
            total[low:end, low:] = gathered_sum
            grad_inputs[low:end, tile] = lane_select(parts, per)
    grad_scores = total[...].astype(bf16)
    grad_maps[:, :states] = dot(grad_scores, maps[:, states:].astype(bf16))
    grad_maps[:, states:] = dot_tn(grad_scores, maps[:, :states].astype(bf16))


def inflow_of(cumulative, rows, place, plan, m):
    here = segment_of(column_position(rows, place), plan, place, m)
    before = segment_of(place[2] - 1, plan, place, m)
    return (here == before).astype(f32) * jnp.exp(cumulative)


def gated_kernel(
    place, plan, small, maps, mixed, entering, conv_out, gate, grad_y, gain, skip, spread, scanned, scaled_y, sums
):
    m = pl.program_id(0)
    rows, width = mixed.shape
    states = maps.shape[1] // 2
    inflow = both_parts(inflow_of(small[:, :LANES], rows, place, plan, m))
    output_map = maps[:, states:].astype(bf16)
    square = jnp.zeros((rows, LANES), f32)
    product = jnp.zeros((rows, LANES), f32)
    for at in range(0, width, LANES):
        tile = slice(at, at + LANES)
        carried = dot(output_map, entering[0, :states, tile]) * dot(inflow, spread[:, tile])
        scan = mixed[:, tile] + carried
        scanned[:, tile] = scan
        conv = conv_out[:, tile]
        gates = gate[:, tile].astype(f32)
        gated = (scan + skip[:, tile] * (conv * jax.nn.sigmoid(conv))) * (gates * jax.nn.sigmoid(gates))
        square = square + gated * gated
        scaled = gain[:, tile] * gated
        put_deal_rows(scaled_y, tile, scaled)
        product = product + grad_y[:, tile].astype(f32) * scaled
    ones = jnp.ones((HALO, LANES), f32)
    pick = lax.broadcasted_iota(jnp.int32, (HALO, rows), 0)
    sums[0] = jnp.where(pick == 0, dot_nt(ones, square, highest), dot_nt(ones, product, highest))


def ungated_kernel(
    inner_all, place, plan, small, maps, scanned, conv_out, gate, grad_y, sums, gain, skip, spread,
    normed_y_t, grads, grad_gate, local, row_part, grad_gain, grad_skip,
):
    m = pl.program_id(0)
    rows, width = scanned.shape
    states = maps.shape[1] // 2
    row = lax.broadcasted_iota(jnp.int32, (rows, rows), 0)
    col = lax.broadcasted_iota(jnp.int32, (rows, rows), 1)
    columns = dot_nt((row == col).astype(f32), sums[0], highest)
    inv = lax.rsqrt(columns[:, :1] / inner_all + epsilon)
    pull = inv * inv * inv * (columns[:, 1:2] / inner_all)
    cumulative = small[:, :LANES]
    inflow = both_parts(inflow_of(cumulative, rows, place, plan, m))
    before = segment_of(place[2] - 1, plan, place, m)
    last = segment_of(place[2] + rows - 1, plan, place, m)
    through = (last == before).astype(f32) * jnp.exp(cumulative[rows - 1 :, :])
    through_parts = both_parts(jnp.broadcast_to(through, (STATE_PAD, LANES)))
    output_map_t = maps[:, states:].T.astype(bf16)

    @pl.when(m == 0)
    def _():
        grad_gain[...] = jnp.zeros_like(grad_gain)
        grad_skip[...] = jnp.zeros_like(grad_skip)

    product = jnp.zeros((rows, LANES), f32)
    for at in range(0, width, LANES):
        tile = slice(at, at + LANES)
        conv = conv_out[:, tile]
        heads_x = conv * jax.nn.sigmoid(conv)
        mixer = scanned[:, tile] + skip[:, tile] * heads_x
        gates = gate[:, tile].astype(f32)
        logistic = jax.nn.sigmoid(gates)
        act = gates * logistic
        gated = mixer * act
        normed = gated * inv
        normed_y_t[tile, :] = (normed * gain[:, tile]).astype(bf16).T
        grad = grad_y[:, tile].astype(f32)
        grad_gain[:, tile] += jnp.sum(grad * normed, axis=0, keepdims=True)
        grad_gated = inv * (grad * gain[:, tile]) - gated * pull
        grad_mixer = grad_gated * act
        grads[:, tile] = grad_mixer.astype(bf16)
        grad_skip[:, tile] += jnp.sum(grad_mixer * heads_x, axis=0, keepdims=True)
        grad_gates = grad_gated * mixer * (logistic * (1.0 + gates * (1.0 - logistic)))
        grad_gate[:, tile] = grad_gates.astype(bf16)
        product = product + grad_gates * gates
        weighted = (grad_mixer * dot(inflow, spread[:, tile])).astype(bf16)
        local[0, :states, tile] = dot(output_map_t, weighted).astype(bf16)
        local[0, states:, tile] = dot(through_parts, spread[:, tile]).astype(bf16)
    row_part[0] = dot_nt(jnp.ones((HALO, LANES), f32), product, highest)


def unscan_kernel(
    place, plan, small, maps, scanned, conv_out, inputs, grads, grad_inputs, grad_maps, entering, leaving,
    skip, scale, spread, grad_conv_out, grad_step, grad_bias, grad_heads,
):
    m = pl.program_id(0)
    rows, width = scanned.shape
    states = maps.shape[1] // 2
    cumulative, step, pre = (small[:, k * LANES : (k + 1) * LANES] for k in range(3))
    here = segment_of(column_position(rows, place), plan, place, m)
    before = segment_of(place[2] - 1, plan, place, m)
    last = segment_of(place[2] + rows - 1, plan, place, m)
    ending = cumulative[rows - 1 :, :]
    fading = both_parts((here == last).astype(f32) * jnp.exp(ending - cumulative))
    inflow = both_parts((here == before).astype(f32) * jnp.exp(cumulative))
    through = (last == before).astype(f32) * jnp.exp(ending)
    step_parts = both_parts(step)
    input_map = maps[:, :states].astype(bf16)

    @pl.when(m == 0)
    def _():
        grad_bias[...] = jnp.zeros_like(grad_bias)
        grad_heads[...] = jnp.zeros_like(grad_heads)

    grad_in, grad_out = grad_maps[:, :states], grad_maps[:, states:]
    grad_cum = jnp.zeros((rows, LANES), f32)
    grad_own = jnp.zeros((rows, LANES), f32)
    ends = jnp.zeros((HALO, LANES), f32)
    for at in range(0, width, LANES):
        tile = slice(at, at + LANES)
        spread_tile = spread[:, tile]
        leave, enter = leaving[0, :states, tile], entering[0, :states, tile]
        fade = dot(fading, spread_tile)
        pulled = fade * dot(input_map, leave)
        values = inputs[:, tile].astype(f32)
        grad = grads[:, tile].astype(f32)
        total = grad_inputs[:, tile] + pulled
        faded = (values * fade).astype(bf16)
        weighted = (grad * dot(inflow, spread_tile)).astype(bf16)
        grad_in = grad_in + dot_nt(faded, leave)
        grad_out = grad_out + dot_nt(weighted, enter)
        conv = conv_out[:, tile]
        logistic = jax.nn.sigmoid(conv)
        heads_x = conv * logistic
        first = both_parts(grad * scanned[:, tile] - values * total)
        second = both_parts(total * heads_x)
        twice = jnp.concatenate([spread[:LANES, tile]] * 2, axis=1)
        grad_cum = grad_cum + dot_nt(first, twice)
        grad_own = grad_own + dot_nt(second, twice)
        fade_sum = jnp.sum(values * pulled, axis=0, keepdims=True)
        through_sum = jnp.sum(leave.astype(f32) * enter.astype(f32), axis=0, keepdims=True)
        pick = lax.broadcasted_iota(jnp.int32, (HALO, LANES), 0)
        edge = both_parts(jnp.where(pick == 0, fade_sum, through_sum))
        ends = ends + dot_nt(edge, twice)
        grad_x = total * dot(step_parts, spread_tile) + skip[:, tile] * grad
        result = grad_x * (logistic * (1.0 + conv * (1.0 - logistic)))
        grad_conv_out[:, tile] = result
        grad_bias[:, tile] += jnp.sum(result, axis=0, keepdims=True)
    for values, start in ((grad_in, width), (grad_out, width + states)):
        conv = conv_out[:, start : start + states]
        result = values * silu_slope(conv)
        grad_conv_out[:, start : start + states] = result
        grad_bias[:, start : start + states] += jnp.sum(result, axis=0, keepdims=True)
    row = lax.broadcasted_iota(jnp.int32, (rows, rows), 0)
    col = lax.broadcasted_iota(jnp.int32, (rows, rows), 1)
    upper = (row <= col).astype(f32)
    grad_rate = dot(upper, grad_cum, highest) + (ends[:1] + through * ends[1:2])
    rate = step * scale[...]
    grad_pre = (grad_rate * scale[...] + grad_own) * jax.nn.sigmoid(pre)
    grad_step[...] = grad_pre
    grad_heads[0:1, :] += jnp.sum(grad_rate * rate, axis=0, keepdims=True)
    grad_heads[1:2, :] += jnp.sum(grad_pre, axis=0, keepdims=True)


def unconv_kernel(
    place, plan, pre, halo, grad_out, after_rows, grad_step, row_part, taps, grad_pre, grad_state, row_sums,
    grad_taps, extended, extended_grad,
):
    m = pl.program_id(0)
    rows = pre.shape[0]
    channels = grad_out.shape[1]
    taps_total = taps.shape[0]
    here = segment_of(column_position(rows, place), plan, place, m)
    behind, ahead = [], []
    for tap in range(taps_total):
        lag = taps_total - 1 - tap
        behind.append((segment_of(column_position(rows, place, -lag), plan, place, m) == here).astype(f32))
        ahead.append((segment_of(column_position(rows, place, lag), plan, place, m) == here).astype(f32))

    @pl.when(m == 0)
    def _():
        grad_taps[...] = jnp.zeros_like(grad_taps)

    total = jnp.zeros((rows, LANES), f32)
    for at in range(0, channels, LANES):
        tile = slice(at, at + LANES)
        extended[:HALO, :] = halo[0, :, tile]
        extended[HALO:, :] = pre[:, tile]
        grad = grad_out[:, tile]
        extended_grad[:rows, :] = grad
        extended_grad[rows:, :] = after_rows[0, :, tile]
        result = jnp.zeros((rows, LANES), f32)
        for tap in range(taps_total):
            lag = taps_total - 1 - tap
            result = result + taps[tap : tap + 1, tile] * extended_grad[lag : lag + rows, :] * ahead[tap]
            begin = HALO - lag
            product = grad * extended[begin : begin + rows, :] * behind[tap]
            grad_taps[tap : tap + 1, tile] += jnp.sum(product, axis=0, keepdims=True)
        grad_pre[:, tile] = result.astype(bf16)
        total = total + result * pre[:, tile]
    grad_pre[:, channels:] = grad_step[...].astype(bf16)
    grad_state[...] = grad_pre[:, channels - grad_state.shape[1] : channels]
    total = total + grad_step[...] * pre[:, channels : channels + LANES]
    row_sums[0] = row_part[0] + dot_nt(jnp.ones((HALO, LANES), f32), total, highest)


def rows_kernel(quarters, first, second, *refs):
    for weight, out in zip(refs[:quarters], refs[quarters:]):
        cut = weight.shape[1] - second.shape[1]
        result = dot_nt(first[...], weight[:, : first.shape[1]]) + dot_nt(second[...], weight[:, cut:])
        put_deal_rows(out.at[0], slice(None), result)


def rows_gradient(first, second, weight, senders, count, edges):
    total = first.shape[0]
    size = lax.axis_size("head")
    width = weight.shape[0] // size
    rows = total // count
    flops = total * (first.shape[1] + second.shape[1]) * width * size
    moved = weight.size + (first.size + second.size) * size
    block = (1, senders, 1, rows // senders, width)
    if edges:
        shape = (1, senders, count, rows // senders, width)
        return call(
            functools.partial(rows_kernel, 2), (count,), (),
            [per_row(first, rows), per_row(second, rows)]
            + [(weight, (width, weight.shape[1]), lambda m, at=at: (at, 0)) for at in (0, size - 1)],
            [(shape, bf16, block, lambda m: (0, 0, m, 0, 0))] * 2, flops=flops, bytes_accessed=moved,
        )
    row_block = lambda array: (array, (rows, array.shape[1]), lambda q, m: (m, 0))
    return call(
        functools.partial(rows_kernel, 1), (size - 2, count), (),
        [row_block(first), row_block(second), (weight, (width, weight.shape[1]), lambda q, m: (q + 1, 0))],
        [
            (
                (size - 2, senders, count, rows // senders, width), bf16, block,
                lambda q, m: (q, 0, m, 0, 0),
            )
        ],
        flops=flops, bytes_accessed=moved,
    )[0]


def column_of(rows_form):
    rows = rows_form.shape[1]
    row = lax.broadcasted_iota(jnp.int32, (rows, rows), 0)
    col = lax.broadcasted_iota(jnp.int32, (rows, rows), 1)
    return dot_nt((row == col).astype(f32), rows_form, highest)[:, :1]


def output_kernel(inner_all, tokens, branch, sums, out):
    inv = lax.rsqrt(column_of(sums[0]) / inner_all + epsilon)
    every = slice(None)
    put_deal_rows(out, every, deal_rows(tokens, every) + deal_rows(branch, every) * inv)


def input_kernel(
    size, place, low, high, middle, up, down, tokens, cot, inverse, sums, gain, out, grad_gain
):
    every = slice(None)
    here = place[0]
    width = tokens.shape[3]
    own = jnp.where(
        here == 0,
        deal_rows(low.at[0], every),
        jnp.where(here == size - 1, deal_rows(high.at[0], every), deal_rows(middle.at[0], every)),
    )
    rows_own = own + deal_rows(up, every) + deal_rows(down, every)
    inv = deal_rows(inverse, every)
    unit = deal_rows(tokens, every) * inv
    own_gain = gain[:, pl.ds(pl.multiple_of(here * width, width), width)]
    total = column_of(sums[0]) / (width * size)
    put_deal_rows(out, every, inv * (rows_own * own_gain - unit * total) + deal_rows(cot, every))
    product = jnp.sum(rows_own * unit, axis=0, keepdims=True)

    @pl.when(pl.program_id(0) == 0)
    def _():
        grad_gain[...] = product

    @pl.when(pl.program_id(0) > 0)
    def _():
        grad_gain[...] += product


def out_kernel(left, right, out):
    out[...] = dot(left[...], right[...]).astype(bf16)


def sent_kernel(columns, count, left, *refs):
    rights, out = refs[:count], refs[count]
    for which, source, target, size in columns:
        out[:, target : target + size] = dot(left[...], rights[which][:, source : source + size]).astype(bf16)


def kept_kernel(columns, count, cut, left, *refs):
    rights, other, outs = refs[:count], refs[count], refs[count + 1 :]
    step = pl.program_id(0)
    high, odd = step >= pl.num_programs(0) // 2, lax.rem(step, 2) == 1
    for which, source, target, size in columns:
        result = dot(left[...], rights[which][:, source : source + size])
        result = (result + other[:, target : target + size].astype(f32)).astype(bf16)
        if target < cut:
            keep, send, sending, start = outs[0], outs[1], high, target
        else:
            keep, send, sending, start = outs[2], outs[3], odd, target - cut
        tile = slice(start, start + size)

        @pl.when(sending)
        def _():
            send[:, tile] = result

        @pl.when(jnp.logical_not(sending))
        def _():
            keep[:, tile] = result


def total_kernel(targets, *refs):
    ins, outs = refs[:2], refs[2:]
    for out, (which, source, target, size) in zip([outs[t[0]] for t in targets], [t[1] for t in targets]):
        tile = slice(source, source + size)
        out[:, target : target + size] = ins[which][:, tile].astype(f32)


def weight_gradient_sent(odd_t, rights, columns, depth):
    total = odd_t.shape[1]
    width = max(target + size for _, _, target, size in columns)
    (sent,) = call(
        functools.partial(sent_kernel, columns, len(rights)), (odd_t.shape[0] // depth,), (),
        [(odd_t, (depth, total), lambda l: (l, 0))] + [entire(right) for right in rights],
        [((odd_t.shape[0], width), bf16, (depth, width), lambda l: (l, 0))],
        flops=2 * odd_t.shape[0] * total * width,
        bytes_accessed=odd_t.shape[0] * (total + width) * 2 + sum(right.size for right in rights) * 2,
    )
    return sent


def weight_gradient_kept(even_t, got, rights, columns, cut, depth):
    blocks = even_t.shape[0] // depth
    total = even_t.shape[1]
    width = got.shape[1]
    top = blocks // 2
    rows = even_t.shape[0] // 2
    half = lambda size, index: ((rows, size), bf16, (depth, size), index)
    return call(
        functools.partial(kept_kernel, columns, len(rights), cut), (blocks,), (),
        [(even_t, (depth, total), lambda l: (l, 0))] + [entire(right) for right in rights]
        + [(got, (depth, width), lambda l: (l, 0))],
        [
            half(cut, lambda l: (jnp.minimum(l, top - 1), 0)),
            half(cut, lambda l: (jnp.maximum(l - top, 0), 0)),
            half(width - cut, lambda l: (l // 2, 0)),
            half(width - cut, lambda l: (l // 2, 0)),
        ],
        flops=2 * even_t.shape[0] * total * width,
        bytes_accessed=even_t.shape[0] * (total + width) * 2 + sum(right.size for right in rights) * 2,
    )


def weight_gradient_parts(mine):
    links = axis_bits("seq")[1:]
    labels = [bit << 1 for bit in range(2 ** len(links))]
    return [
        Scattered(mine[0], mine[1], [x for x in labels if not x & links[-1]], links[::-1]),
        Scattered(mine[2], mine[3], [x for x in labels if not x & links[0]], links),
    ]


def weight_gradient_total(parts, results, depth):
    ins = [array for part in parts for array in part.finish()]
    targets = [(at, column) for at, (_, columns) in enumerate(results) for column in columns]
    return call(
        functools.partial(total_kernel, targets), (1,), (), [entire(a) for a in ins],
        [((depth, size), f32, (depth, size), lambda *_: (0, 0)) for size, _ in results],
        bytes_accessed=sum(a.size for a in ins) * 6,
    )


def per_device(
    tokens,
    cotangent,
    lengths,
    deal_order,
    norm_gain,
    proj_gate,
    proj_inner,
    proj_state,
    proj_step,
    conv_inner,
    conv_inner_bias,
    conv_state,
    conv_state_bias,
    step_bias,
    decay_log,
    skip_gain,
    inner_gain,
    proj_out,
):
    batch_count = lengths.shape[0]
    rows_local, width_own = tokens.shape
    tok_dev = rows_local // batch_count
    seq_index = lax.axis_index("seq")
    head_index = lax.axis_index("head")
    seq_size = lax.axis_size("seq")
    head_size = lax.axis_size("head")
    heads_own = proj_step.shape[1]
    inner_own = proj_inner.shape[1]
    head_width = inner_own // heads_own
    states = proj_state.shape[1] // 2
    taps_total = conv_inner.shape[0]
    width_all = width_own * head_size
    inner_all = inner_own * head_size
    depth = width_all // seq_size
    channels = inner_own + 2 * states
    per = LANES // head_width
    rows = tok_dev
    grid = (batch_count,)

    place = jnp.stack(
        [head_index, seq_index, seq_index * tok_dev, jnp.int32(tok_dev * seq_size)]
    ).astype(jnp.int32)
    plan = (jnp.cumsum(lengths, axis=1) - lengths).astype(jnp.int32)
    scalars = (place, plan)

    piece = tok_dev // seq_size
    dealt_row = deal_order.reshape(batch_count, seq_size, piece) + (
        jnp.arange(batch_count, dtype=jnp.int32) * tok_dev
    )[:, None, None]
    picks = (
        jnp.transpose(dealt_row, (1, 0, 2)).reshape(rows_local, 1) == jnp.arange(rows_local)[None, :]
    ).astype(bf16)
    deal_shape = (seq_size, batch_count, piece, width_own)

    def dealt(values):
        values = dot(picks, values).astype(bf16).reshape(seq_size, batch_count * piece, width_own)
        values = lax.all_to_all(values, "seq", split_axis=0, concat_axis=0, tiled=True)
        return values.reshape(deal_shape)

    def sent_back(values):
        values = values.reshape(seq_size, -1, width_own)
        return lax.all_to_all(values, "seq", split_axis=0, concat_axis=0, tiled=True)

    def put_back(values):
        return dot_tn(picks, values.reshape(rows_local, width_own)).astype(bf16)

    deal_tokens = dealt(tokens)
    lines = LineGather(deal_tokens)
    lines.advance()
    deal_cot = dealt(cotangent)

    full_in = lax.all_gather(
        jnp.concatenate(
            [proj_inner, proj_state, proj_step, jnp.zeros((depth, 2 * LANES - heads_own), bf16), proj_gate],
            axis=1,
        ),
        "seq", axis=0, tiled=True,
    )
    full_out = lax.all_gather(after(proj_out, lines.up, lines.down), "seq", axis=1, tiled=True)

    lines = lines.finish()
    normed, even_t, odd_t, own_t, inv_rms = all_features(deal_tokens, lines, place, norm_gain[None, :], depth)
    cot_lines = LineGather(after(deal_cot, lines[0][-1], lines[1][-1]))

    taps = jnp.concatenate([conv_inner, conv_state], axis=1)
    bias = jnp.concatenate([conv_inner_bias, conv_state_bias])[None, :]
    pad = LANES - heads_own
    step_bias_row = jnp.pad(step_bias, (0, pad))[None, :]
    scale = jnp.pad(-jnp.exp(decay_log), (0, pad))[None, :]
    spread = (
        jnp.arange(2 * LANES)[:, None] % LANES == jnp.arange(inner_own)[None, :] // head_width
    ).astype(bf16)
    skip = jnp.repeat(skip_gain, head_width)[None, :]
    gain = inner_gain[None, :]

    pre_width = channels + 2 * LANES
    (pre,) = cot_lines.advance(dot(normed, full_in[:, :pre_width]))
    halo = passed_along(pre.reshape(batch_count, tok_dev, -1)[:, tok_dev - HALO :], "seq", 1)
    gate = dot(normed, full_in[:, pre_width:]).astype(bf16)
    halo, gate = lax.optimization_barrier((halo, gate))
    conv_out, small, inputs, maps, fresh = call(
        functools.partial(conv_kernel, inner_own), grid, scalars,
        [per_row(pre, rows), per_step(halo)]
        + [entire(a) for a in (taps, bias, step_bias_row, scale, spread)],
        [
            row_out(rows_local, rows, channels, f32),
            row_out(rows_local, rows, 3 * LANES, f32),
            row_out(rows_local, rows, inner_own, bf16),
            row_out(rows_local, rows, 2 * states, f32),
            step_out(batch_count, (states + STATE_PAD, inner_own), bf16),
        ],
        scratch=[pltpu.VMEM((rows + HALO, LANES), f32)],
        flops=rows_local * inner_own * 2000, bytes_accessed=rows_local * inner_own * 20,
    )
    conv_out, small, inputs, maps, fresh = cot_lines.advance(conv_out, small, inputs, maps, fresh)
    scan_ins = [per_row(small, rows), per_row(maps, rows)]
    (mixed,) = call(
        functools.partial(mix_kernel, per), grid, scalars, scan_ins + [per_row(inputs, rows)],
        [row_out(rows_local, rows, inner_own, f32)],
        flops=rows_local * inner_own * 2500, bytes_accessed=rows_local * inner_own * 6,
    )
    cot_lines.advance()

    entering, mixed, (flat_cot, grad_y) = scan_before(
        fresh, states, False,
        [lambda: mixed, lambda _: cotangent_products(deal_cot, cot_lines.finish(), place, full_out)],
    )
    vectors = [entire(gain), entire(skip), entire(spread)]
    scanned, scaled_y, sums = call(
        gated_kernel, grid, scalars,
        scan_ins
        + [per_row(mixed, rows), per_step(entering), per_row(conv_out, rows), per_row(gate, rows)]
        + [per_row(grad_y, rows)] + vectors,
        [
            row_out(rows_local, rows, inner_own, f32),
            deal_out(seq_size, batch_count, piece, inner_own, bf16),
            step_out(batch_count, (HALO, rows), f32),
        ],
        flops=rows_local * inner_own * 1500, bytes_accessed=rows_local * inner_own * 8,
    )
    out_rows = dot(scaled_y.reshape(rows_local, inner_own), full_out).astype(bf16)
    sums = sums + swapped(sums, "head", 1)
    for bit in axis_bits("head")[1:]:
        other, out_rows = lax.optimization_barrier((swapped(sums, "head", bit), out_rows))
        sums = sums + other
    branch = lax.psum_scatter(
        out_rows.reshape(deal_shape[:3] + (width_all,)), "head", scatter_dimension=3, tiled=True
    )

    normed_y_t, grads, grad_gate, local, row_part, grad_gain, grad_skip = call(
        functools.partial(ungated_kernel, inner_all), grid, scalars,
        scan_ins
        + [per_row(array, rows) for array in (scanned, conv_out, gate, grad_y)]
        + [per_step(sums)] + vectors,
        [((inner_own, rows_local), bf16, (inner_own, rows), lambda m, *_: (0, m))]
        + [row_out(rows_local, rows, inner_own, bf16)] * 2
        + [step_out(batch_count, (states + STATE_PAD, inner_own), bf16)]
        + [step_out(batch_count, (HALO, rows), f32)]
        + [sum_out((1, inner_own))] * 2,
        flops=rows_local * inner_own * 2000, bytes_accessed=rows_local * inner_own * 24,
    )
    grad_inputs, grad_maps = call(
        functools.partial(unmix_kernel, per), grid, scalars,
        scan_ins + [per_row(inputs, rows), per_row(grads, rows)],
        [row_out(rows_local, rows, inner_own, f32), row_out(rows_local, rows, 2 * states, f32)],
        scratch=[pltpu.VMEM((rows, rows), f32)],
        flops=rows_local * inner_own * 4000, bytes_accessed=rows_local * inner_own * 8,
    )
    (grad_out,) = call(
        out_kernel, (head_size,), (),
        [entire(normed_y_t), (flat_cot, (rows_local, width_own), lambda q: (0, q))],
        [((inner_own, width_all), bf16, (inner_own, width_own), lambda q: (0, q))],
        flops=2 * rows_local * inner_own * width_all, bytes_accessed=rows_local * width_all * 6,
    )
    leaving, grad_inputs, grad_out = scan_before(
        local, states, True, [lambda: grad_inputs, lambda _: grad_out]
    )

    grad_out = lax.psum_scatter(grad_out, "seq", scatter_dimension=1, tiled=True)
    grad_conv_out, grad_step, grad_bias, grad_heads = call(
        unscan_kernel, grid, scalars,
        scan_ins
        + [per_row(a, rows) for a in (scanned, conv_out, inputs, grads)]
        + [per_row(grad_inputs, rows), per_row(grad_maps, rows)]
        + [per_step(entering), per_step(leaving), entire(skip), entire(scale), entire(spread)],
        [
            row_out(rows_local, rows, channels, f32),
            row_out(rows_local, rows, LANES, f32),
            sum_out((1, channels)),
            sum_out((HALO, LANES)),
        ],
        flops=rows_local * inner_own * 4000, bytes_accessed=rows_local * inner_own * 28,
    )
    after_rows = passed_along(grad_conv_out.reshape(batch_count, tok_dev, channels)[:, :HALO], "seq", -1)
    after_rows, branch = lax.optimization_barrier((after_rows, branch))
    grad_pre, grad_state, row_dots, grad_taps = call(
        unconv_kernel, grid, scalars,
        [per_row(pre, rows), per_step(halo), per_row(grad_conv_out, rows), per_step(after_rows)]
        + [per_row(grad_step, rows), per_step(row_part), entire(taps)],
        [
            row_out(rows_local, rows, channels + LANES, bf16),
            row_out(rows_local, rows, 2 * states, bf16),
            step_out(batch_count, (HALO, rows), f32),
            sum_out((taps_total, channels)),
        ],
        scratch=[pltpu.VMEM((rows + HALO, LANES), f32)] * 2,
        flops=rows_local * inner_own * 100, bytes_accessed=rows_local * inner_own * 14,
    )
    columns = [
        (0, 0, 0, inner_own), (1, 0, inner_own, inner_own), (0, channels, 2 * inner_own, LANES)
    ]
    fill = lambda row: jnp.pad(row, ((0, 0), (0, channels - row.shape[1])))
    state_small = jnp.concatenate([grad_taps[:, inner_own:], grad_bias[:, inner_own:]])
    row_dots = jnp.concatenate([row_dots[:, 0, :], state_small.reshape(-1, rows)])
    packed = jnp.concatenate(
        [grad_taps, grad_bias, fill(grad_gain), fill(grad_skip), fill(grad_heads[:2].reshape(1, 2 * LANES))]
    )
    packed = packed + swapped(packed, "seq", 1)
    seq_bits, head_bits = axis_bits("seq"), axis_bits("head")
    sent = weight_gradient_sent(odd_t, [grad_pre, grad_gate], columns, depth)
    others = [
        swapped(row_dots, "head", head_bits[0]), swapped(packed, "seq", seq_bits[1]),
        swapped(grad_state, "head", head_bits[0]),
    ]
    others, sent = lax.optimization_barrier((others, sent))
    row_dots, packed, grad_state = row_dots + others[0], packed + others[1], added(grad_state, others[2])
    got = swapped(sent, "seq", 1)
    grad_rows = lambda first, edges: rows_gradient(
        first, grad_gate, full_in, seq_size, batch_count, edges
    )
    low, high = grad_rows(after(grad_pre, sent), True)
    other, low, high = lax.optimization_barrier((swapped(packed, "seq", seq_bits[2]), low, high))
    packed = packed + other
    for bit in seq_bits[3:]:
        packed = packed + swapped(packed, "seq", bit)
    rows_line = LineScatter([low[0], high[0]])
    mine = weight_gradient_kept(even_t, after(got, low), [grad_pre, grad_gate], columns, inner_own, depth)
    rows_line.middle = grad_rows(after(grad_pre, mine[0]), False)
    others = [swapped(row_dots, "head", head_bits[1]), swapped(grad_state, "head", head_bits[1])]
    *mine, rows_line.middle, branch, others = rows_line.advance(*mine, rows_line.middle, branch, others)
    row_dots, grad_state = row_dots + others[0], added(grad_state, others[1])
    for bit in head_bits[2:]:
        row_dots = row_dots + swapped(row_dots, "head", bit)
        grad_state = added(grad_state, swapped(grad_state, "head", bit))
    (grad_w_state,) = call(
        out_kernel, (1,), (), [entire(own_t), entire(grad_state)], [sum_out((width_own, 2 * states), bf16)],
        flops=2 * rows_local * width_own * 2 * states, bytes_accessed=rows_local * (width_own + 2 * states) * 2,
    )
    state_small = row_dots[batch_count:].reshape(-1, 2 * states).astype(bf16)
    row_dots = row_dots[:batch_count, None, :]
    pad_rows = -state_small.shape[0] % 16
    grad_w_state = jnp.concatenate([grad_w_state, jnp.pad(state_small, ((0, pad_rows), (0, 0)))])
    grad_w_state = added(grad_w_state, swapped(grad_w_state, "seq", 1))
    parts = weight_gradient_parts(mine)
    for part in parts:
        part.send()
    grad_w_state, grad_out = rows_line.advance(grad_w_state, grad_out)
    other = swapped(grad_w_state, "seq", seq_bits[1])
    (out_rows,) = call(
        functools.partial(output_kernel, inner_all), grid, (),
        [per_deal(deal_tokens), per_deal(branch), per_step(sums)],
        [deal_out(seq_size, batch_count, piece, width_own, bf16)],
        bytes_accessed=rows_local * width_own * 6,
    )
    out_rows = sent_back(out_rows)
    for part in parts:
        part.receive()
    pairs = rows_line.advance(*[part.pair for part in parts], other, out_rows)
    other, out_rows = pairs[-2:]
    grad_w_state = added(grad_w_state, other)
    other = swapped(grad_w_state, "seq", seq_bits[2])
    for part, pair in zip(parts, pairs):
        part.pair = pair
        part.send()
    grad_out = grad_out.astype(f32)
    up, down = rows_line.finish()
    middle = rows_line.middle
    grad_rows_in, grad_norm_gain = call(
        functools.partial(input_kernel, head_size), grid, (place,),
        [per_deal_of(low), per_deal_of(high)]
        + [
            (
                middle, (1, seq_size, 1, piece, width_own),
                lambda m, place: (jnp.clip(place[0] - 1, 0, head_size - 3), 0, m, 0, 0),
            )
        ]
        + [per_deal(a) for a in (up, down, deal_tokens, deal_cot, inv_rms)]
        + [per_step(row_dots), entire(norm_gain[None, :])],
        [deal_out(seq_size, batch_count, piece, width_own, bf16), sum_out((1, width_own))],
        bytes_accessed=rows_local * width_own * 16,
    )
    parts[0].got, parts[1].got, other = after_all((parts[0].got, parts[1].got, other), (grad_rows_in,))
    grad_w_state = added(grad_w_state, other)
    for part in parts:
        part.receive()
        while part.left:
            part.send()
            part.receive()
    grad_inner, grad_w_gate, grad_w_step = weight_gradient_total(
        parts,
        [
            (inner_own, [(0, 0, 0, inner_own)]),
            (inner_own, [(1, 0, 0, inner_own)]),
            (LANES, [(1, inner_own, 0, LANES)]),
        ],
        depth,
    )
    for bit in seq_bits[3:]:
        grad_w_state = added(grad_w_state, swapped(grad_w_state, "seq", bit))
    out_back = put_back(out_rows)
    grad_w_state = grad_w_state.astype(f32)
    state_sums = grad_w_state[width_own : width_own + taps_total + 1]
    gain_high = grad_norm_gain.astype(bf16)
    gain_low = (grad_norm_gain - gain_high.astype(f32)).astype(bf16)
    gain_rows = jnp.pad(jnp.concatenate([gain_high, gain_low]), ((0, HALO - 2), (0, 0)))
    own_rows = batch_count * piece
    grad_back = sent_back(
        jnp.concatenate(
            [
                grad_rows_in.reshape(seq_size, own_rows, width_own),
                jnp.broadcast_to(gain_rows, (seq_size, HALO, width_own)),
            ],
            axis=1,
        )
    )
    grad_norm_gain = jnp.sum(grad_back[:, own_rows : own_rows + 2].astype(f32), axis=(0, 1))
    grad_back = put_back(grad_back[:, :own_rows])
    state_own = 2 * states // head_size
    state_sums = lax.dynamic_slice_in_dim(state_sums, head_index * state_own, state_own, 1)
    return (
        out_back,
        grad_back,
        grad_norm_gain,
        grad_w_gate,
        grad_inner,
        grad_w_state[:width_own],
        grad_w_step[:, :heads_own],
        packed[:taps_total, :inner_own],
        packed[taps_total, :inner_own],
        state_sums[:taps_total],
        state_sums[taps_total],
        packed[taps_total + 3, LANES : LANES + heads_own],
        packed[taps_total + 3, :heads_own],
        jnp.sum(packed[taps_total + 2, :inner_own].reshape(heads_own, head_width), axis=1),
        packed[taps_total + 1, :inner_own],
        grad_out,
    )


def solution(mesh):
    return jax.shard_map(
        per_device,
        mesh=mesh,
        in_specs=(
            P("seq", "head"),
            P("seq", "head"),
            P(),
            P("seq"),
            P(),
            P("seq", "head"),
            P("seq", "head"),
            P("seq", None),
            P("seq", "head"),
            P(None, "head"),
            P("head"),
            P(),
            P(),
            P("head"),
            P("head"),
            P("head"),
            P("head"),
            P("head", "seq"),
        ),
        out_specs=(
            P("seq", "head"),
            P("seq", "head"),
            P("head"),
            P("seq", "head"),
            P("seq", "head"),
            P("head", None),
            P("seq", "head"),
            P(None, "head"),
            P("head"),
            P(None, "head"),
            P("head"),
            P("head"),
            P("head"),
            P("head"),
            P("head"),
            P("head", "seq"),
        ),
        check_vma=False,
    )
```

```python
import functools
import math
import jax
import jax.numpy as jnp
from jax import lax
from jax.experimental import pallas as pl
from jax.experimental.pallas import tpu as pltpu
from jax.sharding import PartitionSpec as P

epsilon = 1e-05
highest = lax.Precision.HIGHEST
f32 = jnp.float32
bf16 = jnp.bfloat16
LANES = 128
HALO = 8
STATE_PAD = 16
HBM_BYTES = 700000
VMEM_SPARE = 10 * 1024 * 1024


def swapped(value, axis, bit):
    return lax.ppermute(value, axis, [(i, i ^ bit) for i in range(lax.axis_size(axis))])


def axis_bits(axis):
    count = lax.axis_size(axis)
    return [1 << k for k in range(count.bit_length() - 1)]


def added(left, right):
    return (left.astype(f32) + right.astype(f32)).astype(left.dtype)


def after(value, *others):
    return lax.optimization_barrier((value, *others))[0]


def after_all(values, others):
    return lax.optimization_barrier((tuple(values), tuple(others)))[0]


class Scattered:
    def __init__(self, keep, send, labels, order):
        rows = keep.shape[0] // len(labels)
        self.pair = (keep.reshape(len(labels), rows, -1), send.reshape(len(labels), rows, -1))
        self.labels, self.left = labels, list(order)

    def send(self):
        self.got = swapped(self.pair[1], "seq", self.left.pop(0))

    def receive(self):
        total = added(self.pair[0], self.got)
        if not self.left:
            self.pair = (total,)
            return
        following, labels = self.left[0], self.labels
        keep_at = [at for at, label in enumerate(labels) if not label & following]
        send_at = [labels.index(labels[at] ^ following) for at in keep_at]
        kept = jnp.concatenate([total[at : at + 1] for at in keep_at])
        sent = jnp.concatenate([total[at : at + 1] for at in send_at])
        self.pair = (kept, sent)
        self.labels = [labels[at] for at in keep_at]

    def finish(self):
        return [self.pair[0][0]]


class LineGather:
    def __init__(self, own):
        self.size = lax.axis_size("head")
        self.up = self.down = own
        self.ups, self.downs = [], []

    def advance(self, *beside):
        step = len(self.ups) + 1
        if step < self.size:
            up = lax.ppermute(self.up, "head", [(i, i + 1) for i in range(step - 1, self.size - 1)])
            down = lax.ppermute(self.down, "head", [(i, i - 1) for i in range(1, self.size - step + 1)])
            if beside:
                (up, down), beside = lax.optimization_barrier(((up, down), beside))
            self.up, self.down = up, down
            self.ups.append(up)
            self.downs.append(down)
        return beside

    def finish(self):
        while len(self.ups) + 1 < self.size:
            self.advance()
        return self.ups, self.downs


class LineScatter:
    def __init__(self, edges, middle=None):
        self.size, self.here = lax.axis_size("head"), lax.axis_index("head")
        self.edges, self.middle = edges, middle
        self.up = self.down = None
        self.step = 0

    def block_of(self, at):
        last = self.size - 1
        inner = lax.dynamic_index_in_dim(self.middle, jnp.clip(at - 1, 0, last - 2), 0, keepdims=False)
        return jnp.where(at <= 0, self.edges[0], jnp.where(at >= last, self.edges[1], inner))

    def advance(self, *beside):
        self.step += 1
        step, size, here = self.step, self.size, self.here
        if step < size:
            if step == 1:
                up, down = self.edges[1], self.edges[0]
            else:
                up = added(self.block_of(here + size - step), self.up)
                down = added(self.block_of(here - size + step), self.down)
            up = lax.ppermute(up, "head", [(i, i + 1) for i in range(step)])
            down = lax.ppermute(down, "head", [(i, i - 1) for i in range(size - step, size)])
            if beside:
                (up, down), beside = lax.optimization_barrier(((up, down), beside))
            self.up, self.down = up, down
        return beside

    def finish(self):
        while self.step + 1 < self.size:
            self.advance()
        return self.up, self.down


def axis_sum(value, axis):
    for bit in axis_bits(axis):
        value = value + swapped(value, axis, bit)
    return value


def passed_along(value, axis, steps):
    count = lax.axis_size(axis)
    initial, last = (max(0, -steps), min(count, count - steps))
    return lax.ppermute(value, axis, [(source, source + steps) for source in range(initial, last)])


def dot(left, right, precision=None):
    return jnp.dot(left, right, preferred_element_type=f32, precision=precision)


def dot_nt(left, right, precision=None):
    return lax.dot_general(
        left, right, (((1,), (1,)), ((), ())), preferred_element_type=f32, precision=precision
    )


def dot_tn(left, right, precision=None):
    return lax.dot_general(
        left, right, (((0,), (0,)), ((), ())), preferred_element_type=f32, precision=precision
    )


def both_parts(values):
    high = values.astype(bf16)
    return jnp.concatenate([high, (values - high.astype(f32)).astype(bf16)], axis=1)


def three_parts(values):
    high = values.astype(bf16)
    rest = values - high.astype(f32)
    middle = rest.astype(bf16)
    return high, middle, (rest - middle.astype(f32)).astype(bf16)


def dot_mask(mask, values):
    return sum(dot(mask, part) for part in three_parts(values))


def silu_slope(values):
    logistic = jax.nn.sigmoid(values)
    return logistic * (1.0 + values * (1.0 - logistic))


def big(shape, dtype):
    return math.prod(shape) * jnp.dtype(dtype).itemsize > HBM_BYTES


def tiled_bytes(shape, dtype):
    *lead, rows, lanes = shape
    size = -(-rows // 8) * 8 * -(-lanes // LANES) * LANES * jnp.dtype(dtype).itemsize
    for count in lead:
        size *= count
    return size


def call(kernel, grid, scalars, ins, outs, scratch=(), flops=0, bytes_accessed=0):
    ins = [(streamed(a) if big(a.shape, a.dtype) else a, block, index) for a, block, index in ins]
    held = [block == array.shape for array, block, _ in ins]
    need = sum(
        (1 if whole else 2) * tiled_bytes(block, array.dtype) for (array, block, _), whole in zip(ins, held)
    )
    need += sum(2 * tiled_bytes(block, dtype) for _, dtype, block, _ in outs)
    need += sum(tiled_bytes(item.shape, item.dtype) for item in scratch)
    return pl.pallas_call(
        kernel,
        grid_spec=pltpu.PrefetchScalarGridSpec(
            num_scalar_prefetch=len(scalars),
            grid=grid,
            in_specs=[
                pl.BlockSpec(block, index, pipeline_mode=pl.Buffered(1) if whole else None)
                for (_, block, index), whole in zip(ins, held)
            ],
            out_specs=[pl.BlockSpec(block, index) for _, _, block, index in outs],
            scratch_shapes=list(scratch),
        ),
        out_shape=[
            (pltpu.HBM if big(shape, dtype) else jax.ShapeDtypeStruct)(shape, dtype) for shape, dtype, _, _ in outs
        ],
        compiler_params=pltpu.CompilerParams(vmem_limit_bytes=need + VMEM_SPARE),
        cost_estimate=pl.CostEstimate(
            flops=int(flops), bytes_accessed=int(bytes_accessed), transcendentals=0
        ),
    )(*scalars, *[array for array, _, _ in ins])


def streamed(array):
    return pltpu.with_memory_space_constraint(array, pltpu.HBM)


def per_row(array, rows):
    return (array, (rows,) + array.shape[1:], lambda m, *_: (m,) + (0,) * (array.ndim - 1))


def per_deal(array):
    return (array, (array.shape[0], 1) + array.shape[2:], lambda m, *_: (0, m, 0, 0))


def per_deal_of(array):
    return (array, (1, array.shape[1], 1) + array.shape[3:], lambda m, *_: (0, 0, m, 0, 0))


def deal_out(senders, count, rows, width, dtype):
    return ((senders, count, rows, width), dtype, (senders, 1, rows, width), lambda m, *_: (0, m, 0, 0))


def deal_rows(ref, tile):
    values = ref[:, 0, :, tile].astype(f32)
    return values.reshape(values.shape[0] * values.shape[1], values.shape[2])


def put_deal_rows(ref, tile, values):
    shape = (ref.shape[0], ref.shape[2], values.shape[1])
    ref[:, 0, :, tile] = values.reshape(shape).astype(ref.dtype)


def per_step(array):
    return (array, (1,) + array.shape[1:], lambda m, *_: (m,) + (0,) * (array.ndim - 1))


def entire(array):
    return (array, array.shape, lambda *_: (0,) * array.ndim)


def row_out(total, rows, width, dtype):
    return ((total, width), dtype, (rows, width), lambda m, *_: (m, 0))


def step_out(count, shape, dtype):
    return ((count,) + shape, dtype, (1,) + shape, lambda m, *_: (m,) + (0,) * len(shape))


def sum_out(shape, dtype=f32):
    return (shape, dtype, shape, lambda *_: (0,) * len(shape))


def joined(earlier, following, states):
    row = lax.broadcasted_iota(jnp.int32, earlier.shape, 0)
    return following[states : states + 1] * earlier + jnp.where(row < states, following, 0.0)


def chip_kernel(states, flags, own, other, total):
    for at in range(own.shape[0]):
        mine, theirs = own[at].astype(f32), other[at].astype(f32)
        later = flags[0] != 0
        first, second = jnp.where(later, theirs, mine), jnp.where(later, mine, theirs)
        total[at] = joined(first, second, states).astype(bf16)


def link_kernel(states, step, last, flags, *refs):
    total, other, refs = refs[0], refs[1], refs[2:]
    later = flags[step] != 0
    if step > 1:
        before, refs = refs[0], refs[1:]
    for at in range(total.shape[0]):
        mine, theirs = total[at].astype(f32), other[at].astype(f32)
        if step == 1:
            row = lax.broadcasted_iota(jnp.int32, mine.shape, 0)
            ahead = jnp.where(row < states, 0.0, 1.0)
            refs[0][at] = jnp.where(later, theirs, ahead).astype(bf16)
        else:
            ahead = before[at].astype(f32)
            refs[0][at] = jnp.where(later, joined(theirs, ahead, states), ahead).astype(bf16)
        if not last:
            first, second = jnp.where(later, theirs, mine), jnp.where(later, mine, theirs)
            refs[1][at] = joined(first, second, states).astype(bf16)


def state_tile(states, flags, ahead, ahead_other, sibling, at):
    odd = flags[flags.shape[0] - 1] != 0
    half = ahead.shape[2]
    tile = slice(at % half, at % half + LANES)
    mine, theirs = ahead[0, :, tile], ahead_other[0, :, tile]
    values = (jnp.where(odd, theirs, mine) if at < half else jnp.where(odd, mine, theirs)).astype(f32)
    near = sibling[0, :, at : at + LANES].astype(f32)
    return jnp.where(flags[0] != 0, joined(values, near, states), values)[:states].astype(bf16)


def scan_before(local, states, reverse, fillers):
    here = lax.axis_index("seq")
    bits = axis_bits("seq")
    count, height, width = local.shape
    passed = [((here & bit) == 0) if reverse else ((here & bit) != 0) for bit in bits]
    flags = jnp.stack(passed + [(here & 1) != 0]).astype(jnp.int32)
    whole = local.shape
    piece = (count, height, width // 2)
    at_step = lambda *_: (0, 0, 0)
    at_core = lambda _, flags: (0, 0, flags[len(bits)])
    half_out = (piece, bf16, piece, at_step)
    moved = local.size * 4
    sibling = swapped(local, "seq", 1)
    (total,) = call(
        functools.partial(chip_kernel, states), (1,), (flags,),
        [(local, piece, at_core), (sibling, piece, at_core)], [half_out], bytes_accessed=moved,
    )
    ahead, filled, beside = None, [], ()
    for step, bit in enumerate(bits[1:], 1):
        other = swapped(total, "seq", bit)
        if step <= len(fillers):
            other, value = lax.optimization_barrier((other, fillers[step - 1](*beside)))
            beside = (value,)
            filled.append(value)
        last = step == len(bits) - 1
        ins = [total, other] + ([] if ahead is None else [ahead])
        results = call(
            functools.partial(link_kernel, states, step, last), (1,), (flags,),
            [(array, piece, at_step) for array in ins], [half_out] * (1 if last else 2),
            bytes_accessed=moved,
        )
        ahead = results[0]
        total = None if last else results[1]
    ahead_other = swapped(ahead, "seq", 1)
    return [(flags, ahead, ahead_other, sibling)] + filled


def columns_of(rows_form):
    rows = rows_form.shape[1]
    row = lax.broadcasted_iota(jnp.int32, (rows, rows), 0)
    col = lax.broadcasted_iota(jnp.int32, (rows, rows), 1)
    same = jnp.where(row == col, 1.0, 0.0).astype(bf16)
    return dot_nt(same.astype(f32), rows_form, highest)


def segment_of(position, plan, place, m):
    found = jnp.full(jnp.shape(position), -1, jnp.int32)
    for k in range(plan.shape[1]):
        found = found + (position >= plan[m, k]).astype(jnp.int32)
    return jnp.where(position >= place[3], -2, found)


def column_position(rows, place, shift=0):
    return place[2] + shift + lax.broadcasted_iota(jnp.int32, (rows, 1), 0)


def row_position(rows, place):
    return place[2] + lax.broadcasted_iota(jnp.int32, (1, rows), 1)


def by_core(values, me, depth):
    count = values.shape[1] // depth
    blocks = [values[:, k * depth : (k + 1) * depth] for k in range(count)]
    odd = (me & 1) != 0
    halves = []
    for at in (0, 1):
        straight, turned = blocks[at::2], blocks[1 - at :: 2]
        half = [jnp.where(odd, b, a) for a, b in zip(straight, turned)]
        bit = 1
        while bit < count // 2:
            flip = ((me >> 1) & bit) != 0
            half = [jnp.where(flip, half[k ^ bit], half[k]) for k in range(len(half))]
            bit *= 2
        halves.append(half[0] if len(half) == 1 else jnp.concatenate(half, axis=1))
    return halves


def half_start(quarter, me, width, depth):
    count = width // depth // 2
    return pl.multiple_of(((quarter * count) ^ ((me >> 1) & ~(count - 1))) * depth, width // 2)


def line_slot(own, ups, downs, z, step):
    if step == 0:
        return deal_rows(own, slice(None))
    up, down = ups[step - 1], downs[len(downs) - step]
    return jnp.where(z >= step, deal_rows(up, slice(None)), deal_rows(down, slice(None)))


def features_kernel(size, depth, place, *refs):
    own, ups, downs = refs[0], refs[1:size], refs[size : 2 * size - 1]
    gain, normed, even_t, odd_t, own_t, inverse = refs[2 * size - 1 :]
    z, me = place[0], place[1]
    width = own.shape[3]
    slots = [line_slot(own, ups, downs, z, step) for step in range(size)]
    square = sum(jnp.sum(slot * slot, axis=1, keepdims=True) for slot in slots)
    inv = lax.rsqrt(square / (width * size) + epsilon)
    put_deal_rows(inverse, slice(None), inv)
    for step, slot in enumerate(slots):
        quarter = lax.rem(z - step + size, size)
        place_at = pl.ds(pl.multiple_of(quarter * width, width), width)
        slot = slot * inv * gain[:, place_at]
        normed[:, place_at] = slot.astype(bf16)
        if step == 0:
            own_t[...] = slot.astype(bf16).T
        first, second = by_core(slot, me, depth)
        at = pl.ds(half_start(quarter, me, width, depth), width // 2)
        even_t[at, :] = first.astype(bf16).T
        odd_t[at, :] = second.astype(bf16).T


def all_features(own, lines, place, gain, depth):
    senders, count, piece, width = own.shape
    rows = senders * piece
    total = rows * count
    size = lax.axis_size("head")
    ups, downs = lines
    half = width * size // 2
    outs = [row_out(total, rows, 2 * half, bf16)]
    outs += [((half, total), bf16, (half, rows), lambda m, *_: (0, m))] * 2
    outs.append(((width, total), bf16, (width, rows), lambda m, *_: (0, m)))
    outs.append(deal_out(senders, count, piece, 1, f32))
    return call(
        functools.partial(features_kernel, size, depth), (count,), (place,),
        [per_deal(array) for array in [own] + ups + downs] + [entire(gain)], outs,
        bytes_accessed=total * width * 2 * 15,
    )


def cotangent_kernel(size, place, *refs):
    own, ups, downs = refs[0], refs[1:size], refs[size : 2 * size - 1]
    weight, every, grad_y = refs[2 * size - 1 :]
    z = place[0]
    width = own.shape[3]
    total = None
    for step in range(size):
        slot = line_slot(own, ups, downs, z, step)
        quarter = lax.rem(z - step + size, size)
        place_at = pl.ds(pl.multiple_of(quarter * width, width), width)
        every[:, place_at] = slot.astype(bf16)
        part = dot_nt(slot.astype(bf16), weight[:, place_at])
        total = part if total is None else total + part
    grad_y[...] = total.astype(bf16)


def cotangent_products(own, lines, place, weight):
    senders, count, piece, width = own.shape
    rows = senders * piece
    total = rows * count
    size = lax.axis_size("head")
    ups, downs = lines
    return call(
        functools.partial(cotangent_kernel, size), (count,), (place,),
        [per_deal(array) for array in [own] + ups + downs] + [entire(weight)],
        [
            row_out(total, rows, width * size, bf16),
            row_out(total, rows, weight.shape[0], bf16),
        ],
        flops=2 * total * width * size * weight.shape[0],
        bytes_accessed=total * width * 2 * 11 + weight.size * 2 + total * weight.shape[0] * 4,
    )


def conv_kernel(
    width, place, plan, pre, halo, taps, bias, step_bias, scale, spread, conv_out, small, inputs, maps, fresh,
    extended,
):
    m = pl.program_id(0)
    rows = pre.shape[0]
    states = maps.shape[1] // 2
    taps_total = taps.shape[0]
    here = segment_of(column_position(rows, place), plan, place, m)
    same = [
        (segment_of(column_position(rows, place, tap + 1 - taps_total), plan, place, m) == here).astype(f32)
        for tap in range(taps_total)
    ]
    before = segment_of(place[2] - 1, plan, place, m)
    last = segment_of(place[2] + rows - 1, plan, place, m)

    step_pre = pre[:, width + 2 * states : width + 2 * states + LANES] + step_bias[...]
    rest = jnp.exp(-jnp.abs(step_pre))
    series = rest * (
        1.0 - rest * (1 / 2 - rest * (1 / 3 - rest * (1 / 4 - rest * (1 / 5 - rest * (1 / 6)))))
    )
    step = jnp.maximum(step_pre, 0.0) + jnp.where(rest < 0.03, series, jnp.log(1.0 + rest))
    row = lax.broadcasted_iota(jnp.int32, (rows, rows), 0)
    col = lax.broadcasted_iota(jnp.int32, (rows, rows), 1)
    lower = jnp.where(row >= col, 1.0, 0.0).astype(bf16)
    cumulative = dot_mask(lower, step * scale[...])
    small[:, :LANES] = cumulative
    small[:, LANES : 2 * LANES] = step
    small[:, 2 * LANES :] = step_pre
    ending = cumulative[rows - 1 :, :]
    fading = (here == last).astype(f32) * jnp.exp(ending - cumulative)
    through = (last == before).astype(f32) * jnp.exp(ending)
    step_parts, fading_parts = both_parts(step), both_parts(fading)
    through_parts = both_parts(jnp.broadcast_to(through, (STATE_PAD, LANES)))

    def conv(at):
        tile = slice(at, at + LANES)
        rows_before = extended.at[at // LANES % 2]
        own = pre[:, tile]
        rows_before[:HALO, :] = halo[0, :, tile]
        rows_before[HALO:, :] = own
        result = bias[:, tile] + taps[taps_total - 1 :, tile] * own
        for tap in range(taps_total - 1):
            start = HALO + tap + 1 - taps_total
            result = result + taps[tap : tap + 1, tile] * rows_before[start : start + rows, :] * same[tap]
        conv_out[:, tile] = result
        return result * jax.nn.sigmoid(result)

    for at in range(0, 2 * states, LANES):
        maps[:, at : at + LANES] = conv(width + at)
    input_map_t = maps[:, :states].T.astype(bf16)
    for at in range(0, width, LANES):
        tile = slice(at, at + LANES)
        values = conv(at) * dot(step_parts, spread[:, tile])
        inputs[:, tile] = values.astype(bf16)
        faded = (values * dot(fading_parts, spread[:, tile])).astype(bf16)
        fresh[0, :states, tile] = dot(input_map_t, faded).astype(bf16)
        fresh[0, states:, tile] = dot(through_parts, spread[:, tile]).astype(bf16)


def allowed_mask(rows, place, plan, m, transposed):
    column = segment_of(column_position(rows, place), plan, place, m)
    across = segment_of(row_position(rows, place), plan, place, m)
    row = lax.broadcasted_iota(jnp.int32, (rows, rows), 0)
    col = lax.broadcasted_iota(jnp.int32, (rows, rows), 1)
    order = (row <= col) if transposed else (row >= col)
    return jnp.where(order & (column == across), 0.0, -1e30)


def lane_select(parts, per):
    lane = lax.broadcasted_iota(jnp.int32, parts[0].shape, 1)
    result = parts[0]
    for at in range(1, per):
        result = jnp.where(lane >= at * (LANES // per), parts[at], result)
    return result


def mix_kernel(per, place, plan, small, maps, inputs, out):
    m = pl.program_id(0)
    rows, width = inputs.shape
    states = maps.shape[1] // 2
    cumulative = small[:, :LANES]
    flat = cumulative.T
    mask = allowed_mask(rows, place, plan, m, False)
    scores = dot_nt(maps[:, states:], maps[:, :states], highest)
    for at in range(0, width, LANES):
        tile = slice(at, at + LANES)
        for low in range(0, rows, LANES):
            end = low + LANES
            parts = []
            for sub in range(per):
                head = at // LANES * per + sub
                decay = jnp.exp(
                    (cumulative[low:end, head : head + 1] - flat[head : head + 1, :end])
                    + mask[low:end, :end]
                )
                mixing = (decay * scores[low:end, :end]).astype(bf16)
                parts.append(dot(mixing, inputs[:end, tile]))
            out[low:end, tile] = lane_select(parts, per)


def unmix_kernel(per, place, plan, small, maps, inputs, grads, grad_inputs, grad_maps, total):
    m = pl.program_id(0)
    rows, width = inputs.shape
    states = maps.shape[1] // 2
    cumulative = small[:, :LANES]
    flat = cumulative.T
    mask = allowed_mask(rows, place, plan, m, True)
    scores = dot_nt(maps[:, :states], maps[:, states:], highest)
    lane = lax.broadcasted_iota(jnp.int32, (LANES, LANES), 1)
    total[...] = jnp.zeros_like(total)
    for at in range(0, width, LANES):
        tile = slice(at, at + LANES)
        for low in range(0, rows, LANES):
            end = low + LANES
            later = grads[low:, tile]
            parts = []
            gathered_sum = total[low:end, low:]
            for sub in range(per):
                head = at // LANES * per + sub
                decay = jnp.exp(
                    (flat[head : head + 1, low:] - cumulative[low:end, head : head + 1])
                    + mask[low:end, low:]
                )
                mixing = (decay * scores[low:end, low:]).astype(bf16)
                parts.append(dot(mixing, later))
                inside = (lane // (LANES // per)) == sub
                own = jnp.where(inside, inputs[low:end, tile].astype(f32), 0.0).astype(bf16)
                gathered_sum = gathered_sum + decay * dot_nt(own, later)
            total[low:end, low:] = gathered_sum
            grad_inputs[low:end, tile] = lane_select(parts, per)
    grad_scores = total[...].astype(bf16)
    grad_maps[:, :states] = dot(grad_scores, maps[:, states:].astype(bf16))
    grad_maps[:, states:] = dot_tn(grad_scores, maps[:, :states].astype(bf16))


def inflow_of(cumulative, rows, place, plan, m):
    here = segment_of(column_position(rows, place), plan, place, m)
    before = segment_of(place[2] - 1, plan, place, m)
    return (here == before).astype(f32) * jnp.exp(cumulative)


def gated_kernel(
    place, plan, flags, small, maps, mixed, ahead, ahead_other, sibling, conv_out, gate, grad_y, gain, skip, spread, scanned, scaled_y, sums
):
    m = pl.program_id(0)
    rows, width = mixed.shape
    states = maps.shape[1] // 2
    inflow = both_parts(inflow_of(small[:, :LANES], rows, place, plan, m))
    output_map = maps[:, states:].astype(bf16)
    square = jnp.zeros((rows, LANES), f32)
    product = jnp.zeros((rows, LANES), f32)
    for at in range(0, width, LANES):
        tile = slice(at, at + LANES)
        entering = state_tile(states, flags, ahead, ahead_other, sibling, at)
        carried = dot(output_map, entering) * dot(inflow, spread[:, tile])
        scan = mixed[:, tile] + carried
        scanned[:, tile] = scan
        conv = conv_out[:, tile]
        gates = gate[:, tile].astype(f32)
        gated = (scan + skip[:, tile] * (conv * jax.nn.sigmoid(conv))) * (gates * jax.nn.sigmoid(gates))
        square = square + gated * gated
        scaled = gain[:, tile] * gated
        put_deal_rows(scaled_y, tile, scaled)
        product = product + grad_y[:, tile].astype(f32) * scaled
    ones = jnp.ones((HALO, LANES), f32)
    pick = lax.broadcasted_iota(jnp.int32, (HALO, rows), 0)
    sums[0] = jnp.where(pick == 0, dot_nt(ones, square, highest), dot_nt(ones, product, highest))


def ungated_kernel(
    inner_all, place, plan, small, maps, scanned, conv_out, gate, grad_y, sums, gain, skip, spread,
    normed_y_t, grads, grad_gate, local, row_part, grad_gain, grad_skip,
):
    m = pl.program_id(0)
    rows, width = scanned.shape
    states = maps.shape[1] // 2
    columns = columns_of(sums[0])
    inv = lax.rsqrt(columns[:, :1] / inner_all + epsilon)
    pull = inv * inv * inv * (columns[:, 1:2] / inner_all)
    cumulative = small[:, :LANES]
    inflow = both_parts(inflow_of(cumulative, rows, place, plan, m))
    before = segment_of(place[2] - 1, plan, place, m)
    last = segment_of(place[2] + rows - 1, plan, place, m)
    through = (last == before).astype(f32) * jnp.exp(cumulative[rows - 1 :, :])
    through_parts = both_parts(jnp.broadcast_to(through, (STATE_PAD, LANES)))
    output_map_t = maps[:, states:].T.astype(bf16)

    @pl.when(m == 0)
    def _():
        grad_gain[...] = jnp.zeros_like(grad_gain)
        grad_skip[...] = jnp.zeros_like(grad_skip)

    product = jnp.zeros((rows, LANES), f32)
    for at in range(0, width, LANES):
        tile = slice(at, at + LANES)
        conv = conv_out[:, tile]
        heads_x = conv * jax.nn.sigmoid(conv)
        mixer = scanned[:, tile] + skip[:, tile] * heads_x
        gates = gate[:, tile].astype(f32)
        logistic = jax.nn.sigmoid(gates)
        act = gates * logistic
        gated = mixer * act
        normed = gated * inv
        normed_y_t[tile, :] = (normed * gain[:, tile]).astype(bf16).T
        grad = grad_y[:, tile].astype(f32)
        grad_gain[:, tile] += jnp.sum(grad * normed, axis=0, keepdims=True)
        grad_gated = inv * (grad * gain[:, tile]) - gated * pull
        grad_mixer = grad_gated * act
        grads[:, tile] = grad_mixer.astype(bf16)
        grad_skip[:, tile] += jnp.sum(grad_mixer * heads_x, axis=0, keepdims=True)
        grad_gates = grad_gated * mixer * (logistic * (1.0 + gates * (1.0 - logistic)))
        grad_gate[:, tile] = grad_gates.astype(bf16)
        product = product + grad_gates * gates
        weighted = (grad_mixer * dot(inflow, spread[:, tile])).astype(bf16)
        local[0, :states, tile] = dot(output_map_t, weighted).astype(bf16)
        local[0, states:, tile] = dot(through_parts, spread[:, tile]).astype(bf16)
    row_part[0] = dot_nt(jnp.ones((HALO, LANES), f32), product, highest)


def unscan_kernel(
    place, plan, flags, flags_back, small, maps, scanned, conv_out, inputs, grads, grad_inputs, grad_maps,
    ahead, ahead_other, sibling, back, back_other, back_sibling, skip, scale, spread, grad_conv_out, grad_step, grad_bias, grad_heads,
):
    m = pl.program_id(0)
    rows, width = scanned.shape
    states = maps.shape[1] // 2
    cumulative, step, pre = (small[:, k * LANES : (k + 1) * LANES] for k in range(3))
    here = segment_of(column_position(rows, place), plan, place, m)
    before = segment_of(place[2] - 1, plan, place, m)
    last = segment_of(place[2] + rows - 1, plan, place, m)
    ending = cumulative[rows - 1 :, :]
    fading = both_parts((here == last).astype(f32) * jnp.exp(ending - cumulative))
    inflow = both_parts((here == before).astype(f32) * jnp.exp(cumulative))
    through = (last == before).astype(f32) * jnp.exp(ending)
    step_parts = both_parts(step)
    input_map = maps[:, :states].astype(bf16)

    @pl.when(m == 0)
    def _():
        grad_bias[...] = jnp.zeros_like(grad_bias)
        grad_heads[...] = jnp.zeros_like(grad_heads)

    grad_in, grad_out = grad_maps[:, :states], grad_maps[:, states:]
    grad_cum = jnp.zeros((rows, LANES), f32)
    grad_own = jnp.zeros((rows, LANES), f32)
    ends = jnp.zeros((HALO, LANES), f32)
    for at in range(0, width, LANES):
        tile = slice(at, at + LANES)
        spread_tile = spread[:, tile]
        leave = state_tile(states, flags_back, back, back_other, back_sibling, at)
        enter = state_tile(states, flags, ahead, ahead_other, sibling, at)
        fade = dot(fading, spread_tile)
        pulled = fade * dot(input_map, leave)
        values = inputs[:, tile].astype(f32)
        grad = grads[:, tile].astype(f32)
        total = grad_inputs[:, tile] + pulled
        faded = (values * fade).astype(bf16)
        weighted = (grad * dot(inflow, spread_tile)).astype(bf16)
        grad_in = grad_in + dot_nt(faded, leave)
        grad_out = grad_out + dot_nt(weighted, enter)
        conv = conv_out[:, tile]
        logistic = jax.nn.sigmoid(conv)
        heads_x = conv * logistic
        first = both_parts(grad * scanned[:, tile] - values * total)
        second = both_parts(total * heads_x)
        twice = jnp.concatenate([spread[:LANES, tile]] * 2, axis=1)
        grad_cum = grad_cum + dot_nt(first, twice)
        grad_own = grad_own + dot_nt(second, twice)
        fade_sum = jnp.sum(values * pulled, axis=0, keepdims=True)
        through_sum = jnp.sum(leave.astype(f32) * enter.astype(f32), axis=0, keepdims=True)
        pick = lax.broadcasted_iota(jnp.int32, (HALO, LANES), 0)
        edge = both_parts(jnp.where(pick == 0, fade_sum, through_sum))
        ends = ends + dot_nt(edge, twice)
        grad_x = total * dot(step_parts, spread_tile) + skip[:, tile] * grad
        result = grad_x * (logistic * (1.0 + conv * (1.0 - logistic)))
        grad_conv_out[:, tile] = result
        grad_bias[:, tile] += jnp.sum(result, axis=0, keepdims=True)
    for values, start in ((grad_in, width), (grad_out, width + states)):
        conv = conv_out[:, start : start + states]
        result = values * silu_slope(conv)
        grad_conv_out[:, start : start + states] = result
        grad_bias[:, start : start + states] += jnp.sum(result, axis=0, keepdims=True)
    row = lax.broadcasted_iota(jnp.int32, (rows, rows), 0)
    col = lax.broadcasted_iota(jnp.int32, (rows, rows), 1)
    upper = jnp.where(row <= col, 1.0, 0.0).astype(bf16)
    grad_rate = dot_mask(upper, grad_cum) + (ends[:1] + through * ends[1:2])
    rate = step * scale[...]
    grad_pre = (grad_rate * scale[...] + grad_own) * jax.nn.sigmoid(pre)
    grad_step[...] = grad_pre
    grad_heads[0:1, :] += jnp.sum(grad_rate * rate, axis=0, keepdims=True)
    grad_heads[1:2, :] += jnp.sum(grad_pre, axis=0, keepdims=True)


def unconv_kernel(
    place, plan, pre, halo, grad_out, after_rows, grad_step, row_part, taps, grad_pre, grad_state, row_sums,
    grad_taps, extended, extended_grad,
):
    m = pl.program_id(0)
    rows = pre.shape[0]
    channels = grad_out.shape[1]
    taps_total = taps.shape[0]
    here = segment_of(column_position(rows, place), plan, place, m)
    behind, ahead = [], []
    for tap in range(taps_total):
        lag = taps_total - 1 - tap
        behind.append((segment_of(column_position(rows, place, -lag), plan, place, m) == here).astype(f32))
        ahead.append((segment_of(column_position(rows, place, lag), plan, place, m) == here).astype(f32))

    @pl.when(m == 0)
    def _():
        grad_taps[...] = jnp.zeros_like(grad_taps)

    total = jnp.zeros((rows, LANES), f32)
    for at in range(0, channels, LANES):
        tile = slice(at, at + LANES)
        rows_before, rows_after = extended.at[at // LANES % 2], extended_grad.at[at // LANES % 2]
        own, grad = pre[:, tile], grad_out[:, tile]
        rows_before[:HALO, :] = halo[0, :, tile]
        rows_before[HALO:, :] = own
        rows_after[:rows, :] = grad
        rows_after[rows:, :] = after_rows[0, :, tile]
        last = taps_total - 1
        result = taps[last:, tile] * grad
        grad_taps[last:, tile] += jnp.sum(grad * own, axis=0, keepdims=True)
        for tap in range(last):
            lag = last - tap
            result = result + taps[tap : tap + 1, tile] * rows_after[lag : lag + rows, :] * ahead[tap]
            begin = HALO - lag
            product = grad * rows_before[begin : begin + rows, :] * behind[tap]
            grad_taps[tap : tap + 1, tile] += jnp.sum(product, axis=0, keepdims=True)
        grad_pre[:, tile] = result.astype(bf16)
        total = total + result * own
    grad_pre[:, channels:] = grad_step[...].astype(bf16)
    grad_state[...] = grad_pre[:, channels - grad_state.shape[1] : channels]
    total = total + grad_step[...] * pre[:, channels : channels + LANES]
    row_sums[0] = row_part[0] + dot_nt(jnp.ones((HALO, LANES), f32), total, highest)


def rows_kernel(quarters, first, second, *refs):
    for weight, out in zip(refs[:quarters], refs[quarters:]):
        cut = weight.shape[1] - second.shape[1]
        result = dot_nt(first[...], weight[:, : first.shape[1]]) + dot_nt(second[...], weight[:, cut:])
        put_deal_rows(out.at[0], slice(None), result)


def rows_gradient(first, second, weight, senders, count, edges):
    total = first.shape[0]
    size = lax.axis_size("head")
    width = weight.shape[0] // size
    rows = total // count
    flops = total * (first.shape[1] + second.shape[1]) * width * size
    moved = weight.size + (first.size + second.size) * size
    block = (1, senders, 1, rows // senders, width)
    if edges:
        shape = (1, senders, count, rows // senders, width)
        return call(
            functools.partial(rows_kernel, 2), (count,), (),
            [per_row(first, rows), per_row(second, rows)]
            + [(weight, (width, weight.shape[1]), lambda m, at=at: (at, 0)) for at in (0, size - 1)],
            [(shape, bf16, block, lambda m: (0, 0, m, 0, 0))] * 2, flops=flops, bytes_accessed=moved,
        )
    row_block = lambda array: (array, (rows, array.shape[1]), lambda q, m: (m, 0))
    return call(
        functools.partial(rows_kernel, 1), (size - 2, count), (),
        [row_block(first), row_block(second), (weight, (width, weight.shape[1]), lambda q, m: (q + 1, 0))],
        [
            (
                (size - 2, senders, count, rows // senders, width), bf16, block,
                lambda q, m: (q, 0, m, 0, 0),
            )
        ],
        flops=flops, bytes_accessed=moved,
    )[0]


def output_kernel(inner_all, tokens, branch, sums, out):
    inv = lax.rsqrt(columns_of(sums[0])[:, :1] / inner_all + epsilon)
    every = slice(None)
    put_deal_rows(out, every, deal_rows(tokens, every) + deal_rows(branch, every) * inv)


def input_kernel(
    size, place, low, high, middle, up, down, tokens, cot, inverse, sums, gain, out, grad_gain
):
    every = slice(None)
    here = place[0]
    width = tokens.shape[3]
    own = jnp.where(
        here == 0,
        deal_rows(low.at[0], every),
        jnp.where(here == size - 1, deal_rows(high.at[0], every), deal_rows(middle.at[0], every)),
    )
    rows_own = own + deal_rows(up, every) + deal_rows(down, every)
    inv = deal_rows(inverse, every)
    unit = deal_rows(tokens, every) * inv
    own_gain = gain[:, pl.ds(pl.multiple_of(here * width, width), width)]
    total = columns_of(sums[0])[:, :1] / (width * size)
    put_deal_rows(out, every, inv * (rows_own * own_gain - unit * total) + deal_rows(cot, every))
    product = jnp.sum(rows_own * unit, axis=0, keepdims=True)

    @pl.when(pl.program_id(0) == 0)
    def _():
        grad_gain[...] = product

    @pl.when(pl.program_id(0) > 0)
    def _():
        grad_gain[...] += product


def out_kernel(left, right, out):
    out[...] = dot(left[...], right[...]).astype(bf16)


def sent_kernel(columns, count, left, *refs):
    rights, out = refs[:count], refs[count]
    for which, source, target, size in columns:
        out[:, target : target + size] = dot(left[...], rights[which][:, source : source + size]).astype(bf16)


def kept_kernel(columns, count, cut, left, *refs):
    rights, other, outs = refs[:count], refs[count], refs[count + 1 :]
    step = pl.program_id(0)
    high, odd = step >= pl.num_programs(0) // 2, lax.rem(step, 2) == 1
    for which, source, target, size in columns:
        result = dot(left[...], rights[which][:, source : source + size])
        result = (result + other[:, target : target + size].astype(f32)).astype(bf16)
        if target < cut:
            keep, send, sending, start = outs[0], outs[1], high, target
        else:
            keep, send, sending, start = outs[2], outs[3], odd, target - cut
        tile = slice(start, start + size)

        @pl.when(sending)
        def _():
            send[:, tile] = result

        @pl.when(jnp.logical_not(sending))
        def _():
            keep[:, tile] = result


def total_kernel(targets, *refs):
    ins, outs = refs[:2], refs[2:]
    for out, (which, source, target, size) in zip([outs[t[0]] for t in targets], [t[1] for t in targets]):
        tile = slice(source, source + size)
        out[:, target : target + size] = ins[which][:, tile].astype(f32)


def weight_gradient_sent(odd_t, rights, columns, depth):
    total = odd_t.shape[1]
    width = max(target + size for _, _, target, size in columns)
    (sent,) = call(
        functools.partial(sent_kernel, columns, len(rights)), (odd_t.shape[0] // depth,), (),
        [(odd_t, (depth, total), lambda l: (l, 0))] + [entire(right) for right in rights],
        [((odd_t.shape[0], width), bf16, (depth, width), lambda l: (l, 0))],
        flops=2 * odd_t.shape[0] * total * width,
        bytes_accessed=odd_t.shape[0] * (total + width) * 2 + sum(right.size for right in rights) * 2,
    )
    return sent


def weight_gradient_kept(even_t, got, rights, columns, cut, depth):
    blocks = even_t.shape[0] // depth
    total = even_t.shape[1]
    width = got.shape[1]
    top = blocks // 2
    rows = even_t.shape[0] // 2
    half = lambda size, index: ((rows, size), bf16, (depth, size), index)
    return call(
        functools.partial(kept_kernel, columns, len(rights), cut), (blocks,), (),
        [(even_t, (depth, total), lambda l: (l, 0))] + [entire(right) for right in rights]
        + [(got, (depth, width), lambda l: (l, 0))],
        [
            half(cut, lambda l: (jnp.minimum(l, top - 1), 0)),
            half(cut, lambda l: (jnp.maximum(l - top, 0), 0)),
            half(width - cut, lambda l: (l // 2, 0)),
            half(width - cut, lambda l: (l // 2, 0)),
        ],
        flops=2 * even_t.shape[0] * total * width,
        bytes_accessed=even_t.shape[0] * (total + width) * 2 + sum(right.size for right in rights) * 2,
    )


def weight_gradient_parts(mine):
    links = axis_bits("seq")[1:]
    labels = [bit << 1 for bit in range(2 ** len(links))]
    return [
        Scattered(mine[0], mine[1], [x for x in labels if not x & links[-1]], links[::-1]),
        Scattered(mine[2], mine[3], [x for x in labels if not x & links[0]], links),
    ]


def weight_gradient_total(parts, results, depth):
    ins = [array for part in parts for array in part.finish()]
    targets = [(at, column) for at, (_, columns) in enumerate(results) for column in columns]
    return call(
        functools.partial(total_kernel, targets), (1,), (), [entire(a) for a in ins],
        [((depth, size), f32, (depth, size), lambda *_: (0, 0)) for size, _ in results],
        bytes_accessed=sum(a.size for a in ins) * 6,
    )


def per_device(
    tokens,
    cotangent,
    lengths,
    deal_order,
    norm_gain,
    proj_gate,
    proj_inner,
    proj_state,
    proj_step,
    conv_inner,
    conv_inner_bias,
    conv_state,
    conv_state_bias,
    step_bias,
    decay_log,
    skip_gain,
    inner_gain,
    proj_out,
):
    batch_count = lengths.shape[0]
    rows_local, width_own = tokens.shape
    tok_dev = rows_local // batch_count
    seq_index = lax.axis_index("seq")
    head_index = lax.axis_index("head")
    seq_size = lax.axis_size("seq")
    head_size = lax.axis_size("head")
    heads_own = proj_step.shape[1]
    inner_own = proj_inner.shape[1]
    head_width = inner_own // heads_own
    states = proj_state.shape[1] // 2
    taps_total = conv_inner.shape[0]
    width_all = width_own * head_size
    inner_all = inner_own * head_size
    depth = width_all // seq_size
    channels = inner_own + 2 * states
    per = LANES // head_width
    rows = tok_dev
    grid = (batch_count,)

    place = jnp.stack(
        [head_index, seq_index, seq_index * tok_dev, jnp.int32(tok_dev * seq_size)]
    ).astype(jnp.int32)
    plan = (jnp.cumsum(lengths, axis=1) - lengths).astype(jnp.int32)
    scalars = (place, plan)

    piece = tok_dev // seq_size
    dealt_row = deal_order.reshape(batch_count, seq_size, piece) + (
        jnp.arange(batch_count, dtype=jnp.int32) * tok_dev
    )[:, None, None]
    picks = (
        jnp.transpose(dealt_row, (1, 0, 2)).reshape(rows_local, 1) == jnp.arange(rows_local)[None, :]
    ).astype(bf16)
    deal_shape = (seq_size, batch_count, piece, width_own)

    def dealt(values):
        values = dot(picks, values).astype(bf16).reshape(seq_size, batch_count * piece, width_own)
        values = lax.all_to_all(values, "seq", split_axis=0, concat_axis=0, tiled=True)
        return values.reshape(deal_shape)

    def sent_back(values):
        values = values.reshape(seq_size, -1, width_own)
        return lax.all_to_all(values, "seq", split_axis=0, concat_axis=0, tiled=True)

    def put_back(values):
        return dot_tn(picks, values.reshape(rows_local, width_own)).astype(bf16)

    deal_tokens = dealt(tokens)
    lines = LineGather(deal_tokens)
    lines.advance()
    deal_cot = dealt(cotangent)

    full_in = lax.all_gather(
        jnp.concatenate(
            [proj_inner, proj_state, proj_step, jnp.zeros((depth, 2 * LANES - heads_own), bf16), proj_gate],
            axis=1,
        ),
        "seq", axis=0, tiled=True,
    )
    full_out = lax.all_gather(after(proj_out, lines.up, lines.down), "seq", axis=1, tiled=True)

    lines = lines.finish()
    normed, even_t, odd_t, own_t, inv_rms = all_features(deal_tokens, lines, place, norm_gain[None, :], depth)
    cot_lines = LineGather(after(deal_cot, lines[0][-1], lines[1][-1]))

    taps = jnp.concatenate([conv_inner, conv_state], axis=1)
    bias = jnp.concatenate([conv_inner_bias, conv_state_bias])[None, :]
    pad = LANES - heads_own
    step_bias_row = jnp.pad(step_bias, (0, pad))[None, :]
    scale = jnp.pad(-jnp.exp(decay_log), (0, pad))[None, :]
    spread = (
        jnp.arange(2 * LANES)[:, None] % LANES == jnp.arange(inner_own)[None, :] // head_width
    ).astype(bf16)
    skip = jnp.repeat(skip_gain, head_width)[None, :]
    gain = inner_gain[None, :]

    pre_width = channels + 2 * LANES
    (pre,) = cot_lines.advance(dot(normed, full_in[:, :pre_width]))
    halo = passed_along(pre.reshape(batch_count, tok_dev, -1)[:, tok_dev - HALO :], "seq", 1)
    gate = dot(normed, full_in[:, pre_width:]).astype(bf16)
    halo, gate = lax.optimization_barrier((halo, gate))
    conv_out, small, inputs, maps, fresh = call(
        functools.partial(conv_kernel, inner_own), grid, scalars,
        [per_row(pre, rows), per_step(halo)]
        + [entire(a) for a in (taps, bias, step_bias_row, scale, spread)],
        [
            row_out(rows_local, rows, channels, f32),
            row_out(rows_local, rows, 3 * LANES, f32),
            row_out(rows_local, rows, inner_own, bf16),
            row_out(rows_local, rows, 2 * states, f32),
            step_out(batch_count, (states + STATE_PAD, inner_own), bf16),
        ],
        scratch=[pltpu.VMEM((2, rows + HALO, LANES), f32)],
        flops=rows_local * inner_own * 2000, bytes_accessed=rows_local * inner_own * 20,
    )
    conv_out, small, inputs, maps, fresh = cot_lines.advance(conv_out, small, inputs, maps, fresh)
    scan_ins = [per_row(small, rows), per_row(maps, rows)]
    (mixed,) = call(
        functools.partial(mix_kernel, per), grid, scalars, scan_ins + [per_row(inputs, rows)],
        [row_out(rows_local, rows, inner_own, f32)],
        flops=rows_local * inner_own * 2500, bytes_accessed=rows_local * inner_own * 6,
    )
    cot_lines.advance()

    entering, mixed, (flat_cot, grad_y) = scan_before(
        fresh, states, False,
        [lambda: mixed, lambda _: cotangent_products(deal_cot, cot_lines.finish(), place, full_out)],
    )
    vectors = [entire(gain), entire(skip), entire(spread)]
    scanned, scaled_y, sums = call(
        gated_kernel, grid, scalars + entering[:1],
        scan_ins
        + [per_row(mixed, rows)] + [per_step(a) for a in entering[1:]]
        + [per_row(conv_out, rows), per_row(gate, rows)]
        + [per_row(grad_y, rows)] + vectors,
        [
            row_out(rows_local, rows, inner_own, f32),
            deal_out(seq_size, batch_count, piece, inner_own, bf16),
            step_out(batch_count, (HALO, rows), f32),
        ],
        flops=rows_local * inner_own * 1500, bytes_accessed=rows_local * inner_own * 8,
    )
    out_rows = dot(scaled_y.reshape(rows_local, inner_own), full_out).astype(bf16)
    sums = sums + swapped(sums, "head", 1)
    for bit in axis_bits("head")[1:]:
        other, out_rows = lax.optimization_barrier((swapped(sums, "head", bit), out_rows))
        sums = sums + other
    branch = lax.psum_scatter(
        out_rows.reshape(deal_shape[:3] + (width_all,)), "head", scatter_dimension=3, tiled=True
    )

    normed_y_t, grads, grad_gate, local, row_part, grad_gain, grad_skip = call(
        functools.partial(ungated_kernel, inner_all), grid, scalars,
        scan_ins
        + [per_row(array, rows) for array in (scanned, conv_out, gate, grad_y)]
        + [per_step(sums)] + vectors,
        [((inner_own, rows_local), bf16, (inner_own, rows), lambda m, *_: (0, m))]
        + [row_out(rows_local, rows, inner_own, bf16)] * 2
        + [step_out(batch_count, (states + STATE_PAD, inner_own), bf16)]
        + [step_out(batch_count, (HALO, rows), f32)]
        + [sum_out((1, inner_own))] * 2,
        flops=rows_local * inner_own * 2000, bytes_accessed=rows_local * inner_own * 24,
    )
    grad_inputs, grad_maps = call(
        functools.partial(unmix_kernel, per), grid, scalars,
        scan_ins + [per_row(inputs, rows), per_row(grads, rows)],
        [row_out(rows_local, rows, inner_own, f32), row_out(rows_local, rows, 2 * states, f32)],
        scratch=[pltpu.VMEM((rows, rows), f32)],
        flops=rows_local * inner_own * 4000, bytes_accessed=rows_local * inner_own * 8,
    )
    (grad_out,) = call(
        out_kernel, (head_size,), (),
        [entire(normed_y_t), (flat_cot, (rows_local, width_own), lambda q: (0, q))],
        [((inner_own, width_all), bf16, (inner_own, width_own), lambda q: (0, q))],
        flops=2 * rows_local * inner_own * width_all, bytes_accessed=rows_local * width_all * 6,
    )
    leaving, grad_inputs, grad_out = scan_before(
        local, states, True, [lambda: grad_inputs, lambda _: grad_out]
    )

    grad_out = lax.psum_scatter(grad_out, "seq", scatter_dimension=1, tiled=True)
    grad_conv_out, grad_step, grad_bias, grad_heads = call(
        unscan_kernel, grid, scalars + entering[:1] + leaving[:1],
        scan_ins
        + [per_row(a, rows) for a in (scanned, conv_out, inputs, grads)]
        + [per_row(grad_inputs, rows), per_row(grad_maps, rows)]
        + [per_step(a) for a in entering[1:] + leaving[1:]] + [entire(skip), entire(scale), entire(spread)],
        [
            row_out(rows_local, rows, channels, f32),
            row_out(rows_local, rows, LANES, f32),
            sum_out((1, channels)),
            sum_out((HALO, LANES)),
        ],
        flops=rows_local * inner_own * 4000, bytes_accessed=rows_local * inner_own * 28,
    )
    after_rows = passed_along(grad_conv_out.reshape(batch_count, tok_dev, channels)[:, :HALO], "seq", -1)
    after_rows, branch = lax.optimization_barrier((after_rows, branch))
    grad_pre, grad_state, row_dots, grad_taps = call(
        unconv_kernel, grid, scalars,
        [per_row(pre, rows), per_step(halo), per_row(grad_conv_out, rows), per_step(after_rows)]
        + [per_row(grad_step, rows), per_step(row_part), entire(taps)],
        [
            row_out(rows_local, rows, channels + LANES, bf16),
            row_out(rows_local, rows, 2 * states, bf16),
            step_out(batch_count, (HALO, rows), f32),
            sum_out((taps_total, channels)),
        ],
        scratch=[pltpu.VMEM((2, rows + HALO, LANES), f32)] * 2,
        flops=rows_local * inner_own * 100, bytes_accessed=rows_local * inner_own * 14,
    )
    columns = [
        (0, 0, 0, inner_own), (1, 0, inner_own, inner_own), (0, channels, 2 * inner_own, LANES)
    ]
    fill = lambda row: jnp.pad(row, ((0, 0), (0, channels - row.shape[1])))
    state_small = jnp.concatenate([grad_taps[:, inner_own:], grad_bias[:, inner_own:]])
    row_dots = jnp.concatenate([row_dots[:, 0, :], state_small.reshape(-1, rows)])
    packed = jnp.concatenate(
        [grad_taps, grad_bias, fill(grad_gain), fill(grad_skip), fill(grad_heads[:2].reshape(1, 2 * LANES))]
    )
    packed = packed + swapped(packed, "seq", 1)
    seq_bits, head_bits = axis_bits("seq"), axis_bits("head")
    sent = weight_gradient_sent(odd_t, [grad_pre, grad_gate], columns, depth)
    others = [
        swapped(row_dots, "head", head_bits[0]), swapped(packed, "seq", seq_bits[1]),
        swapped(grad_state, "head", head_bits[0]),
    ]
    others, sent = lax.optimization_barrier((others, sent))
    row_dots, packed, grad_state = row_dots + others[0], packed + others[1], added(grad_state, others[2])
    got = swapped(sent, "seq", 1)
    grad_rows = lambda first, edges: rows_gradient(
        first, grad_gate, full_in, seq_size, batch_count, edges
    )
    low, high = grad_rows(after(grad_pre, sent), True)
    other, low, high = lax.optimization_barrier((swapped(packed, "seq", seq_bits[2]), low, high))
    packed = packed + other
    for bit in seq_bits[3:]:
        packed = packed + swapped(packed, "seq", bit)
    rows_line = LineScatter([low[0], high[0]])
    mine = weight_gradient_kept(even_t, after(got, low), [grad_pre, grad_gate], columns, inner_own, depth)
    rows_line.middle = grad_rows(after(grad_pre, mine[0]), False)
    others = [swapped(row_dots, "head", head_bits[1]), swapped(grad_state, "head", head_bits[1])]
    *mine, rows_line.middle, branch, grad_out, others = rows_line.advance(
        *mine, rows_line.middle, branch, grad_out, others
    )
    row_dots, grad_state = row_dots + others[0], added(grad_state, others[1])
    for bit in head_bits[2:]:
        row_dots = row_dots + swapped(row_dots, "head", bit)
        grad_state = added(grad_state, swapped(grad_state, "head", bit))
    (grad_w_state,) = call(
        out_kernel, (1,), (), [entire(own_t), entire(grad_state)], [sum_out((width_own, 2 * states), bf16)],
        flops=2 * rows_local * width_own * 2 * states, bytes_accessed=rows_local * (width_own + 2 * states) * 2,
    )
    state_small = row_dots[batch_count:].reshape(-1, 2 * states).astype(bf16)
    row_dots = row_dots[:batch_count, None, :]
    pad_rows = -state_small.shape[0] % 16
    grad_w_state = jnp.concatenate([grad_w_state, jnp.pad(state_small, ((0, pad_rows), (0, 0)))])
    grad_w_state = added(grad_w_state, swapped(grad_w_state, "seq", 1))
    parts = weight_gradient_parts(mine)
    for part in parts:
        part.send()
    (grad_w_state,) = rows_line.advance(grad_w_state)
    other = swapped(grad_w_state, "seq", seq_bits[1])
    (out_rows,) = call(
        functools.partial(output_kernel, inner_all), grid, (),
        [per_deal(deal_tokens), per_deal(branch), per_step(sums)],
        [deal_out(seq_size, batch_count, piece, width_own, bf16)],
        bytes_accessed=rows_local * width_own * 6,
    )
    out_rows = sent_back(out_rows)
    for part in parts:
        part.receive()
    pairs = rows_line.advance(*[part.pair for part in parts], other, out_rows)
    other, out_rows = pairs[-2:]
    grad_w_state = added(grad_w_state, other)
    other = swapped(grad_w_state, "seq", seq_bits[2])
    for part, pair in zip(parts, pairs):
        part.pair = pair
        part.send()
    grad_out = grad_out.astype(f32)
    up, down = rows_line.finish()
    middle = rows_line.middle
    grad_rows_in, grad_norm_gain = call(
        functools.partial(input_kernel, head_size), grid, (place,),
        [per_deal_of(low), per_deal_of(high)]
        + [
            (
                middle, (1, seq_size, 1, piece, width_own),
                lambda m, place: (jnp.clip(place[0] - 1, 0, head_size - 3), 0, m, 0, 0),
            )
        ]
        + [per_deal(a) for a in (up, down, deal_tokens, deal_cot, inv_rms)]
        + [per_step(row_dots), entire(norm_gain[None, :])],
        [deal_out(seq_size, batch_count, piece, width_own, bf16), sum_out((1, width_own))],
        bytes_accessed=rows_local * width_own * 16,
    )
    parts[0].got, parts[1].got, other = after_all((parts[0].got, parts[1].got, other), (grad_rows_in,))
    grad_w_state = added(grad_w_state, other)
    for part in parts:
        part.receive()
        while part.left:
            part.send()
            part.receive()
    grad_inner, grad_w_gate, grad_w_step = weight_gradient_total(
        parts,
        [
            (inner_own, [(0, 0, 0, inner_own)]),
            (inner_own, [(1, 0, 0, inner_own)]),
            (LANES, [(1, inner_own, 0, LANES)]),
        ],
        depth,
    )
    for bit in seq_bits[3:]:
        grad_w_state = added(grad_w_state, swapped(grad_w_state, "seq", bit))
    out_back = put_back(out_rows)
    grad_w_state = grad_w_state.astype(f32)
    state_sums = grad_w_state[width_own : width_own + taps_total + 1]
    gain_high = grad_norm_gain.astype(bf16)
    gain_low = (grad_norm_gain - gain_high.astype(f32)).astype(bf16)
    gain_rows = jnp.pad(jnp.concatenate([gain_high, gain_low]), ((0, HALO - 2), (0, 0)))
    own_rows = batch_count * piece
    grad_back = sent_back(
        jnp.concatenate(
            [
                grad_rows_in.reshape(seq_size, own_rows, width_own),
                jnp.broadcast_to(gain_rows, (seq_size, HALO, width_own)),
            ],
            axis=1,
        )
    )
    grad_norm_gain = jnp.sum(grad_back[:, own_rows : own_rows + 2].astype(f32), axis=(0, 1))
    grad_back = put_back(grad_back[:, :own_rows])
    state_own = 2 * states // head_size
    state_sums = lax.dynamic_slice_in_dim(state_sums, head_index * state_own, state_own, 1)
    return (
        out_back,
        grad_back,
        grad_norm_gain,
        grad_w_gate,
        grad_inner,
        grad_w_state[:width_own],
        grad_w_step[:, :heads_own],
        packed[:taps_total, :inner_own],
        packed[taps_total, :inner_own],
        state_sums[:taps_total],
        state_sums[taps_total],
        packed[taps_total + 3, LANES : LANES + heads_own],
        packed[taps_total + 3, :heads_own],
        jnp.sum(packed[taps_total + 2, :inner_own].reshape(heads_own, head_width), axis=1),
        packed[taps_total + 1, :inner_own],
        grad_out,
    )


def solution(mesh):
    return jax.shard_map(
        per_device,
        mesh=mesh,
        in_specs=(
            P("seq", "head"),
            P("seq", "head"),
            P(),
            P("seq"),
            P(),
            P("seq", "head"),
            P("seq", "head"),
            P("seq", None),
            P("seq", "head"),
            P(None, "head"),
            P("head"),
            P(),
            P(),
            P("head"),
            P("head"),
            P("head"),
            P("head"),
            P("head", "seq"),
        ),
        out_specs=(
            P("seq", "head"),
            P("seq", "head"),
            P("head"),
            P("seq", "head"),
            P("seq", "head"),
            P("head", None),
            P("seq", "head"),
            P(None, "head"),
            P("head"),
            P(None, "head"),
            P("head"),
            P("head"),
            P("head"),
            P("head"),
            P("head"),
            P("head", "seq"),
        ),
        check_vma=False,
    )
```

```python
import functools
import math
import jax
import jax.numpy as jnp
from jax import lax
from jax.experimental import pallas as pl
from jax.experimental.pallas import tpu as pltpu
from jax.sharding import PartitionSpec as P

epsilon = 1e-05
highest = lax.Precision.HIGHEST
f32 = jnp.float32
bf16 = jnp.bfloat16
LANES = 128
HALO = 8
STATE_PAD = 16
HBM_BYTES = 700000
VMEM_SPARE = 10 * 1024 * 1024


def swapped(value, axis, bit):
    return lax.ppermute(value, axis, [(i, i ^ bit) for i in range(lax.axis_size(axis))])


def axis_bits(axis):
    count = lax.axis_size(axis)
    return [1 << k for k in range(count.bit_length() - 1)]


def added(left, right):
    return (left.astype(f32) + right.astype(f32)).astype(left.dtype)


def after(value, *others):
    return lax.optimization_barrier((value, *others))[0]


def after_all(values, others):
    return lax.optimization_barrier((tuple(values), tuple(others)))[0]


class Scattered:
    def __init__(self, keep, send, labels, order):
        rows = keep.shape[0] // len(labels)
        self.pair = (keep.reshape(len(labels), rows, -1), send.reshape(len(labels), rows, -1))
        self.labels, self.left = labels, list(order)

    def send(self):
        self.got = swapped(self.pair[1], "seq", self.left.pop(0))

    def receive(self):
        total = added(self.pair[0], self.got)
        if not self.left:
            self.pair = (total,)
            return
        following, labels = self.left[0], self.labels
        keep_at = [at for at, label in enumerate(labels) if not label & following]
        send_at = [labels.index(labels[at] ^ following) for at in keep_at]
        kept = jnp.concatenate([total[at : at + 1] for at in keep_at])
        sent = jnp.concatenate([total[at : at + 1] for at in send_at])
        self.pair = (kept, sent)
        self.labels = [labels[at] for at in keep_at]

    def finish(self):
        return [self.pair[0][0]]


class LineGather:
    def __init__(self, own):
        self.size = lax.axis_size("head")
        self.up = self.down = own
        self.ups, self.downs = [], []

    def advance(self, *beside):
        step = len(self.ups) + 1
        if step < self.size:
            up = lax.ppermute(self.up, "head", [(i, i + 1) for i in range(step - 1, self.size - 1)])
            down = lax.ppermute(self.down, "head", [(i, i - 1) for i in range(1, self.size - step + 1)])
            if beside:
                (up, down), beside = lax.optimization_barrier(((up, down), beside))
            self.up, self.down = up, down
            self.ups.append(up)
            self.downs.append(down)
        return beside

    def finish(self):
        while len(self.ups) + 1 < self.size:
            self.advance()
        return self.ups, self.downs


class LineScatter:
    def __init__(self, edges, middle=None):
        self.size, self.here = lax.axis_size("head"), lax.axis_index("head")
        self.edges, self.middle = edges, middle
        self.up = self.down = None
        self.step = 0

    def block_of(self, at):
        last = self.size - 1
        inner = lax.dynamic_index_in_dim(self.middle, jnp.clip(at - 1, 0, last - 2), 0, keepdims=False)
        return jnp.where(at <= 0, self.edges[0], jnp.where(at >= last, self.edges[1], inner))

    def advance(self, *beside):
        self.step += 1
        step, size, here = self.step, self.size, self.here
        if step < size:
            if step == 1:
                up, down = self.edges[1], self.edges[0]
            else:
                up = added(self.block_of(here + size - step), self.up)
                down = added(self.block_of(here - size + step), self.down)
            up = lax.ppermute(up, "head", [(i, i + 1) for i in range(step)])
            down = lax.ppermute(down, "head", [(i, i - 1) for i in range(size - step, size)])
            if beside:
                (up, down), beside = lax.optimization_barrier(((up, down), beside))
            self.up, self.down = up, down
        return beside

    def finish(self):
        while self.step + 1 < self.size:
            self.advance()
        return self.up, self.down


def axis_sum(value, axis):
    for bit in axis_bits(axis):
        value = value + swapped(value, axis, bit)
    return value


def passed_along(value, axis, steps):
    count = lax.axis_size(axis)
    initial, last = (max(0, -steps), min(count, count - steps))
    return lax.ppermute(value, axis, [(source, source + steps) for source in range(initial, last)])


def dot(left, right, precision=None):
    return jnp.dot(left, right, preferred_element_type=f32, precision=precision)


def dot_nt(left, right, precision=None):
    return lax.dot_general(
        left, right, (((1,), (1,)), ((), ())), preferred_element_type=f32, precision=precision
    )


def dot_tn(left, right, precision=None):
    return lax.dot_general(
        left, right, (((0,), (0,)), ((), ())), preferred_element_type=f32, precision=precision
    )


def both_parts(values):
    high = values.astype(bf16)
    return jnp.concatenate([high, (values - high.astype(f32)).astype(bf16)], axis=1)


def three_parts(values):
    high = values.astype(bf16)
    rest = values - high.astype(f32)
    middle = rest.astype(bf16)
    return high, middle, (rest - middle.astype(f32)).astype(bf16)


def dot_mask(mask, values):
    return sum(dot(mask, part) for part in three_parts(values))


def silu_slope(values):
    logistic = jax.nn.sigmoid(values)
    return logistic * (1.0 + values * (1.0 - logistic))


def big(shape, dtype):
    return math.prod(shape) * jnp.dtype(dtype).itemsize > HBM_BYTES


def tiled_bytes(shape, dtype):
    *lead, rows, lanes = shape
    size = -(-rows // 8) * 8 * -(-lanes // LANES) * LANES * jnp.dtype(dtype).itemsize
    for count in lead:
        size *= count
    return size


def call(kernel, grid, scalars, ins, outs, scratch=(), flops=0, bytes_accessed=0):
    ins = [(streamed(a) if big(a.shape, a.dtype) else a, block, index) for a, block, index in ins]
    held = [block == array.shape for array, block, _ in ins]
    need = sum(
        (1 if whole else 2) * tiled_bytes(block, array.dtype) for (array, block, _), whole in zip(ins, held)
    )
    need += sum(2 * tiled_bytes(block, dtype) for _, dtype, block, _ in outs)
    need += sum(tiled_bytes(item.shape, item.dtype) for item in scratch)
    return pl.pallas_call(
        kernel,
        grid_spec=pltpu.PrefetchScalarGridSpec(
            num_scalar_prefetch=len(scalars),
            grid=grid,
            in_specs=[
                pl.BlockSpec(block, index, pipeline_mode=pl.Buffered(1) if whole else None)
                for (_, block, index), whole in zip(ins, held)
            ],
            out_specs=[pl.BlockSpec(block, index) for _, _, block, index in outs],
            scratch_shapes=list(scratch),
        ),
        out_shape=[
            (pltpu.HBM if big(shape, dtype) else jax.ShapeDtypeStruct)(shape, dtype) for shape, dtype, _, _ in outs
        ],
        compiler_params=pltpu.CompilerParams(vmem_limit_bytes=need + VMEM_SPARE),
        cost_estimate=pl.CostEstimate(
            flops=int(flops), bytes_accessed=int(bytes_accessed), transcendentals=0
        ),
    )(*scalars, *[array for array, _, _ in ins])


def streamed(array):
    return pltpu.with_memory_space_constraint(array, pltpu.HBM)


def per_row(array, rows):
    return (array, (rows,) + array.shape[1:], lambda m, *_: (m,) + (0,) * (array.ndim - 1))


def per_deal(array):
    return (array, (array.shape[0], 1) + array.shape[2:], lambda m, *_: (0, m, 0, 0))


def per_deal_of(array):
    return (array, (1, array.shape[1], 1) + array.shape[3:], lambda m, *_: (0, 0, m, 0, 0))


def deal_out(senders, count, rows, width, dtype):
    return ((senders, count, rows, width), dtype, (senders, 1, rows, width), lambda m, *_: (0, m, 0, 0))


def deal_rows(ref, tile):
    values = ref[:, 0, :, tile].astype(f32)
    return values.reshape(values.shape[0] * values.shape[1], values.shape[2])


def put_deal_rows(ref, tile, values):
    shape = (ref.shape[0], ref.shape[2], values.shape[1])
    ref[:, 0, :, tile] = values.reshape(shape).astype(ref.dtype)


def per_step(array):
    return (array, (1,) + array.shape[1:], lambda m, *_: (m,) + (0,) * (array.ndim - 1))


def entire(array):
    return (array, array.shape, lambda *_: (0,) * array.ndim)


def row_out(total, rows, width, dtype):
    return ((total, width), dtype, (rows, width), lambda m, *_: (m, 0))


def step_out(count, shape, dtype):
    return ((count,) + shape, dtype, (1,) + shape, lambda m, *_: (m,) + (0,) * len(shape))


def sum_out(shape, dtype=f32):
    return (shape, dtype, shape, lambda *_: (0,) * len(shape))


def joined(earlier, following, states):
    row = lax.broadcasted_iota(jnp.int32, earlier.shape, 0)
    return following[states : states + 1] * earlier + jnp.where(row < states, following, 0.0)


def chip_kernel(states, flags, own, other, total):
    for at in range(own.shape[0]):
        mine, theirs = own[at].astype(f32), other[at].astype(f32)
        later = flags[0] != 0
        first, second = jnp.where(later, theirs, mine), jnp.where(later, mine, theirs)
        total[at] = joined(first, second, states).astype(bf16)


def link_kernel(states, step, last, flags, *refs):
    total, other, refs = refs[0], refs[1], refs[2:]
    later = flags[step] != 0
    if step > 1:
        before, refs = refs[0], refs[1:]
    for at in range(total.shape[0]):
        mine, theirs = total[at].astype(f32), other[at].astype(f32)
        if step == 1:
            row = lax.broadcasted_iota(jnp.int32, mine.shape, 0)
            ahead = jnp.where(row < states, 0.0, 1.0)
            refs[0][at] = jnp.where(later, theirs, ahead).astype(bf16)
        else:
            ahead = before[at].astype(f32)
            refs[0][at] = jnp.where(later, joined(theirs, ahead, states), ahead).astype(bf16)
        if not last:
            first, second = jnp.where(later, theirs, mine), jnp.where(later, mine, theirs)
            refs[1][at] = joined(first, second, states).astype(bf16)


def state_tile(states, flags, ahead, ahead_other, sibling, at):
    odd = flags[flags.shape[0] - 1] != 0
    half = ahead.shape[2]
    tile = slice(at % half, at % half + LANES)
    mine, theirs = ahead[0, :, tile], ahead_other[0, :, tile]
    values = (jnp.where(odd, theirs, mine) if at < half else jnp.where(odd, mine, theirs)).astype(f32)
    near = sibling[0, :, at : at + LANES].astype(f32)
    return jnp.where(flags[0] != 0, joined(values, near, states), values)[:states].astype(bf16)


def scan_before(local, states, reverse, fillers):
    here = lax.axis_index("seq")
    bits = axis_bits("seq")
    count, height, width = local.shape
    passed = [((here & bit) == 0) if reverse else ((here & bit) != 0) for bit in bits]
    flags = jnp.stack(passed + [(here & 1) != 0]).astype(jnp.int32)
    whole = local.shape
    piece = (count, height, width // 2)
    at_step = lambda *_: (0, 0, 0)
    at_core = lambda _, flags: (0, 0, flags[len(bits)])
    half_out = (piece, bf16, piece, at_step)
    moved = local.size * 4
    sibling = swapped(local, "seq", 1)
    (total,) = call(
        functools.partial(chip_kernel, states), (1,), (flags,),
        [(local, piece, at_core), (sibling, piece, at_core)], [half_out], bytes_accessed=moved,
    )
    ahead, filled, beside = None, [], ()
    for step, bit in enumerate(bits[1:], 1):
        other = swapped(total, "seq", bit)
        if step <= len(fillers):
            other, value = lax.optimization_barrier((other, fillers[step - 1](*beside)))
            beside = (value,)
            filled.append(value)
        last = step == len(bits) - 1
        ins = [total, other] + ([] if ahead is None else [ahead])
        results = call(
            functools.partial(link_kernel, states, step, last), (1,), (flags,),
            [(array, piece, at_step) for array in ins], [half_out] * (1 if last else 2),
            bytes_accessed=moved,
        )
        ahead = results[0]
        total = None if last else results[1]
    ahead_other = swapped(ahead, "seq", 1)
    return [(flags, ahead, ahead_other, sibling)] + filled


def columns_of(rows_form):
    rows = rows_form.shape[1]
    row = lax.broadcasted_iota(jnp.int32, (rows, rows), 0)
    col = lax.broadcasted_iota(jnp.int32, (rows, rows), 1)
    same = jnp.where(row == col, 1.0, 0.0).astype(bf16)
    return dot_nt(same.astype(f32), rows_form, highest)


def segment_of(position, plan, place, m):
    found = jnp.full(jnp.shape(position), -1, jnp.int32)
    for k in range(plan.shape[1]):
        found = found + (position >= plan[m, k]).astype(jnp.int32)
    return jnp.where(position >= place[3], -2, found)


def column_position(rows, place, shift=0):
    return place[2] + shift + lax.broadcasted_iota(jnp.int32, (rows, 1), 0)


def row_position(rows, place):
    return place[2] + lax.broadcasted_iota(jnp.int32, (1, rows), 1)


def by_core(values, me, depth):
    count = values.shape[1] // depth
    blocks = [values[:, k * depth : (k + 1) * depth] for k in range(count)]
    odd = (me & 1) != 0
    halves = []
    for at in (0, 1):
        straight, turned = blocks[at::2], blocks[1 - at :: 2]
        half = [jnp.where(odd, b, a) for a, b in zip(straight, turned)]
        bit = 1
        while bit < count // 2:
            flip = ((me >> 1) & bit) != 0
            half = [jnp.where(flip, half[k ^ bit], half[k]) for k in range(len(half))]
            bit *= 2
        halves.append(half[0] if len(half) == 1 else jnp.concatenate(half, axis=1))
    return halves


def half_start(quarter, me, width, depth):
    count = width // depth // 2
    return pl.multiple_of(((quarter * count) ^ ((me >> 1) & ~(count - 1))) * depth, width // 2)


def line_slot(own, ups, downs, z, step):
    if step == 0:
        return deal_rows(own, slice(None))
    up, down = ups[step - 1], downs[len(downs) - step]
    return jnp.where(z >= step, deal_rows(up, slice(None)), deal_rows(down, slice(None)))


def features_kernel(size, depth, place, *refs):
    own, ups, downs = refs[0], refs[1:size], refs[size : 2 * size - 1]
    gain, normed, even_t, odd_t, own_t, inverse = refs[2 * size - 1 :]
    z, me = place[0], place[1]
    width = own.shape[3]
    slots = [line_slot(own, ups, downs, z, step) for step in range(size)]
    square = sum(jnp.sum(slot * slot, axis=1, keepdims=True) for slot in slots)
    inv = lax.rsqrt(square / (width * size) + epsilon)
    put_deal_rows(inverse, slice(None), inv)
    for step, slot in enumerate(slots):
        quarter = lax.rem(z - step + size, size)
        place_at = pl.ds(pl.multiple_of(quarter * width, width), width)
        slot = slot * inv * gain[:, place_at]
        normed[:, place_at] = slot.astype(bf16)
        if step == 0:
            own_t[...] = slot.astype(bf16).T
        first, second = by_core(slot, me, depth)
        at = pl.ds(half_start(quarter, me, width, depth), width // 2)
        even_t[at, :] = first.astype(bf16).T
        odd_t[at, :] = second.astype(bf16).T


def all_features(own, lines, place, gain, depth):
    senders, count, piece, width = own.shape
    rows = senders * piece
    total = rows * count
    size = lax.axis_size("head")
    ups, downs = lines
    half = width * size // 2
    outs = [row_out(total, rows, 2 * half, bf16)]
    outs += [((half, total), bf16, (half, rows), lambda m, *_: (0, m))] * 2
    outs.append(((width, total), bf16, (width, rows), lambda m, *_: (0, m)))
    outs.append(deal_out(senders, count, piece, 1, f32))
    return call(
        functools.partial(features_kernel, size, depth), (count,), (place,),
        [per_deal(array) for array in [own] + ups + downs] + [entire(gain)], outs,
        bytes_accessed=total * width * 2 * 15,
    )


def cotangent_kernel(size, place, *refs):
    own, ups, downs = refs[0], refs[1:size], refs[size : 2 * size - 1]
    weight, every, grad_y = refs[2 * size - 1 :]
    z = place[0]
    width = own.shape[3]
    total = None
    for step in range(size):
        slot = line_slot(own, ups, downs, z, step)
        quarter = lax.rem(z - step + size, size)
        place_at = pl.ds(pl.multiple_of(quarter * width, width), width)
        every[:, place_at] = slot.astype(bf16)
        part = dot_nt(slot.astype(bf16), weight[:, place_at])
        total = part if total is None else total + part
    grad_y[...] = total.astype(bf16)


def cotangent_products(own, lines, place, weight):
    senders, count, piece, width = own.shape
    rows = senders * piece
    total = rows * count
    size = lax.axis_size("head")
    ups, downs = lines
    return call(
        functools.partial(cotangent_kernel, size), (count,), (place,),
        [per_deal(array) for array in [own] + ups + downs] + [entire(weight)],
        [
            row_out(total, rows, width * size, bf16),
            row_out(total, rows, weight.shape[0], bf16),
        ],
        flops=2 * total * width * size * weight.shape[0],
        bytes_accessed=total * width * 2 * 11 + weight.size * 2 + total * weight.shape[0] * 4,
    )


def conv_kernel(
    width, place, plan, pre, halo, taps, bias, step_bias, scale, spread, conv_out, small, inputs, maps, fresh,
    extended,
):
    m = pl.program_id(0)
    rows = pre.shape[0]
    states = maps.shape[1] // 2
    taps_total = taps.shape[0]
    here = segment_of(column_position(rows, place), plan, place, m)
    same = [
        (segment_of(column_position(rows, place, tap + 1 - taps_total), plan, place, m) == here).astype(f32)
        for tap in range(taps_total)
    ]
    before = segment_of(place[2] - 1, plan, place, m)
    last = segment_of(place[2] + rows - 1, plan, place, m)

    step_pre = pre[:, width + 2 * states : width + 2 * states + LANES] + step_bias[...]
    rest = jnp.exp(-jnp.abs(step_pre))
    series = rest * (
        1.0 - rest * (1 / 2 - rest * (1 / 3 - rest * (1 / 4 - rest * (1 / 5 - rest * (1 / 6)))))
    )
    step = jnp.maximum(step_pre, 0.0) + jnp.where(rest < 0.03, series, jnp.log(1.0 + rest))
    row = lax.broadcasted_iota(jnp.int32, (rows, rows), 0)
    col = lax.broadcasted_iota(jnp.int32, (rows, rows), 1)
    lower = jnp.where(row >= col, 1.0, 0.0).astype(bf16)
    cumulative = dot_mask(lower, step * scale[...])
    small[:, :LANES] = cumulative
    small[:, LANES : 2 * LANES] = step
    small[:, 2 * LANES :] = step_pre
    ending = cumulative[rows - 1 :, :]
    fading = (here == last).astype(f32) * jnp.exp(ending - cumulative)
    through = (last == before).astype(f32) * jnp.exp(ending)
    step_parts, fading_parts = both_parts(step), both_parts(fading)
    through_parts = both_parts(jnp.broadcast_to(through, (STATE_PAD, LANES)))

    def conv(at):
        tile = slice(at, at + LANES)
        rows_before = extended.at[at // LANES % 2]
        own = pre[:, tile]
        rows_before[:HALO, :] = halo[0, :, tile]
        rows_before[HALO:, :] = own
        result = bias[:, tile] + taps[taps_total - 1 :, tile] * own
        for tap in range(taps_total - 1):
            start = HALO + tap + 1 - taps_total
            result = result + taps[tap : tap + 1, tile] * rows_before[start : start + rows, :] * same[tap]
        conv_out[:, tile] = result
        return result * jax.nn.sigmoid(result)

    for at in range(0, 2 * states, LANES):
        maps[:, at : at + LANES] = conv(width + at)
    input_map_t = maps[:, :states].T.astype(bf16)
    for at in range(0, width, LANES):
        tile = slice(at, at + LANES)
        values = conv(at) * dot(step_parts, spread[:, tile])
        inputs[:, tile] = values.astype(bf16)
        faded = (values * dot(fading_parts, spread[:, tile])).astype(bf16)
        fresh[0, :states, tile] = dot(input_map_t, faded).astype(bf16)
        fresh[0, states:, tile] = dot(through_parts, spread[:, tile]).astype(bf16)


def allowed_mask(rows, place, plan, m, transposed):
    column = segment_of(column_position(rows, place), plan, place, m)
    across = segment_of(row_position(rows, place), plan, place, m)
    row = lax.broadcasted_iota(jnp.int32, (rows, rows), 0)
    col = lax.broadcasted_iota(jnp.int32, (rows, rows), 1)
    order = (row <= col) if transposed else (row >= col)
    return jnp.where(order & (column == across), 0.0, -1e30)


def lane_select(parts, per):
    lane = lax.broadcasted_iota(jnp.int32, parts[0].shape, 1)
    result = parts[0]
    for at in range(1, per):
        result = jnp.where(lane >= at * (LANES // per), parts[at], result)
    return result


def mix_kernel(per, place, plan, small, maps, inputs, out):
    m = pl.program_id(0)
    rows, width = inputs.shape
    states = maps.shape[1] // 2
    cumulative = small[:, :LANES]
    flat = cumulative.T
    mask = allowed_mask(rows, place, plan, m, False)
    scores = dot_nt(maps[:, states:], maps[:, :states], highest)
    for at in range(0, width, LANES):
        tile = slice(at, at + LANES)
        for low in range(0, rows, LANES):
            end = low + LANES
            parts = []
            for sub in range(per):
                head = at // LANES * per + sub
                decay = jnp.exp(
                    (cumulative[low:end, head : head + 1] - flat[head : head + 1, :end])
                    + mask[low:end, :end]
                )
                mixing = (decay * scores[low:end, :end]).astype(bf16)
                parts.append(dot(mixing, inputs[:end, tile]))
            out[low:end, tile] = lane_select(parts, per)


def unmix_kernel(per, place, plan, small, maps, inputs, grads, grad_inputs, grad_maps, total):
    m = pl.program_id(0)
    rows, width = inputs.shape
    states = maps.shape[1] // 2
    cumulative = small[:, :LANES]
    flat = cumulative.T
    mask = allowed_mask(rows, place, plan, m, True)
    scores = dot_nt(maps[:, :states], maps[:, states:], highest)
    lane = lax.broadcasted_iota(jnp.int32, (LANES, LANES), 1)
    total[...] = jnp.zeros_like(total)
    for at in range(0, width, LANES):
        tile = slice(at, at + LANES)
        for low in range(0, rows, LANES):
            end = low + LANES
            later = grads[low:, tile]
            parts = []
            gathered_sum = total[low:end, low:]
            for sub in range(per):
                head = at // LANES * per + sub
                decay = jnp.exp(
                    (flat[head : head + 1, low:] - cumulative[low:end, head : head + 1])
                    + mask[low:end, low:]
                )
                mixing = (decay * scores[low:end, low:]).astype(bf16)
                parts.append(dot(mixing, later))
                inside = (lane // (LANES // per)) == sub
                own = jnp.where(inside, inputs[low:end, tile].astype(f32), 0.0).astype(bf16)
                gathered_sum = gathered_sum + decay * dot_nt(own, later)
            total[low:end, low:] = gathered_sum
            grad_inputs[low:end, tile] = lane_select(parts, per)
    grad_scores = total[...].astype(bf16)
    grad_maps[:, :states] = dot(grad_scores, maps[:, states:].astype(bf16))
    grad_maps[:, states:] = dot_tn(grad_scores, maps[:, :states].astype(bf16))


def inflow_of(cumulative, rows, place, plan, m):
    here = segment_of(column_position(rows, place), plan, place, m)
    before = segment_of(place[2] - 1, plan, place, m)
    return (here == before).astype(f32) * jnp.exp(cumulative)


def gated_kernel(
    place, plan, flags, small, maps, mixed, ahead, ahead_other, sibling, conv_out, gate, grad_y, gain, skip, spread, scanned, scaled_y, sums
):
    m = pl.program_id(0)
    rows, width = mixed.shape
    states = maps.shape[1] // 2
    inflow = both_parts(inflow_of(small[:, :LANES], rows, place, plan, m))
    output_map = maps[:, states:].astype(bf16)
    square = jnp.zeros((rows, LANES), f32)
    product = jnp.zeros((rows, LANES), f32)
    for at in range(0, width, LANES):
        tile = slice(at, at + LANES)
        entering = state_tile(states, flags, ahead, ahead_other, sibling, at)
        carried = dot(output_map, entering) * dot(inflow, spread[:, tile])
        scan = mixed[:, tile] + carried
        scanned[:, tile] = scan
        conv = conv_out[:, tile]
        gates = gate[:, tile].astype(f32)
        gated = (scan + skip[:, tile] * (conv * jax.nn.sigmoid(conv))) * (gates * jax.nn.sigmoid(gates))
        square = square + gated * gated
        scaled = gain[:, tile] * gated
        put_deal_rows(scaled_y, tile, scaled)
        product = product + grad_y[:, tile].astype(f32) * scaled
    ones = jnp.ones((HALO, LANES), f32)
    pick = lax.broadcasted_iota(jnp.int32, (HALO, rows), 0)
    sums[0] = jnp.where(pick == 0, dot_nt(ones, square, highest), dot_nt(ones, product, highest))


def ungated_kernel(
    inner_all, place, plan, small, maps, scanned, conv_out, gate, grad_y, sums, gain, skip, spread,
    normed_y_t, grads, grad_gate, local, row_part, grad_gain, grad_skip,
):
    m = pl.program_id(0)
    rows, width = scanned.shape
    states = maps.shape[1] // 2
    columns = columns_of(sums[0])
    inv = lax.rsqrt(columns[:, :1] / inner_all + epsilon)
    pull = inv * inv * inv * (columns[:, 1:2] / inner_all)
    cumulative = small[:, :LANES]
    inflow = both_parts(inflow_of(cumulative, rows, place, plan, m))
    before = segment_of(place[2] - 1, plan, place, m)
    last = segment_of(place[2] + rows - 1, plan, place, m)
    through = (last == before).astype(f32) * jnp.exp(cumulative[rows - 1 :, :])
    through_parts = both_parts(jnp.broadcast_to(through, (STATE_PAD, LANES)))
    output_map_t = maps[:, states:].T.astype(bf16)

    @pl.when(m == 0)
    def _():
        grad_gain[...] = jnp.zeros_like(grad_gain)
        grad_skip[...] = jnp.zeros_like(grad_skip)

    product = jnp.zeros((rows, LANES), f32)
    for at in range(0, width, LANES):
        tile = slice(at, at + LANES)
        conv = conv_out[:, tile]
        heads_x = conv * jax.nn.sigmoid(conv)
        mixer = scanned[:, tile] + skip[:, tile] * heads_x
        gates = gate[:, tile].astype(f32)
        logistic = jax.nn.sigmoid(gates)
        act = gates * logistic
        gated = mixer * act
        normed = gated * inv
        normed_y_t[tile, :] = (normed * gain[:, tile]).astype(bf16).T
        grad = grad_y[:, tile].astype(f32)
        grad_gain[:, tile] += jnp.sum(grad * normed, axis=0, keepdims=True)
        grad_gated = inv * (grad * gain[:, tile]) - gated * pull
        grad_mixer = grad_gated * act
        grads[:, tile] = grad_mixer.astype(bf16)
        grad_skip[:, tile] += jnp.sum(grad_mixer * heads_x, axis=0, keepdims=True)
        grad_gates = grad_gated * mixer * (logistic * (1.0 + gates * (1.0 - logistic)))
        grad_gate[:, tile] = grad_gates.astype(bf16)
        product = product + grad_gates * gates
        weighted = (grad_mixer * dot(inflow, spread[:, tile])).astype(bf16)
        local[0, :states, tile] = dot(output_map_t, weighted).astype(bf16)
        local[0, states:, tile] = dot(through_parts, spread[:, tile]).astype(bf16)
    row_part[0] = dot_nt(jnp.ones((HALO, LANES), f32), product, highest)


def unscan_kernel(
    place, plan, flags, flags_back, small, maps, scanned, conv_out, inputs, grads, grad_inputs, grad_maps,
    ahead, ahead_other, sibling, back, back_other, back_sibling, skip, scale, spread, grad_conv_out, grad_step, grad_bias, grad_heads,
):
    m = pl.program_id(0)
    rows, width = scanned.shape
    states = maps.shape[1] // 2
    cumulative, step, pre = (small[:, k * LANES : (k + 1) * LANES] for k in range(3))
    here = segment_of(column_position(rows, place), plan, place, m)
    before = segment_of(place[2] - 1, plan, place, m)
    last = segment_of(place[2] + rows - 1, plan, place, m)
    ending = cumulative[rows - 1 :, :]
    fading = both_parts((here == last).astype(f32) * jnp.exp(ending - cumulative))
    inflow = both_parts((here == before).astype(f32) * jnp.exp(cumulative))
    through = (last == before).astype(f32) * jnp.exp(ending)
    step_parts = both_parts(step)
    input_map = maps[:, :states].astype(bf16)

    @pl.when(m == 0)
    def _():
        grad_bias[...] = jnp.zeros_like(grad_bias)
        grad_heads[...] = jnp.zeros_like(grad_heads)

    grad_in, grad_out = grad_maps[:, :states], grad_maps[:, states:]
    grad_cum = jnp.zeros((rows, LANES), f32)
    grad_own = jnp.zeros((rows, LANES), f32)
    ends = jnp.zeros((HALO, LANES), f32)
    for at in range(0, width, LANES):
        tile = slice(at, at + LANES)
        spread_tile = spread[:, tile]
        leave = state_tile(states, flags_back, back, back_other, back_sibling, at)
        enter = state_tile(states, flags, ahead, ahead_other, sibling, at)
        fade = dot(fading, spread_tile)
        pulled = fade * dot(input_map, leave)
        values = inputs[:, tile].astype(f32)
        grad = grads[:, tile].astype(f32)
        total = grad_inputs[:, tile] + pulled
        faded = (values * fade).astype(bf16)
        weighted = (grad * dot(inflow, spread_tile)).astype(bf16)
        grad_in = grad_in + dot_nt(faded, leave)
        grad_out = grad_out + dot_nt(weighted, enter)
        conv = conv_out[:, tile]
        logistic = jax.nn.sigmoid(conv)
        heads_x = conv * logistic
        first = both_parts(grad * scanned[:, tile] - values * total)
        second = both_parts(total * heads_x)
        twice = jnp.concatenate([spread[:LANES, tile]] * 2, axis=1)
        grad_cum = grad_cum + dot_nt(first, twice)
        grad_own = grad_own + dot_nt(second, twice)
        fade_sum = jnp.sum(values * pulled, axis=0, keepdims=True)
        through_sum = jnp.sum(leave.astype(f32) * enter.astype(f32), axis=0, keepdims=True)
        pick = lax.broadcasted_iota(jnp.int32, (HALO, LANES), 0)
        edge = both_parts(jnp.where(pick == 0, fade_sum, through_sum))
        ends = ends + dot_nt(edge, twice)
        grad_x = total * dot(step_parts, spread_tile) + skip[:, tile] * grad
        result = grad_x * (logistic * (1.0 + conv * (1.0 - logistic)))
        grad_conv_out[:, tile] = result
        grad_bias[:, tile] += jnp.sum(result, axis=0, keepdims=True)
    for values, start in ((grad_in, width), (grad_out, width + states)):
        conv = conv_out[:, start : start + states]
        result = values * silu_slope(conv)
        grad_conv_out[:, start : start + states] = result
        grad_bias[:, start : start + states] += jnp.sum(result, axis=0, keepdims=True)
    row = lax.broadcasted_iota(jnp.int32, (rows, rows), 0)
    col = lax.broadcasted_iota(jnp.int32, (rows, rows), 1)
    upper = jnp.where(row <= col, 1.0, 0.0).astype(bf16)
    grad_rate = dot_mask(upper, grad_cum) + (ends[:1] + through * ends[1:2])
    rate = step * scale[...]
    grad_pre = (grad_rate * scale[...] + grad_own) * jax.nn.sigmoid(pre)
    grad_step[...] = grad_pre
    grad_heads[0:1, :] += jnp.sum(grad_rate * rate, axis=0, keepdims=True)
    grad_heads[1:2, :] += jnp.sum(grad_pre, axis=0, keepdims=True)


def unconv_kernel(
    place, plan, pre, halo, grad_out, after_rows, grad_step, row_part, taps, grad_pre, grad_state, row_sums,
    grad_taps, extended, extended_grad,
):
    m = pl.program_id(0)
    rows = pre.shape[0]
    channels = grad_out.shape[1]
    taps_total = taps.shape[0]
    here = segment_of(column_position(rows, place), plan, place, m)
    behind, ahead = [], []
    for tap in range(taps_total):
        lag = taps_total - 1 - tap
        behind.append((segment_of(column_position(rows, place, -lag), plan, place, m) == here).astype(f32))
        ahead.append((segment_of(column_position(rows, place, lag), plan, place, m) == here).astype(f32))

    @pl.when(m == 0)
    def _():
        grad_taps[...] = jnp.zeros_like(grad_taps)

    total = jnp.zeros((rows, LANES), f32)
    for at in range(0, channels, LANES):
        tile = slice(at, at + LANES)
        rows_before, rows_after = extended.at[at // LANES % 2], extended_grad.at[at // LANES % 2]
        own, grad = pre[:, tile], grad_out[:, tile]
        rows_before[:HALO, :] = halo[0, :, tile]
        rows_before[HALO:, :] = own
        rows_after[:rows, :] = grad
        rows_after[rows:, :] = after_rows[0, :, tile]
        last = taps_total - 1
        result = taps[last:, tile] * grad
        grad_taps[last:, tile] += jnp.sum(grad * own, axis=0, keepdims=True)
        for tap in range(last):
            lag = last - tap
            result = result + taps[tap : tap + 1, tile] * rows_after[lag : lag + rows, :] * ahead[tap]
            begin = HALO - lag
            product = grad * rows_before[begin : begin + rows, :] * behind[tap]
            grad_taps[tap : tap + 1, tile] += jnp.sum(product, axis=0, keepdims=True)
        grad_pre[:, tile] = result.astype(bf16)
        total = total + result * own
    grad_pre[:, channels:] = grad_step[...].astype(bf16)
    grad_state[...] = grad_pre[:, channels - grad_state.shape[1] : channels]
    total = total + grad_step[...] * pre[:, channels : channels + LANES]
    row_sums[0] = row_part[0] + dot_nt(jnp.ones((HALO, LANES), f32), total, highest)


def rows_kernel(quarters, first, second, *refs):
    for weight, out in zip(refs[:quarters], refs[quarters:]):
        cut = weight.shape[1] - second.shape[1]
        result = dot_nt(first[...], weight[:, : first.shape[1]]) + dot_nt(second[...], weight[:, cut:])
        put_deal_rows(out.at[0], slice(None), result)


def rows_gradient(first, second, weight, senders, count, edges):
    total = first.shape[0]
    size = lax.axis_size("head")
    width = weight.shape[0] // size
    rows = total // count
    flops = total * (first.shape[1] + second.shape[1]) * width * size
    moved = weight.size + (first.size + second.size) * size
    block = (1, senders, 1, rows // senders, width)
    if edges:
        shape = (1, senders, count, rows // senders, width)
        return call(
            functools.partial(rows_kernel, 2), (count,), (),
            [per_row(first, rows), per_row(second, rows)]
            + [(weight, (width, weight.shape[1]), lambda m, at=at: (at, 0)) for at in (0, size - 1)],
            [(shape, bf16, block, lambda m: (0, 0, m, 0, 0))] * 2, flops=flops, bytes_accessed=moved,
        )
    row_block = lambda array: (array, (rows, array.shape[1]), lambda q, m: (m, 0))
    return call(
        functools.partial(rows_kernel, 1), (size - 2, count), (),
        [row_block(first), row_block(second), (weight, (width, weight.shape[1]), lambda q, m: (q + 1, 0))],
        [
            (
                (size - 2, senders, count, rows // senders, width), bf16, block,
                lambda q, m: (q, 0, m, 0, 0),
            )
        ],
        flops=flops, bytes_accessed=moved,
    )[0]


def output_kernel(inner_all, tokens, branch, sums, out):
    inv = lax.rsqrt(columns_of(sums[0])[:, :1] / inner_all + epsilon)
    every = slice(None)
    put_deal_rows(out, every, deal_rows(tokens, every) + deal_rows(branch, every) * inv)


def input_kernel(
    size, place, low, high, middle, up, down, tokens, cot, inverse, sums, gain, out, grad_gain
):
    every = slice(None)
    here = place[0]
    width = tokens.shape[3]
    own = jnp.where(
        here == 0,
        deal_rows(low.at[0], every),
        jnp.where(here == size - 1, deal_rows(high.at[0], every), deal_rows(middle.at[0], every)),
    )
    rows_own = own + deal_rows(up, every) + deal_rows(down, every)
    inv = deal_rows(inverse, every)
    unit = deal_rows(tokens, every) * inv
    own_gain = gain[:, pl.ds(pl.multiple_of(here * width, width), width)]
    total = columns_of(sums[0])[:, :1] / (width * size)
    put_deal_rows(out, every, inv * (rows_own * own_gain - unit * total) + deal_rows(cot, every))
    product = jnp.sum(rows_own * unit, axis=0, keepdims=True)

    @pl.when(pl.program_id(0) == 0)
    def _():
        grad_gain[...] = product

    @pl.when(pl.program_id(0) > 0)
    def _():
        grad_gain[...] += product


def out_kernel(left, right, out):
    out[...] = dot(left[...], right[...]).astype(bf16)


def sent_kernel(columns, count, left, *refs):
    rights, out = refs[:count], refs[count]
    for which, source, target, size in columns:
        out[:, target : target + size] = dot(left[...], rights[which][:, source : source + size]).astype(bf16)


def kept_kernel(columns, count, cut, left, *refs):
    rights, other, outs = refs[:count], refs[count], refs[count + 1 :]
    step = pl.program_id(0)
    high, odd = step >= pl.num_programs(0) // 2, lax.rem(step, 2) == 1
    for which, source, target, size in columns:
        result = dot(left[...], rights[which][:, source : source + size])
        result = (result + other[:, target : target + size].astype(f32)).astype(bf16)
        if target < cut:
            keep, send, sending, start = outs[0], outs[1], high, target
        else:
            keep, send, sending, start = outs[2], outs[3], odd, target - cut
        tile = slice(start, start + size)

        @pl.when(sending)
        def _():
            send[:, tile] = result

        @pl.when(jnp.logical_not(sending))
        def _():
            keep[:, tile] = result


def total_kernel(targets, *refs):
    ins, outs = refs[:2], refs[2:]
    for out, (which, source, target, size) in zip([outs[t[0]] for t in targets], [t[1] for t in targets]):
        tile = slice(source, source + size)
        out[:, target : target + size] = ins[which][:, tile].astype(f32)


def weight_gradient_sent(odd_t, rights, columns, depth):
    total = odd_t.shape[1]
    width = max(target + size for _, _, target, size in columns)
    (sent,) = call(
        functools.partial(sent_kernel, columns, len(rights)), (odd_t.shape[0] // depth,), (),
        [(odd_t, (depth, total), lambda l: (l, 0))] + [entire(right) for right in rights],
        [((odd_t.shape[0], width), bf16, (depth, width), lambda l: (l, 0))],
        flops=2 * odd_t.shape[0] * total * width,
        bytes_accessed=odd_t.shape[0] * (total + width) * 2 + sum(right.size for right in rights) * 2,
    )
    return sent


def weight_gradient_kept(even_t, got, rights, columns, cut, depth):
    blocks = even_t.shape[0] // depth
    total = even_t.shape[1]
    width = got.shape[1]
    top = blocks // 2
    rows = even_t.shape[0] // 2
    half = lambda size, index: ((rows, size), bf16, (depth, size), index)
    return call(
        functools.partial(kept_kernel, columns, len(rights), cut), (blocks,), (),
        [(even_t, (depth, total), lambda l: (l, 0))] + [entire(right) for right in rights]
        + [(got, (depth, width), lambda l: (l, 0))],
        [
            half(cut, lambda l: (jnp.minimum(l, top - 1), 0)),
            half(cut, lambda l: (jnp.maximum(l - top, 0), 0)),
            half(width - cut, lambda l: (l // 2, 0)),
            half(width - cut, lambda l: (l // 2, 0)),
        ],
        flops=2 * even_t.shape[0] * total * width,
        bytes_accessed=even_t.shape[0] * (total + width) * 2 + sum(right.size for right in rights) * 2,
    )


def weight_gradient_parts(mine):
    links = axis_bits("seq")[1:]
    labels = [bit << 1 for bit in range(2 ** len(links))]
    return [
        Scattered(mine[0], mine[1], [x for x in labels if not x & links[-1]], links[::-1]),
        Scattered(mine[2], mine[3], [x for x in labels if not x & links[0]], links),
    ]


def weight_gradient_total(parts, results, depth):
    ins = [array for part in parts for array in part.finish()]
    targets = [(at, column) for at, (_, columns) in enumerate(results) for column in columns]
    return call(
        functools.partial(total_kernel, targets), (1,), (), [entire(a) for a in ins],
        [((depth, size), f32, (depth, size), lambda *_: (0, 0)) for size, _ in results],
        bytes_accessed=sum(a.size for a in ins) * 6,
    )


def per_device(
    tokens,
    cotangent,
    lengths,
    deal_order,
    norm_gain,
    proj_gate,
    proj_inner,
    proj_state,
    proj_step,
    conv_inner,
    conv_inner_bias,
    conv_state,
    conv_state_bias,
    step_bias,
    decay_log,
    skip_gain,
    inner_gain,
    proj_out,
):
    batch_count = lengths.shape[0]
    rows_local, width_own = tokens.shape
    tok_dev = rows_local // batch_count
    seq_index = lax.axis_index("seq")
    head_index = lax.axis_index("head")
    seq_size = lax.axis_size("seq")
    head_size = lax.axis_size("head")
    heads_own = proj_step.shape[1]
    inner_own = proj_inner.shape[1]
    head_width = inner_own // heads_own
    states = proj_state.shape[1] // 2
    taps_total = conv_inner.shape[0]
    width_all = width_own * head_size
    inner_all = inner_own * head_size
    depth = width_all // seq_size
    channels = inner_own + 2 * states
    per = LANES // head_width
    rows = tok_dev
    grid = (batch_count,)

    place = jnp.stack(
        [head_index, seq_index, seq_index * tok_dev, jnp.int32(tok_dev * seq_size)]
    ).astype(jnp.int32)
    plan = (jnp.cumsum(lengths, axis=1) - lengths).astype(jnp.int32)
    scalars = (place, plan)

    piece = tok_dev // seq_size
    dealt_row = deal_order.reshape(batch_count, seq_size, piece) + (
        jnp.arange(batch_count, dtype=jnp.int32) * tok_dev
    )[:, None, None]
    picks = (
        jnp.transpose(dealt_row, (1, 0, 2)).reshape(rows_local, 1) == jnp.arange(rows_local)[None, :]
    ).astype(bf16)
    deal_shape = (seq_size, batch_count, piece, width_own)

    def dealt(values):
        values = dot(picks, values).astype(bf16).reshape(seq_size, batch_count * piece, width_own)
        values = lax.all_to_all(values, "seq", split_axis=0, concat_axis=0, tiled=True)
        return values.reshape(deal_shape)

    def sent_back(values):
        values = values.reshape(seq_size, -1, width_own)
        return lax.all_to_all(values, "seq", split_axis=0, concat_axis=0, tiled=True)

    def put_back(values):
        return dot_tn(picks, values.reshape(rows_local, width_own)).astype(bf16)

    deal_tokens = dealt(tokens)
    lines = LineGather(deal_tokens)
    lines.advance()
    deal_cot = dealt(cotangent)

    full_in = lax.all_gather(
        jnp.concatenate(
            [proj_inner, proj_state, jnp.pad(proj_step, ((0, 0), (0, 2 * LANES - heads_own))), proj_gate],
            axis=1,
        ),
        "seq", axis=0, tiled=True,
    )
    full_out = lax.all_gather(after(proj_out, lines.up, lines.down), "seq", axis=1, tiled=True)

    lines = lines.finish()
    normed, even_t, odd_t, own_t, inv_rms = all_features(deal_tokens, lines, place, norm_gain[None, :], depth)
    cot_lines = LineGather(after(deal_cot, lines[0][-1], lines[1][-1]))

    taps = jnp.concatenate([conv_inner, conv_state], axis=1)
    bias = jnp.concatenate([conv_inner_bias, conv_state_bias])[None, :]
    pad = LANES - heads_own
    step_bias_row = jnp.pad(step_bias, (0, pad))[None, :]
    scale = jnp.pad(-jnp.exp(decay_log), (0, pad))[None, :]
    spread = (
        jnp.arange(2 * LANES)[:, None] % LANES == jnp.arange(inner_own)[None, :] // head_width
    ).astype(bf16)
    skip = jnp.repeat(skip_gain, head_width)[None, :]
    gain = inner_gain[None, :]

    pre_width = channels + 2 * LANES
    (pre,) = cot_lines.advance(dot(normed, full_in[:, :pre_width]))
    halo = passed_along(pre.reshape(batch_count, tok_dev, -1)[:, tok_dev - HALO :], "seq", 1)
    gate = dot(normed, full_in[:, pre_width:]).astype(bf16)
    halo, gate = lax.optimization_barrier((halo, gate))
    conv_out, small, inputs, maps, fresh = call(
        functools.partial(conv_kernel, inner_own), grid, scalars,
        [per_row(pre, rows), per_step(halo)]
        + [entire(a) for a in (taps, bias, step_bias_row, scale, spread)],
        [
            row_out(rows_local, rows, channels, f32),
            row_out(rows_local, rows, 3 * LANES, f32),
            row_out(rows_local, rows, inner_own, bf16),
            row_out(rows_local, rows, 2 * states, f32),
            step_out(batch_count, (states + STATE_PAD, inner_own), bf16),
        ],
        scratch=[pltpu.VMEM((2, rows + HALO, LANES), f32)],
        flops=rows_local * inner_own * 2000, bytes_accessed=rows_local * inner_own * 20,
    )
    conv_out, small, inputs, maps, fresh = cot_lines.advance(conv_out, small, inputs, maps, fresh)
    scan_ins = [per_row(small, rows), per_row(maps, rows)]
    (mixed,) = call(
        functools.partial(mix_kernel, per), grid, scalars, scan_ins + [per_row(inputs, rows)],
        [row_out(rows_local, rows, inner_own, f32)],
        flops=rows_local * inner_own * 2500, bytes_accessed=rows_local * inner_own * 6,
    )
    cot_lines.advance()

    entering, mixed, (flat_cot, grad_y) = scan_before(
        fresh, states, False,
        [lambda: mixed, lambda _: cotangent_products(deal_cot, cot_lines.finish(), place, full_out)],
    )
    vectors = [entire(gain), entire(skip), entire(spread)]
    scanned, scaled_y, sums = call(
        gated_kernel, grid, scalars + entering[:1],
        scan_ins
        + [per_row(mixed, rows)] + [per_step(a) for a in entering[1:]]
        + [per_row(conv_out, rows), per_row(gate, rows)]
        + [per_row(grad_y, rows)] + vectors,
        [
            row_out(rows_local, rows, inner_own, f32),
            deal_out(seq_size, batch_count, piece, inner_own, bf16),
            step_out(batch_count, (HALO, rows), f32),
        ],
        flops=rows_local * inner_own * 1500, bytes_accessed=rows_local * inner_own * 8,
    )
    out_rows = dot(scaled_y.reshape(rows_local, inner_own), full_out).astype(bf16)
    sums = sums + swapped(sums, "head", 1)
    for bit in axis_bits("head")[1:]:
        other, out_rows = lax.optimization_barrier((swapped(sums, "head", bit), out_rows))
        sums = sums + other
    branch = lax.psum_scatter(
        out_rows.reshape(deal_shape[:3] + (width_all,)), "head", scatter_dimension=3, tiled=True
    )

    normed_y_t, grads, grad_gate, local, row_part, grad_gain, grad_skip = call(
        functools.partial(ungated_kernel, inner_all), grid, scalars,
        scan_ins
        + [per_row(array, rows) for array in (scanned, conv_out, gate, grad_y)]
        + [per_step(sums)] + vectors,
        [((inner_own, rows_local), bf16, (inner_own, rows), lambda m, *_: (0, m))]
        + [row_out(rows_local, rows, inner_own, bf16)] * 2
        + [step_out(batch_count, (states + STATE_PAD, inner_own), bf16)]
        + [step_out(batch_count, (HALO, rows), f32)]
        + [sum_out((1, inner_own))] * 2,
        flops=rows_local * inner_own * 2000, bytes_accessed=rows_local * inner_own * 24,
    )
    grad_inputs, grad_maps = call(
        functools.partial(unmix_kernel, per), grid, scalars,
        scan_ins + [per_row(inputs, rows), per_row(grads, rows)],
        [row_out(rows_local, rows, inner_own, f32), row_out(rows_local, rows, 2 * states, f32)],
        scratch=[pltpu.VMEM((rows, rows), f32)],
        flops=rows_local * inner_own * 4000, bytes_accessed=rows_local * inner_own * 8,
    )
    (grad_out,) = call(
        out_kernel, (head_size,), (),
        [entire(normed_y_t), (flat_cot, (rows_local, width_own), lambda q: (0, q))],
        [((inner_own, width_all), bf16, (inner_own, width_own), lambda q: (0, q))],
        flops=2 * rows_local * inner_own * width_all, bytes_accessed=rows_local * width_all * 6,
    )
    leaving, grad_inputs, grad_out = scan_before(
        local, states, True, [lambda: grad_inputs, lambda _: grad_out]
    )

    grad_out = lax.psum_scatter(grad_out, "seq", scatter_dimension=1, tiled=True)
    grad_conv_out, grad_step, grad_bias, grad_heads = call(
        unscan_kernel, grid, scalars + entering[:1] + leaving[:1],
        scan_ins
        + [per_row(a, rows) for a in (scanned, conv_out, inputs, grads)]
        + [per_row(grad_inputs, rows), per_row(grad_maps, rows)]
        + [per_step(a) for a in entering[1:] + leaving[1:]] + [entire(skip), entire(scale), entire(spread)],
        [
            row_out(rows_local, rows, channels, f32),
            row_out(rows_local, rows, LANES, f32),
            sum_out((1, channels)),
            sum_out((HALO, LANES)),
        ],
        flops=rows_local * inner_own * 4000, bytes_accessed=rows_local * inner_own * 28,
    )
    after_rows = passed_along(grad_conv_out.reshape(batch_count, tok_dev, channels)[:, :HALO], "seq", -1)
    after_rows, branch = lax.optimization_barrier((after_rows, branch))
    grad_pre, grad_state, row_dots, grad_taps = call(
        unconv_kernel, grid, scalars,
        [per_row(pre, rows), per_step(halo), per_row(grad_conv_out, rows), per_step(after_rows)]
        + [per_row(grad_step, rows), per_step(row_part), entire(taps)],
        [
            row_out(rows_local, rows, channels + LANES, bf16),
            row_out(rows_local, rows, 2 * states, bf16),
            step_out(batch_count, (HALO, rows), f32),
            sum_out((taps_total, channels)),
        ],
        scratch=[pltpu.VMEM((2, rows + HALO, LANES), f32)] * 2,
        flops=rows_local * inner_own * 100, bytes_accessed=rows_local * inner_own * 14,
    )
    columns = [
        (0, 0, 0, inner_own), (1, 0, inner_own, inner_own), (0, channels, 2 * inner_own, LANES)
    ]
    fill = lambda row: jnp.pad(row, ((0, 0), (0, channels - row.shape[1])))
    state_small = jnp.concatenate([grad_taps[:, inner_own:], grad_bias[:, inner_own:]])
    row_dots = jnp.concatenate([row_dots[:, 0, :], state_small.reshape(-1, rows)])
    packed = jnp.concatenate(
        [grad_taps, grad_bias, fill(grad_gain), fill(grad_skip), fill(grad_heads[:2].reshape(1, 2 * LANES))]
    )
    packed = packed + swapped(packed, "seq", 1)
    seq_bits, head_bits = axis_bits("seq"), axis_bits("head")
    sent = weight_gradient_sent(odd_t, [grad_pre, grad_gate], columns, depth)
    others = [
        swapped(row_dots, "head", head_bits[0]), swapped(packed, "seq", seq_bits[1]),
        swapped(grad_state, "head", head_bits[0]),
    ]
    others, sent = lax.optimization_barrier((others, sent))
    row_dots, packed, grad_state = row_dots + others[0], packed + others[1], added(grad_state, others[2])
    got = swapped(sent, "seq", 1)
    grad_rows = lambda first, edges: rows_gradient(
        first, grad_gate, full_in, seq_size, batch_count, edges
    )
    low, high = grad_rows(after(grad_pre, sent), True)
    other, low, high = lax.optimization_barrier((swapped(packed, "seq", seq_bits[2]), low, high))
    packed = packed + other
    for bit in seq_bits[3:]:
        packed = packed + swapped(packed, "seq", bit)
    rows_line = LineScatter([low[0], high[0]])
    mine = weight_gradient_kept(even_t, after(got, low), [grad_pre, grad_gate], columns, inner_own, depth)
    rows_line.middle = grad_rows(after(grad_pre, mine[0]), False)
    others = [swapped(row_dots, "head", head_bits[1]), swapped(grad_state, "head", head_bits[1])]
    *mine, rows_line.middle, branch, grad_out, others = rows_line.advance(
        *mine, rows_line.middle, branch, grad_out, others
    )
    row_dots, grad_state = row_dots + others[0], added(grad_state, others[1])
    for bit in head_bits[2:]:
        row_dots = row_dots + swapped(row_dots, "head", bit)
        grad_state = added(grad_state, swapped(grad_state, "head", bit))
    (grad_w_state,) = call(
        out_kernel, (1,), (), [entire(own_t), entire(grad_state)], [sum_out((width_own, 2 * states), bf16)],
        flops=2 * rows_local * width_own * 2 * states, bytes_accessed=rows_local * (width_own + 2 * states) * 2,
    )
    state_small = row_dots[batch_count:].reshape(-1, 2 * states).astype(bf16)
    row_dots = row_dots[:batch_count, None, :]
    pad_rows = -state_small.shape[0] % 16
    grad_w_state = jnp.concatenate([grad_w_state, jnp.pad(state_small, ((0, pad_rows), (0, 0)))])
    grad_w_state = added(grad_w_state, swapped(grad_w_state, "seq", 1))
    parts = weight_gradient_parts(mine)
    for part in parts:
        part.send()
    (grad_w_state,) = rows_line.advance(grad_w_state)
    other = swapped(grad_w_state, "seq", seq_bits[1])
    (out_rows,) = call(
        functools.partial(output_kernel, inner_all), grid, (),
        [per_deal(deal_tokens), per_deal(branch), per_step(sums)],
        [deal_out(seq_size, batch_count, piece, width_own, bf16)],
        bytes_accessed=rows_local * width_own * 6,
    )
    out_rows = sent_back(out_rows)
    for part in parts:
        part.receive()
    *pairs, out_rows = rows_line.advance(*[part.pair for part in parts], out_rows)
    for part, pair in zip(parts, pairs):
        part.pair = pair
        part.send()
    grad_out = grad_out.astype(f32)
    up, down = rows_line.finish()
    middle = rows_line.middle
    grad_rows_in, grad_norm_gain = call(
        functools.partial(input_kernel, head_size), grid, (place,),
        [per_deal_of(low), per_deal_of(high)]
        + [
            (
                middle, (1, seq_size, 1, piece, width_own),
                lambda m, place: (jnp.clip(place[0] - 1, 0, head_size - 3), 0, m, 0, 0),
            )
        ]
        + [per_deal(a) for a in (up, down, deal_tokens, deal_cot, inv_rms)]
        + [per_step(row_dots), entire(norm_gain[None, :])],
        [deal_out(seq_size, batch_count, piece, width_own, bf16), sum_out((1, width_own))],
        bytes_accessed=rows_local * width_own * 16,
    )
    parts[0].got, parts[1].got, other = after_all((parts[0].got, parts[1].got, other), (grad_rows_in,))
    grad_w_state = added(grad_w_state, other)
    grad_w_state = added(grad_w_state, swapped(grad_w_state, "seq", seq_bits[2]))
    for part in parts:
        part.receive()
        while part.left:
            part.send()
            part.receive()
    grad_inner, grad_w_gate, grad_w_step = weight_gradient_total(
        parts,
        [
            (inner_own, [(0, 0, 0, inner_own)]),
            (inner_own, [(1, 0, 0, inner_own)]),
            (LANES, [(1, inner_own, 0, LANES)]),
        ],
        depth,
    )
    for bit in seq_bits[3:]:
        grad_w_state = added(grad_w_state, swapped(grad_w_state, "seq", bit))
    out_back = put_back(out_rows)
    grad_w_state = grad_w_state.astype(f32)
    state_sums = grad_w_state[width_own : width_own + taps_total + 1]
    gain_high = grad_norm_gain.astype(bf16)
    gain_low = (grad_norm_gain - gain_high.astype(f32)).astype(bf16)
    gain_rows = jnp.pad(jnp.concatenate([gain_high, gain_low]), ((0, HALO - 2), (0, 0)))
    own_rows = batch_count * piece
    grad_back = sent_back(
        jnp.concatenate(
            [
                grad_rows_in.reshape(seq_size, own_rows, width_own),
                jnp.broadcast_to(gain_rows, (seq_size, HALO, width_own)),
            ],
            axis=1,
        )
    )
    grad_norm_gain = jnp.sum(grad_back[:, own_rows : own_rows + 2].astype(f32), axis=(0, 1))
    grad_back = put_back(grad_back[:, :own_rows])
    state_own = 2 * states // head_size
    state_sums = lax.dynamic_slice_in_dim(state_sums, head_index * state_own, state_own, 1)
    return (
        out_back,
        grad_back,
        grad_norm_gain,
        grad_w_gate,
        grad_inner,
        grad_w_state[:width_own],
        grad_w_step[:, :heads_own],
        packed[:taps_total, :inner_own],
        packed[taps_total, :inner_own],
        state_sums[:taps_total],
        state_sums[taps_total],
        packed[taps_total + 3, LANES : LANES + heads_own],
        packed[taps_total + 3, :heads_own],
        jnp.sum(packed[taps_total + 2, :inner_own].reshape(heads_own, head_width), axis=1),
        packed[taps_total + 1, :inner_own],
        grad_out,
    )


def solution(mesh):
    return jax.shard_map(
        per_device,
        mesh=mesh,
        in_specs=(
            P("seq", "head"),
            P("seq", "head"),
            P(),
            P("seq"),
            P(),
            P("seq", "head"),
            P("seq", "head"),
            P("seq", None),
            P("seq", "head"),
            P(None, "head"),
            P("head"),
            P(),
            P(),
            P("head"),
            P("head"),
            P("head"),
            P("head"),
            P("head", "seq"),
        ),
        out_specs=(
            P("seq", "head"),
            P("seq", "head"),
            P("head"),
            P("seq", "head"),
            P("seq", "head"),
            P("head", None),
            P("seq", "head"),
            P(None, "head"),
            P("head"),
            P(None, "head"),
            P("head"),
            P("head"),
            P("head"),
            P("head"),
            P("head"),
            P("head", "seq"),
        ),
        check_vma=False,
    )
```

```python
import functools
import math
import jax
import jax.numpy as jnp
from jax import lax
from jax.experimental import pallas as pl
from jax.experimental.pallas import tpu as pltpu
from jax.sharding import PartitionSpec as P

epsilon = 1e-05
highest = lax.Precision.HIGHEST
f32 = jnp.float32
bf16 = jnp.bfloat16
LANES = 128
HALO = 8
STATE_PAD = 16
HBM_BYTES = 700000
VMEM_SPARE = 10 * 1024 * 1024


def swapped(value, axis, bit):
    return lax.ppermute(value, axis, [(i, i ^ bit) for i in range(lax.axis_size(axis))])


def axis_bits(axis):
    count = lax.axis_size(axis)
    return [1 << k for k in range(count.bit_length() - 1)]


def added(left, right):
    return (left.astype(f32) + right.astype(f32)).astype(left.dtype)


def after(value, *others):
    return lax.optimization_barrier((value, *others))[0]


def after_all(values, others):
    return lax.optimization_barrier((tuple(values), tuple(others)))[0]


class Scattered:
    def __init__(self, keep, send, labels, order):
        rows = keep.shape[0] // len(labels)
        self.pair = (keep.reshape(len(labels), rows, -1), send.reshape(len(labels), rows, -1))
        self.labels, self.left = labels, list(order)

    def send(self):
        self.got = swapped(self.pair[1], "seq", self.left.pop(0))

    def receive(self):
        total = added(self.pair[0], self.got)
        if not self.left:
            self.pair = (total,)
            return
        following, labels = self.left[0], self.labels
        keep_at = [at for at, label in enumerate(labels) if not label & following]
        send_at = [labels.index(labels[at] ^ following) for at in keep_at]
        kept = jnp.concatenate([total[at : at + 1] for at in keep_at])
        sent = jnp.concatenate([total[at : at + 1] for at in send_at])
        self.pair = (kept, sent)
        self.labels = [labels[at] for at in keep_at]

    def finish(self):
        return [self.pair[0][0]]


class LineGather:
    def __init__(self, own):
        self.size = lax.axis_size("head")
        self.up = self.down = own
        self.ups, self.downs = [], []

    def advance(self, *beside):
        step = len(self.ups) + 1
        if step < self.size:
            up = lax.ppermute(self.up, "head", [(i, i + 1) for i in range(step - 1, self.size - 1)])
            down = lax.ppermute(self.down, "head", [(i, i - 1) for i in range(1, self.size - step + 1)])
            if beside:
                (up, down), beside = lax.optimization_barrier(((up, down), beside))
            self.up, self.down = up, down
            self.ups.append(up)
            self.downs.append(down)
        return beside

    def finish(self):
        while len(self.ups) + 1 < self.size:
            self.advance()
        return self.ups, self.downs


class LineScatter:
    def __init__(self, edges, middle=None):
        self.size, self.here = lax.axis_size("head"), lax.axis_index("head")
        self.edges, self.middle = edges, middle
        self.up = self.down = None
        self.step = 0

    def block_of(self, at):
        last = self.size - 1
        inner = lax.dynamic_index_in_dim(self.middle, jnp.clip(at - 1, 0, last - 2), 0, keepdims=False)
        return jnp.where(at <= 0, self.edges[0], jnp.where(at >= last, self.edges[1], inner))

    def advance(self, *beside):
        self.step += 1
        step, size, here = self.step, self.size, self.here
        if step < size:
            if step == 1:
                up, down = self.edges[1], self.edges[0]
            else:
                up = added(self.block_of(here + size - step), self.up)
                down = added(self.block_of(here - size + step), self.down)
            up = lax.ppermute(up, "head", [(i, i + 1) for i in range(step)])
            down = lax.ppermute(down, "head", [(i, i - 1) for i in range(size - step, size)])
            if beside:
                (up, down), beside = lax.optimization_barrier(((up, down), beside))
            self.up, self.down = up, down
        return beside

    def finish(self):
        while self.step + 1 < self.size:
            self.advance()
        return self.up, self.down


def axis_sum(value, axis):
    for bit in axis_bits(axis):
        value = value + swapped(value, axis, bit)
    return value


def passed_along(value, axis, steps):
    count = lax.axis_size(axis)
    initial, last = (max(0, -steps), min(count, count - steps))
    return lax.ppermute(value, axis, [(source, source + steps) for source in range(initial, last)])


def dot(left, right, precision=None):
    return jnp.dot(left, right, preferred_element_type=f32, precision=precision)


def dot_nt(left, right, precision=None):
    return lax.dot_general(
        left, right, (((1,), (1,)), ((), ())), preferred_element_type=f32, precision=precision
    )


def dot_tn(left, right, precision=None):
    return lax.dot_general(
        left, right, (((0,), (0,)), ((), ())), preferred_element_type=f32, precision=precision
    )


def both_parts(values):
    high = values.astype(bf16)
    return jnp.concatenate([high, (values - high.astype(f32)).astype(bf16)], axis=1)


def three_parts(values):
    high = values.astype(bf16)
    rest = values - high.astype(f32)
    middle = rest.astype(bf16)
    return high, middle, (rest - middle.astype(f32)).astype(bf16)


def dot_mask(mask, values):
    return sum(dot(mask, part) for part in three_parts(values))


def silu_slope(values):
    logistic = jax.nn.sigmoid(values)
    return logistic * (1.0 + values * (1.0 - logistic))


def big(shape, dtype):
    return math.prod(shape) * jnp.dtype(dtype).itemsize > HBM_BYTES


def tiled_bytes(shape, dtype):
    *lead, rows, lanes = shape
    size = -(-rows // 8) * 8 * -(-lanes // LANES) * LANES * jnp.dtype(dtype).itemsize
    for count in lead:
        size *= count
    return size


def call(kernel, grid, scalars, ins, outs, scratch=(), flops=0, bytes_accessed=0):
    ins = [(streamed(a) if big(a.shape, a.dtype) else a, block, index) for a, block, index in ins]
    held = [block == array.shape for array, block, _ in ins]
    need = sum(
        (1 if whole else 2) * tiled_bytes(block, array.dtype) for (array, block, _), whole in zip(ins, held)
    )
    need += sum(2 * tiled_bytes(block, dtype) for _, dtype, block, _ in outs)
    need += sum(tiled_bytes(item.shape, item.dtype) for item in scratch)
    return pl.pallas_call(
        kernel,
        grid_spec=pltpu.PrefetchScalarGridSpec(
            num_scalar_prefetch=len(scalars),
            grid=grid,
            in_specs=[
                pl.BlockSpec(block, index, pipeline_mode=pl.Buffered(1) if whole else None)
                for (_, block, index), whole in zip(ins, held)
            ],
            out_specs=[pl.BlockSpec(block, index) for _, _, block, index in outs],
            scratch_shapes=list(scratch),
        ),
        out_shape=[
            (pltpu.HBM if big(shape, dtype) else jax.ShapeDtypeStruct)(shape, dtype) for shape, dtype, _, _ in outs
        ],
        compiler_params=pltpu.CompilerParams(vmem_limit_bytes=need + VMEM_SPARE),
        cost_estimate=pl.CostEstimate(
            flops=int(flops), bytes_accessed=int(bytes_accessed), transcendentals=0
        ),
    )(*scalars, *[array for array, _, _ in ins])


def streamed(array):
    return pltpu.with_memory_space_constraint(array, pltpu.HBM)


def per_row(array, rows):
    return (array, (rows,) + array.shape[1:], lambda m, *_: (m,) + (0,) * (array.ndim - 1))


def per_deal(array):
    return (array, (array.shape[0], 1) + array.shape[2:], lambda m, *_: (0, m, 0, 0))


def per_deal_of(array):
    return (array, (1, array.shape[1], 1) + array.shape[3:], lambda m, *_: (0, 0, m, 0, 0))


def deal_out(senders, count, rows, width, dtype):
    return ((senders, count, rows, width), dtype, (senders, 1, rows, width), lambda m, *_: (0, m, 0, 0))


def deal_rows(ref, tile):
    values = ref[:, 0, :, tile].astype(f32)
    return values.reshape(values.shape[0] * values.shape[1], values.shape[2])


def put_deal_rows(ref, tile, values):
    shape = (ref.shape[0], ref.shape[2], values.shape[1])
    ref[:, 0, :, tile] = values.reshape(shape).astype(ref.dtype)


def per_step(array):
    return (array, (1,) + array.shape[1:], lambda m, *_: (m,) + (0,) * (array.ndim - 1))


def entire(array):
    return (array, array.shape, lambda *_: (0,) * array.ndim)


def row_out(total, rows, width, dtype):
    return ((total, width), dtype, (rows, width), lambda m, *_: (m, 0))


def step_out(count, shape, dtype):
    return ((count,) + shape, dtype, (1,) + shape, lambda m, *_: (m,) + (0,) * len(shape))


def sum_out(shape, dtype=f32):
    return (shape, dtype, shape, lambda *_: (0,) * len(shape))


def joined(earlier, following, states):
    row = lax.broadcasted_iota(jnp.int32, earlier.shape, 0)
    return following[states : states + 1] * earlier + jnp.where(row < states, following, 0.0)


def chip_kernel(states, flags, own, other, total):
    for at in range(own.shape[0]):
        mine, theirs = own[at].astype(f32), other[at].astype(f32)
        later = flags[0] != 0
        first, second = jnp.where(later, theirs, mine), jnp.where(later, mine, theirs)
        total[at] = joined(first, second, states).astype(bf16)


def link_kernel(states, step, last, flags, *refs):
    total, other, refs = refs[0], refs[1], refs[2:]
    later = flags[step] != 0
    if step > 1:
        before, refs = refs[0], refs[1:]
    for at in range(total.shape[0]):
        mine, theirs = total[at].astype(f32), other[at].astype(f32)
        if step == 1:
            row = lax.broadcasted_iota(jnp.int32, mine.shape, 0)
            ahead = jnp.where(row < states, 0.0, 1.0)
            refs[0][at] = jnp.where(later, theirs, ahead).astype(bf16)
        else:
            ahead = before[at].astype(f32)
            refs[0][at] = jnp.where(later, joined(theirs, ahead, states), ahead).astype(bf16)
        if not last:
            first, second = jnp.where(later, theirs, mine), jnp.where(later, mine, theirs)
            refs[1][at] = joined(first, second, states).astype(bf16)


def state_tile(states, flags, ahead, ahead_other, sibling, at):
    odd = flags[flags.shape[0] - 1] != 0
    half = ahead.shape[2]
    tile = slice(at % half, at % half + LANES)
    mine, theirs = ahead[0, :, tile], ahead_other[0, :, tile]
    values = (jnp.where(odd, theirs, mine) if at < half else jnp.where(odd, mine, theirs)).astype(f32)
    near = sibling[0, :, at : at + LANES].astype(f32)
    return jnp.where(flags[0] != 0, joined(values, near, states), values)[:states].astype(bf16)


def scan_before(local, states, reverse, fillers):
    here = lax.axis_index("seq")
    bits = axis_bits("seq")
    count, height, width = local.shape
    passed = [((here & bit) == 0) if reverse else ((here & bit) != 0) for bit in bits]
    flags = jnp.stack(passed + [(here & 1) != 0]).astype(jnp.int32)
    whole = local.shape
    piece = (count, height, width // 2)
    at_step = lambda *_: (0, 0, 0)
    at_core = lambda _, flags: (0, 0, flags[len(bits)])
    half_out = (piece, bf16, piece, at_step)
    moved = local.size * 4
    sibling = swapped(local, "seq", 1)
    (total,) = call(
        functools.partial(chip_kernel, states), (1,), (flags,),
        [(local, piece, at_core), (sibling, piece, at_core)], [half_out], bytes_accessed=moved,
    )
    ahead, filled, beside = None, [], ()
    for step, bit in enumerate(bits[1:], 1):
        other = swapped(total, "seq", bit)
        if step <= len(fillers):
            other, value = lax.optimization_barrier((other, fillers[step - 1](*beside)))
            beside = (value,)
            filled.append(value)
        last = step == len(bits) - 1
        ins = [total, other] + ([] if ahead is None else [ahead])
        results = call(
            functools.partial(link_kernel, states, step, last), (1,), (flags,),
            [(array, piece, at_step) for array in ins], [half_out] * (1 if last else 2),
            bytes_accessed=moved,
        )
        ahead = results[0]
        total = None if last else results[1]
    ahead_other = swapped(ahead, "seq", 1)
    return [(flags, ahead, ahead_other, sibling)] + filled


def columns_of(rows_form):
    rows = rows_form.shape[1]
    row = lax.broadcasted_iota(jnp.int32, (rows, rows), 0)
    col = lax.broadcasted_iota(jnp.int32, (rows, rows), 1)
    same = jnp.where(row == col, 1.0, 0.0).astype(bf16)
    return dot_nt(same.astype(f32), rows_form, highest)


def segment_of(position, plan, place, m):
    found = jnp.full(jnp.shape(position), -1, jnp.int32)
    for k in range(plan.shape[1]):
        found = found + (position >= plan[m, k]).astype(jnp.int32)
    return jnp.where(position >= place[3], -2, found)


def column_position(rows, place, shift=0):
    return place[2] + shift + lax.broadcasted_iota(jnp.int32, (rows, 1), 0)


def row_position(rows, place):
    return place[2] + lax.broadcasted_iota(jnp.int32, (1, rows), 1)


def by_core(values, me, depth):
    count = values.shape[1] // depth
    blocks = [values[:, k * depth : (k + 1) * depth] for k in range(count)]
    odd = (me & 1) != 0
    halves = []
    for at in (0, 1):
        straight, turned = blocks[at::2], blocks[1 - at :: 2]
        half = [jnp.where(odd, b, a) for a, b in zip(straight, turned)]
        bit = 1
        while bit < count // 2:
            flip = ((me >> 1) & bit) != 0
            half = [jnp.where(flip, half[k ^ bit], half[k]) for k in range(len(half))]
            bit *= 2
        halves.append(half[0] if len(half) == 1 else jnp.concatenate(half, axis=1))
    return halves


def half_start(quarter, me, width, depth):
    count = width // depth // 2
    return pl.multiple_of(((quarter * count) ^ ((me >> 1) & ~(count - 1))) * depth, width // 2)


def line_slot(own, ups, downs, z, step):
    if step == 0:
        return deal_rows(own, slice(None))
    up, down = ups[step - 1], downs[len(downs) - step]
    return jnp.where(z >= step, deal_rows(up, slice(None)), deal_rows(down, slice(None)))


def features_kernel(size, depth, place, *refs):
    own, ups, downs = refs[0], refs[1:size], refs[size : 2 * size - 1]
    gain, normed, even_t, odd_t, own_t, inverse = refs[2 * size - 1 :]
    z, me = place[0], place[1]
    width = own.shape[3]
    slots = [line_slot(own, ups, downs, z, step) for step in range(size)]
    square = sum(jnp.sum(slot * slot, axis=1, keepdims=True) for slot in slots)
    inv = lax.rsqrt(square / (width * size) + epsilon)
    put_deal_rows(inverse, slice(None), inv)
    for step, slot in enumerate(slots):
        quarter = lax.rem(z - step + size, size)
        place_at = pl.ds(pl.multiple_of(quarter * width, width), width)
        slot = slot * inv * gain[:, place_at]
        normed[:, place_at] = slot.astype(bf16)
        if step == 0:
            own_t[...] = slot.astype(bf16).T
        first, second = by_core(slot, me, depth)
        at = pl.ds(half_start(quarter, me, width, depth), width // 2)
        even_t[at, :] = first.astype(bf16).T
        odd_t[at, :] = second.astype(bf16).T


def all_features(own, lines, place, gain, depth):
    senders, count, piece, width = own.shape
    rows = senders * piece
    total = rows * count
    size = lax.axis_size("head")
    ups, downs = lines
    half = width * size // 2
    outs = [row_out(total, rows, 2 * half, bf16)]
    outs += [((half, total), bf16, (half, rows), lambda m, *_: (0, m))] * 2
    outs.append(((width, total), bf16, (width, rows), lambda m, *_: (0, m)))
    outs.append(deal_out(senders, count, piece, 1, f32))
    return call(
        functools.partial(features_kernel, size, depth), (count,), (place,),
        [per_deal(array) for array in [own] + ups + downs] + [entire(gain)], outs,
        bytes_accessed=total * width * 2 * 15,
    )


def cotangent_kernel(size, place, *refs):
    own, ups, downs = refs[0], refs[1:size], refs[size : 2 * size - 1]
    weight, every, grad_y = refs[2 * size - 1 :]
    z = place[0]
    width = own.shape[3]
    total = None
    for step in range(size):
        slot = line_slot(own, ups, downs, z, step)
        quarter = lax.rem(z - step + size, size)
        place_at = pl.ds(pl.multiple_of(quarter * width, width), width)
        every[:, place_at] = slot.astype(bf16)
        part = dot_nt(slot.astype(bf16), weight[:, place_at])
        total = part if total is None else total + part
    grad_y[...] = total.astype(bf16)


def cotangent_products(own, lines, place, weight):
    senders, count, piece, width = own.shape
    rows = senders * piece
    total = rows * count
    size = lax.axis_size("head")
    ups, downs = lines
    return call(
        functools.partial(cotangent_kernel, size), (count,), (place,),
        [per_deal(array) for array in [own] + ups + downs] + [entire(weight)],
        [
            row_out(total, rows, width * size, bf16),
            row_out(total, rows, weight.shape[0], bf16),
        ],
        flops=2 * total * width * size * weight.shape[0],
        bytes_accessed=total * width * 2 * 11 + weight.size * 2 + total * weight.shape[0] * 4,
    )


def conv_kernel(
    width, place, plan, pre, halo, taps, bias, step_bias, scale, spread, conv_out, small, inputs, maps, fresh,
    extended,
):
    m = pl.program_id(0)
    rows = pre.shape[0]
    states = maps.shape[1] // 2
    taps_total = taps.shape[0]
    here = segment_of(column_position(rows, place), plan, place, m)
    same = [
        (segment_of(column_position(rows, place, tap + 1 - taps_total), plan, place, m) == here).astype(f32)
        for tap in range(taps_total)
    ]
    before = segment_of(place[2] - 1, plan, place, m)
    last = segment_of(place[2] + rows - 1, plan, place, m)

    step_pre = pre[:, width + 2 * states : width + 2 * states + LANES] + step_bias[...]
    rest = jnp.exp(-jnp.abs(step_pre))
    series = rest * (
        1.0 - rest * (1 / 2 - rest * (1 / 3 - rest * (1 / 4 - rest * (1 / 5 - rest * (1 / 6)))))
    )
    step = jnp.maximum(step_pre, 0.0) + jnp.where(rest < 0.03, series, jnp.log(1.0 + rest))
    row = lax.broadcasted_iota(jnp.int32, (rows, rows), 0)
    col = lax.broadcasted_iota(jnp.int32, (rows, rows), 1)
    lower = jnp.where(row >= col, 1.0, 0.0).astype(bf16)
    cumulative = dot_mask(lower, step * scale[...])
    small[:, :LANES] = cumulative
    small[:, LANES : 2 * LANES] = step
    small[:, 2 * LANES :] = step_pre
    ending = cumulative[rows - 1 :, :]
    fading = (here == last).astype(f32) * jnp.exp(ending - cumulative)
    through = (last == before).astype(f32) * jnp.exp(ending)
    step_parts, fading_parts = both_parts(step), both_parts(fading)
    through_parts = both_parts(jnp.broadcast_to(through, (STATE_PAD, LANES)))

    def conv(at):
        tile = slice(at, at + LANES)
        rows_before = extended.at[at // LANES % 2]
        own = pre[:, tile]
        rows_before[:HALO, :] = halo[0, :, tile]
        rows_before[HALO:, :] = own
        result = bias[:, tile] + taps[taps_total - 1 :, tile] * own
        for tap in range(taps_total - 1):
            start = HALO + tap + 1 - taps_total
            result = result + taps[tap : tap + 1, tile] * rows_before[start : start + rows, :] * same[tap]
        conv_out[:, tile] = result
        return result * jax.nn.sigmoid(result)

    for at in range(0, 2 * states, LANES):
        maps[:, at : at + LANES] = conv(width + at)
    input_map_t = maps[:, :states].T.astype(bf16)
    for at in range(0, width, LANES):
        tile = slice(at, at + LANES)
        values = conv(at) * dot(step_parts, spread[:, tile])
        inputs[:, tile] = values.astype(bf16)
        faded = (values * dot(fading_parts, spread[:, tile])).astype(bf16)
        fresh[0, :states, tile] = dot(input_map_t, faded).astype(bf16)
        fresh[0, states:, tile] = dot(through_parts, spread[:, tile]).astype(bf16)


def allowed_mask(rows, place, plan, m, transposed):
    column = segment_of(column_position(rows, place), plan, place, m)
    across = segment_of(row_position(rows, place), plan, place, m)
    row = lax.broadcasted_iota(jnp.int32, (rows, rows), 0)
    col = lax.broadcasted_iota(jnp.int32, (rows, rows), 1)
    order = (row <= col) if transposed else (row >= col)
    return jnp.where(order & (column == across), 0.0, -1e30)


def lane_select(parts, per):
    lane = lax.broadcasted_iota(jnp.int32, parts[0].shape, 1)
    result = parts[0]
    for at in range(1, per):
        result = jnp.where(lane >= at * (LANES // per), parts[at], result)
    return result


def mix_kernel(per, place, plan, small, maps, inputs, out):
    m = pl.program_id(0)
    rows, width = inputs.shape
    states = maps.shape[1] // 2
    cumulative = small[:, :LANES]
    flat = cumulative.T
    mask = allowed_mask(rows, place, plan, m, False)
    scores = dot_nt(maps[:, states:], maps[:, :states], highest)
    for at in range(0, width, LANES):
        tile = slice(at, at + LANES)
        for low in range(0, rows, LANES):
            end = low + LANES
            parts = []
            for sub in range(per):
                head = at // LANES * per + sub
                decay = jnp.exp(
                    (cumulative[low:end, head : head + 1] - flat[head : head + 1, :end])
                    + mask[low:end, :end]
                )
                mixing = (decay * scores[low:end, :end]).astype(bf16)
                parts.append(dot(mixing, inputs[:end, tile]))
            out[low:end, tile] = lane_select(parts, per)


def unmix_kernel(per, place, plan, small, maps, inputs, grads, grad_inputs, grad_maps, total):
    m = pl.program_id(0)
    rows, width = inputs.shape
    states = maps.shape[1] // 2
    cumulative = small[:, :LANES]
    flat = cumulative.T
    mask = allowed_mask(rows, place, plan, m, True)
    scores = dot_nt(maps[:, :states], maps[:, states:], highest)
    lane = lax.broadcasted_iota(jnp.int32, (LANES, LANES), 1)
    total[...] = jnp.zeros_like(total)
    for at in range(0, width, LANES):
        tile = slice(at, at + LANES)
        for low in range(0, rows, LANES):
            end = low + LANES
            later = grads[low:, tile]
            parts = []
            gathered_sum = total[low:end, low:]
            for sub in range(per):
                head = at // LANES * per + sub
                decay = jnp.exp(
                    (flat[head : head + 1, low:] - cumulative[low:end, head : head + 1])
                    + mask[low:end, low:]
                )
                mixing = (decay * scores[low:end, low:]).astype(bf16)
                parts.append(dot(mixing, later))
                inside = (lane // (LANES // per)) == sub
                own = jnp.where(inside, inputs[low:end, tile].astype(f32), 0.0).astype(bf16)
                gathered_sum = gathered_sum + decay * dot_nt(own, later)
            total[low:end, low:] = gathered_sum
            grad_inputs[low:end, tile] = lane_select(parts, per)
    grad_scores = total[...].astype(bf16)
    grad_maps[:, :states] = dot(grad_scores, maps[:, states:].astype(bf16))
    grad_maps[:, states:] = dot_tn(grad_scores, maps[:, :states].astype(bf16))


def inflow_of(cumulative, rows, place, plan, m):
    here = segment_of(column_position(rows, place), plan, place, m)
    before = segment_of(place[2] - 1, plan, place, m)
    return (here == before).astype(f32) * jnp.exp(cumulative)


def gated_kernel(
    place, plan, flags, small, maps, mixed, ahead, ahead_other, sibling, conv_out, gate, grad_y, gain, skip, spread, scanned, scaled_y, sums
):
    m = pl.program_id(0)
    rows, width = mixed.shape
    states = maps.shape[1] // 2
    inflow = both_parts(inflow_of(small[:, :LANES], rows, place, plan, m))
    output_map = maps[:, states:].astype(bf16)
    square = jnp.zeros((rows, LANES), f32)
    product = jnp.zeros((rows, LANES), f32)
    for at in range(0, width, LANES):
        tile = slice(at, at + LANES)
        entering = state_tile(states, flags, ahead, ahead_other, sibling, at)
        carried = dot(output_map, entering) * dot(inflow, spread[:, tile])
        scan = mixed[:, tile] + carried
        scanned[:, tile] = scan
        conv = conv_out[:, tile]
        gates = gate[:, tile].astype(f32)
        gated = (scan + skip[:, tile] * (conv * jax.nn.sigmoid(conv))) * (gates * jax.nn.sigmoid(gates))
        square = square + gated * gated
        scaled = gain[:, tile] * gated
        put_deal_rows(scaled_y, tile, scaled)
        product = product + grad_y[:, tile].astype(f32) * scaled
    ones = jnp.ones((HALO, LANES), f32)
    pick = lax.broadcasted_iota(jnp.int32, (HALO, rows), 0)
    sums[0] = jnp.where(pick == 0, dot_nt(ones, square, highest), dot_nt(ones, product, highest))


def ungated_kernel(
    inner_all, place, plan, small, maps, scanned, conv_out, gate, grad_y, sums, gain, skip, spread,
    normed_y_t, grads, grad_gate, local, row_part, grad_gain, grad_skip,
):
    m = pl.program_id(0)
    rows, width = scanned.shape
    states = maps.shape[1] // 2
    columns = columns_of(sums[0])
    inv = lax.rsqrt(columns[:, :1] / inner_all + epsilon)
    pull = inv * inv * inv * (columns[:, 1:2] / inner_all)
    cumulative = small[:, :LANES]
    inflow = both_parts(inflow_of(cumulative, rows, place, plan, m))
    before = segment_of(place[2] - 1, plan, place, m)
    last = segment_of(place[2] + rows - 1, plan, place, m)
    through = (last == before).astype(f32) * jnp.exp(cumulative[rows - 1 :, :])
    through_parts = both_parts(jnp.broadcast_to(through, (STATE_PAD, LANES)))
    output_map_t = maps[:, states:].T.astype(bf16)

    @pl.when(m == 0)
    def _():
        grad_gain[...] = jnp.zeros_like(grad_gain)
        grad_skip[...] = jnp.zeros_like(grad_skip)

    product = jnp.zeros((rows, LANES), f32)
    for at in range(0, width, LANES):
        tile = slice(at, at + LANES)
        conv = conv_out[:, tile]
        heads_x = conv * jax.nn.sigmoid(conv)
        mixer = scanned[:, tile] + skip[:, tile] * heads_x
        gates = gate[:, tile].astype(f32)
        logistic = jax.nn.sigmoid(gates)
        act = gates * logistic
        gated = mixer * act
        normed = gated * inv
        normed_y_t[tile, :] = (normed * gain[:, tile]).astype(bf16).T
        grad = grad_y[:, tile].astype(f32)
        grad_gain[:, tile] += jnp.sum(grad * normed, axis=0, keepdims=True)
        grad_gated = inv * (grad * gain[:, tile]) - gated * pull
        grad_mixer = grad_gated * act
        grads[:, tile] = grad_mixer.astype(bf16)
        grad_skip[:, tile] += jnp.sum(grad_mixer * heads_x, axis=0, keepdims=True)
        grad_gates = grad_gated * mixer * (logistic * (1.0 + gates * (1.0 - logistic)))
        grad_gate[:, tile] = grad_gates.astype(bf16)
        product = product + grad_gates * gates
        weighted = (grad_mixer * dot(inflow, spread[:, tile])).astype(bf16)
        local[0, :states, tile] = dot(output_map_t, weighted).astype(bf16)
        local[0, states:, tile] = dot(through_parts, spread[:, tile]).astype(bf16)
    row_part[0] = dot_nt(jnp.ones((HALO, LANES), f32), product, highest)


def unscan_kernel(
    place, plan, flags, flags_back, small, maps, scanned, conv_out, inputs, grads, grad_inputs, grad_maps,
    ahead, ahead_other, sibling, back, back_other, back_sibling, skip, scale, spread, grad_conv_out, grad_step, grad_bias, grad_heads,
):
    m = pl.program_id(0)
    rows, width = scanned.shape
    states = maps.shape[1] // 2
    cumulative, step, pre = (small[:, k * LANES : (k + 1) * LANES] for k in range(3))
    here = segment_of(column_position(rows, place), plan, place, m)
    before = segment_of(place[2] - 1, plan, place, m)
    last = segment_of(place[2] + rows - 1, plan, place, m)
    ending = cumulative[rows - 1 :, :]
    fading = both_parts((here == last).astype(f32) * jnp.exp(ending - cumulative))
    inflow = both_parts((here == before).astype(f32) * jnp.exp(cumulative))
    through = (last == before).astype(f32) * jnp.exp(ending)
    step_parts = both_parts(step)
    input_map = maps[:, :states].astype(bf16)

    @pl.when(m == 0)
    def _():
        grad_bias[...] = jnp.zeros_like(grad_bias)
        grad_heads[...] = jnp.zeros_like(grad_heads)

    grad_in, grad_out = grad_maps[:, :states], grad_maps[:, states:]
    grad_cum = jnp.zeros((rows, LANES), f32)
    grad_own = jnp.zeros((rows, LANES), f32)
    ends = jnp.zeros((HALO, LANES), f32)
    for at in range(0, width, LANES):
        tile = slice(at, at + LANES)
        spread_tile = spread[:, tile]
        leave = state_tile(states, flags_back, back, back_other, back_sibling, at)
        enter = state_tile(states, flags, ahead, ahead_other, sibling, at)
        fade = dot(fading, spread_tile)
        pulled = fade * dot(input_map, leave)
        values = inputs[:, tile].astype(f32)
        grad = grads[:, tile].astype(f32)
        total = grad_inputs[:, tile] + pulled
        faded = (values * fade).astype(bf16)
        weighted = (grad * dot(inflow, spread_tile)).astype(bf16)
        grad_in = grad_in + dot_nt(faded, leave)
        grad_out = grad_out + dot_nt(weighted, enter)
        conv = conv_out[:, tile]
        logistic = jax.nn.sigmoid(conv)
        heads_x = conv * logistic
        first = both_parts(grad * scanned[:, tile] - values * total)
        second = both_parts(total * heads_x)
        twice = jnp.concatenate([spread[:LANES, tile]] * 2, axis=1)
        grad_cum = grad_cum + dot_nt(first, twice)
        grad_own = grad_own + dot_nt(second, twice)
        fade_sum = jnp.sum(values * pulled, axis=0, keepdims=True)
        through_sum = jnp.sum(leave.astype(f32) * enter.astype(f32), axis=0, keepdims=True)
        pick = lax.broadcasted_iota(jnp.int32, (HALO, LANES), 0)
        edge = both_parts(jnp.where(pick == 0, fade_sum, through_sum))
        ends = ends + dot_nt(edge, twice)
        grad_x = total * dot(step_parts, spread_tile) + skip[:, tile] * grad
        result = grad_x * (logistic * (1.0 + conv * (1.0 - logistic)))
        grad_conv_out[:, tile] = result
        grad_bias[:, tile] += jnp.sum(result, axis=0, keepdims=True)
    for values, start in ((grad_in, width), (grad_out, width + states)):
        conv = conv_out[:, start : start + states]
        result = values * silu_slope(conv)
        grad_conv_out[:, start : start + states] = result
        grad_bias[:, start : start + states] += jnp.sum(result, axis=0, keepdims=True)
    row = lax.broadcasted_iota(jnp.int32, (rows, rows), 0)
    col = lax.broadcasted_iota(jnp.int32, (rows, rows), 1)
    upper = jnp.where(row <= col, 1.0, 0.0).astype(bf16)
    grad_rate = dot_mask(upper, grad_cum) + (ends[:1] + through * ends[1:2])
    rate = step * scale[...]
    grad_pre = (grad_rate * scale[...] + grad_own) * jax.nn.sigmoid(pre)
    grad_step[...] = grad_pre
    grad_heads[0:1, :] += jnp.sum(grad_rate * rate, axis=0, keepdims=True)
    grad_heads[1:2, :] += jnp.sum(grad_pre, axis=0, keepdims=True)


def unconv_kernel(
    place, plan, pre, halo, grad_out, after_rows, grad_step, row_part, taps, grad_pre, grad_state, row_sums,
    grad_taps, extended, extended_grad,
):
    m = pl.program_id(0)
    rows = pre.shape[0]
    channels = grad_out.shape[1]
    taps_total = taps.shape[0]
    here = segment_of(column_position(rows, place), plan, place, m)
    behind, ahead = [], []
    for tap in range(taps_total):
        lag = taps_total - 1 - tap
        behind.append((segment_of(column_position(rows, place, -lag), plan, place, m) == here).astype(f32))
        ahead.append((segment_of(column_position(rows, place, lag), plan, place, m) == here).astype(f32))

    @pl.when(m == 0)
    def _():
        grad_taps[...] = jnp.zeros_like(grad_taps)

    total = jnp.zeros((rows, LANES), f32)
    for at in range(0, channels, LANES):
        tile = slice(at, at + LANES)
        rows_before, rows_after = extended.at[at // LANES % 2], extended_grad.at[at // LANES % 2]
        own, grad = pre[:, tile], grad_out[:, tile]
        rows_before[:HALO, :] = halo[0, :, tile]
        rows_before[HALO:, :] = own
        rows_after[:rows, :] = grad
        rows_after[rows:, :] = after_rows[0, :, tile]
        last = taps_total - 1
        result = taps[last:, tile] * grad
        grad_taps[last:, tile] += jnp.sum(grad * own, axis=0, keepdims=True)
        for tap in range(last):
            lag = last - tap
            result = result + taps[tap : tap + 1, tile] * rows_after[lag : lag + rows, :] * ahead[tap]
            begin = HALO - lag
            product = grad * rows_before[begin : begin + rows, :] * behind[tap]
            grad_taps[tap : tap + 1, tile] += jnp.sum(product, axis=0, keepdims=True)
        grad_pre[:, tile] = result.astype(bf16)
        total = total + result * own
    grad_pre[:, channels:] = grad_step[...].astype(bf16)
    grad_state[...] = grad_pre[:, channels - grad_state.shape[1] : channels]
    total = total + grad_step[...] * pre[:, channels : channels + LANES]
    row_sums[0] = row_part[0] + dot_nt(jnp.ones((HALO, LANES), f32), total, highest)


def rows_kernel(quarters, first, second, *refs):
    for weight, out in zip(refs[:quarters], refs[quarters:]):
        cut = weight.shape[1] - second.shape[1]
        result = dot_nt(first[...], weight[:, : first.shape[1]]) + dot_nt(second[...], weight[:, cut:])
        put_deal_rows(out.at[0], slice(None), result)


def rows_gradient(first, second, weight, senders, count, edges):
    total = first.shape[0]
    size = lax.axis_size("head")
    width = weight.shape[0] // size
    rows = total // count
    flops = total * (first.shape[1] + second.shape[1]) * width * size
    moved = weight.size + (first.size + second.size) * size
    block = (1, senders, 1, rows // senders, width)
    if edges:
        shape = (1, senders, count, rows // senders, width)
        return call(
            functools.partial(rows_kernel, 2), (count,), (),
            [per_row(first, rows), per_row(second, rows)]
            + [(weight, (width, weight.shape[1]), lambda m, at=at: (at, 0)) for at in (0, size - 1)],
            [(shape, bf16, block, lambda m: (0, 0, m, 0, 0))] * 2, flops=flops, bytes_accessed=moved,
        )
    row_block = lambda array: (array, (rows, array.shape[1]), lambda q, m: (m, 0))
    return call(
        functools.partial(rows_kernel, 1), (size - 2, count), (),
        [row_block(first), row_block(second), (weight, (width, weight.shape[1]), lambda q, m: (q + 1, 0))],
        [
            (
                (size - 2, senders, count, rows // senders, width), bf16, block,
                lambda q, m: (q, 0, m, 0, 0),
            )
        ],
        flops=flops, bytes_accessed=moved,
    )[0]


def output_kernel(inner_all, tokens, branch, sums, out):
    inv = lax.rsqrt(columns_of(sums[0])[:, :1] / inner_all + epsilon)
    every = slice(None)
    put_deal_rows(out, every, deal_rows(tokens, every) + deal_rows(branch, every) * inv)


def input_kernel(
    size, place, low, high, middle, up, down, tokens, cot, inverse, sums, gain, out, grad_gain
):
    every = slice(None)
    here = place[0]
    width = tokens.shape[3]
    own = jnp.where(
        here == 0,
        deal_rows(low.at[0], every),
        jnp.where(here == size - 1, deal_rows(high.at[0], every), deal_rows(middle.at[0], every)),
    )
    rows_own = own + deal_rows(up, every) + deal_rows(down, every)
    inv = deal_rows(inverse, every)
    unit = deal_rows(tokens, every) * inv
    own_gain = gain[:, pl.ds(pl.multiple_of(here * width, width), width)]
    total = columns_of(sums[0])[:, :1] / (width * size)
    put_deal_rows(out, every, inv * (rows_own * own_gain - unit * total) + deal_rows(cot, every))
    product = jnp.sum(rows_own * unit, axis=0, keepdims=True)

    @pl.when(pl.program_id(0) == 0)
    def _():
        grad_gain[...] = product

    @pl.when(pl.program_id(0) > 0)
    def _():
        grad_gain[...] += product


def out_kernel(left, right, out):
    out[...] = dot(left[...], right[...]).astype(bf16)


def sent_kernel(columns, count, left, *refs):
    rights, out = refs[:count], refs[count]
    for which, source, target, size in columns:
        out[:, target : target + size] = dot(left[...], rights[which][:, source : source + size]).astype(bf16)


def kept_kernel(columns, count, cut, left, *refs):
    rights, other, outs = refs[:count], refs[count], refs[count + 1 :]
    step = pl.program_id(0)
    high, odd = step >= pl.num_programs(0) // 2, lax.rem(step, 2) == 1
    for which, source, target, size in columns:
        result = dot(left[...], rights[which][:, source : source + size])
        result = (result + other[:, target : target + size].astype(f32)).astype(bf16)
        if target < cut:
            keep, send, sending, start = outs[0], outs[1], high, target
        else:
            keep, send, sending, start = outs[2], outs[3], odd, target - cut
        tile = slice(start, start + size)

        @pl.when(sending)
        def _():
            send[:, tile] = result

        @pl.when(jnp.logical_not(sending))
        def _():
            keep[:, tile] = result


def total_kernel(targets, *refs):
    ins, outs = refs[:2], refs[2:]
    for out, (which, source, target, size) in zip([outs[t[0]] for t in targets], [t[1] for t in targets]):
        tile = slice(source, source + size)
        out[:, target : target + size] = ins[which][:, tile].astype(f32)


def weight_gradient_sent(odd_t, rights, columns, depth):
    total = odd_t.shape[1]
    width = max(target + size for _, _, target, size in columns)
    (sent,) = call(
        functools.partial(sent_kernel, columns, len(rights)), (odd_t.shape[0] // depth,), (),
        [(odd_t, (depth, total), lambda l: (l, 0))] + [entire(right) for right in rights],
        [((odd_t.shape[0], width), bf16, (depth, width), lambda l: (l, 0))],
        flops=2 * odd_t.shape[0] * total * width,
        bytes_accessed=odd_t.shape[0] * (total + width) * 2 + sum(right.size for right in rights) * 2,
    )
    return sent


def weight_gradient_kept(even_t, got, rights, columns, cut, depth):
    blocks = even_t.shape[0] // depth
    total = even_t.shape[1]
    width = got.shape[1]
    top = blocks // 2
    rows = even_t.shape[0] // 2
    half = lambda size, index: ((rows, size), bf16, (depth, size), index)
    return call(
        functools.partial(kept_kernel, columns, len(rights), cut), (blocks,), (),
        [(even_t, (depth, total), lambda l: (l, 0))] + [entire(right) for right in rights]
        + [(got, (depth, width), lambda l: (l, 0))],
        [
            half(cut, lambda l: (jnp.minimum(l, top - 1), 0)),
            half(cut, lambda l: (jnp.maximum(l - top, 0), 0)),
            half(width - cut, lambda l: (l // 2, 0)),
            half(width - cut, lambda l: (l // 2, 0)),
        ],
        flops=2 * even_t.shape[0] * total * width,
        bytes_accessed=even_t.shape[0] * (total + width) * 2 + sum(right.size for right in rights) * 2,
    )


def weight_gradient_parts(mine):
    links = axis_bits("seq")[1:]
    labels = [bit << 1 for bit in range(2 ** len(links))]
    return [
        Scattered(mine[0], mine[1], [x for x in labels if not x & links[-1]], links[::-1]),
        Scattered(mine[2], mine[3], [x for x in labels if not x & links[0]], links),
    ]


def weight_gradient_total(parts, results, depth):
    ins = [array for part in parts for array in part.finish()]
    targets = [(at, column) for at, (_, columns) in enumerate(results) for column in columns]
    return call(
        functools.partial(total_kernel, targets), (1,), (), [entire(a) for a in ins],
        [((depth, size), f32, (depth, size), lambda *_: (0, 0)) for size, _ in results],
        bytes_accessed=sum(a.size for a in ins) * 6,
    )


def per_device(
    tokens,
    cotangent,
    lengths,
    deal_order,
    norm_gain,
    proj_gate,
    proj_inner,
    proj_state,
    proj_step,
    conv_inner,
    conv_inner_bias,
    conv_state,
    conv_state_bias,
    step_bias,
    decay_log,
    skip_gain,
    inner_gain,
    proj_out,
):
    batch_count = lengths.shape[0]
    rows_local, width_own = tokens.shape
    tok_dev = rows_local // batch_count
    seq_index = lax.axis_index("seq")
    head_index = lax.axis_index("head")
    seq_size = lax.axis_size("seq")
    head_size = lax.axis_size("head")
    heads_own = proj_step.shape[1]
    inner_own = proj_inner.shape[1]
    head_width = inner_own // heads_own
    states = proj_state.shape[1] // 2
    taps_total = conv_inner.shape[0]
    width_all = width_own * head_size
    inner_all = inner_own * head_size
    depth = width_all // seq_size
    channels = inner_own + 2 * states
    per = LANES // head_width
    rows = tok_dev
    grid = (batch_count,)

    place = jnp.stack(
        [head_index, seq_index, seq_index * tok_dev, jnp.int32(tok_dev * seq_size)]
    ).astype(jnp.int32)
    plan = (jnp.cumsum(lengths, axis=1) - lengths).astype(jnp.int32)
    scalars = (place, plan)

    piece = tok_dev // seq_size
    dealt_row = deal_order.reshape(batch_count, seq_size, piece) + (
        jnp.arange(batch_count, dtype=jnp.int32) * tok_dev
    )[:, None, None]
    picks = (
        jnp.transpose(dealt_row, (1, 0, 2)).reshape(rows_local, 1) == jnp.arange(rows_local)[None, :]
    ).astype(bf16)
    deal_shape = (seq_size, batch_count, piece, width_own)

    def dealt(values):
        values = dot(picks, values).astype(bf16).reshape(seq_size, batch_count * piece, width_own)
        values = lax.all_to_all(values, "seq", split_axis=0, concat_axis=0, tiled=True)
        return values.reshape(deal_shape)

    def sent_back(values):
        values = values.reshape(seq_size, -1, width_own)
        return lax.all_to_all(values, "seq", split_axis=0, concat_axis=0, tiled=True)

    def put_back(values):
        return dot_tn(picks, values.reshape(rows_local, width_own)).astype(bf16)

    deal_tokens = dealt(tokens)
    lines = LineGather(deal_tokens)
    lines.advance()
    deal_cot = dealt(cotangent)

    full_in = lax.all_gather(
        jnp.concatenate(
            [proj_inner, proj_state, jnp.pad(proj_step, ((0, 0), (0, 2 * LANES - heads_own))), proj_gate],
            axis=1,
        ),
        "seq", axis=0, tiled=True,
    )
    full_out = lax.all_gather(after(proj_out, lines.up, lines.down), "seq", axis=1, tiled=True)

    lines = lines.finish()
    normed, even_t, odd_t, own_t, inv_rms = all_features(deal_tokens, lines, place, norm_gain[None, :], depth)
    cot_lines = LineGather(after(deal_cot, lines[0][-1], lines[1][-1]))

    taps = jnp.concatenate([conv_inner, conv_state], axis=1)
    bias = jnp.concatenate([conv_inner_bias, conv_state_bias])[None, :]
    pad = LANES - heads_own
    step_bias_row = jnp.pad(step_bias, (0, pad))[None, :]
    scale = jnp.pad(-jnp.exp(decay_log), (0, pad))[None, :]
    spread = (
        jnp.arange(2 * LANES)[:, None] % LANES == jnp.arange(inner_own)[None, :] // head_width
    ).astype(bf16)
    skip = jnp.repeat(skip_gain, head_width)[None, :]
    gain = inner_gain[None, :]

    pre_width = channels + 2 * LANES
    (pre,) = cot_lines.advance(dot(normed, full_in[:, :pre_width]))
    halo = passed_along(pre.reshape(batch_count, tok_dev, -1)[:, tok_dev - HALO :], "seq", 1)
    gate = dot(normed, full_in[:, pre_width:]).astype(bf16)
    halo, gate = lax.optimization_barrier((halo, gate))
    conv_out, small, inputs, maps, fresh = call(
        functools.partial(conv_kernel, inner_own), grid, scalars,
        [per_row(pre, rows), per_step(halo)]
        + [entire(a) for a in (taps, bias, step_bias_row, scale, spread)],
        [
            row_out(rows_local, rows, channels, f32),
            row_out(rows_local, rows, 3 * LANES, f32),
            row_out(rows_local, rows, inner_own, bf16),
            row_out(rows_local, rows, 2 * states, f32),
            step_out(batch_count, (states + STATE_PAD, inner_own), bf16),
        ],
        scratch=[pltpu.VMEM((2, rows + HALO, LANES), f32)],
        flops=rows_local * inner_own * 2000, bytes_accessed=rows_local * inner_own * 20,
    )
    conv_out, small, inputs, maps, fresh = cot_lines.advance(conv_out, small, inputs, maps, fresh)
    scan_ins = [per_row(small, rows), per_row(maps, rows)]
    (mixed,) = call(
        functools.partial(mix_kernel, per), grid, scalars, scan_ins + [per_row(inputs, rows)],
        [row_out(rows_local, rows, inner_own, f32)],
        flops=rows_local * inner_own * 2500, bytes_accessed=rows_local * inner_own * 6,
    )
    cot_lines.advance()

    entering, mixed, (flat_cot, grad_y) = scan_before(
        fresh, states, False,
        [lambda: mixed, lambda _: cotangent_products(deal_cot, cot_lines.finish(), place, full_out)],
    )
    vectors = [entire(gain), entire(skip), entire(spread)]
    scanned, scaled_y, sums = call(
        gated_kernel, grid, scalars + entering[:1],
        scan_ins
        + [per_row(mixed, rows)] + [per_step(a) for a in entering[1:]]
        + [per_row(conv_out, rows), per_row(gate, rows)]
        + [per_row(grad_y, rows)] + vectors,
        [
            row_out(rows_local, rows, inner_own, f32),
            deal_out(seq_size, batch_count, piece, inner_own, bf16),
            step_out(batch_count, (HALO, rows), f32),
        ],
        flops=rows_local * inner_own * 1500, bytes_accessed=rows_local * inner_own * 8,
    )
    out_rows = dot(scaled_y.reshape(rows_local, inner_own), full_out).astype(bf16)
    sums = sums + swapped(sums, "head", 1)
    for bit in axis_bits("head")[1:]:
        other, out_rows = lax.optimization_barrier((swapped(sums, "head", bit), out_rows))
        sums = sums + other
    branch = lax.psum_scatter(
        out_rows.reshape(deal_shape[:3] + (width_all,)), "head", scatter_dimension=3, tiled=True
    )

    normed_y_t, grads, grad_gate, local, row_part, grad_gain, grad_skip = call(
        functools.partial(ungated_kernel, inner_all), grid, scalars,
        scan_ins
        + [per_row(array, rows) for array in (scanned, conv_out, gate, grad_y)]
        + [per_step(sums)] + vectors,
        [((inner_own, rows_local), bf16, (inner_own, rows), lambda m, *_: (0, m))]
        + [row_out(rows_local, rows, inner_own, bf16)] * 2
        + [step_out(batch_count, (states + STATE_PAD, inner_own), bf16)]
        + [step_out(batch_count, (HALO, rows), f32)]
        + [sum_out((1, inner_own))] * 2,
        flops=rows_local * inner_own * 2000, bytes_accessed=rows_local * inner_own * 24,
    )
    grad_inputs, grad_maps = call(
        functools.partial(unmix_kernel, per), grid, scalars,
        scan_ins + [per_row(inputs, rows), per_row(grads, rows)],
        [row_out(rows_local, rows, inner_own, f32), row_out(rows_local, rows, 2 * states, f32)],
        scratch=[pltpu.VMEM((rows, rows), f32)],
        flops=rows_local * inner_own * 4000, bytes_accessed=rows_local * inner_own * 8,
    )
    (grad_out,) = call(
        out_kernel, (head_size,), (),
        [entire(normed_y_t), (flat_cot, (rows_local, width_own), lambda q: (0, q))],
        [((inner_own, width_all), bf16, (inner_own, width_own), lambda q: (0, q))],
        flops=2 * rows_local * inner_own * width_all, bytes_accessed=rows_local * width_all * 6,
    )
    leaving, grad_inputs, grad_out = scan_before(
        local, states, True, [lambda: grad_inputs, lambda _: grad_out]
    )

    grad_out = lax.psum_scatter(grad_out, "seq", scatter_dimension=1, tiled=True)
    grad_conv_out, grad_step, grad_bias, grad_heads = call(
        unscan_kernel, grid, scalars + entering[:1] + leaving[:1],
        scan_ins
        + [per_row(a, rows) for a in (scanned, conv_out, inputs, grads)]
        + [per_row(grad_inputs, rows), per_row(grad_maps, rows)]
        + [per_step(a) for a in entering[1:] + leaving[1:]] + [entire(skip), entire(scale), entire(spread)],
        [
            row_out(rows_local, rows, channels, f32),
            row_out(rows_local, rows, LANES, f32),
            sum_out((1, channels)),
            sum_out((HALO, LANES)),
        ],
        flops=rows_local * inner_own * 4000, bytes_accessed=rows_local * inner_own * 28,
    )
    after_rows = passed_along(grad_conv_out.reshape(batch_count, tok_dev, channels)[:, :HALO], "seq", -1)
    after_rows, branch = lax.optimization_barrier((after_rows, branch))
    grad_pre, grad_state, row_dots, grad_taps = call(
        unconv_kernel, grid, scalars,
        [per_row(pre, rows), per_step(halo), per_row(grad_conv_out, rows), per_step(after_rows)]
        + [per_row(grad_step, rows), per_step(row_part), entire(taps)],
        [
            row_out(rows_local, rows, channels + LANES, bf16),
            row_out(rows_local, rows, 2 * states, bf16),
            step_out(batch_count, (HALO, rows), f32),
            sum_out((taps_total, channels)),
        ],
        scratch=[pltpu.VMEM((2, rows + HALO, LANES), f32)] * 2,
        flops=rows_local * inner_own * 100, bytes_accessed=rows_local * inner_own * 14,
    )
    columns = [
        (0, 0, 0, inner_own), (1, 0, inner_own, inner_own), (0, channels, 2 * inner_own, LANES)
    ]
    fill = lambda row: jnp.pad(row, ((0, 0), (0, channels - row.shape[1])))
    state_small = jnp.concatenate([grad_taps[:, inner_own:], grad_bias[:, inner_own:]])
    row_dots = jnp.concatenate([row_dots[:, 0, :], state_small.reshape(-1, rows)])
    packed = jnp.concatenate(
        [grad_taps, grad_bias, fill(grad_gain), fill(grad_skip), fill(grad_heads[:2].reshape(1, 2 * LANES))]
    )
    packed = packed + swapped(packed, "seq", 1)
    seq_bits, head_bits = axis_bits("seq"), axis_bits("head")
    sent = weight_gradient_sent(odd_t, [grad_pre, grad_gate], columns, depth)
    others = [
        swapped(row_dots, "head", head_bits[0]), swapped(packed, "seq", seq_bits[1]),
        swapped(grad_state, "head", head_bits[0]),
    ]
    others, sent = lax.optimization_barrier((others, sent))
    row_dots, packed, grad_state = row_dots + others[0], packed + others[1], added(grad_state, others[2])
    got = swapped(sent, "seq", 1)
    grad_rows = lambda first, edges: rows_gradient(
        first, grad_gate, full_in, seq_size, batch_count, edges
    )
    low, high = grad_rows(after(grad_pre, sent), True)
    other, low, high = lax.optimization_barrier((swapped(packed, "seq", seq_bits[2]), low, high))
    packed = packed + other
    for bit in seq_bits[3:]:
        packed = packed + swapped(packed, "seq", bit)
    rows_line = LineScatter([low[0], high[0]])
    mine = weight_gradient_kept(even_t, after(got, low), [grad_pre, grad_gate], columns, inner_own, depth)
    rows_line.middle = grad_rows(after(grad_pre, mine[0]), False)
    others = [swapped(row_dots, "head", head_bits[1]), swapped(grad_state, "head", head_bits[1])]
    *mine, rows_line.middle, branch, grad_out, others = rows_line.advance(
        *mine, rows_line.middle, branch, grad_out, others
    )
    row_dots, grad_state = row_dots + others[0], added(grad_state, others[1])
    for bit in head_bits[2:]:
        row_dots = row_dots + swapped(row_dots, "head", bit)
        grad_state = added(grad_state, swapped(grad_state, "head", bit))
    (grad_w_state,) = call(
        out_kernel, (1,), (), [entire(own_t), entire(grad_state)], [sum_out((width_own, 2 * states), bf16)],
        flops=2 * rows_local * width_own * 2 * states, bytes_accessed=rows_local * (width_own + 2 * states) * 2,
    )
    state_small = row_dots[batch_count:].reshape(-1, 2 * states).astype(bf16)
    row_dots = row_dots[:batch_count, None, :]
    pad_rows = -state_small.shape[0] % 16
    grad_w_state = jnp.concatenate([grad_w_state, jnp.pad(state_small, ((0, pad_rows), (0, 0)))])
    grad_w_state = added(grad_w_state, swapped(grad_w_state, "seq", 1))
    parts = weight_gradient_parts(mine)
    for part in parts:
        part.send()
    (grad_w_state,) = rows_line.advance(grad_w_state)
    other = swapped(grad_w_state, "seq", seq_bits[1])
    (out_rows,) = call(
        functools.partial(output_kernel, inner_all), grid, (),
        [per_deal(deal_tokens), per_deal(branch), per_step(sums)],
        [deal_out(seq_size, batch_count, piece, width_own, bf16)],
        bytes_accessed=rows_local * width_own * 6,
    )
    out_rows = sent_back(out_rows)
    for part in parts:
        part.receive()
    *pairs, out_rows = rows_line.advance(*[part.pair for part in parts], out_rows)
    for part, pair in zip(parts, pairs):
        part.pair = pair
        part.send()
    up, down = rows_line.finish()
    middle = rows_line.middle
    grad_rows_in, grad_norm_gain = call(
        functools.partial(input_kernel, head_size), grid, (place,),
        [per_deal_of(low), per_deal_of(high)]
        + [
            (
                middle, (1, seq_size, 1, piece, width_own),
                lambda m, place: (jnp.clip(place[0] - 1, 0, head_size - 3), 0, m, 0, 0),
            )
        ]
        + [per_deal(a) for a in (up, down, deal_tokens, deal_cot, inv_rms)]
        + [per_step(row_dots), entire(norm_gain[None, :])],
        [deal_out(seq_size, batch_count, piece, width_own, bf16), sum_out((1, width_own))],
        bytes_accessed=rows_local * width_own * 16,
    )
    grad_out = after(grad_out, grad_rows_in).astype(f32)
    parts[0].got, parts[1].got, other = after_all((parts[0].got, parts[1].got, other), (grad_rows_in,))
    grad_w_state = added(grad_w_state, other)
    grad_w_state = added(grad_w_state, swapped(grad_w_state, "seq", seq_bits[2]))
    for part in parts:
        part.receive()
        while part.left:
            part.send()
            part.receive()
    grad_inner, grad_w_gate, grad_w_step = weight_gradient_total(
        parts,
        [
            (inner_own, [(0, 0, 0, inner_own)]),
            (inner_own, [(1, 0, 0, inner_own)]),
            (LANES, [(1, inner_own, 0, LANES)]),
        ],
        depth,
    )
    for bit in seq_bits[3:]:
        grad_w_state = added(grad_w_state, swapped(grad_w_state, "seq", bit))
    out_back = put_back(out_rows)
    grad_w_state = grad_w_state.astype(f32)
    state_sums = grad_w_state[width_own : width_own + taps_total + 1]
    gain_high = grad_norm_gain.astype(bf16)
    gain_low = (grad_norm_gain - gain_high.astype(f32)).astype(bf16)
    gain_rows = jnp.pad(jnp.concatenate([gain_high, gain_low]), ((0, HALO - 2), (0, 0)))
    own_rows = batch_count * piece
    grad_back = sent_back(
        jnp.concatenate(
            [
                grad_rows_in.reshape(seq_size, own_rows, width_own),
                jnp.broadcast_to(gain_rows, (seq_size, HALO, width_own)),
            ],
            axis=1,
        )
    )
    grad_norm_gain = jnp.sum(grad_back[:, own_rows : own_rows + 2].astype(f32), axis=(0, 1))
    grad_back = put_back(grad_back[:, :own_rows])
    state_own = 2 * states // head_size
    state_sums = lax.dynamic_slice_in_dim(state_sums, head_index * state_own, state_own, 1)
    return (
        out_back,
        grad_back,
        grad_norm_gain,
        grad_w_gate,
        grad_inner,
        grad_w_state[:width_own],
        grad_w_step[:, :heads_own],
        packed[:taps_total, :inner_own],
        packed[taps_total, :inner_own],
        state_sums[:taps_total],
        state_sums[taps_total],
        packed[taps_total + 3, LANES : LANES + heads_own],
        packed[taps_total + 3, :heads_own],
        jnp.sum(packed[taps_total + 2, :inner_own].reshape(heads_own, head_width), axis=1),
        packed[taps_total + 1, :inner_own],
        grad_out,
    )


def solution(mesh):
    return jax.shard_map(
        per_device,
        mesh=mesh,
        in_specs=(
            P("seq", "head"),
            P("seq", "head"),
            P(),
            P("seq"),
            P(),
            P("seq", "head"),
            P("seq", "head"),
            P("seq", None),
            P("seq", "head"),
            P(None, "head"),
            P("head"),
            P(),
            P(),
            P("head"),
            P("head"),
            P("head"),
            P("head"),
            P("head", "seq"),
        ),
        out_specs=(
            P("seq", "head"),
            P("seq", "head"),
            P("head"),
            P("seq", "head"),
            P("seq", "head"),
            P("head", None),
            P("seq", "head"),
            P(None, "head"),
            P("head"),
            P(None, "head"),
            P("head"),
            P("head"),
            P("head"),
            P("head"),
            P("head"),
            P("head", "seq"),
        ),
        check_vma=False,
    )
```
